32 devices in a mesh: dp: 16 (over z, y, x), mp: 2 (over core).
Axes of the slice: x: 2, y: 2, z: 4, core: 2. Of those that a mesh axis runs over, the one named last changes fastest.
Arguments:
- tokens: bfloat16 [32768, 768], P(('dp', 'mp')), may hold values from -7.2 to 7.2
- cotangent: bfloat16 [32768, 768], P(('dp', 'mp')), may hold values from -6 to 6
- seg_lengths: int32 [64, 8], P('dp'), may hold values from 1 to 256, 480 in all within a row
- w_qkv: float32 [768, 3, 768], P('dp', None, 'mp'), may hold values from -0.21875 to 0.21875
- w_out: float32 [768, 768], P(('mp', 'dp')), may hold values from -0.625 to 0.625
- w_up: float32 [768, 3072], P('dp', 'mp'), may hold values from -0.21875 to 0.21875
- w_down: float32 [3072, 768], P(('mp', 'dp')), may hold values from -0.109375 to 0.109375
- head_bias: float32 [2, 768], P(None, ('mp', 'dp')), may hold values from -1 to 1
- ffn_bias: float32 [3072], P(('mp', 'dp')), may hold values from -1 to 1
- norm_bias: float32 [6, 768], P(None, ('dp', 'mp')), may hold values from -1 to 3
- qkv_rows: float32 [768], P('dp'), may hold values from 1474.56 to 23592.96
- qkv_cols: float32 [3, 768], P(None, 'mp'), may hold values from 2949.12 to 11796.48
- out_rows: float32 [768], P(('mp', 'dp')), may hold values from 1474.56 to 23592.96
- out_cols: float32 [768], replicated, may hold values from 2949.12 to 11796.48
- up_rows: float32 [768], P('dp'), may hold values from 1966.08 to 31457.28
- up_cols: float32 [3072], P('mp'), may hold values from 3932.16 to 15728.64
- down_rows: float32 [3072], P(('mp', 'dp')), may hold values from 5898.24 to 94371.84
- down_cols: float32 [768], replicated, may hold values from 11796.48 to 47185.92
- head_bias_sq: float32 [2, 768], P(None, ('mp', 'dp')), may hold values from 655.36 to 6553.6
- ffn_bias_sq: float32 [3072], P(('mp', 'dp')), may hold values from 2949.12 to 11796.48
- norm_sq: float32 [6, 768], P(None, ('dp', 'mp')), may hold values from 16384 to 131072
Outputs:
- layer_out: bfloat16 [32768, 768], P(('dp', 'mp'))
- pooled: float32 [64, 8, 768], P(('dp', 'mp'))
- input_grad: float32 [32768, 768], P(('dp', 'mp'))
- qkv_grad: float32 [768, 3, 768], P('dp', None, 'mp')
- out_grad: float32 [768, 768], P(('mp', 'dp'))
- up_grad: float32 [768, 3072], P('dp', 'mp')
- down_grad: float32 [3072, 768], P(('mp', 'dp'))
- head_bias_grad: float32 [2, 768], P(None, ('mp', 'dp'))
- ffn_bias_grad: float32 [3072], P(('mp', 'dp'))
- norm_grad: float32 [6, 768], P(None, ('dp', 'mp'))
- qkv_rows_new: float32 [768], P('dp')
- qkv_cols_new: float32 [3, 768], P(None, 'mp')
- out_rows_new: float32 [768], P(('mp', 'dp'))
- out_cols_new: float32 [768], replicated
- up_rows_new: float32 [768], P('dp')
- up_cols_new: float32 [3072], P('mp')
- down_rows_new: float32 [3072], P(('mp', 'dp'))
- down_cols_new: float32 [768], replicated
- head_bias_sq_new: float32 [2, 768], P(None, ('mp', 'dp'))
- ffn_bias_sq_new: float32 [3072], P(('mp', 'dp'))
- norm_sq_new: float32 [6, 768], P(None, ('dp', 'mp'))
- qkv_new: float32 [768, 3, 768], P('dp', None, 'mp')
- out_new: float32 [768, 768], P(('mp', 'dp'))
- up_new: float32 [768, 3072], P('dp', 'mp')
- down_new: float32 [3072, 768], P(('mp', 'dp'))
- head_bias_new: float32 [2, 768], P(None, ('mp', 'dp'))
- ffn_bias_new: float32 [3072], P(('mp', 'dp'))
- norm_new: float32 [6, 768], P(None, ('dp', 'mp'))
The draws below stay inside these ranges and needn't reach their ends.
Inputs may be any that keep to these rules, and one draw needn't show every extreme that they name: `seg_lengths`: in each row the 8 lengths sum to 480 and the largest is exactly 256; the positions after them are padding.
All inputs are finite; a program needn't handle non-finite values.
Results may differ from the reference program's by a relative error of at most 0.015.
Values may be sent and summed in bfloat16 or wider, within the bound.
A program may use at most 192 MiB of HBM per device.

```python
import math
import jax
import jax.numpy as jnp
import numpy as np
from jax import lax

D = 768
H = 12
HD = 64
FF = 3072
LEN = 512
SEGS = 8
ROWS_DEV = 4
ROWS_ALL = 64
TOKENS = 32768
N_DP = 16


def rising(count, level):
    place = jnp.arange(count, dtype=jnp.float32) / max(count - 1, 1)
    return level * jnp.exp(place * math.log(4.0))


def factor_draw(key, count):
    return jnp.exp(jax.random.uniform(key, (count,), jnp.float32, -0.69, 0.69))


def draw_tokens(key, part):
    key = jax.random.fold_in(key, 3)
    place = jnp.arange(D, dtype=jnp.float32) / (D - 1)
    base = jnp.clip(jax.random.normal(key, (TOKENS, D), jnp.float32), -4.0, 4.0)
    ramp = 0.6 * jnp.exp(place * math.log(3.0))
    return (base * ramp[None, :]).astype(jnp.bfloat16)


def draw_norm_bias(key, part):
    key = jax.random.fold_in(key, 5)
    gain_key, shift_key = jax.random.split(key)
    place = jnp.arange(D, dtype=jnp.float32) / (D - 1)
    gains = 0.6 * jnp.exp(place * math.log(3.0))[None, :] * jax.random.uniform(gain_key, (2, D), jnp.float32, 0.85, 1.15)
    shifts = jnp.clip(0.3 * jax.random.normal(shift_key, (4, D), jnp.float32), -1.0, 1.0)
    return jnp.stack([shifts[0], shifts[1], gains[0], shifts[2], gains[1], shifts[3]])


def draw_qkv_rows(key, part):
    key = jax.random.fold_in(key, 11)
    factor = factor_draw(key, D)
    return rising(D, 0.09 * TOKENS) * factor


def draw_out_rows(key, part):
    key = jax.random.fold_in(key, 13)
    factor = factor_draw(key, D)
    return rising(D, 0.09 * TOKENS) * factor


def draw_up_rows(key, part):
    key = jax.random.fold_in(key, 17)
    factor = factor_draw(key, D)
    return rising(D, 0.12 * TOKENS) * factor


def draw_down_rows(key, part):
    key = jax.random.fold_in(key, 19)
    factor = factor_draw(key, FF)
    return rising(FF, 0.36 * TOKENS) * factor


def levels(rng, dims, cuts, smallest, high):
    level, own = 1.0, jax.random.fold_in(rng, 6)
    for dim, shards_of in cuts:
        steps = jnp.exp(jax.random.uniform(jax.random.fold_in(own, dim), (shards_of,), jnp.float32, smallest / len(cuts), high / len(cuts)))
        level = level * jnp.repeat(steps, dims[dim] // shards_of).reshape([-1 if axis == dim else 1 for axis in range(len(dims))])
    return level


def length_profile(number_of, total, limit, slope):
    portions = [(1 << 20) // math.isqrt(grade ** slope) + 1 for grade in range(2, number_of + 1)]
    surplus, holding = total - limit - (number_of - 1), [1] * (number_of - 1)
    while surplus > 0:
        movable = [i for i in range(number_of - 1) if holding[i] < limit]
        pool, left = sum([portions[i] for i in movable]), surplus
        for i in movable:
            addition = min(limit - holding[i], max(1, left * portions[i] // pool), surplus)
            holding[i] = holding[i] + addition
            surplus = surplus - addition
    return np.array([limit] + holding)


def uneven_parts(key, count, total, most, slope):
    if count == 2:
        one = jax.random.randint(key, (), max(1, total - most), min(most, total - 1) + 1)
        return jnp.stack([one, total - one])
    tallies = jnp.asarray(length_profile(count, total, most, slope), jnp.int32)
    couples = (count - 1) // 2
    source_of, sink = tallies[1:1 + 2 * couples:2], tallies[2:2 + 2 * couples:2]
    margin = jnp.minimum(source_of - 1, most - sink)
    shifted = jax.random.randint(jax.random.fold_in(key, 1), (couples,), 0, 1 << 20) % (margin + 1)
    tallies = tallies.at[1:1 + 2 * couples:2].set(source_of - shifted).at[2:2 + 2 * couples:2].set(sink + shifted)
    return tallies[jax.random.permutation(jax.random.fold_in(key, 2), count)]


def normal_values(stream_key, dims, deviation, reach, pieces=(), kind=jnp.bfloat16):
    entries = jax.random.normal(stream_key, dims, jnp.float32) * deviation
    if len(pieces) > 0:
        entries = levels(stream_key, dims, pieces, -0.22, 0.18) * entries
    return jnp.clip(entries, min=-reach, max=reach).astype(kind)


def setup_inputs(seed: int = 0) -> dict:
    seeds = jax.random.split(jax.random.key(seed), 22)
    return {
        "tokens": draw_tokens(jax.random.fold_in(seeds[21], 71), 0),
        "cotangent": normal_values(seeds[1], (TOKENS, D), 1.0, 6.0, ((0, 32),)),
        "seg_lengths": jax.vmap(lambda own: uneven_parts(own, SEGS, LEN - LEN // 16, LEN // 2, 2))(jax.random.split(seeds[2], ROWS_ALL)).reshape((ROWS_ALL, SEGS)).astype(jnp.int32),
        "w_qkv": normal_values(seeds[3], (D, 3, D), D ** -0.5, 0.21875, ((0, 16), (2, 2)), jnp.float32),
        "w_out": normal_values(seeds[4], (D, D), (D // 8) ** -0.5, 0.625, ((0, 32),), jnp.float32),
        "w_up": normal_values(seeds[5], (D, FF), D ** -0.5, 0.21875, ((0, 16), (1, 2)), jnp.float32),
        "w_down": normal_values(seeds[6], (FF, D), FF ** -0.5, 0.109375, ((0, 32),), jnp.float32),
        "head_bias": normal_values(seeds[7], (2, D), 0.3, 1.0, ((1, 32),), jnp.float32),
        "ffn_bias": normal_values(seeds[8], (FF,), 0.3, 1.0, ((0, 32),), jnp.float32),
        "norm_bias": draw_norm_bias(jax.random.fold_in(seeds[21], 71), 0),
        "qkv_rows": draw_qkv_rows(jax.random.fold_in(seeds[21], 71), 0),
        "qkv_cols": jnp.clip(jnp.exp(math.log(11796.48) - 1.3862944 * jax.random.uniform(seeds[11], (3, D), jnp.float32) ** levels(seeds[11], (3, D), ((1, 2),), -0.2, 0.2)), 2949.12, 11796.48),
        "out_rows": draw_out_rows(jax.random.fold_in(seeds[21], 71), 0),
        "out_cols": jnp.clip(jnp.exp(jax.random.uniform(seeds[13], (D,), jnp.float32, math.log(2949.12), math.log(11796.48))), 2949.12, 11796.48),
        "up_rows": draw_up_rows(jax.random.fold_in(seeds[21], 71), 0),
        "up_cols": jnp.clip(jnp.exp(math.log(15728.64) - 1.3862944 * jax.random.uniform(seeds[15], (FF,), jnp.float32) ** levels(seeds[15], (FF,), ((0, 2),), -0.2, 0.2)), 3932.16, 15728.64),
        "down_rows": draw_down_rows(jax.random.fold_in(seeds[21], 71), 0),
        "down_cols": jnp.clip(jnp.exp(jax.random.uniform(seeds[17], (D,), jnp.float32, math.log(11796.48), math.log(47185.92))), 11796.48, 47185.92),
        "head_bias_sq": jnp.clip(jnp.exp(math.log(6553.6) - 2.3025851 * jax.random.uniform(seeds[18], (2, D), jnp.float32) ** levels(seeds[18], (2, D), ((1, 32),), -0.2, 0.2)), 655.36, 6553.6),
        "ffn_bias_sq": jnp.clip(jnp.exp(math.log(11796.48) - 1.3862944 * jax.random.uniform(seeds[19], (FF,), jnp.float32) ** levels(seeds[19], (FF,), ((0, 32),), -0.2, 0.2)), 2949.12, 11796.48),
        "norm_sq": jnp.clip(jnp.exp(math.log(131072.0) - 2.0794415 * jax.random.uniform(seeds[20], (6, D), jnp.float32) ** levels(seeds[20], (6, D), ((1, 32),), -0.2, 0.2)), 16384.0, 131072.0),
    }


EPS_NORM = 1e-12
EPS_SQUARE = 1e-30
DECAY = 0.5
RATE = 3.0
CLIP = 0.3
HIGHEST = lax.Precision.HIGHEST

@jax.custom_vjp
def low(v):
    return lax.optimization_barrier(v.astype(jnp.bfloat16)).astype(jnp.float32)

@jax.custom_vjp
def low_back(v):
    return v

def low_keep(v):
    return (low(v), None)

def low_pass(kept, grad):
    return (grad,)

def back_keep(v):
    return (v, None)

def back_low(kept, grad):
    return (low(grad),)
low.defvjp(low_keep, low_pass)
low_back.defvjp(back_keep, back_low)

def layer_norm(values, gain, shift):
    center = values - lax.optimization_barrier(jnp.mean(values, axis=-1, keepdims=True))
    spread = lax.optimization_barrier(jnp.mean(center * center, axis=-1, keepdims=True))
    return center * lax.rsqrt(spread + EPS_NORM) * gain + shift

def segment_ids(lengths, length):
    bounds = jnp.cumsum(lengths, axis=-1).astype(jnp.int32)
    places = jnp.arange(length, dtype=jnp.int32)
    return lax.optimization_barrier(jnp.sum((places[None, :, None] >= bounds[:, None, :]).astype(jnp.int32), axis=-1))

def block_forward(params, block_x, block_ids):
    w_qkv, w_out, w_up, w_down, head_bias, ffn_bias, norm_bias = params
    rows = block_x.shape[0]
    flat = block_x.reshape(rows * LEN, D)
    projected = jnp.dot(flat, w_qkv.reshape(D, 3 * D), precision=HIGHEST).reshape(rows * LEN, 3, D)
    offsets = jnp.stack([head_bias[0], jnp.zeros_like(head_bias[0]), head_bias[1]])
    projected = low(low_back(projected + offsets))
    split = projected.reshape(rows, LEN, 3, H, HD)
    queries = split[:, :, 0]
    keys_in = split[:, :, 1]
    values_in = split[:, :, 2]
    scores = low_back(jnp.einsum('rqhd,rkhd->rhqk', queries, keys_in, precision=HIGHEST) * HD ** (-0.5))
    same = (block_ids[:, :, None] == block_ids[:, None, :])[:, None]
    probs = jax.nn.softmax(jnp.where(same, scores, -1e+30), axis=-1)
    context = jnp.einsum('rhqk,rkhd->rqhd', low(probs), values_in, precision=HIGHEST).reshape(rows * LEN, D)
    context = low(low_back(context))
    attended = low_back(jnp.dot(context, w_out, precision=HIGHEST) + norm_bias[0])
    hidden = layer_norm(flat + attended, norm_bias[2], norm_bias[3])
    inner = low_back(jnp.dot(low(hidden), w_up, precision=HIGHEST) + ffn_bias)
    activated = low(jax.nn.gelu(inner, approximate=False))
    branch = low_back(jnp.dot(activated, w_down, precision=HIGHEST) + norm_bias[1])
    output = layer_norm(hidden + branch, norm_bias[4], norm_bias[5])
    return output.reshape(rows, LEN, D)

def factored_step(weight, grad, rows_old, cols_old):
    count = weight.shape[0]
    matrix = grad.reshape(count, -1)
    squared = matrix * matrix + EPS_SQUARE
    rows_new = DECAY * rows_old + (1.0 - DECAY) * lax.optimization_barrier(jnp.mean(squared, axis=1))
    cols_new = DECAY * cols_old.reshape(-1) + (1.0 - DECAY) * lax.optimization_barrier(jnp.mean(squared, axis=0))
    estimate = rows_new[:, None] * cols_new[None, :] / jnp.mean(rows_new)
    update = matrix / jnp.sqrt(estimate)
    update_rms = jnp.sqrt(jnp.mean(update * update))
    stride = RATE * jnp.sqrt(jnp.mean(weight * weight)) / jnp.maximum(1.0, update_rms / CLIP)
    return (rows_new, cols_new.reshape(cols_old.shape), weight - stride * update.reshape(weight.shape))

def vector_step(weight, grad, second_old):
    second = DECAY * second_old + (1.0 - DECAY) * (grad * grad + EPS_SQUARE)
    update = grad / jnp.sqrt(second)
    update_rms = jnp.sqrt(jnp.mean(update * update))
    stride = RATE * jnp.sqrt(jnp.mean(weight * weight)) / jnp.maximum(1.0, update_rms / CLIP)
    return (second, weight - stride * update)

def reference(tokens, cotangent, seg_lengths, w_qkv, w_out, w_up, w_down, head_bias, ffn_bias, norm_bias, qkv_rows, qkv_cols, out_rows, out_cols, up_rows, up_cols, down_rows, down_cols, head_bias_sq, ffn_bias_sq, norm_sq):
    ids = segment_ids(seg_lengths, LEN)
    masters = (w_qkv, w_out, w_up, w_down, head_bias, ffn_bias, norm_bias)

    def forward(params, inputs):
        rounded = tuple((low(param) for param in params))
        blocks = inputs.reshape(N_DP, ROWS_DEV, LEN, D)
        block_ids = ids.reshape(N_DP, ROWS_DEV, LEN)
        step = jax.checkpoint(lambda pair: block_forward(rounded, pair[0], pair[1]))
        return lax.map(step, (blocks, block_ids)).reshape(TOKENS, D)
    output, backward = jax.vjp(forward, masters, tokens.astype(jnp.float32))
    grads, input_grad = backward(cotangent.astype(jnp.float32))
    member = (ids[:, None, :] == jnp.arange(SEGS, dtype=jnp.int32)[None, :, None]).astype(jnp.float32)
    pooled = jnp.einsum('rsl,rld->rsd', member, output.reshape(ROWS_ALL, LEN, D), precision=HIGHEST)
    pooled = pooled / seg_lengths[:, :, None].astype(jnp.float32)
    g_qkv, g_out, g_up, g_down, g_head, g_ffn, g_norm = grads
    qkv_r, qkv_c, qkv_new = factored_step(w_qkv, g_qkv, qkv_rows, qkv_cols)
    out_r, out_c, out_new = factored_step(w_out, g_out, out_rows, out_cols)
    up_r, up_c, up_new = factored_step(w_up, g_up, up_rows, up_cols)
    down_r, down_c, down_new = factored_step(w_down, g_down, down_rows, down_cols)
    head_s, head_new = vector_step(head_bias, g_head, head_bias_sq)
    ffn_s, ffn_new = vector_step(ffn_bias, g_ffn, ffn_bias_sq)
    norm_s, norm_new = vector_step(norm_bias, g_norm, norm_sq)
    return (output.astype(jnp.bfloat16), pooled, input_grad, g_qkv, g_out, g_up, g_down, g_head, g_ffn, g_norm, qkv_r, qkv_c, out_r, out_c, up_r, up_c, down_r, down_c, head_s, ffn_s, norm_s, qkv_new, out_new, up_new, down_new, head_new, ffn_new, norm_new)
```

```python
import functools

import jax
import jax.numpy as jnp
from jax import lax
from jax.experimental import pallas as pl
from jax.experimental.pallas import tpu as pltpu
from jax.sharding import PartitionSpec as P

D = 768
HD = 64
FF = 3072
LEN = 512
SEGS = 8

EPS_NORM = 1e-12
EPS_SQUARE = 1e-30
DECAY = 0.5
RATE = 3.0
CLIP = 0.3

MESH = pl.DeviceIdType.MESH
BF = jnp.bfloat16
F32 = jnp.float32
EVERY = slice(None)


class Place:
    def __init__(self):
        d = lax.axis_index("dp")
        self.m = lax.axis_index("mp")
        self.z, self.y, self.x = d // 4, (d // 2) % 2, d % 2

    def at(self, axis, step):
        size = 4 if axis == "z" else 2
        spot = {"z": self.z, "y": self.y, "x": self.x, "m": self.m}
        spot[axis] = (spot[axis] + step) % size
        return spot

    @staticmethod
    def device(spot):
        return (spot["z"] * 4 + spot["y"] * 2 + spot["x"], spot["m"])


def steps_of(axis):
    return (1, 2, 3) if axis == "z" else (1,)


def greet(place):
    barrier = pltpu.get_barrier_semaphore()
    count = 0
    for axis in "zyxm":
        for step in steps_of(axis):
            pl.semaphore_signal(
                barrier, inc=1, device_id=place.device(place.at(axis, step)), device_id_type=MESH
            )
            count += 1
    pl.semaphore_wait(barrier, count)


def column_parts(cols):
    tiles = cols // 128
    first = tiles // 3
    parts = [("yzx", 0, first * 128)] if first else []
    return parts + [("zxy", first * 128, cols - first * 128)]


class Gatherer:
    def __init__(self, place, shard, full, part, sems, base):
        order, start, width = part
        self.place, self.shard, self.full = place, shard, full
        self.cols = pl.ds(start, width)
        self.order = order + "m"
        self.sems, self.base = sems, base

    def view(self, spot):
        return self.full.at[spot["m"], spot["z"], spot["y"], spot["x"], :, self.cols]

    def copies(self, stage):
        place, axis = self.place, self.order[stage]
        out = []
        for step in steps_of(axis):
            spot = {"z": place.z, "y": place.y, "x": place.x, "m": place.m}
            for done in self.order[:stage]:
                spot[done] = EVERY
            target = place.at(axis, step)
            send, recv = self.sems
            slot = self.base + 4 * stage + step
            source = self.shard.at[:, self.cols] if stage == 0 else self.view(spot)
            sent = pltpu.make_async_remote_copy(
                source, self.view(spot), send.at[slot], recv.at[slot],
                device_id=place.device(target), device_id_type=MESH)
            spot = dict(spot)
            spot[axis] = place.at(axis, -step)[axis]
            arrives = pltpu.make_async_remote_copy(
                self.view(spot), self.view(spot), send.at[slot], recv.at[slot],
                device_id=place.device(target), device_id_type=MESH)
            out.append((sent, arrives))
        return out

    def start(self, stage):
        for sent, _ in self.copies(stage):
            sent.start()

    def arrived(self, stage):
        for _, arrives in self.copies(stage):
            arrives.wait_recv()

    def finish(self):
        for stage in range(4):
            for sent, _ in self.copies(stage):
                sent.wait_send()


def gather_kernel(count, *refs):
    shards, fulls = refs[:count], refs[count:2 * count]
    cast = refs[2 * count:3 * count]
    send, recv, local = refs[3 * count:]
    place = Place()
    greet(place)
    paths, base = [], 0
    locals_ = []
    for index in range(count):
        rows = shards[index].shape[0]
        held = cast[index].shape[0]
        value = shards[index][...]
        if held != rows:
            value = jnp.concatenate([value, jnp.zeros((held - rows, value.shape[1]), F32)], 0)
        cast[index][...] = value.astype(cast[index].dtype)
        own = pltpu.make_async_copy(
            cast[index], fulls[index].at[place.m, place.z, place.y, place.x], local.at[index])
        own.start()
        locals_.append(own)
        group = []
        for part in column_parts(cast[index].shape[1]):
            group.append(Gatherer(place, cast[index], fulls[index], part, (send, recv), base))
            base += 16
        for path in group:
            path.start(0)
        paths.append(group)
    for own in locals_:
        own.wait()
    for turn in range(count + 3):
        for index in range(count):
            stage = turn - index + 1
            if 1 <= stage <= 3:
                for path in paths[index]:
                    path.arrived(stage - 1)
                    path.start(stage)
    for group in paths:
        for path in group:
            path.arrived(3)
    for group in paths:
        for path in group:
            path.finish()


def gather(shards, kinds):
    held = [(s.shape[0] + (-s.shape[0]) % (16 if k == BF else 8), s.shape[1])
            for s, k in zip(shards, kinds)]
    count = len(shards)
    slots = 16 * sum(len(column_parts(h[1])) for h in held)
    outs = pl.pallas_call(
        functools.partial(gather_kernel, count),
        out_shape=[jax.ShapeDtypeStruct((2, 4, 2, 2) + h, k) for h, k in zip(held, kinds)],
        in_specs=[pl.BlockSpec(memory_space=pltpu.VMEM)] * count,
        out_specs=[pl.BlockSpec(memory_space=pl.ANY)] * count,
        scratch_shapes=[pltpu.VMEM(h, k) for h, k in zip(held, kinds)] + [
            pltpu.SemaphoreType.DMA((slots,)),
            pltpu.SemaphoreType.DMA((slots,)),
            pltpu.SemaphoreType.DMA((count,)),
        ],
        compiler_params=pltpu.CompilerParams(
            collective_id=0, has_side_effects=True, vmem_limit_bytes=48 << 20),
        name="gather_weights",
    )(*shards)
    return outs


class Scatterer:
    def __init__(self, place, held, part, slots, sems, base):
        order, start, width = part
        self.place, self.held = place, held
        self.order = order[::-1]
        self.start_col, self.width = start, width
        self.cols = pl.ds(start, width)
        self.slots = slots
        self.sems, self.base = sems, base

    def view(self, spot):
        return self.held.at[spot["z"], spot["y"], spot["x"], :, self.cols]

    def copies(self, stage):
        place, axis = self.place, self.order[stage]
        out = []
        for step in steps_of(axis):
            spot = {"z": EVERY, "y": EVERY, "x": EVERY}
            for done in self.order[:stage]:
                spot[done] = getattr(place, done)
            target = place.at(axis, step)
            spot[axis] = target[axis]
            send, recv = self.sems
            slot = self.base + 4 * stage + step
            land = self.slots[stage].at[step - 1]
            out.append(pltpu.make_async_remote_copy(
                self.view(spot), land, send.at[slot], recv.at[slot],
                device_id=place.device(target), device_id_type=MESH))
        return out

    def start(self, stage):
        for sent in self.copies(stage):
            sent.start()

    def add(self, stage, result=None):
        place, axis = self.place, self.order[stage]
        for sent in self.copies(stage):
            sent.wait_recv()
        left = [name for name in "zyx" if name not in self.order[:stage + 1]]
        sizes = [4 if name == "z" else 2 for name in left]
        total = 1
        for size in sizes:
            total *= size
        slots = self.slots[stage]
        arrivals = len(steps_of(axis))

        def one(index):
            spot = {name: getattr(place, name) for name in "zyx"}
            inner = []
            rest = index
            for name, size in reversed(list(zip(left, sizes))):
                spot[name] = rest % size
                inner.insert(0, rest % size)
                rest = rest // size
            where = (spot["z"], spot["y"], spot["x"], EVERY, self.cols)
            value = self.held[where].astype(F32)
            for arrival in range(arrivals):
                value = value + slots[tuple([arrival] + inner)].astype(F32)
            if result is None:
                self.held[where] = value.astype(self.held.dtype)
            else:
                result[:, self.cols] = value[:result.shape[0]]

        if total == 1:
            one(0)
        else:
            pl.loop(0, total)(one)

    def finish(self):
        for stage in range(3):
            for sent in self.copies(stage):
                sent.wait_send()


def slot_shapes(part, rows):
    order, _, width = part
    order = order[::-1]
    shapes = []
    for stage in range(3):
        left = [4 if name == "z" else 2 for name in "zyx" if name not in order[:stage + 1]]
        shapes.append((len(steps_of(order[stage])), *left, rows, width))
    return shapes


def scatter_kernel(count, parts, *refs):
    fulls, results = refs[:count], refs[count:2 * count]
    rest = list(refs[2 * count:])
    held = [rest.pop(0) for _ in range(count)]
    other = [rest.pop(0) for _ in range(count)]
    slots = [[[rest.pop(0) for _ in range(3)] for _ in parts[index]] for index in range(count)]
    send, recv, local = rest
    place = Place()
    greet(place)
    partner = place.device(place.at("m", 1))
    base = 0
    groups, swaps, owns = [], [], []
    for index in range(count):
        swap = pltpu.make_async_remote_copy(
            fulls[index].at[1 - place.m], other[index], send.at[base], recv.at[base],
            device_id=partner, device_id_type=MESH)
        swap.start()
        own = pltpu.make_async_copy(fulls[index].at[place.m], held[index], local.at[index])
        own.start()
        swaps.append(swap)
        owns.append(own)
        base += 1
        group = []
        for number, part in enumerate(parts[index]):
            group.append(Scatterer(place, held[index], part, slots[index][number], (send, recv), base))
            base += 12
        groups.append(group)
    for turn in range(count + 3):
        for index in range(count):
            stage = turn - index
            if stage == 0:
                owns[index].wait()
                swaps[index].wait_recv()

                @pl.loop(0, 16)
                def _(block):
                    where = (block // 4, (block // 2) % 2, block % 2)
                    held[index][where] = (
                        held[index][where].astype(F32) + other[index][where].astype(F32)
                    ).astype(held[index].dtype)

                for path in groups[index]:
                    path.start(0)
            elif 1 <= stage <= 3:
                for path in groups[index]:
                    path.add(stage - 1, results[index] if stage == 3 else None)
                    if stage < 3:
                        path.start(stage)
    for index in range(count):
        swaps[index].wait_send()
        for path in groups[index]:
            path.finish()


def scatter(fulls, rows):
    count = len(fulls)
    parts = [column_parts(f.shape[-1]) for f in fulls]
    slots = []
    for full, own in zip(fulls, parts):
        for part in own:
            slots += [pltpu.VMEM(s, full.dtype) for s in slot_shapes(part, full.shape[-2])]
    sems = sum(1 + 12 * len(own) for own in parts)
    return pl.pallas_call(
        functools.partial(scatter_kernel, count, parts),
        out_shape=[jax.ShapeDtypeStruct((r, f.shape[-1]), F32) for r, f in zip(rows, fulls)],
        in_specs=[pl.BlockSpec(memory_space=pl.ANY)] * count,
        out_specs=[pl.BlockSpec(memory_space=pltpu.VMEM)] * count,
        scratch_shapes=[pltpu.VMEM(f.shape[1:], f.dtype) for f in fulls] * 2 + slots + [
            pltpu.SemaphoreType.DMA((sems,)),
            pltpu.SemaphoreType.DMA((sems,)),
            pltpu.SemaphoreType.DMA((count,)),
        ],
        compiler_params=pltpu.CompilerParams(
            collective_id=1, has_side_effects=True, vmem_limit_bytes=56 << 20),
        name="scatter_grads",
    )(*fulls)


def layer_norm(values, gain, shift):
    center = values - jnp.mean(values, axis=-1, keepdims=True)
    spread = jnp.mean(center * center, axis=-1, keepdims=True)
    return center * lax.rsqrt(spread + EPS_NORM) * gain + shift


def gelu_exact(values):
    return jax.nn.gelu(values, approximate=False)


def segment_ids(lengths, length):
    bounds = jnp.cumsum(lengths, axis=-1)
    places = jnp.arange(length, dtype=jnp.int32)
    return jnp.sum((places[None, :, None] >= bounds[:, None, :]).astype(jnp.int32), axis=-1)


def row_scores(packed, row_ids):
    scores = jnp.einsum(
        "qhd,khd->hqk", packed[:, 0], packed[:, 1], preferred_element_type=F32
    ) * HD ** (-0.5)
    same = row_ids[:, None] == row_ids[None, :]
    return jnp.where(same[None], scores, -1e30)


def attend_row(packed, row_ids):
    scores = row_scores(packed, row_ids)
    peak = jnp.max(scores, axis=-1, keepdims=True)
    raised = jnp.exp(scores - peak)
    total = jnp.sum(raised, axis=-1, keepdims=True)
    probs = raised / total
    context = jnp.einsum(
        "hqk,khd->qhd", probs.astype(BF), packed[:, 2], preferred_element_type=F32
    )
    return (
        context.astype(BF).reshape(context.shape[0], -1),
        (peak + jnp.log(total))[..., 0],
    )


def attend_back(packed, grad_context, log_total, row_ids):
    scores = row_scores(packed, row_ids)
    probs = jnp.exp(scores - log_total[..., None])
    grad_values = jnp.einsum(
        "hqk,qhd->khd", probs.astype(BF), grad_context, preferred_element_type=F32
    )
    grad_probs = jnp.einsum(
        "qhd,khd->hqk", grad_context, packed[:, 2], preferred_element_type=F32
    )
    inner_sum = jnp.sum(probs * grad_probs, axis=-1, keepdims=True)
    grad_scores = (probs * (grad_probs - inner_sum)).astype(BF)
    grad_queries = jnp.einsum(
        "hqk,khd->qhd", grad_scores, packed[:, 1], preferred_element_type=F32
    ) * HD ** (-0.5)
    grad_keys = jnp.einsum(
        "hqk,qhd->khd", grad_scores, packed[:, 0], preferred_element_type=F32
    ) * HD ** (-0.5)
    return jnp.stack([grad_queries, grad_keys, grad_values], axis=1).astype(BF)


def fast_mesh():
    return lax.axis_size("dp") == 16 and lax.axis_size("mp") == 2


def gather_all(shards, kinds):
    if fast_mesh():
        full = gather(shards, kinds)
        return [f.reshape(2, 16, *f.shape[-2:])[:, :, :s.shape[0]] for f, s in zip(full, shards)]
    both = [lax.all_gather(s.astype(k), "dp", axis=0) for s, k in zip(shards, kinds)]
    return [lax.all_gather(s, "mp", axis=0) for s in both]


def scatter_all(fulls):
    if fast_mesh():
        rows = [f.shape[-2] for f in fulls]
        held = [r + (-r) % (16 if f.dtype == BF else 8) for r, f in zip(rows, fulls)]
        padded = [
            jnp.pad(f, ((0, 0), (0, 0), (0, h - r), (0, 0))).reshape(2, 4, 2, 2, h, f.shape[-1])
            for f, h, r in zip(fulls, held, rows)
        ]
        return scatter(padded, rows)
    out = []
    for full in fulls:
        own = lax.psum_scatter(full.astype(F32), "mp", scatter_dimension=0)
        out.append(lax.psum_scatter(own, "dp", scatter_dimension=0))
    return out


def pack_small(head, ffn, norm):
    flat = jnp.concatenate([head.reshape(-1), ffn.reshape(-1), norm.reshape(-1)])
    rows = -(-flat.shape[0] // 1024) * 8
    return jnp.pad(flat, (0, rows * 128 - flat.shape[0])).reshape(rows, 128)


def body(
    tokens, cotangent, seg_lengths, w_qkv, w_out, w_up, w_down, head_bias, ffn_bias, norm_bias,
    qkv_rows, qkv_cols, out_rows, out_cols, up_rows, up_cols, down_rows, down_cols,
    head_bias_sq, ffn_bias_sq, norm_sq,
):
    f32 = F32
    cores = lax.axis_size("mp")
    data = lax.axis_size("dp")
    core = lax.axis_index("mp")
    own_tokens = tokens.shape[0]
    own_rows = own_tokens // LEN
    ids = segment_ids(seg_lengths, LEN)
    own_ids = lax.dynamic_slice_in_dim(ids, core * own_rows, own_rows, 0)
    own_lengths = lax.dynamic_slice_in_dim(seg_lengths, core * own_rows, own_rows, 0)
    rows_qkv = w_qkv.shape[0]
    half = w_qkv.shape[2]
    n_head, n_ffn, n_norm = head_bias.size, ffn_bias.size, norm_bias.size
    small, qkv_g, out_g, up_g, down_g = gather_all(
        [pack_small(head_bias, ffn_bias, norm_bias), w_qkv.reshape(rows_qkv, -1), w_out, w_up, w_down],
        [f32, BF, BF, BF, BF],
    )
    small = small.reshape(cores, data, -1).astype(BF).astype(f32)
    head_full = small[:, :, :n_head].reshape(cores, data, 2, -1).transpose(2, 0, 1, 3).reshape(2, D)
    ffn_full = small[:, :, n_head:n_head + n_ffn].reshape(-1)
    norm_full = small[:, :, n_head + n_ffn:n_head + n_ffn + n_norm]
    norm_full = norm_full.reshape(cores, data, 6, -1).transpose(2, 1, 0, 3).reshape(6, D)
    qkv_weight = qkv_g.reshape(cores, D, 3, half).transpose(1, 2, 0, 3).reshape(D, 3 * D)
    out_weight = out_g.reshape(D, D)
    up_weight = up_g.reshape(cores, D, FF // cores).transpose(1, 0, 2).reshape(D, FF)
    down_weight = down_g.reshape(FF, D)
    heads = D // HD
    offsets = jnp.stack([head_full[0], jnp.zeros_like(head_full[0]), head_full[1]])
    projected = jnp.dot(tokens, qkv_weight, preferred_element_type=f32).reshape(-1, 3, D) + offsets
    packed_rows = projected.astype(BF).reshape(own_rows, LEN, 3, heads, HD)
    context_rows, log_totals = lax.map(
        lambda pair: attend_row(pair[0], pair[1]), (packed_rows, own_ids)
    )
    context = context_rows.reshape(own_tokens, D)
    attended = jnp.dot(context, out_weight, preferred_element_type=f32) + norm_full[0]
    hidden, norm_one_back = jax.vjp(
        layer_norm, tokens.astype(f32) + attended, norm_full[2], norm_full[3]
    )
    hidden_b = hidden.astype(BF)
    inner = jnp.dot(hidden_b, up_weight, preferred_element_type=f32) + ffn_full
    activated, gelu_back = jax.vjp(gelu_exact, inner)
    activated_b = activated.astype(BF)
    branch = jnp.dot(activated_b, down_weight, preferred_element_type=f32) + norm_full[1]
    output, norm_two_back = jax.vjp(layer_norm, hidden + branch, norm_full[4], norm_full[5])
    member = (own_ids[:, None, :] == jnp.arange(SEGS, dtype=jnp.int32)[None, :, None]).astype(f32)
    pooled = jnp.einsum(
        "rsl,rld->rsd", member, output.reshape(own_rows, LEN, D), precision=lax.Precision.HIGHEST
    )
    pooled = pooled / own_lengths[:, :, None].astype(f32)
    grad_res_two, grad_gain_two, grad_shift_two = norm_two_back(cotangent.astype(f32))
    grad_branch = grad_res_two.astype(BF)
    grad_bias_down = jnp.sum(grad_branch.astype(f32), axis=0)
    grad_act = jnp.dot(grad_branch, down_weight.T, preferred_element_type=f32)
    grad_down = jnp.dot(activated_b.T, grad_branch, preferred_element_type=f32)
    grad_inner = gelu_back(grad_act)[0].astype(BF)
    grad_bias_up = jnp.sum(grad_inner.astype(f32), axis=0)
    grad_up = jnp.dot(hidden_b.T, grad_inner, preferred_element_type=f32)
    grad_hidden = grad_res_two + jnp.dot(grad_inner, up_weight.T, preferred_element_type=f32)
    grad_res_one, grad_gain_one, grad_shift_one = norm_one_back(grad_hidden)
    grad_attended = grad_res_one.astype(BF)
    grad_bias_out = jnp.sum(grad_attended.astype(f32), axis=0)
    grad_context = jnp.dot(grad_attended, out_weight.T, preferred_element_type=f32).astype(BF)
    grad_out = jnp.dot(context.T, grad_attended, preferred_element_type=f32)
    grad_rows = lax.map(
        lambda item: attend_back(item[0], item[1], item[2], item[3]),
        (packed_rows, grad_context.reshape(own_rows, LEN, heads, HD), log_totals, own_ids),
    )
    grad_packed = grad_rows.reshape(own_tokens, 3, D)
    grad_head = jnp.stack(
        [
            jnp.sum(grad_packed[:, 0].astype(f32), axis=0),
            jnp.sum(grad_packed[:, 2].astype(f32), axis=0),
        ]
    )
    grad_flat = grad_packed.reshape(own_tokens, 3 * D)
    grad_qkv = jnp.dot(tokens.T, grad_flat, preferred_element_type=f32)
    input_grad = grad_res_one + jnp.dot(grad_flat, qkv_weight.T, preferred_element_type=f32)
    norm_terms = jnp.stack(
        [grad_bias_out, grad_bias_down, grad_gain_one, grad_shift_one, grad_gain_two, grad_shift_two]
    )
    small_grads = jnp.concatenate(
        [
            grad_head.reshape(2, cores, data, -1).transpose(1, 2, 0, 3).reshape(cores, data, -1),
            grad_bias_up.reshape(cores, data, -1),
            norm_terms.reshape(6, data, cores, -1).transpose(2, 1, 0, 3).reshape(cores, data, -1),
        ],
        axis=-1,
    )
    small_rows = -(-small_grads.shape[-1] // 1024) * 8
    small_grads = jnp.pad(
        small_grads, ((0, 0), (0, 0), (0, small_rows * 128 - small_grads.shape[-1]))
    ).reshape(cores, data, small_rows, 128)
    qkv_blocks = grad_qkv.astype(BF).reshape(data, rows_qkv, 3, cores, half)
    red_small, red_qkv, red_out, red_up, red_down = scatter_all(
        [
            small_grads,
            qkv_blocks.transpose(3, 0, 1, 2, 4).reshape(cores, data, rows_qkv, 3 * half),
            grad_out.astype(BF).reshape(cores, data, -1, D),
            grad_up.astype(BF).reshape(data, rows_qkv, cores, -1).transpose(2, 0, 1, 3),
            grad_down.astype(BF).reshape(cores, data, -1, D),
        ]
    )
    red_small = red_small.reshape(-1)
    red_head = red_small[:n_head].reshape(head_bias.shape)
    red_ffn = red_small[n_head:n_head + n_ffn]
    norm_grad = red_small[n_head + n_ffn:n_head + n_ffn + n_norm].reshape(norm_bias.shape)
    weights_flat = [w_qkv.reshape(rows_qkv, -1), w_out, w_up, w_down]
    grads_flat = [red_qkv, red_out, red_up, red_down]
    rows_old = [qkv_rows, out_rows, up_rows, down_rows]
    cols_old = [qkv_cols.reshape(-1), out_cols, up_cols, down_cols]
    col_count = [3 * D, D, FF, D]
    row_count = [D, D, D, FF]
    row_share = [cores, 1, cores, 1]
    squares = [grad * grad + EPS_SQUARE for grad in grads_flat]
    row_parts = [jnp.sum(square, axis=1) for square in squares]
    col_parts = [jnp.sum(square, axis=0) for square in squares]
    vec_weights = [head_bias, ffn_bias, norm_bias]
    vec_grads = [red_head, red_ffn, norm_grad]
    vec_old = [head_bias_sq, ffn_bias_sq, norm_sq]
    vec_counts = [2 * D, FF, 6 * D]
    vec_second = [
        DECAY * old + (1.0 - DECAY) * (grad * grad + EPS_SQUARE)
        for old, grad in zip(vec_old, vec_grads)
    ]
    vec_update = [grad * lax.rsqrt(second) for grad, second in zip(vec_grads, vec_second)]
    weight_parts = [jnp.sum(weight * weight) for weight in weights_flat + vec_weights]
    vec_parts = [jnp.sum(update * update) for update in vec_update]
    row_qkv, row_up = lax.psum((row_parts[0], row_parts[2]), "mp")
    col_qkv, col_up = lax.psum((col_parts[0], col_parts[2]), "dp")
    col_out, col_down = lax.psum((col_parts[1], col_parts[3]), ("dp", "mp"))
    row_sums = [row_qkv, row_parts[1], row_up, row_parts[3]]
    col_sums = [col_qkv, col_out, col_up, col_down]
    rows_new = [
        DECAY * rows_old[index] + (1.0 - DECAY) * row_sums[index] / col_count[index]
        for index in range(4)
    ]
    cols_new = [
        DECAY * cols_old[index] + (1.0 - DECAY) * col_sums[index] / row_count[index]
        for index in range(4)
    ]
    ratio_parts = [
        jnp.sum(
            grads_flat[index]
            * grads_flat[index]
            / (rows_new[index][:, None] * cols_new[index][None, :])
        )
        for index in range(4)
    ]
    extra_parts = (
        [jnp.sum(rows_new[index]) / row_share[index] for index in range(4)]
        + weight_parts
        + vec_parts
    )
    totals = lax.psum(jnp.stack(ratio_parts + extra_parts), ("dp", "mp"))
    row_means = [totals[4 + index] / row_count[index] for index in range(4)]
    weight_totals = [totals[8 + index] for index in range(7)]
    vec_totals = [totals[15 + index] for index in range(3)]
    new_mats = []
    for index in range(4):
        entries = row_count[index] * col_count[index]
        estimate = rows_new[index][:, None] * cols_new[index][None, :] / row_means[index]
        update = grads_flat[index] / jnp.sqrt(estimate)
        update_rms = jnp.sqrt(row_means[index] * totals[index] / entries)
        stride = (
            RATE * jnp.sqrt(weight_totals[index] / entries) / jnp.maximum(1.0, update_rms / CLIP)
        )
        new_mats.append(weights_flat[index] - stride * update)
    new_vecs = []
    for index in range(3):
        update_rms = jnp.sqrt(vec_totals[index] / vec_counts[index])
        stride = (
            RATE
            * jnp.sqrt(weight_totals[4 + index] / vec_counts[index])
            / jnp.maximum(1.0, update_rms / CLIP)
        )
        new_vecs.append(vec_weights[index] - stride * vec_update[index])
    return (
        output.astype(BF),
        pooled,
        input_grad,
        red_qkv.reshape(w_qkv.shape),
        red_out,
        red_up,
        red_down,
        red_head,
        red_ffn,
        norm_grad,
        rows_new[0],
        cols_new[0].reshape(qkv_cols.shape),
        rows_new[1],
        cols_new[1],
        rows_new[2],
        cols_new[2],
        rows_new[3],
        cols_new[3],
        vec_second[0],
        vec_second[1],
        vec_second[2],
        new_mats[0].reshape(w_qkv.shape),
        new_mats[1],
        new_mats[2],
        new_mats[3],
        new_vecs[0],
        new_vecs[1],
        new_vecs[2],
    )


def solution(mesh):
    return jax.shard_map(
        body,
        mesh=mesh,
        in_specs=(
            P(("dp", "mp"), None),
            P(("dp", "mp"), None),
            P("dp", None),
            P("dp", None, "mp"),
            P(("mp", "dp"), None),
            P("dp", "mp"),
            P(("mp", "dp"), None),
            P(None, ("mp", "dp")),
            P(("mp", "dp")),
            P(None, ("dp", "mp")),
            P("dp"),
            P(None, "mp"),
            P(("mp", "dp")),
            P(),
            P("dp"),
            P("mp"),
            P(("mp", "dp")),
            P(),
            P(None, ("mp", "dp")),
            P(("mp", "dp")),
            P(None, ("dp", "mp")),
        ),
        out_specs=(
            P(("dp", "mp"), None),
            P(("dp", "mp"), None, None),
            P(("dp", "mp"), None),
            P("dp", None, "mp"),
            P(("mp", "dp"), None),
            P("dp", "mp"),
            P(("mp", "dp"), None),
            P(None, ("mp", "dp")),
            P(("mp", "dp")),
            P(None, ("dp", "mp")),
            P("dp"),
            P(None, "mp"),
            P(("mp", "dp")),
            P(),
            P("dp"),
            P("mp"),
            P(("mp", "dp")),
            P(),
            P(None, ("mp", "dp")),
            P(("mp", "dp")),
            P(None, ("dp", "mp")),
            P("dp", None, "mp"),
            P(("mp", "dp"), None),
            P("dp", "mp"),
            P(("mp", "dp"), None),
            P(None, ("mp", "dp")),
            P(("mp", "dp")),
            P(None, ("dp", "mp")),
        ),
        check_vma=False,
    )
```

```python
import functools

import jax
import jax.numpy as jnp
from jax import lax
from jax.experimental import pallas as pl
from jax.experimental.pallas import tpu as pltpu
from jax.sharding import PartitionSpec as P

D = 768
HD = 64
FF = 3072
LEN = 512
SEGS = 8

EPS_NORM = 1e-12
EPS_SQUARE = 1e-30
DECAY = 0.5
RATE = 3.0
CLIP = 0.3

MESH = pl.DeviceIdType.MESH
BF = jnp.bfloat16
F32 = jnp.float32
EVERY = slice(None)


class Place:
    def __init__(self):
        d = lax.axis_index("dp")
        self.m = lax.axis_index("mp")
        self.z, self.y, self.x = d // 4, (d // 2) % 2, d % 2

    def at(self, axis, step):
        size = 4 if axis == "z" else 2
        spot = {"z": self.z, "y": self.y, "x": self.x, "m": self.m}
        spot[axis] = (spot[axis] + step) % size
        return spot

    @staticmethod
    def device(spot):
        return (spot["z"] * 4 + spot["y"] * 2 + spot["x"], spot["m"])


def steps_of(axis):
    return (1, 2, 3) if axis == "z" else (1,)


def greet(place):
    barrier = pltpu.get_barrier_semaphore()
    count = 0
    for axis in "zyxm":
        for step in steps_of(axis):
            pl.semaphore_signal(
                barrier, inc=1, device_id=place.device(place.at(axis, step)), device_id_type=MESH
            )
            count += 1
    pl.semaphore_wait(barrier, count)


def column_parts(cols):
    tiles = cols // 128
    first = tiles // 3
    parts = [("yzx", 0, first * 128)] if first else []
    return parts + [("zxy", first * 128, cols - first * 128)]


class Gatherer:
    def __init__(self, place, shard, full, part, sems, base):
        order, start, width = part
        self.place, self.shard, self.full = place, shard, full
        self.cols = pl.ds(start, width)
        self.order = order + "m"
        self.sems, self.base = sems, base

    def view(self, spot):
        return self.full.at[spot["m"], spot["z"], spot["y"], spot["x"], :, self.cols]

    def copies(self, stage):
        place, axis = self.place, self.order[stage]
        out = []
        for step in steps_of(axis):
            spot = {"z": place.z, "y": place.y, "x": place.x, "m": place.m}
            for done in self.order[:stage]:
                spot[done] = EVERY
            target = place.at(axis, step)
            send, recv = self.sems
            slot = self.base + 4 * stage + step
            source = self.shard.at[:, self.cols] if stage == 0 else self.view(spot)
            sent = pltpu.make_async_remote_copy(
                source, self.view(spot), send.at[slot], recv.at[slot],
                device_id=place.device(target), device_id_type=MESH)
            spot = dict(spot)
            spot[axis] = place.at(axis, -step)[axis]
            arrives = pltpu.make_async_remote_copy(
                self.view(spot), self.view(spot), send.at[slot], recv.at[slot],
                device_id=place.device(target), device_id_type=MESH)
            out.append((sent, arrives))
        return out

    def start(self, stage):
        for sent, _ in self.copies(stage):
            sent.start()

    def arrived(self, stage):
        for _, arrives in self.copies(stage):
            arrives.wait_recv()

    def finish(self):
        for stage in range(4):
            for sent, _ in self.copies(stage):
                sent.wait_send()


def weight_sums_of(weights, small):
    parts = []
    for weight in weights:
        value = weight[...]
        if value.ndim == 3:
            parts.append(sum(all_sum(value[:, part] * value[:, part]) for part in range(3)))
        else:
            parts.append(all_sum(value * value))
    return scalars([jnp.zeros((1, 1), F32)] * 11 + parts + small_sums(small))


def gather_kernel(*refs):
    refs = list(refs)
    take = lambda number: [refs.pop(0) for _ in range(number)]
    weights = take(4)
    head, ffn, norm = take(3)
    fulls = take(5)
    sums = refs.pop(0)
    cast = take(5)
    send, recv, local = refs
    count = 5
    half = weights[0].shape[2]
    place_small(cast[0], norm[...], head[...], ffn[...], 0.0)
    for part in range(3):
        cast[1][:, part * half:(part + 1) * half] = weights[0][:, part, :].astype(BF)
    value = weights[1][...]
    held = cast[2].shape[0]
    cast[2][...] = jnp.concatenate(
        [value, jnp.zeros((held - value.shape[0], value.shape[1]), F32)], 0).astype(BF)
    cast[3][...] = weights[2][...].astype(BF)
    cast[4][...] = weights[3][...].astype(BF)
    place = Place()
    greet(place)
    paths, base = [], 0
    locals_ = []
    for index in range(count):
        own = pltpu.make_async_copy(
            cast[index], fulls[index].at[place.m, place.z, place.y, place.x], local.at[index])
        own.start()
        locals_.append(own)
        group = []
        for part in column_parts(cast[index].shape[1]):
            group.append(Gatherer(place, cast[index], fulls[index], part, (send, recv), base))
            base += 16
        for path in group:
            path.start(0)
        paths.append(group)
    for own in locals_:
        own.wait()
    sums[...] = weight_sums_of(weights, cast[0][...])
    for turn in range(count + 3):
        for index in range(count):
            stage = turn - index + 1
            if 1 <= stage <= 3:
                for path in paths[index]:
                    path.arrived(stage - 1)
                    path.start(stage)
    for group in paths:
        for path in group:
            path.arrived(3)
    for group in paths:
        for path in group:
            path.finish()


def gather(weights, vectors):
    qkv, out, up, down = weights
    held = [(16, 128), (qkv.shape[0], 3 * qkv.shape[2]), (32, out.shape[1]), up.shape, down.shape]
    kinds = [F32, BF, BF, BF, BF]
    slots = 16 * sum(len(column_parts(h[1])) for h in held)
    vmem = pl.BlockSpec(memory_space=pltpu.VMEM)
    return pl.pallas_call(
        gather_kernel,
        out_shape=[jax.ShapeDtypeStruct((2, 4, 2, 2) + h, k) for h, k in zip(held, kinds)]
        + [jax.ShapeDtypeStruct((8, 128), F32)],
        in_specs=[vmem] * 7,
        out_specs=[pl.BlockSpec(memory_space=pl.ANY)] * 5 + [vmem],
        scratch_shapes=[pltpu.VMEM(h, k) for h, k in zip(held, kinds)] + [
            pltpu.SemaphoreType.DMA((slots,)),
            pltpu.SemaphoreType.DMA((slots,)),
            pltpu.SemaphoreType.DMA((5,)),
        ],
        compiler_params=pltpu.CompilerParams(
            collective_id=0, has_side_effects=True, vmem_limit_bytes=48 << 20),
        name="gather_weights",
    )(*weights, *vectors)


class Scatterer:
    def __init__(self, place, held, part, slots, sems, base):
        order, start, width = part
        self.place, self.held = place, held
        self.order = order[::-1]
        self.start_col, self.width = start, width
        self.cols = pl.ds(start, width)
        self.slots = slots
        self.sems, self.base = sems, base

    def view(self, spot):
        return self.held.at[spot["z"], spot["y"], spot["x"], :, self.cols]

    def copies(self, stage):
        place, axis = self.place, self.order[stage]
        out = []
        for step in steps_of(axis):
            spot = {"z": EVERY, "y": EVERY, "x": EVERY}
            for done in self.order[:stage]:
                spot[done] = getattr(place, done)
            target = place.at(axis, step)
            spot[axis] = target[axis]
            send, recv = self.sems
            slot = self.base + 4 * stage + step
            land = self.slots[stage].at[step - 1]
            out.append(pltpu.make_async_remote_copy(
                self.view(spot), land, send.at[slot], recv.at[slot],
                device_id=place.device(target), device_id_type=MESH))
        return out

    def start(self, stage):
        for sent in self.copies(stage):
            sent.start()

    def add(self, stage, result=None):
        place, axis = self.place, self.order[stage]
        for sent in self.copies(stage):
            sent.wait_recv()
        left = [name for name in "zyx" if name not in self.order[:stage + 1]]
        sizes = [4 if name == "z" else 2 for name in left]
        total = 1
        for size in sizes:
            total *= size
        slots = self.slots[stage]
        arrivals = len(steps_of(axis))

        def one(index):
            spot = {name: getattr(place, name) for name in "zyx"}
            inner = []
            rest = index
            for name, size in reversed(list(zip(left, sizes))):
                spot[name] = rest % size
                inner.insert(0, rest % size)
                rest = rest // size
            where = (spot["z"], spot["y"], spot["x"], EVERY, self.cols)
            value = self.held[where].astype(F32)
            for arrival in range(arrivals):
                value = value + slots[tuple([arrival] + inner)].astype(F32)
            if result is None:
                self.held[where] = value.astype(self.held.dtype)
            else:
                result[:, self.cols] = value[:result.shape[0]]

        if total == 1:
            one(0)
        else:
            pl.loop(0, total)(one)

    def finish(self):
        for stage in range(3):
            for sent in self.copies(stage):
                sent.wait_send()


def slot_shapes(part, rows):
    order, _, width = part
    order = order[::-1]
    shapes = []
    for stage in range(3):
        left = [4 if name == "z" else 2 for name in "zyx" if name not in order[:stage + 1]]
        shapes.append((len(steps_of(order[stage])), *left, rows, width))
    return shapes


def to_column(row):
    count = row.shape[1]
    here = lax.broadcasted_iota(jnp.int32, (count, count), 0)
    there = lax.broadcasted_iota(jnp.int32, (count, count), 1)
    return jnp.sum(jnp.where(here == there, row, 0.0), axis=1, keepdims=True)


def to_row(column):
    count = column.shape[0]
    here = lax.broadcasted_iota(jnp.int32, (count, count), 0)
    there = lax.broadcasted_iota(jnp.int32, (count, count), 1)
    return jnp.sum(jnp.where(here == there, column, 0.0), axis=0, keepdims=True)


def put_line(ref, line, row):
    for tile in range(row.shape[1] // 128):
        ref[line + tile:line + tile + 1, :] = row[:, tile * 128:(tile + 1) * 128]


def get_line(ref, line, width):
    tiles = width // 128
    return jnp.concatenate([ref[line + t:line + t + 1, :] for t in range(tiles)], axis=1)


def scalars(values):
    lane = lax.broadcasted_iota(jnp.int32, (8, 128), 1)
    out = jnp.zeros((8, 128), F32)
    for index, value in enumerate(values):
        out = jnp.where(lane == index, value, out)
    return out


def all_sum(values):
    return jnp.sum(jnp.sum(values, axis=1, keepdims=True), axis=0, keepdims=True)


class Exchange:
    def __init__(self, place, mine, land, sems, base):
        self.place, self.mine, self.land = place, mine, land
        self.sems, self.base = sems, base
        self.sent = []

    def swap(self, stage, axis):
        place = self.place
        send, recv = self.sems
        own = place.z if axis == "z" else 0
        for step in steps_of(axis):
            slot = self.base + 4 * stage + step
            copy = pltpu.make_async_remote_copy(
                self.mine.at[stage], self.land.at[stage, own], send.at[slot], recv.at[slot],
                device_id=place.device(place.at(axis, step)), device_id_type=MESH)
            copy.start()
            self.sent.append(copy)
        if axis == "z":
            self.land[stage, place.z] = self.mine[stage]
        for step in steps_of(axis):
            slot = self.base + 4 * stage + step
            spot = (place.z - step) % 4 if axis == "z" else 0
            pltpu.make_async_remote_copy(
                self.mine.at[stage], self.land.at[stage, spot], send.at[slot], recv.at[slot],
                device_id=place.device(place.at(axis, step)), device_id_type=MESH).wait_recv()
        if axis == "z":
            land = self.land
            return (land[stage, 0] + land[stage, 1]) + (land[stage, 2] + land[stage, 3])
        return self.mine[stage] + self.land[stage, 0]

    def finish(self):
        for copy in self.sent:
            copy.wait_send()


def add_up(exchange, value, picked=None):
    exchange.mine[0] = value
    total = exchange.swap(0, "m")
    if picked is not None:
        total = jnp.where(picked, total, value)
    for stage, axis in ((1, "x"), (2, "y"), (3, "z")):
        exchange.mine[stage] = total
        total = exchange.swap(stage, axis)
    return total


QKV_LINE, UP_LINE, OUT_LINE, DOWN_LINE, ROW_LINE = 0, 9, 21, 27, 33
LINES = 40
WIDTHS = (3 * D // 2, D, FF // 2, D)
COL_LINES = (QKV_LINE, OUT_LINE, UP_LINE, DOWN_LINE)
COL_COUNT = (3 * D, D, FF, D)
ROW_COUNT = (D, D, D, FF)


def new_rows_cols(grads, rows_old, cols_old, lines):
    rows_new, cols_new = [], []
    for index in range(4):
        if index in (0, 2):
            line = ROW_LINE + index // 2
            count = rows_old[index].shape[1]
            row_sum = to_column(lines[line:line + 1, :count])
        else:
            grad = grads[index][...]
            row_sum = jnp.sum(grad * grad + EPS_SQUARE, axis=1, keepdims=True)
        rows_new.append(
            DECAY * to_column(rows_old[index][...]) + (1.0 - DECAY) * row_sum / COL_COUNT[index])
        col_sum = get_line(lines, COL_LINES[index], WIDTHS[index])
        if index == 0:
            old = cols_old[0]
            old = jnp.concatenate([old[0:1, :], old[1:2, :], old[2:3, :]], axis=1)
        else:
            old = cols_old[index][...]
        cols_new.append(DECAY * old + (1.0 - DECAY) * col_sum / ROW_COUNT[index])
    return rows_new, cols_new


def place_small(ref, norm, head, ffn, fill):
    ref[...] = jnp.full(ref.shape, fill, F32)
    ref[0:6, 0:norm.shape[1]] = norm
    ref[6:8, 0:head.shape[1]] = head
    ref[8:9, 0:ffn.shape[1]] = ffn


def small_update(grad, old):
    second = DECAY * old + (1.0 - DECAY) * (grad * grad + EPS_SQUARE)
    return second, grad * lax.rsqrt(second)


def small_sums(values):
    line = lax.broadcasted_iota(jnp.int32, values.shape, 0)
    square = values * values
    return [
        all_sum(jnp.where((line >= 6) & (line < 8), square, 0.0)),
        all_sum(jnp.where(line == 8, square, 0.0)),
        all_sum(jnp.where(line < 6, square, 0.0)),
    ]


def scatter_kernel(count, parts, *refs):
    refs = list(refs)
    take = lambda number: [refs.pop(0) for _ in range(number)]
    fulls = take(count)
    rows_old, cols_old = take(4), take(4)
    head_sq, ffn_sq, norm_sq, weight_sums = take(4)
    results = take(count)
    lines, totals = take(2)
    held, other = take(count), take(count)
    slots = [[take(3) for _ in parts[index]] for index in range(count)]
    mine_one, land_one, mine_two, land_two, old_small = take(5)
    send, recv, local = refs
    place = Place()
    greet(place)
    partner = place.device(place.at("m", 1))
    base = 0
    groups, swaps, owns = [], [], []
    for index in range(count):
        swap = pltpu.make_async_remote_copy(
            fulls[index].at[1 - place.m], other[index], send.at[base], recv.at[base],
            device_id=partner, device_id_type=MESH)
        swap.start()
        own = pltpu.make_async_copy(fulls[index].at[place.m], held[index], local.at[index])
        own.start()
        swaps.append(swap)
        owns.append(own)
        base += 1
        group = []
        for number, part in enumerate(parts[index]):
            group.append(Scatterer(place, held[index], part, slots[index][number], (send, recv), base))
            base += 12
        groups.append(group)
    for turn in range(count + 3):
        for index in range(count):
            stage = turn - index
            if stage == 0:
                owns[index].wait()
                swaps[index].wait_recv()

                @pl.loop(0, 16)
                def _(block):
                    where = (block // 4, (block // 2) % 2, block % 2)
                    held[index][where] = (
                        held[index][where].astype(F32) + other[index][where].astype(F32)
                    ).astype(held[index].dtype)

                for path in groups[index]:
                    path.start(0)
            elif 1 <= stage <= 3:
                for path in groups[index]:
                    path.add(stage - 1, results[index] if stage == 3 else None)
                    if stage < 3:
                        path.start(stage)
    small, grads = results[0], results[1:]
    lines[...] = jnp.zeros(lines.shape, F32)
    for index in range(4):
        grad = grads[index][...]
        square = grad * grad + EPS_SQUARE
        put_line(lines, COL_LINES[index], jnp.sum(square, axis=0, keepdims=True))
        if index in (0, 2):
            line = ROW_LINE + index // 2
            lines[line:line + 1, 0:grad.shape[0]] = to_row(jnp.sum(square, axis=1, keepdims=True))
    first = Exchange(place, mine_one, land_one, (send, recv), base)
    line = lax.broadcasted_iota(jnp.int32, lines.shape, 0)
    value = lines[...]
    first.mine[0] = value
    paired = jnp.where(line >= OUT_LINE, first.swap(0, "m"), value)
    total = paired
    for stage, axis in ((1, "x"), (2, "y"), (3, "z")):
        first.mine[stage] = total
        total = first.swap(stage, axis)
    lines[...] = jnp.where(line >= ROW_LINE, paired, total)
    rows_new, cols_new = new_rows_cols(grads, rows_old, cols_old, lines)
    ratios, row_totals = [], []
    for index in range(4):
        grad = grads[index][...]
        scaled = jnp.sum(grad * grad * (1.0 / cols_new[index]), axis=1, keepdims=True)
        ratios.append(jnp.sum(scaled / rows_new[index], axis=0, keepdims=True))
        share = 0.5 if index in (0, 2) else 1.0
        row_totals.append(jnp.sum(rows_new[index], axis=0, keepdims=True) * share)
    place_small(old_small, norm_sq[...], head_sq[...], ffn_sq[...], 1.0)
    _, update = small_update(small[...], old_small[...])
    second = Exchange(place, mine_two, land_two, (send, recv), base + 16)
    totals[...] = add_up(
        second, scalars(ratios + row_totals + small_sums(update)) + weight_sums[...])
    for index in range(count):
        swaps[index].wait_send()
        for path in groups[index]:
            path.finish()
    first.finish()
    second.finish()


def scatter(fulls, rows, rows_old, cols_old, squares, weight_sums):
    count = len(fulls)
    parts = [column_parts(f.shape[-1]) for f in fulls]
    slots = []
    for full, own in zip(fulls, parts):
        for part in own:
            slots += [pltpu.VMEM(s, full.dtype) for s in slot_shapes(part, full.shape[-2])]
    sems = sum(1 + 12 * len(own) for own in parts) + 32
    vmem = pl.BlockSpec(memory_space=pltpu.VMEM)
    outs = [jax.ShapeDtypeStruct((r, f.shape[-1]), F32) for r, f in zip(rows, fulls)]
    outs += [jax.ShapeDtypeStruct((LINES, 128), F32), jax.ShapeDtypeStruct((8, 128), F32)]
    return pl.pallas_call(
        functools.partial(scatter_kernel, count, parts),
        out_shape=outs,
        in_specs=[pl.BlockSpec(memory_space=pl.ANY)] * count + [vmem] * 12,
        out_specs=[vmem] * len(outs),
        scratch_shapes=[pltpu.VMEM(f.shape[1:], f.dtype) for f in fulls] * 2 + slots + [
            pltpu.VMEM((4, LINES, 128), F32),
            pltpu.VMEM((4, 4, LINES, 128), F32),
            pltpu.VMEM((4, 8, 128), F32),
            pltpu.VMEM((4, 4, 8, 128), F32),
            pltpu.VMEM((16, 128), F32),
            pltpu.SemaphoreType.DMA((sems,)),
            pltpu.SemaphoreType.DMA((sems,)),
            pltpu.SemaphoreType.DMA((count,)),
        ],
        compiler_params=pltpu.CompilerParams(
            collective_id=1, has_side_effects=True, vmem_limit_bytes=56 << 20),
        name="scatter_grads",
    )(*fulls, *rows_old, *cols_old, *squares, weight_sums)


def step_kernel(*refs):
    refs = list(refs)
    take = lambda number: [refs.pop(0) for _ in range(number)]
    grads = take(4)
    small, lines, totals = take(3)
    weights, rows_old, cols_old = take(4), take(4), take(4)
    head, ffn, norm, head_sq, ffn_sq, norm_sq = take(6)
    grads_out = take(4)
    head_grad, ffn_grad, norm_grad = take(3)
    rows_out, cols_out = take(4), take(4)
    head_second, ffn_second, norm_second = take(3)
    weights_out = take(4)
    head_new, ffn_new, norm_new = take(3)
    old_small, weight_small = refs
    half = D // 2
    rows_new, cols_new = new_rows_cols(grads, rows_old, cols_old, lines)
    total = lambda lane: totals[0:1, lane:lane + 1]
    for index in range(4):
        rows_out[index][...] = to_row(rows_new[index])
        if index == 0:
            for part in range(3):
                cols_out[0][part:part + 1, :] = cols_new[0][:, part * half:(part + 1) * half]
        else:
            cols_out[index][...] = cols_new[index]
        entries = ROW_COUNT[index] * COL_COUNT[index]
        row_mean = total(4 + index) / ROW_COUNT[index]
        update_rms = jnp.sqrt(row_mean * total(index) / entries)
        stride = (
            RATE * jnp.sqrt(total(11 + index) / entries) / jnp.maximum(1.0, update_rms / CLIP))
        scale_rows = lax.rsqrt(rows_new[index] / row_mean) * stride
        scale_cols = lax.rsqrt(cols_new[index])
        if index == 0:
            for part in range(3):
                cut = slice(part * half, (part + 1) * half)
                grad = grads[0][:, cut]
                grads_out[0][:, part, :] = grad
                weights_out[0][:, part, :] = (
                    weights[0][:, part, :] - grad * scale_rows * scale_cols[:, cut])
        else:
            grad = grads[index][...]
            grads_out[index][...] = grad
            weights_out[index][...] = weights[index][...] - grad * scale_rows * scale_cols
    place_small(old_small, norm_sq[...], head_sq[...], ffn_sq[...], 1.0)
    place_small(weight_small, norm[...], head[...], ffn[...], 0.0)
    grad = small[...]
    second, update = small_update(grad, old_small[...])
    line = lax.broadcasted_iota(jnp.int32, grad.shape, 0)
    counts = (2 * D, FF, 6 * D)
    strides = []
    for index in range(3):
        update_rms = jnp.sqrt(total(8 + index) / counts[index])
        strides.append(
            RATE * jnp.sqrt(total(15 + index) / counts[index])
            / jnp.maximum(1.0, update_rms / CLIP))
    stride = jnp.where(line < 6, strides[2], jnp.where(line < 8, strides[0], strides[1]))
    fresh = weight_small[...] - stride * update
    for values, (norm_ref, head_ref, ffn_ref) in (
        (grad, (norm_grad, head_grad, ffn_grad)),
        (second, (norm_second, head_second, ffn_second)),
        (fresh, (norm_new, head_new, ffn_new)),
    ):
        norm_ref[...] = values[0:6, 0:norm_ref.shape[1]]
        head_ref[...] = values[6:8, 0:head_ref.shape[1]]
        ffn_ref[...] = values[8:9, 0:ffn_ref.shape[1]]


def step(reduced, lines, totals, weights, rows_old, cols_old, vectors, squares):
    vmem = pl.BlockSpec(memory_space=pltpu.VMEM)
    small, grads = reduced[0], reduced[1:]
    shapes = [w.shape for w in weights] + [v.shape for v in vectors]
    shapes += [r.shape for r in rows_old] + [c.shape for c in cols_old]
    shapes += [v.shape for v in vectors] + [w.shape for w in weights] + [v.shape for v in vectors]
    operands = [*grads, small, lines, totals, *weights, *rows_old, *cols_old, *vectors, *squares]
    return pl.pallas_call(
        step_kernel,
        out_shape=[jax.ShapeDtypeStruct(s, F32) for s in shapes],
        in_specs=[vmem] * len(operands),
        out_specs=[vmem] * len(shapes),
        scratch_shapes=[pltpu.VMEM((16, 128), F32), pltpu.VMEM((16, 128), F32)],
        compiler_params=pltpu.CompilerParams(vmem_limit_bytes=32 << 20),
        name="adafactor_step",
    )(*operands)


def layer_norm(values, gain, shift):
    center = values - jnp.mean(values, axis=-1, keepdims=True)
    spread = jnp.mean(center * center, axis=-1, keepdims=True)
    return center * lax.rsqrt(spread + EPS_NORM) * gain + shift


def gelu_exact(values):
    return jax.nn.gelu(values, approximate=False)


def segment_ids(lengths, length):
    bounds = jnp.cumsum(lengths, axis=-1)
    places = jnp.arange(length, dtype=jnp.int32)
    return jnp.sum((places[None, :, None] >= bounds[:, None, :]).astype(jnp.int32), axis=-1)


def row_scores(packed, row_ids):
    scores = jnp.einsum(
        "qhd,khd->hqk", packed[:, 0], packed[:, 1], preferred_element_type=F32
    ) * HD ** (-0.5)
    same = row_ids[:, None] == row_ids[None, :]
    return jnp.where(same[None], scores, -1e30)


def attend_row(packed, row_ids):
    scores = row_scores(packed, row_ids)
    peak = jnp.max(scores, axis=-1, keepdims=True)
    raised = jnp.exp(scores - peak)
    total = jnp.sum(raised, axis=-1, keepdims=True)
    probs = raised / total
    context = jnp.einsum(
        "hqk,khd->qhd", probs.astype(BF), packed[:, 2], preferred_element_type=F32
    )
    return (
        context.astype(BF).reshape(context.shape[0], -1),
        (peak + jnp.log(total))[..., 0],
    )


def attend_back(packed, grad_context, log_total, row_ids):
    scores = row_scores(packed, row_ids)
    probs = jnp.exp(scores - log_total[..., None])
    grad_values = jnp.einsum(
        "hqk,qhd->khd", probs.astype(BF), grad_context, preferred_element_type=F32
    )
    grad_probs = jnp.einsum(
        "qhd,khd->hqk", grad_context, packed[:, 2], preferred_element_type=F32
    )
    inner_sum = jnp.sum(probs * grad_probs, axis=-1, keepdims=True)
    grad_scores = (probs * (grad_probs - inner_sum)).astype(BF)
    grad_queries = jnp.einsum(
        "hqk,khd->qhd", grad_scores, packed[:, 1], preferred_element_type=F32
    ) * HD ** (-0.5)
    grad_keys = jnp.einsum(
        "hqk,qhd->khd", grad_scores, packed[:, 0], preferred_element_type=F32
    ) * HD ** (-0.5)
    return jnp.stack([grad_queries, grad_keys, grad_values], axis=1).astype(BF)


def fast_mesh():
    return lax.axis_size("dp") == 16 and lax.axis_size("mp") == 2


def small_block(norm, head, ffn):
    wide = lambda v: jnp.pad(v, [(0, 0)] * (v.ndim - 1) + [(0, 128 - v.shape[-1])])
    block = jnp.concatenate([wide(norm), wide(head), wide(ffn)], axis=-2)
    return jnp.pad(block, [(0, 0)] * (block.ndim - 2) + [(0, 16 - block.shape[-2]), (0, 0)])


def gather_plain(weights, vectors):
    head, ffn, norm = vectors
    qkv, out, up, down = (w.astype(BF) for w in weights)
    full = []
    for shard in (small_block(norm, head, ffn), qkv.reshape(qkv.shape[0], -1), out, up, down):
        full.append(lax.all_gather(lax.all_gather(shard, "dp", axis=0), "mp", axis=0))
    return full


def scatter_plain(fulls):
    out = []
    for full in fulls:
        own = lax.psum_scatter(full.astype(F32), "mp", scatter_dimension=0)
        out.append(lax.psum_scatter(own, "dp", scatter_dimension=0))
    return out


def body(
    tokens, cotangent, seg_lengths, w_qkv, w_out, w_up, w_down, head_bias, ffn_bias, norm_bias,
    qkv_rows, qkv_cols, out_rows, out_cols, up_rows, up_cols, down_rows, down_cols,
    head_bias_sq, ffn_bias_sq, norm_sq,
):
    f32 = F32
    cores = lax.axis_size("mp")
    data = lax.axis_size("dp")
    core = lax.axis_index("mp")
    own_tokens = tokens.shape[0]
    own_rows = own_tokens // LEN
    ids = segment_ids(seg_lengths, LEN)
    own_ids = lax.dynamic_slice_in_dim(ids, core * own_rows, own_rows, 0)
    own_lengths = lax.dynamic_slice_in_dim(seg_lengths, core * own_rows, own_rows, 0)
    rows_qkv = w_qkv.shape[0]
    half = w_qkv.shape[2]
    fast = data == 16 and cores == 2
    weights = [w_qkv, w_out, w_up, w_down]
    vectors = [head_bias, ffn_bias.reshape(1, -1), norm_bias]
    if fast:
        *gathered, weight_sums = gather(weights, vectors)
        gathered = [g.reshape(cores, data, *g.shape[-2:]) for g in gathered]
        gathered[2] = gathered[2][:, :, :w_out.shape[0]]
    else:
        gathered = gather_plain(weights, vectors)
    small, qkv_g, out_g, up_g, down_g = gathered
    small = small.astype(BF).astype(f32)
    own_head, own_ffn, own_norm = head_bias.shape[1], ffn_bias.shape[0], norm_bias.shape[1]
    norm_full = small[:, :, 0:6, :own_norm].transpose(2, 1, 0, 3).reshape(6, D)
    head_full = small[:, :, 6:8, :own_head].transpose(2, 0, 1, 3).reshape(2, D)
    ffn_full = small[:, :, 8, :own_ffn].reshape(-1)
    qkv_weight = qkv_g.reshape(cores, D, 3, half).transpose(1, 2, 0, 3).reshape(D, 3 * D)
    out_weight = out_g.reshape(D, D)
    up_weight = up_g.reshape(cores, D, FF // cores).transpose(1, 0, 2).reshape(D, FF)
    down_weight = down_g.reshape(FF, D)
    heads = D // HD
    offsets = jnp.stack([head_full[0], jnp.zeros_like(head_full[0]), head_full[1]])
    projected = jnp.dot(tokens, qkv_weight, preferred_element_type=f32).reshape(-1, 3, D) + offsets
    packed_rows = projected.astype(BF).reshape(own_rows, LEN, 3, heads, HD)
    context_rows, log_totals = lax.map(
        lambda pair: attend_row(pair[0], pair[1]), (packed_rows, own_ids)
    )
    context = context_rows.reshape(own_tokens, D)
    attended = jnp.dot(context, out_weight, preferred_element_type=f32) + norm_full[0]
    hidden, norm_one_back = jax.vjp(
        layer_norm, tokens.astype(f32) + attended, norm_full[2], norm_full[3]
    )
    hidden_b = hidden.astype(BF)
    inner = jnp.dot(hidden_b, up_weight, preferred_element_type=f32) + ffn_full
    activated, gelu_back = jax.vjp(gelu_exact, inner)
    activated_b = activated.astype(BF)
    branch = jnp.dot(activated_b, down_weight, preferred_element_type=f32) + norm_full[1]
    output, norm_two_back = jax.vjp(layer_norm, hidden + branch, norm_full[4], norm_full[5])
    member = (own_ids[:, None, :] == jnp.arange(SEGS, dtype=jnp.int32)[None, :, None]).astype(f32)
    pooled = jnp.einsum(
        "rsl,rld->rsd", member, output.reshape(own_rows, LEN, D), precision=lax.Precision.HIGHEST
    )
    pooled = pooled / own_lengths[:, :, None].astype(f32)
    grad_res_two, grad_gain_two, grad_shift_two = norm_two_back(cotangent.astype(f32))
    grad_branch = grad_res_two.astype(BF)
    grad_bias_down = jnp.sum(grad_branch.astype(f32), axis=0)
    grad_act = jnp.dot(grad_branch, down_weight.T, preferred_element_type=f32)
    grad_down = jnp.dot(activated_b.T, grad_branch, preferred_element_type=f32)
    grad_inner = gelu_back(grad_act)[0].astype(BF)
    grad_bias_up = jnp.sum(grad_inner.astype(f32), axis=0)
    grad_up = jnp.dot(hidden_b.T, grad_inner, preferred_element_type=f32)
    grad_hidden = grad_res_two + jnp.dot(grad_inner, up_weight.T, preferred_element_type=f32)
    grad_res_one, grad_gain_one, grad_shift_one = norm_one_back(grad_hidden)
    grad_attended = grad_res_one.astype(BF)
    grad_bias_out = jnp.sum(grad_attended.astype(f32), axis=0)
    grad_context = jnp.dot(grad_attended, out_weight.T, preferred_element_type=f32).astype(BF)
    grad_out = jnp.dot(context.T, grad_attended, preferred_element_type=f32)
    grad_rows = lax.map(
        lambda item: attend_back(item[0], item[1], item[2], item[3]),
        (packed_rows, grad_context.reshape(own_rows, LEN, heads, HD), log_totals, own_ids),
    )
    grad_packed = grad_rows.reshape(own_tokens, 3, D)
    grad_head = jnp.stack(
        [
            jnp.sum(grad_packed[:, 0].astype(f32), axis=0),
            jnp.sum(grad_packed[:, 2].astype(f32), axis=0),
        ]
    )
    grad_flat = grad_packed.reshape(own_tokens, 3 * D)
    grad_qkv = jnp.dot(tokens.T, grad_flat, preferred_element_type=f32)
    input_grad = grad_res_one + jnp.dot(grad_flat, qkv_weight.T, preferred_element_type=f32)
    norm_terms = jnp.stack(
        [grad_bias_out, grad_bias_down, grad_gain_one, grad_shift_one, grad_gain_two, grad_shift_two]
    )
    small_grads = small_block(
        norm_terms.reshape(6, data, cores, -1).transpose(2, 1, 0, 3),
        grad_head.reshape(2, cores, data, -1).transpose(1, 2, 0, 3),
        grad_bias_up.reshape(cores, data, 1, -1),
    )
    qkv_blocks = grad_qkv.astype(BF).reshape(data, rows_qkv, 3, cores, half)
    fulls = [
        small_grads,
        qkv_blocks.transpose(3, 0, 1, 2, 4).reshape(cores, data, rows_qkv, 3 * half),
        grad_out.astype(BF).reshape(cores, data, -1, D),
        grad_up.astype(BF).reshape(data, rows_qkv, cores, -1).transpose(2, 0, 1, 3),
        grad_down.astype(BF).reshape(cores, data, -1, D),
    ]
    if fast:
        fulls[2] = jnp.pad(fulls[2], ((0, 0), (0, 0), (0, 32 - w_out.shape[0]), (0, 0)))
        fulls = [f.reshape(2, 4, 2, 2, *f.shape[-2:]) for f in fulls]
        rows_old = [v.reshape(1, -1) for v in (qkv_rows, out_rows, up_rows, down_rows)]
        cols_old = [qkv_cols] + [v.reshape(1, -1) for v in (out_cols, up_cols, down_cols)]
        old = [head_bias_sq, ffn_bias_sq.reshape(1, -1), norm_sq]
        *reduced, lines, totals = scatter(
            fulls, [16, rows_qkv, w_out.shape[0], rows_qkv, w_down.shape[0]],
            rows_old, cols_old, old, weight_sums)
        new = step(reduced, lines, totals, weights, rows_old, cols_old, vectors, old)
        grads, (g_head, g_ffn, g_norm) = new[:4], new[4:7]
        rows_new, cols_new = [r.reshape(-1) for r in new[7:11]], new[11:15]
        cols_new = [cols_new[0]] + [c.reshape(-1) for c in cols_new[1:]]
        (s_head, s_ffn, s_norm), mats = new[15:18], new[18:22]
        n_head, n_ffn, n_norm = new[22:25]
        stats = [v for pair in zip(rows_new, cols_new) for v in pair]
        return (
            output.astype(BF), pooled, input_grad, *grads, g_head, g_ffn.reshape(-1), g_norm, *stats,
            s_head, s_ffn.reshape(-1), s_norm, *mats, n_head, n_ffn.reshape(-1), n_norm,
        )
    red_small, red_qkv, red_out, red_up, red_down = scatter_plain(fulls)
    norm_grad = red_small[0:6, :own_norm]
    red_head = red_small[6:8, :own_head]
    red_ffn = red_small[8, :own_ffn]
    weights_flat = [w_qkv.reshape(rows_qkv, -1), w_out, w_up, w_down]
    grads_flat = [red_qkv, red_out, red_up, red_down]
    rows_old = [qkv_rows, out_rows, up_rows, down_rows]
    cols_old = [qkv_cols.reshape(-1), out_cols, up_cols, down_cols]
    col_count = [3 * D, D, FF, D]
    row_count = [D, D, D, FF]
    row_share = [cores, 1, cores, 1]
    squares = [grad * grad + EPS_SQUARE for grad in grads_flat]
    row_parts = [jnp.sum(square, axis=1) for square in squares]
    col_parts = [jnp.sum(square, axis=0) for square in squares]
    vec_weights = [head_bias, ffn_bias, norm_bias]
    vec_grads = [red_head, red_ffn, norm_grad]
    vec_old = [head_bias_sq, ffn_bias_sq, norm_sq]
    vec_counts = [2 * D, FF, 6 * D]
    vec_second = [
        DECAY * old + (1.0 - DECAY) * (grad * grad + EPS_SQUARE)
        for old, grad in zip(vec_old, vec_grads)
    ]
    vec_update = [grad * lax.rsqrt(second) for grad, second in zip(vec_grads, vec_second)]
    weight_parts = [jnp.sum(weight * weight) for weight in weights_flat + vec_weights]
    vec_parts = [jnp.sum(update * update) for update in vec_update]
    row_qkv, row_up = lax.psum((row_parts[0], row_parts[2]), "mp")
    col_qkv, col_up = lax.psum((col_parts[0], col_parts[2]), "dp")
    col_out, col_down = lax.psum((col_parts[1], col_parts[3]), ("dp", "mp"))
    row_sums = [row_qkv, row_parts[1], row_up, row_parts[3]]
    col_sums = [col_qkv, col_out, col_up, col_down]
    rows_new = [
        DECAY * rows_old[index] + (1.0 - DECAY) * row_sums[index] / col_count[index]
        for index in range(4)
    ]
    cols_new = [
        DECAY * cols_old[index] + (1.0 - DECAY) * col_sums[index] / row_count[index]
        for index in range(4)
    ]
    ratio_parts = [
        jnp.sum(
            grads_flat[index]
            * grads_flat[index]
            / (rows_new[index][:, None] * cols_new[index][None, :])
        )
        for index in range(4)
    ]
    extra_parts = (
        [jnp.sum(rows_new[index]) / row_share[index] for index in range(4)]
        + weight_parts
        + vec_parts
    )
    totals = lax.psum(jnp.stack(ratio_parts + extra_parts), ("dp", "mp"))
    row_means = [totals[4 + index] / row_count[index] for index in range(4)]
    weight_totals = [totals[8 + index] for index in range(7)]
    vec_totals = [totals[15 + index] for index in range(3)]
    new_mats = []
    for index in range(4):
        entries = row_count[index] * col_count[index]
        estimate = rows_new[index][:, None] * cols_new[index][None, :] / row_means[index]
        update = grads_flat[index] / jnp.sqrt(estimate)
        update_rms = jnp.sqrt(row_means[index] * totals[index] / entries)
        stride = (
            RATE * jnp.sqrt(weight_totals[index] / entries) / jnp.maximum(1.0, update_rms / CLIP)
        )
        new_mats.append(weights_flat[index] - stride * update)
    new_vecs = []
    for index in range(3):
        update_rms = jnp.sqrt(vec_totals[index] / vec_counts[index])
        stride = (
            RATE
            * jnp.sqrt(weight_totals[4 + index] / vec_counts[index])
            / jnp.maximum(1.0, update_rms / CLIP)
        )
        new_vecs.append(vec_weights[index] - stride * vec_update[index])
    return (
        output.astype(BF),
        pooled,
        input_grad,
        red_qkv.reshape(w_qkv.shape),
        red_out,
        red_up,
        red_down,
        red_head,
        red_ffn,
        norm_grad,
        rows_new[0],
        cols_new[0].reshape(qkv_cols.shape),
        rows_new[1],
        cols_new[1],
        rows_new[2],
        cols_new[2],
        rows_new[3],
        cols_new[3],
        vec_second[0],
        vec_second[1],
        vec_second[2],
        new_mats[0].reshape(w_qkv.shape),
        new_mats[1],
        new_mats[2],
        new_mats[3],
        new_vecs[0],
        new_vecs[1],
        new_vecs[2],
    )


def solution(mesh):
    return jax.shard_map(
        body,
        mesh=mesh,
        in_specs=(
            P(("dp", "mp"), None),
            P(("dp", "mp"), None),
            P("dp", None),
            P("dp", None, "mp"),
            P(("mp", "dp"), None),
            P("dp", "mp"),
            P(("mp", "dp"), None),
            P(None, ("mp", "dp")),
            P(("mp", "dp")),
            P(None, ("dp", "mp")),
            P("dp"),
            P(None, "mp"),
            P(("mp", "dp")),
            P(),
            P("dp"),
            P("mp"),
            P(("mp", "dp")),
            P(),
            P(None, ("mp", "dp")),
            P(("mp", "dp")),
            P(None, ("dp", "mp")),
        ),
        out_specs=(
            P(("dp", "mp"), None),
            P(("dp", "mp"), None, None),
            P(("dp", "mp"), None),
            P("dp", None, "mp"),
            P(("mp", "dp"), None),
            P("dp", "mp"),
            P(("mp", "dp"), None),
            P(None, ("mp", "dp")),
            P(("mp", "dp")),
            P(None, ("dp", "mp")),
            P("dp"),
            P(None, "mp"),
            P(("mp", "dp")),
            P(),
            P("dp"),
            P("mp"),
            P(("mp", "dp")),
            P(),
            P(None, ("mp", "dp")),
            P(("mp", "dp")),
            P(None, ("dp", "mp")),
            P("dp", None, "mp"),
            P(("mp", "dp"), None),
            P("dp", "mp"),
            P(("mp", "dp"), None),
            P(None, ("mp", "dp")),
            P(("mp", "dp")),
            P(None, ("dp", "mp")),
        ),
        check_vma=False,
    )
```

```python
import functools

import jax
import jax.numpy as jnp
from jax import lax
from jax.experimental import pallas as pl
from jax.experimental.pallas import tpu as pltpu
from jax.sharding import PartitionSpec as P

D = 768
HD = 64
FF = 3072
LEN = 512
SEGS = 8

EPS_NORM = 1e-12
EPS_SQUARE = 1e-30
DECAY = 0.5
RATE = 3.0
CLIP = 0.3

MESH = pl.DeviceIdType.MESH
BF = jnp.bfloat16
F32 = jnp.float32
EVERY = slice(None)


class Place:
    def __init__(self):
        d = lax.axis_index("dp")
        self.m = lax.axis_index("mp")
        self.z, self.y, self.x = d // 4, (d // 2) % 2, d % 2

    def at(self, axis, step):
        size = 4 if axis == "z" else 2
        spot = {"z": self.z, "y": self.y, "x": self.x, "m": self.m}
        spot[axis] = (spot[axis] + step) % size
        return spot

    @staticmethod
    def device(spot):
        return (spot["z"] * 4 + spot["y"] * 2 + spot["x"], spot["m"])


def steps_of(axis):
    return (1, 2, 3) if axis == "z" else (1,)


def greet(place):
    barrier = pltpu.get_barrier_semaphore()
    count = 0
    for axis in "zyxm":
        for step in steps_of(axis):
            pl.semaphore_signal(
                barrier, inc=1, device_id=place.device(place.at(axis, step)), device_id_type=MESH
            )
            count += 1
    pl.semaphore_wait(barrier, count)


def column_parts(cols):
    tiles = cols // 128
    first = tiles // 3
    parts = [("yzx", 0, first * 128)] if first else []
    return parts + [("zxy", first * 128, cols - first * 128)]


class Gatherer:
    def __init__(self, place, shard, full, part, sems, base):
        order, start, width = part
        self.place, self.shard, self.full = place, shard, full
        self.cols = pl.ds(start, width)
        self.order = order + "m"
        self.sems, self.base = sems, base

    def view(self, spot):
        return self.full.at[spot["m"], spot["z"], spot["y"], spot["x"], :, self.cols]

    def copies(self, stage):
        place, axis = self.place, self.order[stage]
        out = []
        for step in steps_of(axis):
            spot = {"z": place.z, "y": place.y, "x": place.x, "m": place.m}
            for done in self.order[:stage]:
                spot[done] = EVERY
            target = place.at(axis, step)
            send, recv = self.sems
            slot = self.base + 4 * stage + step
            source = self.shard.at[:, self.cols] if stage == 0 else self.view(spot)
            sent = pltpu.make_async_remote_copy(
                source, self.view(spot), send.at[slot], recv.at[slot],
                device_id=place.device(target), device_id_type=MESH)
            spot = dict(spot)
            spot[axis] = place.at(axis, -step)[axis]
            arrives = pltpu.make_async_remote_copy(
                self.view(spot), self.view(spot), send.at[slot], recv.at[slot],
                device_id=place.device(target), device_id_type=MESH)
            out.append((sent, arrives))
        return out

    def start(self, stage):
        for sent, _ in self.copies(stage):
            sent.start()

    def arrived(self, stage):
        for _, arrives in self.copies(stage):
            arrives.wait_recv()

    def finish(self):
        for stage in range(4):
            for sent, _ in self.copies(stage):
                sent.wait_send()


def weight_sums_of(weights, small):
    parts = []
    for weight in weights:
        value = weight[...]
        if value.ndim == 3:
            parts.append(sum(all_sum(value[:, part] * value[:, part]) for part in range(3)))
        else:
            parts.append(all_sum(value * value))
    return scalars([jnp.zeros((1, 1), F32)] * 11 + parts + small_sums(small))


def gather_kernel(*refs):
    refs = list(refs)
    take = lambda number: [refs.pop(0) for _ in range(number)]
    weights = take(4)
    head, ffn, norm = take(3)
    fulls = take(5)
    sums = refs.pop(0)
    cast = take(5)
    send, recv, local = refs
    count = 5
    half = weights[0].shape[2]
    place_small(cast[0], norm[...], head[...], ffn[...], 0.0)
    for part in range(3):
        cast[1][:, part * half:(part + 1) * half] = weights[0][:, part, :].astype(BF)
    value = weights[1][...]
    held = cast[2].shape[0]
    cast[2][...] = jnp.concatenate(
        [value, jnp.zeros((held - value.shape[0], value.shape[1]), F32)], 0).astype(BF)
    cast[3][...] = weights[2][...].astype(BF)
    cast[4][...] = weights[3][...].astype(BF)
    place = Place()
    greet(place)
    paths, base = [], 0
    locals_ = []
    for index in range(count):
        own = pltpu.make_async_copy(
            cast[index], fulls[index].at[place.m, place.z, place.y, place.x], local.at[index])
        own.start()
        locals_.append(own)
        group = []
        for part in column_parts(cast[index].shape[1]):
            group.append(Gatherer(place, cast[index], fulls[index], part, (send, recv), base))
            base += 16
        for path in group:
            path.start(0)
        paths.append(group)
    for own in locals_:
        own.wait()
    sums[...] = weight_sums_of(weights, cast[0][...])
    for turn in range(count + 3):
        for index in range(count):
            stage = turn - index + 1
            if 1 <= stage <= 3:
                for path in paths[index]:
                    path.arrived(stage - 1)
                    path.start(stage)
    for group in paths:
        for path in group:
            path.arrived(3)
    for group in paths:
        for path in group:
            path.finish()


def gather(weights, vectors):
    qkv, out, up, down = weights
    held = [(16, 128), (qkv.shape[0], 3 * qkv.shape[2]), (32, out.shape[1]), up.shape, down.shape]
    kinds = [F32, BF, BF, BF, BF]
    slots = 16 * sum(len(column_parts(h[1])) for h in held)
    vmem = pl.BlockSpec(memory_space=pltpu.VMEM)
    return pl.pallas_call(
        gather_kernel,
        out_shape=[jax.ShapeDtypeStruct((2, 4, 2, 2) + h, k) for h, k in zip(held, kinds)]
        + [jax.ShapeDtypeStruct((8, 128), F32)],
        in_specs=[vmem] * 7,
        out_specs=[pl.BlockSpec(memory_space=pl.ANY)] * 5 + [vmem],
        scratch_shapes=[pltpu.VMEM(h, k) for h, k in zip(held, kinds)] + [
            pltpu.SemaphoreType.DMA((slots,)),
            pltpu.SemaphoreType.DMA((slots,)),
            pltpu.SemaphoreType.DMA((5,)),
        ],
        compiler_params=pltpu.CompilerParams(
            collective_id=0, has_side_effects=True, vmem_limit_bytes=48 << 20),
        name="gather_weights",
    )(*weights, *vectors)


class Scatterer:
    def __init__(self, place, held, part, slots, sems, base):
        order, start, width = part
        self.place, self.held = place, held
        self.order = order[::-1]
        self.start_col, self.width = start, width
        self.cols = pl.ds(start, width)
        self.slots = slots
        self.sems, self.base = sems, base

    def view(self, spot):
        return self.held.at[spot["z"], spot["y"], spot["x"], :, self.cols]

    def copies(self, stage):
        place, axis = self.place, self.order[stage]
        out = []
        for step in steps_of(axis):
            spot = {"z": EVERY, "y": EVERY, "x": EVERY}
            for done in self.order[:stage]:
                spot[done] = getattr(place, done)
            target = place.at(axis, step)
            spot[axis] = target[axis]
            send, recv = self.sems
            slot = self.base + 4 * stage + step
            land = self.slots[stage].at[step - 1]
            out.append(pltpu.make_async_remote_copy(
                self.view(spot), land, send.at[slot], recv.at[slot],
                device_id=place.device(target), device_id_type=MESH))
        return out

    def start(self, stage):
        for sent in self.copies(stage):
            sent.start()

    def add(self, stage, result=None):
        place, axis = self.place, self.order[stage]
        for sent in self.copies(stage):
            sent.wait_recv()
        left = [name for name in "zyx" if name not in self.order[:stage + 1]]
        sizes = [4 if name == "z" else 2 for name in left]
        total = 1
        for size in sizes:
            total *= size
        slots = self.slots[stage]
        arrivals = len(steps_of(axis))

        def one(index):
            spot = {name: getattr(place, name) for name in "zyx"}
            inner = []
            rest = index
            for name, size in reversed(list(zip(left, sizes))):
                spot[name] = rest % size
                inner.insert(0, rest % size)
                rest = rest // size
            where = (spot["z"], spot["y"], spot["x"], EVERY, self.cols)
            value = self.held[where].astype(F32)
            for arrival in range(arrivals):
                value = value + slots[tuple([arrival] + inner)].astype(F32)
            if result is None:
                self.held[where] = value.astype(self.held.dtype)
            else:
                result[:, self.cols] = value[:result.shape[0]]

        if total == 1:
            one(0)
        else:
            pl.loop(0, total)(one)

    def finish(self):
        for stage in range(3):
            for sent in self.copies(stage):
                sent.wait_send()


def slot_shapes(part, rows):
    order, _, width = part
    order = order[::-1]
    shapes = []
    for stage in range(3):
        left = [4 if name == "z" else 2 for name in "zyx" if name not in order[:stage + 1]]
        shapes.append((len(steps_of(order[stage])), *left, rows, width))
    return shapes


def to_column(row):
    count = row.shape[1]
    here = lax.broadcasted_iota(jnp.int32, (count, count), 0)
    there = lax.broadcasted_iota(jnp.int32, (count, count), 1)
    return jnp.sum(jnp.where(here == there, row, 0.0), axis=1, keepdims=True)


def to_row(column):
    count = column.shape[0]
    here = lax.broadcasted_iota(jnp.int32, (count, count), 0)
    there = lax.broadcasted_iota(jnp.int32, (count, count), 1)
    return jnp.sum(jnp.where(here == there, column, 0.0), axis=0, keepdims=True)


def put_line(ref, line, row):
    for tile in range(row.shape[1] // 128):
        ref[line + tile:line + tile + 1, :] = row[:, tile * 128:(tile + 1) * 128]


def get_line(ref, line, width):
    tiles = width // 128
    return jnp.concatenate([ref[line + t:line + t + 1, :] for t in range(tiles)], axis=1)


def scalars(values):
    lane = lax.broadcasted_iota(jnp.int32, (8, 128), 1)
    out = jnp.zeros((8, 128), F32)
    for index, value in enumerate(values):
        out = jnp.where(lane == index, value, out)
    return out


def all_sum(values):
    return jnp.sum(jnp.sum(values, axis=1, keepdims=True), axis=0, keepdims=True)


class Exchange:
    def __init__(self, place, mine, land, sems, base):
        self.place, self.mine, self.land = place, mine, land
        self.sems, self.base = sems, base
        self.sent = []

    def swap(self, stage, axis):
        place = self.place
        send, recv = self.sems
        own = place.z if axis == "z" else 0
        for step in steps_of(axis):
            slot = self.base + 4 * stage + step
            copy = pltpu.make_async_remote_copy(
                self.mine.at[stage], self.land.at[stage, own], send.at[slot], recv.at[slot],
                device_id=place.device(place.at(axis, step)), device_id_type=MESH)
            copy.start()
            self.sent.append(copy)
        if axis == "z":
            self.land[stage, place.z] = self.mine[stage]
        for step in steps_of(axis):
            slot = self.base + 4 * stage + step
            spot = (place.z - step) % 4 if axis == "z" else 0
            pltpu.make_async_remote_copy(
                self.mine.at[stage], self.land.at[stage, spot], send.at[slot], recv.at[slot],
                device_id=place.device(place.at(axis, step)), device_id_type=MESH).wait_recv()
        if axis == "z":
            land = self.land
            return (land[stage, 0] + land[stage, 1]) + (land[stage, 2] + land[stage, 3])
        return self.mine[stage] + self.land[stage, 0]

    def finish(self):
        for copy in self.sent:
            copy.wait_send()


def add_up(exchange, value, picked=None):
    exchange.mine[0] = value
    total = exchange.swap(0, "m")
    if picked is not None:
        total = jnp.where(picked, total, value)
    for stage, axis in ((1, "x"), (2, "y"), (3, "z")):
        exchange.mine[stage] = total
        total = exchange.swap(stage, axis)
    return total


QKV_LINE, UP_LINE, OUT_LINE, DOWN_LINE, ROW_LINE = 0, 9, 21, 27, 33
LINES = 40
WIDTHS = (3 * D // 2, D, FF // 2, D)
COL_LINES = (QKV_LINE, OUT_LINE, UP_LINE, DOWN_LINE)
COL_COUNT = (3 * D, D, FF, D)
ROW_COUNT = (D, D, D, FF)


def new_rows_cols(grads, rows_old, cols_old, lines):
    rows_new, cols_new = [], []
    for index in range(4):
        if index in (0, 2):
            line = ROW_LINE + index // 2
            count = rows_old[index].shape[1]
            row_sum = to_column(lines[line:line + 1, :count])
        else:
            grad = grads[index][...]
            row_sum = jnp.sum(grad * grad + EPS_SQUARE, axis=1, keepdims=True)
        rows_new.append(
            DECAY * to_column(rows_old[index][...]) + (1.0 - DECAY) * row_sum / COL_COUNT[index])
        col_sum = get_line(lines, COL_LINES[index], WIDTHS[index])
        if index == 0:
            old = cols_old[0]
            old = jnp.concatenate([old[0:1, :], old[1:2, :], old[2:3, :]], axis=1)
        else:
            old = cols_old[index][...]
        cols_new.append(DECAY * old + (1.0 - DECAY) * col_sum / ROW_COUNT[index])
    return rows_new, cols_new


def place_small(ref, norm, head, ffn, fill):
    ref[...] = jnp.full(ref.shape, fill, F32)
    ref[0:6, 0:norm.shape[1]] = norm
    ref[6:8, 0:head.shape[1]] = head
    ref[8:9, 0:ffn.shape[1]] = ffn


def small_update(grad, old):
    second = DECAY * old + (1.0 - DECAY) * (grad * grad + EPS_SQUARE)
    return second, grad * lax.rsqrt(second)


def small_sums(values):
    line = lax.broadcasted_iota(jnp.int32, values.shape, 0)
    square = values * values
    return [
        all_sum(jnp.where((line >= 6) & (line < 8), square, 0.0)),
        all_sum(jnp.where(line == 8, square, 0.0)),
        all_sum(jnp.where(line < 6, square, 0.0)),
    ]


def scatter_kernel(count, parts, *refs):
    refs = list(refs)
    take = lambda number: [refs.pop(0) for _ in range(number)]
    fulls = take(count)
    rows_old, cols_old = take(4), take(4)
    head_sq, ffn_sq, norm_sq, weight_sums = take(4)
    results = take(count)
    lines, totals = take(2)
    held, other = take(count), take(count)
    slots = [[take(3) for _ in parts[index]] for index in range(count)]
    mine_one, land_one, mine_two, land_two, old_small = take(5)
    send, recv, local = refs
    place = Place()
    greet(place)
    partner = place.device(place.at("m", 1))
    base = 0
    groups, swaps, owns = [], [], []
    for index in range(count):
        swap = pltpu.make_async_remote_copy(
            fulls[index].at[1 - place.m], other[index], send.at[base], recv.at[base],
            device_id=partner, device_id_type=MESH)
        swap.start()
        own = pltpu.make_async_copy(fulls[index].at[place.m], held[index], local.at[index])
        own.start()
        swaps.append(swap)
        owns.append(own)
        base += 1
        group = []
        for number, part in enumerate(parts[index]):
            group.append(Scatterer(place, held[index], part, slots[index][number], (send, recv), base))
            base += 12
        groups.append(group)
    for turn in range(count + 3):
        for index in range(count):
            stage = turn - index
            if stage == 0:
                owns[index].wait()
                swaps[index].wait_recv()

                @pl.loop(0, 16)
                def _(block):
                    where = (block // 4, (block // 2) % 2, block % 2)
                    held[index][where] = (
                        held[index][where].astype(F32) + other[index][where].astype(F32)
                    ).astype(held[index].dtype)

                for path in groups[index]:
                    path.start(0)
            elif 1 <= stage <= 3:
                for path in groups[index]:
                    path.add(stage - 1, results[index] if stage == 3 else None)
                    if stage < 3:
                        path.start(stage)
    small, grads = results[0], results[1:]
    lines[...] = jnp.zeros(lines.shape, F32)
    for index in range(4):
        grad = grads[index][...]
        square = grad * grad + EPS_SQUARE
        put_line(lines, COL_LINES[index], jnp.sum(square, axis=0, keepdims=True))
        if index in (0, 2):
            line = ROW_LINE + index // 2
            lines[line:line + 1, 0:grad.shape[0]] = to_row(jnp.sum(square, axis=1, keepdims=True))
    first = Exchange(place, mine_one, land_one, (send, recv), base)
    line = lax.broadcasted_iota(jnp.int32, lines.shape, 0)
    value = lines[...]
    first.mine[0] = value
    paired = jnp.where(line >= OUT_LINE, first.swap(0, "m"), value)
    total = paired
    for stage, axis in ((1, "x"), (2, "y"), (3, "z")):
        first.mine[stage] = total
        total = first.swap(stage, axis)
    lines[...] = jnp.where(line >= ROW_LINE, paired, total)
    rows_new, cols_new = new_rows_cols(grads, rows_old, cols_old, lines)
    ratios, row_totals = [], []
    for index in range(4):
        grad = grads[index][...]
        scaled = jnp.sum(grad * grad * (1.0 / cols_new[index]), axis=1, keepdims=True)
        ratios.append(jnp.sum(scaled / rows_new[index], axis=0, keepdims=True))
        share = 0.5 if index in (0, 2) else 1.0
        row_totals.append(jnp.sum(rows_new[index], axis=0, keepdims=True) * share)
    place_small(old_small, norm_sq[...], head_sq[...], ffn_sq[...], 1.0)
    _, update = small_update(small[...], old_small[...])
    second = Exchange(place, mine_two, land_two, (send, recv), base + 16)
    totals[...] = add_up(
        second, scalars(ratios + row_totals + small_sums(update)) + weight_sums[...])
    for index in range(count):
        swaps[index].wait_send()
        for path in groups[index]:
            path.finish()
    first.finish()
    second.finish()


def scatter(fulls, rows, rows_old, cols_old, squares, weight_sums):
    count = len(fulls)
    parts = [column_parts(f.shape[-1]) for f in fulls]
    slots = []
    for full, own in zip(fulls, parts):
        for part in own:
            slots += [pltpu.VMEM(s, full.dtype) for s in slot_shapes(part, full.shape[-2])]
    sems = sum(1 + 12 * len(own) for own in parts) + 32
    vmem = pl.BlockSpec(memory_space=pltpu.VMEM)
    outs = [jax.ShapeDtypeStruct((r, f.shape[-1]), F32) for r, f in zip(rows, fulls)]
    outs += [jax.ShapeDtypeStruct((LINES, 128), F32), jax.ShapeDtypeStruct((8, 128), F32)]
    return pl.pallas_call(
        functools.partial(scatter_kernel, count, parts),
        out_shape=outs,
        in_specs=[pl.BlockSpec(memory_space=pl.ANY)] * count + [vmem] * 12,
        out_specs=[vmem] * len(outs),
        scratch_shapes=[pltpu.VMEM(f.shape[1:], f.dtype) for f in fulls] * 2 + slots + [
            pltpu.VMEM((4, LINES, 128), F32),
            pltpu.VMEM((4, 4, LINES, 128), F32),
            pltpu.VMEM((4, 8, 128), F32),
            pltpu.VMEM((4, 4, 8, 128), F32),
            pltpu.VMEM((16, 128), F32),
            pltpu.SemaphoreType.DMA((sems,)),
            pltpu.SemaphoreType.DMA((sems,)),
            pltpu.SemaphoreType.DMA((count,)),
        ],
        compiler_params=pltpu.CompilerParams(
            collective_id=1, has_side_effects=True, vmem_limit_bytes=56 << 20),
        name="scatter_grads",
    )(*fulls, *rows_old, *cols_old, *squares, weight_sums)


def step_kernel(*refs):
    refs = list(refs)
    take = lambda number: [refs.pop(0) for _ in range(number)]
    grads = take(4)
    small, lines, totals = take(3)
    weights, rows_old, cols_old = take(4), take(4), take(4)
    head, ffn, norm, head_sq, ffn_sq, norm_sq = take(6)
    grads_out = take(4)
    head_grad, ffn_grad, norm_grad = take(3)
    rows_out, cols_out = take(4), take(4)
    head_second, ffn_second, norm_second = take(3)
    weights_out = take(4)
    head_new, ffn_new, norm_new = take(3)
    old_small, weight_small = refs
    half = D // 2
    rows_new, cols_new = new_rows_cols(grads, rows_old, cols_old, lines)
    total = lambda lane: totals[0:1, lane:lane + 1]
    for index in range(4):
        rows_out[index][...] = to_row(rows_new[index])
        if index == 0:
            for part in range(3):
                cols_out[0][part:part + 1, :] = cols_new[0][:, part * half:(part + 1) * half]
        else:
            cols_out[index][...] = cols_new[index]
        entries = ROW_COUNT[index] * COL_COUNT[index]
        row_mean = total(4 + index) / ROW_COUNT[index]
        update_rms = jnp.sqrt(row_mean * total(index) / entries)
        stride = (
            RATE * jnp.sqrt(total(11 + index) / entries) / jnp.maximum(1.0, update_rms / CLIP))
        scale_rows = lax.rsqrt(rows_new[index] / row_mean) * stride
        scale_cols = lax.rsqrt(cols_new[index])
        if index == 0:
            for part in range(3):
                cut = slice(part * half, (part + 1) * half)
                grad = grads[0][:, cut]
                grads_out[0][:, part, :] = grad
                weights_out[0][:, part, :] = (
                    weights[0][:, part, :] - grad * scale_rows * scale_cols[:, cut])
        else:
            grad = grads[index][...]
            grads_out[index][...] = grad
            weights_out[index][...] = weights[index][...] - grad * scale_rows * scale_cols
    place_small(old_small, norm_sq[...], head_sq[...], ffn_sq[...], 1.0)
    place_small(weight_small, norm[...], head[...], ffn[...], 0.0)
    grad = small[...]
    second, update = small_update(grad, old_small[...])
    line = lax.broadcasted_iota(jnp.int32, grad.shape, 0)
    counts = (2 * D, FF, 6 * D)
    strides = []
    for index in range(3):
        update_rms = jnp.sqrt(total(8 + index) / counts[index])
        strides.append(
            RATE * jnp.sqrt(total(15 + index) / counts[index])
            / jnp.maximum(1.0, update_rms / CLIP))
    stride = jnp.where(line < 6, strides[2], jnp.where(line < 8, strides[0], strides[1]))
    fresh = weight_small[...] - stride * update
    for values, (norm_ref, head_ref, ffn_ref) in (
        (grad, (norm_grad, head_grad, ffn_grad)),
        (second, (norm_second, head_second, ffn_second)),
        (fresh, (norm_new, head_new, ffn_new)),
    ):
        norm_ref[...] = values[0:6, 0:norm_ref.shape[1]]
        head_ref[...] = values[6:8, 0:head_ref.shape[1]]
        ffn_ref[...] = values[8:9, 0:ffn_ref.shape[1]]


def step(reduced, lines, totals, weights, rows_old, cols_old, vectors, squares):
    vmem = pl.BlockSpec(memory_space=pltpu.VMEM)
    small, grads = reduced[0], reduced[1:]
    shapes = [w.shape for w in weights] + [v.shape for v in vectors]
    shapes += [r.shape for r in rows_old] + [c.shape for c in cols_old]
    shapes += [v.shape for v in vectors] + [w.shape for w in weights] + [v.shape for v in vectors]
    operands = [*grads, small, lines, totals, *weights, *rows_old, *cols_old, *vectors, *squares]
    return pl.pallas_call(
        step_kernel,
        out_shape=[jax.ShapeDtypeStruct(s, F32) for s in shapes],
        in_specs=[vmem] * len(operands),
        out_specs=[vmem] * len(shapes),
        scratch_shapes=[pltpu.VMEM((16, 128), F32), pltpu.VMEM((16, 128), F32)],
        compiler_params=pltpu.CompilerParams(vmem_limit_bytes=32 << 20),
        name="adafactor_step",
    )(*operands)


HALF = D // 2
QKV_HALF = 3 * HALF
VMEM = pl.BlockSpec(memory_space=pltpu.VMEM)
SMEM = pl.BlockSpec(memory_space=pltpu.SMEM)


def dot(a, b):
    return jnp.dot(a, b, preferred_element_type=F32)


def dot_last(a, b):
    return lax.dot_general(a, b, (((1,), (1,)), ((), ())), preferred_element_type=F32)


def dot_first(a, b):
    return lax.dot_general(a, b, (((0,), (0,)), ((), ())), preferred_element_type=F32)


def ids_at(lengths, row, places):
    bound = jnp.int32(0)
    ids = jnp.zeros(places.shape, jnp.int32)
    for segment in range(SEGS):
        bound = bound + lengths[row, segment]
        ids = ids + (places >= bound).astype(jnp.int32)
    return ids


def set_bias(bias, lengths, row):
    down = ids_at(lengths, row, lax.broadcasted_iota(jnp.int32, (LEN, 1), 0))
    across = ids_at(lengths, row, lax.broadcasted_iota(jnp.int32, (1, LEN), 1))
    bias[...] = jnp.where(down == across, 0.0, -1e30)


def half_masks():
    lane = lax.broadcasted_iota(jnp.int32, (1, 128), 1)
    return [((lane // HD) == half).astype(F32).astype(BF) for half in range(2)]


def slab(ref, core, row, part, pair):
    return ref[core, pl.ds(pl.multiple_of(row * LEN, LEN), LEN),
               pl.ds(pl.multiple_of(part * HALF + pair * 128, 128), 128)]


def project(tokens, weight, offsets, qkv, row):
    rows = pl.ds(pl.multiple_of(row * LEN, LEN), LEN)
    values = tokens[rows, :]
    for core in range(2):
        for part in range(3):
            cut = slice(part * HALF, (part + 1) * HALF)
            out = (dot(values, weight[core, :, cut]) + offsets[core, :, cut]).astype(BF)
            if part == 0:
                out = out * jnp.asarray(HD ** -0.5, BF)
            qkv[core, rows, cut] = out


def attend(qkv, bias, context, lse, held, row):
    rows = pl.ds(pl.multiple_of(row * LEN, LEN), LEN)
    lane = lax.broadcasted_iota(jnp.int32, (LEN, 128), 1)
    held[...] = jnp.zeros(held.shape, F32)

    @pl.loop(0, 6)
    def _(item):
        core, pair = item // 3, item % 3
        queries, keys, values = (slab(qkv, core, row, part, pair) for part in range(3))
        wide = jnp.concatenate([values, jnp.ones_like(values)], axis=1)
        outs = []
        logs = held[...]
        for half, mask in enumerate(half_masks()):
            scores = dot_last(queries * mask, keys) + bias[...]
            peak = jnp.max(scores, axis=1, keepdims=True)
            raised = jnp.exp(scores - peak).astype(BF)
            both = dot(raised, wide)
            total = both[:, 128:]
            outs.append(both[:, :128] / total)
            logs = jnp.where(lane == item * 2 + half, peak + jnp.log(total), logs)
        held[...] = logs
        context[rows, pl.ds(pl.multiple_of(item * 128, 128), 128)] = jnp.where(
            lane < HD, outs[0], outs[1]).astype(BF)

    lse[row] = held[...].T[0:16, :]


def forward_kernel(tokens, weight, offsets, lengths, qkv, context, lse, bias, held):
    core = lax.axis_index("mp")

    @pl.loop(0, 2)
    def _(row):
        set_bias(bias, lengths, core * 2 + row)
        project(tokens, weight, offsets, qkv, row)
        attend(qkv, bias, context, lse, held, row)


def forward(tokens, weight, offsets, lengths):
    count = tokens.shape[0]
    return pl.pallas_call(
        forward_kernel,
        out_shape=[
            jax.ShapeDtypeStruct((2, count, QKV_HALF), BF),
            jax.ShapeDtypeStruct((count, D), BF),
            jax.ShapeDtypeStruct((count // LEN, 16, LEN), F32),
        ],
        in_specs=[VMEM, VMEM, VMEM, SMEM],
        out_specs=[VMEM] * 3,
        scratch_shapes=[pltpu.VMEM((LEN, LEN), F32), pltpu.VMEM((LEN, 128), F32)],
        compiler_params=pltpu.CompilerParams(vmem_limit_bytes=56 << 20),
        name="project_attend",
    )(tokens, weight, offsets, lengths)


def gelu_both(inner):
    cdf = 0.5 * (1.0 + lax.erf(inner * 0.7071067811865476))
    density = 0.3989422804014327 * jnp.exp(-0.5 * inner * inner)
    return inner * cdf, cdf + inner * density


def norm_parts(values):
    center = values - jnp.mean(values, axis=-1, keepdims=True)
    scale = lax.rsqrt(jnp.mean(center * center, axis=-1, keepdims=True) + EPS_NORM)
    return center * scale, scale


def norm_back(grad, normed, scale, gain):
    scaled = grad * gain
    mean = jnp.mean(scaled, axis=-1, keepdims=True)
    along = jnp.mean(scaled * normed, axis=-1, keepdims=True)
    return (
        (scaled - mean - normed * along) * scale,
        jnp.sum(grad * normed, axis=0, keepdims=True),
        jnp.sum(grad, axis=0, keepdims=True),
    )


CHUNK = 512


def middle(row, core, tokens, context, cotangent, lengths, w_out, w_up, w_down, ffn, norm, layer_out,
           pooled, hidden_b, act, grad_branch, grad_inner, grad_attended, grad_context,
           grad_one, delta, norm_sums, ffn_sums, slope, branch, hidden, normed_one, grad_two):
    rows = pl.ds(pl.multiple_of(row * LEN, LEN), LEN)
    attended = dot(context[rows, :], w_out[...]) + norm[0:1, :]
    normed, scale_one = norm_parts(tokens[rows, :].astype(F32) + attended)
    normed_one[...] = normed
    value = normed * norm[2:3, :] + norm[3:4, :]
    hidden[...] = value
    hidden_b[rows, :] = value.astype(BF)
    branch[...] = jnp.zeros(branch.shape, F32)
    for chunk in range(FF // CHUNK):
        core_of, start = chunk * CHUNK // (FF // 2), chunk * CHUNK % (FF // 2)
        cols = slice(chunk * CHUNK, (chunk + 1) * CHUNK)
        up = w_up[core_of, :, start:start + CHUNK]
        value, slope_value = gelu_both(dot(hidden_b[rows, :], up) + ffn[:, cols])
        value = value.astype(BF)
        act[rows, cols] = value
        slope[:, cols] = slope_value.astype(BF)
        branch[...] += dot(value, w_down[cols, :])
    normed, scale = norm_parts(hidden[...] + branch[...] + norm[1:2, :])
    output = normed * norm[4:5, :] + norm[5:6, :]
    high = output.astype(BF)
    layer_out[rows, :] = high
    low = (output - high.astype(F32)).astype(BF)
    place = lax.broadcasted_iota(jnp.int32, (SEGS, LEN), 1)
    segment = lax.broadcasted_iota(jnp.int32, (SEGS, 1), 0)
    ids = ids_at(lengths, core * 2 + row, place)
    member = (ids == segment).astype(F32)
    sizes = jnp.sum(member, axis=1, keepdims=True)
    member = member.astype(BF)
    pooled[row] = (dot(member, high) + dot(member, low)) / sizes
    back, gain, shift = norm_back(cotangent[rows, :].astype(F32), normed, scale, norm[4:5, :])
    norm_sums[4:5, :] += gain
    norm_sums[5:6, :] += shift
    grad_two[...] = back
    back = back.astype(BF)
    grad_branch[rows, :] = back
    norm_sums[1:2, :] += jnp.sum(back.astype(F32), axis=0, keepdims=True)
    for chunk in range(FF // CHUNK):
        core_of, start = chunk * CHUNK // (FF // 2), chunk * CHUNK % (FF // 2)
        cols = slice(chunk * CHUNK, (chunk + 1) * CHUNK)
        value = dot_last(grad_branch[rows, :], w_down[cols, :])
        value = (value * slope[:, cols].astype(F32)).astype(BF)
        grad_inner[rows, cols] = value
        ffn_sums[:, cols] += jnp.sum(value.astype(F32), axis=0, keepdims=True)
        grad_two[...] += dot_last(value, w_up[core_of, :, start:start + CHUNK])
    back, gain, shift = norm_back(grad_two[...], normed_one[...], scale_one, norm[2:3, :])
    norm_sums[2:3, :] += gain
    norm_sums[3:4, :] += shift
    grad_one[rows, :] = back
    back = back.astype(BF)
    grad_attended[rows, :] = back
    norm_sums[0:1, :] += jnp.sum(back.astype(F32), axis=0, keepdims=True)
    back = dot_last(back, w_out[...]).astype(BF)
    grad_context[rows, :] = back
    product = back.astype(F32) * context[rows, :].astype(F32)
    high = product.astype(BF)
    low = (product - high.astype(F32)).astype(BF)
    head = lax.broadcasted_iota(jnp.int32, (16, D), 0)
    member = (lax.broadcasted_iota(jnp.int32, (16, D), 1) // HD == head).astype(F32).astype(BF)
    delta[row] = dot_last(member, high) + dot_last(member, low)


def middle_kernel(*refs):
    core = lax.axis_index("mp")
    norm_sums, ffn_sums = refs[19], refs[20]
    norm_sums[...] = jnp.zeros(norm_sums.shape, F32)
    ffn_sums[...] = jnp.zeros(ffn_sums.shape, F32)

    @pl.loop(0, 2)
    def _(row):
        middle(row, core, *refs)


def middle_call(tokens, context, cotangent, lengths, w_out, w_up, w_down, ffn, norm):
    count = tokens.shape[0]
    shape = jax.ShapeDtypeStruct
    return pl.pallas_call(
        middle_kernel,
        out_shape=[
            shape((count, D), BF),
            shape((count // LEN, SEGS, D), F32),
            shape((count, D), BF),
            shape((count, FF), BF),
            shape((count, D), BF),
            shape((count, FF), BF),
            shape((count, D), BF),
            shape((count, D), BF),
            shape((count, D), F32),
            shape((count // LEN, 16, LEN), F32),
            shape((8, D), F32),
            shape((1, FF), F32),
        ],
        in_specs=[VMEM] * 3 + [SMEM] + [VMEM] * 5,
        out_specs=[VMEM] * 12,
        scratch_shapes=[
            pltpu.VMEM((LEN, FF), BF),
            pltpu.VMEM((LEN, D), F32),
            pltpu.VMEM((LEN, D), F32),
            pltpu.VMEM((LEN, D), F32),
            pltpu.VMEM((LEN, D), F32),
        ],
        compiler_params=pltpu.CompilerParams(vmem_limit_bytes=60 << 20),
        name="feed_forward",
    )(tokens, context, cotangent, lengths, w_out, w_up, w_down, ffn, norm)


def weight_grads_kernel(context, hidden_b, act, grad_branch, grad_inner, grad_attended,
                        out_grad, up_grad, down_grad, flipped):
    flipped[...] = hidden_b[...].T

    @pl.loop(0, FF // CHUNK)
    def _(chunk):
        half_chunks = FF // 2 // CHUNK
        cols = pl.ds(pl.multiple_of(chunk * CHUNK, CHUNK), CHUNK)
        local = pl.ds(pl.multiple_of((chunk % half_chunks) * CHUNK, CHUNK), CHUNK)
        up_grad[chunk // half_chunks, :, local] = dot(flipped[...], grad_inner[:, cols]).astype(BF)
        down_grad[cols, :] = dot_first(act[:, cols], grad_branch[...]).astype(BF)

    flipped[...] = context[...].T
    value = dot(flipped[...], grad_attended[...])
    rows, held = D // out_grad.shape[0], out_grad.shape[1]
    for block in range(out_grad.shape[0]):
        piece = value[block * rows:(block + 1) * rows, :]
        if held > rows:
            piece = jnp.concatenate([piece, jnp.zeros((held - rows, D), F32)], axis=0)
        out_grad[block] = piece.astype(BF)


def weight_grads(context, hidden_b, act, grad_branch, grad_inner, grad_attended, blocks, held):
    shape = jax.ShapeDtypeStruct
    return pl.pallas_call(
        weight_grads_kernel,
        out_shape=[shape((blocks, held, D), BF), shape((2, D, FF // 2), BF), shape((FF, D), BF)],
        in_specs=[VMEM] * 6,
        out_specs=[VMEM] * 3,
        scratch_shapes=[pltpu.VMEM((D, context.shape[0]), BF)],
        compiler_params=pltpu.CompilerParams(vmem_limit_bytes=60 << 20),
        name="weight_grads",
    )(context, hidden_b, act, grad_branch, grad_inner, grad_attended)


def attend_back(qkv, grad_context, lse, delta, bias, grad_qkv, grad_head, row):
    rows = pl.ds(pl.multiple_of(row * LEN, LEN), LEN)
    lane = lax.broadcasted_iota(jnp.int32, (LEN, 128), 1)

    @pl.loop(0, 6)
    def _(item):
        core, pair = item // 3, item % 3
        queries, keys, values = (slab(qkv, core, row, part, pair) for part in range(3))
        wide = pl.ds(pl.multiple_of(item * 128, 128), 128)
        grad = grad_context[rows, wide]
        flipped = keys.T
        grads_k, grads_v, grads_q = [], [], []
        for half, mask in enumerate(half_masks()):
            head = item * 2 + half
            scores = dot_last(keys * mask, queries) + bias[...] - lse[row, pl.ds(head, 1), :]
            probs = jnp.exp(scores)
            grad_probs = dot_last(values * mask, grad)
            grad_scores = (probs * (grad_probs - delta[row, pl.ds(head, 1), :])).astype(BF)
            grads_v.append(dot(probs.astype(BF), grad))
            grads_k.append(dot(grad_scores, queries))
            grads_q.append(dot(flipped[half * HD:(half + 1) * HD, :], grad_scores))
        grad_q = (jnp.concatenate(grads_q, axis=0).T * HD ** -0.5).astype(BF)
        grad_k = jnp.where(lane < HD, grads_k[0], grads_k[1]).astype(BF)
        grad_v = jnp.where(lane < HD, grads_v[0], grads_v[1]).astype(BF)
        for part, value in enumerate((grad_q, grad_k, grad_v)):
            grad_qkv[core, rows, pl.ds(pl.multiple_of(part * HALF + pair * 128, 128), 128)] = value
        grad_head[0:1, wide] += jnp.sum(grad_q.astype(F32), axis=0, keepdims=True)
        grad_head[1:2, wide] += jnp.sum(grad_v.astype(F32), axis=0, keepdims=True)


def backward_kernel(tokens, qkv, grad_context, lse, delta, lengths, weight, grad_one,
                    qkv_grad, input_grad, grad_head, grad_qkv, bias, flipped):
    core = lax.axis_index("mp")
    grad_head[...] = jnp.zeros(grad_head.shape, F32)

    @pl.loop(0, 2)
    def _(row):
        set_bias(bias, lengths, core * 2 + row)
        attend_back(qkv, grad_context, lse, delta, bias, grad_qkv, grad_head, row)
        rows = pl.ds(pl.multiple_of(row * LEN, LEN), LEN)
        input_grad[rows, :] = (
            grad_one[rows, :]
            + dot_last(grad_qkv[0, rows, :], weight[0])
            + dot_last(grad_qkv[1, rows, :], weight[1])
        )

    flipped[...] = tokens[...].T
    for core_of in range(2):
        for part in range(3):
            cut = slice(part * HALF, (part + 1) * HALF)
            qkv_grad[core_of, :, cut] = dot(flipped[...], grad_qkv[core_of, :, cut]).astype(BF)


def backward(tokens, qkv, grad_context, lse, delta, lengths, weight, grad_one):
    count = tokens.shape[0]
    shape = jax.ShapeDtypeStruct
    return pl.pallas_call(
        backward_kernel,
        out_shape=[shape((2, D, QKV_HALF), BF), shape((count, D), F32), shape((2, D), F32)],
        in_specs=[VMEM] * 5 + [SMEM] + [VMEM] * 2,
        out_specs=[VMEM] * 3,
        scratch_shapes=[
            pltpu.VMEM((2, count, QKV_HALF), BF),
            pltpu.VMEM((LEN, LEN), F32),
            pltpu.VMEM((D, count), BF),
        ],
        compiler_params=pltpu.CompilerParams(vmem_limit_bytes=60 << 20),
        name="attend_back",
    )(tokens, qkv, grad_context, lse, delta, lengths, weight, grad_one)


def small_block(norm, head, ffn):
    wide = lambda v: jnp.pad(v, [(0, 0)] * (v.ndim - 1) + [(0, 128 - v.shape[-1])])
    block = jnp.concatenate([wide(norm), wide(head), wide(ffn)], axis=-2)
    return jnp.pad(block, [(0, 0)] * (block.ndim - 2) + [(0, 16 - block.shape[-2]), (0, 0)])


def gather_plain(weights, vectors):
    head, ffn, norm = vectors
    qkv, out, up, down = (w.astype(BF) for w in weights)
    full = []
    for shard in (small_block(norm, head, ffn), qkv.reshape(qkv.shape[0], -1), out, up, down):
        full.append(lax.all_gather(lax.all_gather(shard, "dp", axis=0), "mp", axis=0))
    return full


def scatter_plain(fulls):
    out = []
    for full in fulls:
        own = lax.psum_scatter(full.astype(F32), "mp", scatter_dimension=0)
        out.append(lax.psum_scatter(own, "dp", scatter_dimension=0))
    return out


def body(
    tokens, cotangent, seg_lengths, w_qkv, w_out, w_up, w_down, head_bias, ffn_bias, norm_bias,
    qkv_rows, qkv_cols, out_rows, out_cols, up_rows, up_cols, down_rows, down_cols,
    head_bias_sq, ffn_bias_sq, norm_sq,
):
    cores = lax.axis_size("mp")
    data = lax.axis_size("dp")
    rows_qkv = w_qkv.shape[0]
    fast = data == 16 and cores == 2
    weights = [w_qkv, w_out, w_up, w_down]
    vectors = [head_bias, ffn_bias.reshape(1, -1), norm_bias]
    if fast:
        *gathered, weight_sums = gather(weights, vectors)
        gathered = [g.reshape(cores, data, *g.shape[-2:]) for g in gathered]
        gathered[2] = gathered[2][:, :, :w_out.shape[0]]
    else:
        gathered = gather_plain(weights, vectors)
    small, qkv_g, out_g, up_g, down_g = gathered
    small = small.astype(BF).astype(F32)
    own_head, own_ffn, own_norm = head_bias.shape[1], ffn_bias.shape[0], norm_bias.shape[1]
    norm_full = small[:, :, 0:6, :own_norm].transpose(2, 1, 0, 3).reshape(6, D)
    head_full = small[:, :, 6:8, :own_head].transpose(2, 0, 1, 3).reshape(2, 2, 1, HALF)
    ffn_full = small[:, :, 8, :own_ffn].reshape(1, FF)
    offsets = jnp.concatenate([head_full[0], jnp.zeros_like(head_full[0]), head_full[1]], axis=-1)
    qkv_full = qkv_g.reshape(2, D, QKV_HALF)
    up_full = up_g.reshape(2, D, FF // 2)
    down_full = down_g.reshape(FF, D)
    out_full = out_g.reshape(D, D)
    norm_full = jnp.pad(norm_full, ((0, 2), (0, 0)))
    qkv, context, lse = forward(tokens, qkv_full, offsets, seg_lengths)
    (layer_out, pooled, hidden_b, act, grad_branch, grad_inner, grad_attended, grad_context,
     grad_one, delta, norm_sums, ffn_sums) = middle_call(
        tokens, context, cotangent, seg_lengths, out_full, up_full, down_full, ffn_full, norm_full)
    rows_out = w_out.shape[0]
    held = 32 if fast else rows_out
    grad_out, grad_up, grad_down = weight_grads(
        context, hidden_b, act, grad_branch, grad_inner, grad_attended, cores * data, held)
    grad_qkv, input_grad, grad_head = backward(
        tokens, qkv, grad_context, lse, delta, seg_lengths, qkv_full, grad_one)
    small_grads = small_block(
        norm_sums[:6].reshape(6, data, cores, -1).transpose(2, 1, 0, 3),
        grad_head.reshape(2, cores, data, -1).transpose(1, 2, 0, 3),
        ffn_sums.reshape(cores, data, 1, -1),
    )
    fulls = [
        small_grads,
        grad_qkv.reshape(cores, data, rows_qkv, QKV_HALF),
        grad_out.reshape(cores, data, held, D),
        grad_up.reshape(cores, data, rows_qkv, FF // 2),
        grad_down.reshape(cores, data, -1, D),
    ]
    if fast:
        fulls = [f.reshape(2, 4, 2, 2, *f.shape[-2:]) for f in fulls]
        rows_old = [v.reshape(1, -1) for v in (qkv_rows, out_rows, up_rows, down_rows)]
        cols_old = [qkv_cols] + [v.reshape(1, -1) for v in (out_cols, up_cols, down_cols)]
        old = [head_bias_sq, ffn_bias_sq.reshape(1, -1), norm_sq]
        *reduced, lines, totals = scatter(
            fulls, [16, rows_qkv, rows_out, rows_qkv, w_down.shape[0]],
            rows_old, cols_old, old, weight_sums)
        new = step(reduced, lines, totals, weights, rows_old, cols_old, vectors, old)
        grads, (g_head, g_ffn, g_norm) = new[:4], new[4:7]
        rows_new, cols_new = [r.reshape(-1) for r in new[7:11]], new[11:15]
        cols_new = [cols_new[0]] + [c.reshape(-1) for c in cols_new[1:]]
        (s_head, s_ffn, s_norm), mats = new[15:18], new[18:22]
        n_head, n_ffn, n_norm = new[22:25]
        stats = [v for pair in zip(rows_new, cols_new) for v in pair]
        return (
            layer_out, pooled, input_grad, *grads, g_head, g_ffn.reshape(-1), g_norm, *stats,
            s_head, s_ffn.reshape(-1), s_norm, *mats, n_head, n_ffn.reshape(-1), n_norm,
        )
    red_small, red_qkv, red_out, red_up, red_down = scatter_plain(fulls)
    norm_grad = red_small[0:6, :own_norm]
    red_head = red_small[6:8, :own_head]
    red_ffn = red_small[8, :own_ffn]
    weights_flat = [w_qkv.reshape(rows_qkv, -1), w_out, w_up, w_down]
    grads_flat = [red_qkv, red_out, red_up, red_down]
    rows_old = [qkv_rows, out_rows, up_rows, down_rows]
    cols_old = [qkv_cols.reshape(-1), out_cols, up_cols, down_cols]
    col_count = [3 * D, D, FF, D]
    row_count = [D, D, D, FF]
    row_share = [cores, 1, cores, 1]
    squares = [grad * grad + EPS_SQUARE for grad in grads_flat]
    row_parts = [jnp.sum(square, axis=1) for square in squares]
    col_parts = [jnp.sum(square, axis=0) for square in squares]
    vec_weights = [head_bias, ffn_bias, norm_bias]
    vec_grads = [red_head, red_ffn, norm_grad]
    vec_old = [head_bias_sq, ffn_bias_sq, norm_sq]
    vec_counts = [2 * D, FF, 6 * D]
    vec_second = [
        DECAY * old + (1.0 - DECAY) * (grad * grad + EPS_SQUARE)
        for old, grad in zip(vec_old, vec_grads)
    ]
    vec_update = [grad * lax.rsqrt(second) for grad, second in zip(vec_grads, vec_second)]
    weight_parts = [jnp.sum(weight * weight) for weight in weights_flat + vec_weights]
    vec_parts = [jnp.sum(update * update) for update in vec_update]
    row_qkv, row_up = lax.psum((row_parts[0], row_parts[2]), "mp")
    col_qkv, col_up = lax.psum((col_parts[0], col_parts[2]), "dp")
    col_out, col_down = lax.psum((col_parts[1], col_parts[3]), ("dp", "mp"))
    row_sums = [row_qkv, row_parts[1], row_up, row_parts[3]]
    col_sums = [col_qkv, col_out, col_up, col_down]
    rows_new = [
        DECAY * rows_old[index] + (1.0 - DECAY) * row_sums[index] / col_count[index]
        for index in range(4)
    ]
    cols_new = [
        DECAY * cols_old[index] + (1.0 - DECAY) * col_sums[index] / row_count[index]
        for index in range(4)
    ]
    ratio_parts = [
        jnp.sum(
            grads_flat[index]
            * grads_flat[index]
            / (rows_new[index][:, None] * cols_new[index][None, :])
        )
        for index in range(4)
    ]
    extra_parts = (
        [jnp.sum(rows_new[index]) / row_share[index] for index in range(4)]
        + weight_parts
        + vec_parts
    )
    totals = lax.psum(jnp.stack(ratio_parts + extra_parts), ("dp", "mp"))
    row_means = [totals[4 + index] / row_count[index] for index in range(4)]
    weight_totals = [totals[8 + index] for index in range(7)]
    vec_totals = [totals[15 + index] for index in range(3)]
    new_mats = []
    for index in range(4):
        entries = row_count[index] * col_count[index]
        estimate = rows_new[index][:, None] * cols_new[index][None, :] / row_means[index]
        update = grads_flat[index] / jnp.sqrt(estimate)
        update_rms = jnp.sqrt(row_means[index] * totals[index] / entries)
        stride = (
            RATE * jnp.sqrt(weight_totals[index] / entries) / jnp.maximum(1.0, update_rms / CLIP)
        )
        new_mats.append(weights_flat[index] - stride * update)
    new_vecs = []
    for index in range(3):
        update_rms = jnp.sqrt(vec_totals[index] / vec_counts[index])
        stride = (
            RATE
            * jnp.sqrt(weight_totals[4 + index] / vec_counts[index])
            / jnp.maximum(1.0, update_rms / CLIP)
        )
        new_vecs.append(vec_weights[index] - stride * vec_update[index])
    return (
        layer_out,
        pooled,
        input_grad,
        red_qkv.reshape(w_qkv.shape),
        red_out,
        red_up,
        red_down,
        red_head,
        red_ffn,
        norm_grad,
        rows_new[0],
        cols_new[0].reshape(qkv_cols.shape),
        rows_new[1],
        cols_new[1],
        rows_new[2],
        cols_new[2],
        rows_new[3],
        cols_new[3],
        vec_second[0],
        vec_second[1],
        vec_second[2],
        new_mats[0].reshape(w_qkv.shape),
        new_mats[1],
        new_mats[2],
        new_mats[3],
        new_vecs[0],
        new_vecs[1],
        new_vecs[2],
    )


def solution(mesh):
    return jax.shard_map(
        body,
        mesh=mesh,
        in_specs=(
            P(("dp", "mp"), None),
            P(("dp", "mp"), None),
            P("dp", None),
            P("dp", None, "mp"),
            P(("mp", "dp"), None),
            P("dp", "mp"),
            P(("mp", "dp"), None),
            P(None, ("mp", "dp")),
            P(("mp", "dp")),
            P(None, ("dp", "mp")),
            P("dp"),
            P(None, "mp"),
            P(("mp", "dp")),
            P(),
            P("dp"),
            P("mp"),
            P(("mp", "dp")),
            P(),
            P(None, ("mp", "dp")),
            P(("mp", "dp")),
            P(None, ("dp", "mp")),
        ),
        out_specs=(
            P(("dp", "mp"), None),
            P(("dp", "mp"), None, None),
            P(("dp", "mp"), None),
            P("dp", None, "mp"),
            P(("mp", "dp"), None),
            P("dp", "mp"),
            P(("mp", "dp"), None),
            P(None, ("mp", "dp")),
            P(("mp", "dp")),
            P(None, ("dp", "mp")),
            P("dp"),
            P(None, "mp"),
            P(("mp", "dp")),
            P(),
            P("dp"),
            P("mp"),
            P(("mp", "dp")),
            P(),
            P(None, ("mp", "dp")),
            P(("mp", "dp")),
            P(None, ("dp", "mp")),
            P("dp", None, "mp"),
            P(("mp", "dp"), None),
            P("dp", "mp"),
            P(("mp", "dp"), None),
            P(None, ("mp", "dp")),
            P(("mp", "dp")),
            P(None, ("dp", "mp")),
        ),
        check_vma=False,
    )
```

```python
import functools

import jax
import jax.numpy as jnp
from jax import lax
from jax.experimental import pallas as pl
from jax.experimental.pallas import tpu as pltpu
from jax.sharding import PartitionSpec as P

D = 768
HD = 64
FF = 3072
LEN = 512
SEGS = 8

EPS_NORM = 1e-12
EPS_SQUARE = 1e-30
DECAY = 0.5
RATE = 3.0
CLIP = 0.3

MESH = pl.DeviceIdType.MESH
BF = jnp.bfloat16
F32 = jnp.float32
EVERY = slice(None)


class Place:
    def __init__(self):
        d = lax.axis_index("dp")
        self.m = lax.axis_index("mp")
        self.z, self.y, self.x = d // 4, (d // 2) % 2, d % 2

    def at(self, axis, step):
        size = 4 if axis == "z" else 2
        spot = {"z": self.z, "y": self.y, "x": self.x, "m": self.m}
        spot[axis] = (spot[axis] + step) % size
        return spot

    @staticmethod
    def device(spot):
        return (spot["z"] * 4 + spot["y"] * 2 + spot["x"], spot["m"])


def steps_of(axis):
    return (1, 2, 3) if axis == "z" else (1,)


def greet(place):
    barrier = pltpu.get_barrier_semaphore()
    count = 0
    for axis in "zyxm":
        for step in steps_of(axis):
            pl.semaphore_signal(
                barrier, inc=1, device_id=place.device(place.at(axis, step)), device_id_type=MESH
            )
            count += 1
    pl.semaphore_wait(barrier, count)


def column_parts(cols):
    tiles = cols // 128
    first = tiles // 3
    parts = [("yzx", 0, first * 128)] if first else []
    return parts + [("zxy", first * 128, cols - first * 128)]


def weight_sums_of(weights, small):
    parts = []
    for weight in weights:
        value = weight[...]
        if value.ndim == 3:
            parts.append(sum(all_sum(value[:, part] * value[:, part]) for part in range(3)))
        else:
            parts.append(all_sum(value * value))
    return scalars([jnp.zeros((1, 1), F32)] * 11 + parts + small_sums(small))


class Scatterer:
    def __init__(self, place, held, part, slots, sems, base):
        order, start, width = part
        self.place, self.held = place, held
        self.order = order[::-1]
        self.start_col, self.width = start, width
        self.cols = pl.ds(start, width)
        self.slots = slots
        self.sems, self.base = sems, base

    def view(self, spot):
        return self.held.at[spot["z"], spot["y"], spot["x"], :, self.cols]

    def copies(self, stage):
        place, axis = self.place, self.order[stage]
        out = []
        for step in steps_of(axis):
            spot = {"z": EVERY, "y": EVERY, "x": EVERY}
            for done in self.order[:stage]:
                spot[done] = getattr(place, done)
            target = place.at(axis, step)
            spot[axis] = target[axis]
            send, recv = self.sems
            slot = self.base + 4 * stage + step
            land = self.slots[stage].at[step - 1]
            out.append(pltpu.make_async_remote_copy(
                self.view(spot), land, send.at[slot], recv.at[slot],
                device_id=place.device(target), device_id_type=MESH))
        return out

    def start(self, stage):
        for sent in self.copies(stage):
            sent.start()

    def add(self, stage, result=None):
        place, axis = self.place, self.order[stage]
        for sent in self.copies(stage):
            sent.wait_recv()
        left = [name for name in "zyx" if name not in self.order[:stage + 1]]
        sizes = [4 if name == "z" else 2 for name in left]
        total = 1
        for size in sizes:
            total *= size
        slots = self.slots[stage]
        arrivals = len(steps_of(axis))

        def one(index):
            spot = {name: getattr(place, name) for name in "zyx"}
            inner = []
            rest = index
            for name, size in reversed(list(zip(left, sizes))):
                spot[name] = rest % size
                inner.insert(0, rest % size)
                rest = rest // size
            where = (spot["z"], spot["y"], spot["x"], EVERY, self.cols)
            value = self.held[where].astype(F32)
            for arrival in range(arrivals):
                value = value + slots[tuple([arrival] + inner)].astype(F32)
            if result is None:
                self.held[where] = value.astype(self.held.dtype)
            else:
                result[:, self.cols] = value[:result.shape[0]]

        if total == 1:
            one(0)
        else:
            pl.loop(0, total)(one)

    def finish(self):
        for stage in range(3):
            for sent in self.copies(stage):
                sent.wait_send()


def slot_shapes(part, rows):
    order, _, width = part
    order = order[::-1]
    shapes = []
    for stage in range(3):
        left = [4 if name == "z" else 2 for name in "zyx" if name not in order[:stage + 1]]
        shapes.append((len(steps_of(order[stage])), *left, rows, width))
    return shapes


def to_column(row):
    count = row.shape[1]
    here = lax.broadcasted_iota(jnp.int32, (count, count), 0)
    there = lax.broadcasted_iota(jnp.int32, (count, count), 1)
    return jnp.sum(jnp.where(here == there, row, 0.0), axis=1, keepdims=True)


def to_row(column):
    count = column.shape[0]
    here = lax.broadcasted_iota(jnp.int32, (count, count), 0)
    there = lax.broadcasted_iota(jnp.int32, (count, count), 1)
    return jnp.sum(jnp.where(here == there, column, 0.0), axis=0, keepdims=True)


def put_line(ref, line, row):
    for tile in range(row.shape[1] // 128):
        ref[line + tile:line + tile + 1, :] = row[:, tile * 128:(tile + 1) * 128]


def get_line(ref, line, width):
    tiles = width // 128
    return jnp.concatenate([ref[line + t:line + t + 1, :] for t in range(tiles)], axis=1)


def scalars(values):
    lane = lax.broadcasted_iota(jnp.int32, (8, 128), 1)
    out = jnp.zeros((8, 128), F32)
    for index, value in enumerate(values):
        out = jnp.where(lane == index, value, out)
    return out


def all_sum(values):
    return jnp.sum(jnp.sum(values, axis=1, keepdims=True), axis=0, keepdims=True)


class Exchange:
    def __init__(self, place, mine, land, sems, base):
        self.place, self.mine, self.land = place, mine, land
        self.sems, self.base = sems, base
        self.sent = []

    def swap(self, stage, axis):
        place = self.place
        send, recv = self.sems
        own = place.z if axis == "z" else 0
        for step in steps_of(axis):
            slot = self.base + 4 * stage + step
            copy = pltpu.make_async_remote_copy(
                self.mine.at[stage], self.land.at[stage, own], send.at[slot], recv.at[slot],
                device_id=place.device(place.at(axis, step)), device_id_type=MESH)
            copy.start()
            self.sent.append(copy)
        if axis == "z":
            self.land[stage, place.z] = self.mine[stage]
        for step in steps_of(axis):
            slot = self.base + 4 * stage + step
            spot = (place.z - step) % 4 if axis == "z" else 0
            pltpu.make_async_remote_copy(
                self.mine.at[stage], self.land.at[stage, spot], send.at[slot], recv.at[slot],
                device_id=place.device(place.at(axis, step)), device_id_type=MESH).wait_recv()
        if axis == "z":
            land = self.land
            return (land[stage, 0] + land[stage, 1]) + (land[stage, 2] + land[stage, 3])
        return self.mine[stage] + self.land[stage, 0]

    def finish(self):
        for copy in self.sent:
            copy.wait_send()


def add_up(exchange, value, picked=None):
    exchange.mine[0] = value
    total = exchange.swap(0, "m")
    if picked is not None:
        total = jnp.where(picked, total, value)
    for stage, axis in ((1, "x"), (2, "y"), (3, "z")):
        exchange.mine[stage] = total
        total = exchange.swap(stage, axis)
    return total


QKV_LINE, UP_LINE, OUT_LINE, DOWN_LINE, ROW_LINE = 0, 9, 21, 27, 33
LINES = 40
WIDTHS = (3 * D // 2, D, FF // 2, D)
COL_LINES = (QKV_LINE, OUT_LINE, UP_LINE, DOWN_LINE)
COL_COUNT = (3 * D, D, FF, D)
ROW_COUNT = (D, D, D, FF)


def pair_cuts():
    out = []
    for pair in range(3):
        for part in range(3):
            start = (pair * 3 + part) * 128
            out.append(((slice(part, part + 1), slice(pair * 128, (pair + 1) * 128)),
                        slice(start, start + 128)))
    return out


def new_rows_cols(grads, rows_old, cols_old, lines):
    rows_new, cols_new = [], []
    for index in range(4):
        if index in (0, 2):
            line = ROW_LINE + index // 2
            count = rows_old[index].shape[1]
            row_sum = to_column(lines[line:line + 1, :count])
        else:
            grad = grads[index][...]
            row_sum = jnp.sum(grad * grad + EPS_SQUARE, axis=1, keepdims=True)
        rows_new.append(
            DECAY * to_column(rows_old[index][...]) + (1.0 - DECAY) * row_sum / COL_COUNT[index])
        col_sum = get_line(lines, COL_LINES[index], WIDTHS[index])
        if index == 0:
            old = jnp.concatenate([cols_old[0][at] for at, _ in pair_cuts()], axis=1)
        else:
            old = cols_old[index][...]
        cols_new.append(DECAY * old + (1.0 - DECAY) * col_sum / ROW_COUNT[index])
    return rows_new, cols_new


def place_small(ref, norm, head, ffn, fill):
    ref[...] = jnp.full(ref.shape, fill, F32)
    ref[0:6, 0:norm.shape[1]] = norm
    ref[6:8, 0:head.shape[1]] = head
    ref[8:9, 0:ffn.shape[1]] = ffn


def small_update(grad, old):
    second = DECAY * old + (1.0 - DECAY) * (grad * grad + EPS_SQUARE)
    return second, grad * lax.rsqrt(second)


def small_sums(values):
    line = lax.broadcasted_iota(jnp.int32, values.shape, 0)
    square = values * values
    return [
        all_sum(jnp.where((line >= 6) & (line < 8), square, 0.0)),
        all_sum(jnp.where(line == 8, square, 0.0)),
        all_sum(jnp.where(line < 6, square, 0.0)),
    ]


def scatter_kernel(count, parts, *refs):
    refs = list(refs)
    take = lambda number: [refs.pop(0) for _ in range(number)]
    fulls = take(count)
    rows_old, cols_old = take(4), take(4)
    head_sq, ffn_sq, norm_sq, weight_sums = take(4)
    results = take(count)
    lines, totals = take(2)
    held, other = take(count), take(count)
    slots = [[take(3) for _ in parts[index]] for index in range(count)]
    mine_one, land_one, mine_two, land_two, old_small = take(5)
    send, recv, local = refs
    place = Place()
    greet(place)
    partner = place.device(place.at("m", 1))
    base = 0
    groups, swaps, owns = [], [], []
    for index in range(count):
        swap = pltpu.make_async_remote_copy(
            fulls[index].at[1 - place.m], other[index], send.at[base], recv.at[base],
            device_id=partner, device_id_type=MESH)
        swap.start()
        own = pltpu.make_async_copy(fulls[index].at[place.m], held[index], local.at[index])
        own.start()
        swaps.append(swap)
        owns.append(own)
        base += 1
        group = []
        for number, part in enumerate(parts[index]):
            group.append(Scatterer(place, held[index], part, slots[index][number], (send, recv), base))
            base += 12
        groups.append(group)
    for turn in range(count + 3):
        for index in range(count):
            stage = turn - index
            if stage == 0:
                owns[index].wait()
                swaps[index].wait_recv()

                @pl.loop(0, 16)
                def _(block):
                    where = (block // 4, (block // 2) % 2, block % 2)
                    held[index][where] = (
                        held[index][where].astype(F32) + other[index][where].astype(F32)
                    ).astype(held[index].dtype)

                for path in groups[index]:
                    path.start(0)
            elif 1 <= stage <= 3:
                for path in groups[index]:
                    path.add(stage - 1, results[index] if stage == 3 else None)
                    if stage < 3:
                        path.start(stage)
    small, grads = results[0], results[1:]
    lines[...] = jnp.zeros(lines.shape, F32)
    for index in range(4):
        grad = grads[index][...]
        square = grad * grad + EPS_SQUARE
        put_line(lines, COL_LINES[index], jnp.sum(square, axis=0, keepdims=True))
        if index in (0, 2):
            line = ROW_LINE + index // 2
            lines[line:line + 1, 0:grad.shape[0]] = to_row(jnp.sum(square, axis=1, keepdims=True))
    first = Exchange(place, mine_one, land_one, (send, recv), base)
    line = lax.broadcasted_iota(jnp.int32, lines.shape, 0)
    value = lines[...]
    first.mine[0] = value
    paired = jnp.where(line >= OUT_LINE, first.swap(0, "m"), value)
    total = paired
    for stage, axis in ((1, "x"), (2, "y"), (3, "z")):
        first.mine[stage] = total
        total = first.swap(stage, axis)
    lines[...] = jnp.where(line >= ROW_LINE, paired, total)
    rows_new, cols_new = new_rows_cols(grads, rows_old, cols_old, lines)
    ratios, row_totals = [], []
    for index in range(4):
        grad = grads[index][...]
        scaled = jnp.sum(grad * grad * (1.0 / cols_new[index]), axis=1, keepdims=True)
        ratios.append(jnp.sum(scaled / rows_new[index], axis=0, keepdims=True))
        share = 0.5 if index in (0, 2) else 1.0
        row_totals.append(jnp.sum(rows_new[index], axis=0, keepdims=True) * share)
    place_small(old_small, norm_sq[...], head_sq[...], ffn_sq[...], 1.0)
    _, update = small_update(small[...], old_small[...])
    second = Exchange(place, mine_two, land_two, (send, recv), base + 16)
    totals[...] = add_up(
        second, scalars(ratios + row_totals + small_sums(update)) + weight_sums[...])
    for index in range(count):
        swaps[index].wait_send()
        for path in groups[index]:
            path.finish()
    first.finish()
    second.finish()


def scatter(fulls, rows, rows_old, cols_old, squares, weight_sums):
    count = len(fulls)
    parts = [column_parts(f.shape[-1]) for f in fulls]
    slots = []
    for full, own in zip(fulls, parts):
        for part in own:
            slots += [pltpu.VMEM(s, full.dtype) for s in slot_shapes(part, full.shape[-2])]
    sems = sum(1 + 12 * len(own) for own in parts) + 32
    vmem = pl.BlockSpec(memory_space=pltpu.VMEM)
    outs = [jax.ShapeDtypeStruct((r, f.shape[-1]), F32) for r, f in zip(rows, fulls)]
    outs += [jax.ShapeDtypeStruct((LINES, 128), F32), jax.ShapeDtypeStruct((8, 128), F32)]
    return pl.pallas_call(
        functools.partial(scatter_kernel, count, parts),
        out_shape=outs,
        in_specs=[pl.BlockSpec(memory_space=pl.ANY)] * count + [vmem] * 12,
        out_specs=[vmem] * len(outs),
        scratch_shapes=[pltpu.VMEM(f.shape[1:], f.dtype) for f in fulls] * 2 + slots + [
            pltpu.VMEM((4, LINES, 128), F32),
            pltpu.VMEM((4, 4, LINES, 128), F32),
            pltpu.VMEM((4, 8, 128), F32),
            pltpu.VMEM((4, 4, 8, 128), F32),
            pltpu.VMEM((16, 128), F32),
            pltpu.SemaphoreType.DMA((sems,)),
            pltpu.SemaphoreType.DMA((sems,)),
            pltpu.SemaphoreType.DMA((count,)),
        ],
        compiler_params=pltpu.CompilerParams(
            collective_id=1, has_side_effects=True, vmem_limit_bytes=56 << 20),
        name="scatter_grads",
    )(*fulls, *rows_old, *cols_old, *squares, weight_sums)


def step_kernel(*refs):
    refs = list(refs)
    take = lambda number: [refs.pop(0) for _ in range(number)]
    grads = take(4)
    small, lines, totals = take(3)
    weights, rows_old, cols_old = take(4), take(4), take(4)
    head, ffn, norm, head_sq, ffn_sq, norm_sq = take(6)
    grads_out = take(4)
    head_grad, ffn_grad, norm_grad = take(3)
    rows_out, cols_out = take(4), take(4)
    head_second, ffn_second, norm_second = take(3)
    weights_out = take(4)
    head_new, ffn_new, norm_new = take(3)
    old_small, weight_small = refs
    rows_new, cols_new = new_rows_cols(grads, rows_old, cols_old, lines)
    total = lambda lane: totals[0:1, lane:lane + 1]
    for index in range(4):
        rows_out[index][...] = to_row(rows_new[index])
        if index == 0:
            for at, cut in pair_cuts():
                cols_out[0][at] = cols_new[0][:, cut]
        else:
            cols_out[index][...] = cols_new[index]
        entries = ROW_COUNT[index] * COL_COUNT[index]
        row_mean = total(4 + index) / ROW_COUNT[index]
        update_rms = jnp.sqrt(row_mean * total(index) / entries)
        stride = (
            RATE * jnp.sqrt(total(11 + index) / entries) / jnp.maximum(1.0, update_rms / CLIP))
        scale_rows = lax.rsqrt(rows_new[index] / row_mean) * stride
        scale_cols = lax.rsqrt(cols_new[index])
        if index == 0:
            for (part, cols), cut in pair_cuts():
                at = (EVERY, part.start, cols)
                grad = grads[0][:, cut]
                grads_out[0][at] = grad
                weights_out[0][at] = weights[0][at] - grad * scale_rows * scale_cols[:, cut]
        else:
            grad = grads[index][...]
            grads_out[index][...] = grad
            weights_out[index][...] = weights[index][...] - grad * scale_rows * scale_cols
    place_small(old_small, norm_sq[...], head_sq[...], ffn_sq[...], 1.0)
    place_small(weight_small, norm[...], head[...], ffn[...], 0.0)
    grad = small[...]
    second, update = small_update(grad, old_small[...])
    line = lax.broadcasted_iota(jnp.int32, grad.shape, 0)
    counts = (2 * D, FF, 6 * D)
    strides = []
    for index in range(3):
        update_rms = jnp.sqrt(total(8 + index) / counts[index])
        strides.append(
            RATE * jnp.sqrt(total(15 + index) / counts[index])
            / jnp.maximum(1.0, update_rms / CLIP))
    stride = jnp.where(line < 6, strides[2], jnp.where(line < 8, strides[0], strides[1]))
    fresh = weight_small[...] - stride * update
    for values, (norm_ref, head_ref, ffn_ref) in (
        (grad, (norm_grad, head_grad, ffn_grad)),
        (second, (norm_second, head_second, ffn_second)),
        (fresh, (norm_new, head_new, ffn_new)),
    ):
        norm_ref[...] = values[0:6, 0:norm_ref.shape[1]]
        head_ref[...] = values[6:8, 0:head_ref.shape[1]]
        ffn_ref[...] = values[8:9, 0:ffn_ref.shape[1]]


def step(reduced, lines, totals, weights, rows_old, cols_old, vectors, squares):
    vmem = pl.BlockSpec(memory_space=pltpu.VMEM)
    small, grads = reduced[0], reduced[1:]
    shapes = [w.shape for w in weights] + [v.shape for v in vectors]
    shapes += [r.shape for r in rows_old] + [c.shape for c in cols_old]
    shapes += [v.shape for v in vectors] + [w.shape for w in weights] + [v.shape for v in vectors]
    operands = [*grads, small, lines, totals, *weights, *rows_old, *cols_old, *vectors, *squares]
    return pl.pallas_call(
        step_kernel,
        out_shape=[jax.ShapeDtypeStruct(s, F32) for s in shapes],
        in_specs=[vmem] * len(operands),
        out_specs=[vmem] * len(shapes),
        scratch_shapes=[pltpu.VMEM((16, 128), F32), pltpu.VMEM((16, 128), F32)],
        compiler_params=pltpu.CompilerParams(vmem_limit_bytes=32 << 20),
        name="adafactor_step",
    )(*operands)


HALF = D // 2
QKV_HALF = 3 * HALF
VMEM = pl.BlockSpec(memory_space=pltpu.VMEM)
SMEM = pl.BlockSpec(memory_space=pltpu.SMEM)


def dot(a, b):
    return jnp.dot(a, b, preferred_element_type=F32)


def dot_last(a, b):
    return lax.dot_general(a, b, (((1,), (1,)), ((), ())), preferred_element_type=F32)


def dot_first(a, b):
    return lax.dot_general(a, b, (((0,), (0,)), ((), ())), preferred_element_type=F32)


def ids_at(lengths, row, places):
    bound = jnp.int32(0)
    ids = jnp.zeros(places.shape, jnp.int32)
    for segment in range(SEGS):
        bound = bound + lengths[row, segment]
        ids = ids + (places >= bound).astype(jnp.int32)
    return ids


def set_bias(bias, lengths, row):
    down = ids_at(lengths, row, lax.broadcasted_iota(jnp.int32, (LEN, 1), 0))
    across = ids_at(lengths, row, lax.broadcasted_iota(jnp.int32, (1, LEN), 1))
    bias[...] = jnp.where(down == across, 0.0, -1e30)


def half_masks():
    lane = lax.broadcasted_iota(jnp.int32, (1, 128), 1)
    return [((lane // HD) == half).astype(F32).astype(BF) for half in range(2)]


PAIR = 3 * 128


def slab(ref, core, row, part, pair):
    return ref[core, pl.ds(pl.multiple_of(row * LEN, LEN), LEN),
               pl.ds(pl.multiple_of(pair * PAIR + part * 128, 128), 128)]


def project(tokens, weight, offsets, qkv, row):
    rows = pl.ds(pl.multiple_of(row * LEN, LEN), LEN)
    values = tokens[rows, :]
    for core in range(2):
        for pair in range(3):
            cut = slice(pair * PAIR, (pair + 1) * PAIR)
            out = (dot(values, weight[core, :, cut]) + offsets[core, :, cut]).astype(BF)
            scale = jnp.where(
                lax.broadcasted_iota(jnp.int32, (1, PAIR), 1) < 128, HD ** -0.5, 1.0).astype(BF)
            qkv[core, rows, cut] = out * scale


def attend(qkv, bias, context, lse, held, row):
    rows = pl.ds(pl.multiple_of(row * LEN, LEN), LEN)
    lane = lax.broadcasted_iota(jnp.int32, (LEN, 128), 1)
    held[...] = jnp.zeros(held.shape, F32)

    @pl.loop(0, 6)
    def _(item):
        core, pair = item // 3, item % 3
        queries, keys, values = (slab(qkv, core, row, part, pair) for part in range(3))
        wide = jnp.concatenate([values, jnp.ones_like(values)], axis=1)
        outs = []
        logs = held[...]
        for half, mask in enumerate(half_masks()):
            scores = dot_last(queries * mask, keys) + bias[...]
            peak = jnp.max(scores, axis=1, keepdims=True)
            raised = jnp.exp(scores - peak).astype(BF)
            both = dot(raised, wide)
            total = both[:, 128:]
            outs.append(both[:, :128] / total)
            logs = jnp.where(lane == item * 2 + half, peak + jnp.log(total), logs)
        held[...] = logs
        context[rows, pl.ds(pl.multiple_of(item * 128, 128), 128)] = jnp.where(
            lane < HD, outs[0], outs[1]).astype(BF)

    lse[row] = held[...].T[0:16, :]


def forward_kernel(tokens, weight, offsets, lengths, qkv, context, lse, bias, held):
    core = lax.axis_index("mp")

    @pl.loop(0, 2)
    def _(row):
        set_bias(bias, lengths, core * 2 + row)
        project(tokens, weight, offsets, qkv, row)
        attend(qkv, bias, context, lse, held, row)


def forward(tokens, weight, offsets, lengths):
    count = tokens.shape[0]
    return pl.pallas_call(
        forward_kernel,
        out_shape=[
            jax.ShapeDtypeStruct((2, count, QKV_HALF), BF),
            jax.ShapeDtypeStruct((count, D), BF),
            jax.ShapeDtypeStruct((count // LEN, 16, LEN), F32),
        ],
        in_specs=[VMEM, VMEM, VMEM, SMEM],
        out_specs=[VMEM] * 3,
        scratch_shapes=[pltpu.VMEM((LEN, LEN), F32), pltpu.VMEM((LEN, 128), F32)],
        compiler_params=pltpu.CompilerParams(vmem_limit_bytes=56 << 20),
        name="project_attend",
    )(tokens, weight, offsets, lengths)


def gelu_both(inner):
    cdf = 0.5 * (1.0 + lax.erf(inner * 0.7071067811865476))
    density = 0.3989422804014327 * jnp.exp(-0.5 * inner * inner)
    return inner * cdf, cdf + inner * density


def norm_parts(values):
    center = values - jnp.mean(values, axis=-1, keepdims=True)
    scale = lax.rsqrt(jnp.mean(center * center, axis=-1, keepdims=True) + EPS_NORM)
    return center * scale, scale


def norm_back(grad, normed, scale, gain):
    scaled = grad * gain
    mean = jnp.mean(scaled, axis=-1, keepdims=True)
    along = jnp.mean(scaled * normed, axis=-1, keepdims=True)
    return (
        (scaled - mean - normed * along) * scale,
        jnp.sum(grad * normed, axis=0, keepdims=True),
        jnp.sum(grad, axis=0, keepdims=True),
    )


CHUNK = 512


def middle(row, core, tokens, context, cotangent, lengths, w_out, w_up, w_down, ffn, norm, layer_out,
           pooled, hidden_b, act, grad_branch, grad_inner, grad_attended, grad_context,
           grad_one, delta, norm_sums, ffn_sums, slope, branch, hidden, normed_one, grad_two):
    rows = pl.ds(pl.multiple_of(row * LEN, LEN), LEN)
    attended = dot(context[rows, :], w_out[...]) + norm[0:1, :]
    normed, scale_one = norm_parts(tokens[rows, :].astype(F32) + attended)
    normed_one[...] = normed
    value = normed * norm[2:3, :] + norm[3:4, :]
    hidden[...] = value
    hidden_b[rows, :] = value.astype(BF)
    branch[...] = jnp.zeros(branch.shape, F32)
    for chunk in range(FF // CHUNK):
        core_of, start = chunk * CHUNK // (FF // 2), chunk * CHUNK % (FF // 2)
        cols = slice(chunk * CHUNK, (chunk + 1) * CHUNK)
        up = w_up[core_of, :, start:start + CHUNK]
        value, slope_value = gelu_both(dot(hidden_b[rows, :], up) + ffn[:, cols])
        value = value.astype(BF)
        act[rows, cols] = value
        slope[:, cols] = slope_value.astype(BF)
        branch[...] += dot(value, w_down[cols, :])
    normed, scale = norm_parts(hidden[...] + branch[...] + norm[1:2, :])
    output = normed * norm[4:5, :] + norm[5:6, :]
    high = output.astype(BF)
    layer_out[rows, :] = high
    low = (output - high.astype(F32)).astype(BF)
    place = lax.broadcasted_iota(jnp.int32, (SEGS, LEN), 1)
    segment = lax.broadcasted_iota(jnp.int32, (SEGS, 1), 0)
    ids = ids_at(lengths, core * 2 + row, place)
    member = (ids == segment).astype(F32)
    sizes = jnp.sum(member, axis=1, keepdims=True)
    member = member.astype(BF)
    pooled[row] = (dot(member, high) + dot(member, low)) / sizes
    back, gain, shift = norm_back(cotangent[rows, :].astype(F32), normed, scale, norm[4:5, :])
    norm_sums[4:5, :] += gain
    norm_sums[5:6, :] += shift
    grad_two[...] = back
    back = back.astype(BF)
    grad_branch[rows, :] = back
    norm_sums[1:2, :] += jnp.sum(back.astype(F32), axis=0, keepdims=True)
    for chunk in range(FF // CHUNK):
        core_of, start = chunk * CHUNK // (FF // 2), chunk * CHUNK % (FF // 2)
        cols = slice(chunk * CHUNK, (chunk + 1) * CHUNK)
        value = dot_last(grad_branch[rows, :], w_down[cols, :])
        value = (value * slope[:, cols].astype(F32)).astype(BF)
        grad_inner[rows, cols] = value
        ffn_sums[:, cols] += jnp.sum(value.astype(F32), axis=0, keepdims=True)
        grad_two[...] += dot_last(value, w_up[core_of, :, start:start + CHUNK])
    back, gain, shift = norm_back(grad_two[...], normed_one[...], scale_one, norm[2:3, :])
    norm_sums[2:3, :] += gain
    norm_sums[3:4, :] += shift
    grad_one[rows, :] = back
    back = back.astype(BF)
    grad_attended[rows, :] = back
    norm_sums[0:1, :] += jnp.sum(back.astype(F32), axis=0, keepdims=True)
    back = dot_last(back, w_out[...]).astype(BF)
    grad_context[rows, :] = back
    product = back.astype(F32) * context[rows, :].astype(F32)
    high = product.astype(BF)
    low = (product - high.astype(F32)).astype(BF)
    head = lax.broadcasted_iota(jnp.int32, (16, D), 0)
    member = (lax.broadcasted_iota(jnp.int32, (16, D), 1) // HD == head).astype(F32).astype(BF)
    delta[row] = dot_last(member, high) + dot_last(member, low)


def middle_kernel(*refs):
    core = lax.axis_index("mp")
    norm_sums, ffn_sums = refs[19], refs[20]
    norm_sums[...] = jnp.zeros(norm_sums.shape, F32)
    ffn_sums[...] = jnp.zeros(ffn_sums.shape, F32)

    @pl.loop(0, 2)
    def _(row):
        middle(row, core, *refs)


def middle_call(tokens, context, cotangent, lengths, w_out, w_up, w_down, ffn, norm):
    count = tokens.shape[0]
    shape = jax.ShapeDtypeStruct
    return pl.pallas_call(
        middle_kernel,
        out_shape=[
            shape((count, D), BF),
            shape((count // LEN, SEGS, D), F32),
            shape((count, D), BF),
            shape((count, FF), BF),
            shape((count, D), BF),
            shape((count, FF), BF),
            shape((count, D), BF),
            shape((count, D), BF),
            shape((count, D), F32),
            shape((count // LEN, 16, LEN), F32),
            shape((8, D), F32),
            shape((1, FF), F32),
        ],
        in_specs=[VMEM] * 3 + [SMEM] + [VMEM] * 5,
        out_specs=[VMEM] * 12,
        scratch_shapes=[
            pltpu.VMEM((LEN, FF), BF),
            pltpu.VMEM((LEN, D), F32),
            pltpu.VMEM((LEN, D), F32),
            pltpu.VMEM((LEN, D), F32),
            pltpu.VMEM((LEN, D), F32),
        ],
        compiler_params=pltpu.CompilerParams(vmem_limit_bytes=60 << 20),
        name="feed_forward",
    )(tokens, context, cotangent, lengths, w_out, w_up, w_down, ffn, norm)


def weight_grads_kernel(context, hidden_b, act, grad_branch, grad_inner, grad_attended,
                        out_grad, up_grad, down_grad):

    @pl.loop(0, FF // CHUNK)
    def _(chunk):
        half_chunks = FF // 2 // CHUNK
        cols = pl.ds(pl.multiple_of(chunk * CHUNK, CHUNK), CHUNK)
        local = pl.ds(pl.multiple_of((chunk % half_chunks) * CHUNK, CHUNK), CHUNK)
        up_grad[chunk // half_chunks, :, local] = dot(hidden_b[...], grad_inner[:, cols]).astype(BF)
        down_grad[cols, :] = dot(act[cols, :], grad_branch[...]).astype(BF)

    value = dot(context[...], grad_attended[...])
    rows, held = D // out_grad.shape[0], out_grad.shape[1]
    for block in range(out_grad.shape[0]):
        piece = value[block * rows:(block + 1) * rows, :]
        if held > rows:
            piece = jnp.concatenate([piece, jnp.zeros((held - rows, D), F32)], axis=0)
        out_grad[block] = piece.astype(BF)


def weight_grads(context, hidden_b, act, grad_branch, grad_inner, grad_attended, blocks, held):
    shape = jax.ShapeDtypeStruct
    return pl.pallas_call(
        weight_grads_kernel,
        out_shape=[shape((blocks, held, D), BF), shape((2, D, FF // 2), BF), shape((FF, D), BF)],
        in_specs=[VMEM] * 6,
        out_specs=[VMEM] * 3,
        compiler_params=pltpu.CompilerParams(vmem_limit_bytes=60 << 20),
        name="weight_grads",
    )(context, hidden_b, act, grad_branch, grad_inner, grad_attended)


def attend_back(qkv, grad_context, lse, delta, bias, grad_qkv, grad_head, row):
    rows = pl.ds(pl.multiple_of(row * LEN, LEN), LEN)
    lane = lax.broadcasted_iota(jnp.int32, (LEN, 128), 1)

    @pl.loop(0, 6)
    def _(item):
        core, pair = item // 3, item % 3
        queries, keys, values = (slab(qkv, core, row, part, pair) for part in range(3))
        wide = pl.ds(pl.multiple_of(item * 128, 128), 128)
        grad = grad_context[rows, wide]
        flipped = keys.T
        grads_k, grads_v, grads_q = [], [], []
        for half, mask in enumerate(half_masks()):
            head = item * 2 + half
            scores = dot_last(keys * mask, queries) + bias[...] - lse[row, pl.ds(head, 1), :]
            probs = jnp.exp(scores)
            grad_probs = dot_last(values * mask, grad)
            grad_scores = (probs * (grad_probs - delta[row, pl.ds(head, 1), :])).astype(BF)
            grads_v.append(dot(probs.astype(BF), grad))
            grads_k.append(dot(grad_scores, queries))
            grads_q.append(dot(flipped[half * HD:(half + 1) * HD, :], grad_scores))
        grad_q = (jnp.concatenate(grads_q, axis=0).T * HD ** -0.5).astype(BF)
        grad_k = jnp.where(lane < HD, grads_k[0], grads_k[1]).astype(BF)
        grad_v = jnp.where(lane < HD, grads_v[0], grads_v[1]).astype(BF)
        for part, value in enumerate((grad_q, grad_k, grad_v)):
            grad_qkv[core, rows, pl.ds(pl.multiple_of(pair * PAIR + part * 128, 128), 128)] = value
        grad_head[0:1, wide] += jnp.sum(grad_q.astype(F32), axis=0, keepdims=True)
        grad_head[1:2, wide] += jnp.sum(grad_v.astype(F32), axis=0, keepdims=True)


def backward_kernel(tokens, qkv, grad_context, lse, delta, lengths, weight, grad_one,
                    qkv_grad, input_grad, grad_head, grad_qkv, bias):
    core = lax.axis_index("mp")
    grad_head[...] = jnp.zeros(grad_head.shape, F32)

    @pl.loop(0, 2)
    def _(row):
        set_bias(bias, lengths, core * 2 + row)
        attend_back(qkv, grad_context, lse, delta, bias, grad_qkv, grad_head, row)
        rows = pl.ds(pl.multiple_of(row * LEN, LEN), LEN)
        input_grad[rows, :] = (
            grad_one[rows, :]
            + dot_last(grad_qkv[0, rows, :], weight[0])
            + dot_last(grad_qkv[1, rows, :], weight[1])
        )

    for core_of in range(2):
        for part in range(3):
            cut = slice(part * HALF, (part + 1) * HALF)
            qkv_grad[core_of, :, cut] = dot(tokens[...], grad_qkv[core_of, :, cut]).astype(BF)


def backward(tokens, qkv, grad_context, lse, delta, lengths, weight, grad_one):
    count = tokens.shape[1]
    shape = jax.ShapeDtypeStruct
    return pl.pallas_call(
        backward_kernel,
        out_shape=[shape((2, D, QKV_HALF), BF), shape((count, D), F32), shape((2, D), F32)],
        in_specs=[VMEM] * 5 + [SMEM] + [VMEM] * 2,
        out_specs=[VMEM] * 3,
        scratch_shapes=[
            pltpu.VMEM((2, count, QKV_HALF), BF),
            pltpu.VMEM((LEN, LEN), F32),
        ],
        compiler_params=pltpu.CompilerParams(vmem_limit_bytes=60 << 20),
        name="attend_back",
    )(tokens, qkv, grad_context, lse, delta, lengths, weight, grad_one)


UP_CHUNK = 512
DOWN_CHUNK = 256


class Spread:
    COUNT = 8

    def __init__(self, place, full, start, width, flip, sems, base, shard=None):
        self.place, self.full, self.shard = place, full, shard
        self.cols = pl.ds(start, width)
        tiles = width // 128
        cut = (tiles // 2 if flip else tiles - tiles // 2) * 128
        self.halves = [("xy", pl.ds(start, cut))]
        if cut < width:
            self.halves.append(("yx", pl.ds(start + cut, width - cut)))
        self.sems, self.base = sems, base

    def view(self, spot, cols):
        return self.full.at[spot["m"], spot["z"], spot["y"], spot["x"], :, cols]

    def copy(self, slot, axis, step, spot, cols, source=None):
        place = self.place
        send, recv = self.sems
        send, recv = send.at[self.base + slot], recv.at[self.base + slot]
        device = place.device(place.at(axis, step))
        view = self.view(spot, cols)
        sent = pltpu.make_async_remote_copy(
            view if source is None else source, view, send, recv,
            device_id=device, device_id_type=MESH)
        land = dict(spot)
        land[axis] = place.at(axis, -step)[axis]
        land = self.view(land, cols)
        arrives = pltpu.make_async_remote_copy(
            land, land, send, recv, device_id=device, device_id_type=MESH)
        return sent, arrives

    def copies(self, stage):
        place = self.place
        here = {"z": place.z, "y": place.y, "x": place.x, "m": place.m}
        if stage == 0:
            source = None if self.shard is None else self.shard.at[:, self.cols]
            return [self.copy(step - 1, "z", step, here, self.cols, source) for step in (1, 2, 3)]
        here["z"] = EVERY
        if stage == 3:
            here["y"] = here["x"] = EVERY
            return [self.copy(7, "m", 1, here, self.cols)]
        out = []
        for number, (order, cols) in enumerate(self.halves):
            spot = dict(here)
            if stage == 2:
                spot[order[0]] = EVERY
            out.append(self.copy(1 + 2 * stage + number, order[stage - 1], 1, spot, cols))
        return out

    def start(self, stage):
        for sent, _ in self.copies(stage):
            sent.start()

    def arrived(self, stage):
        for _, arrives in self.copies(stage):
            arrives.wait_recv()

    def finish(self):
        for stage in range(4):
            for sent, _ in self.copies(stage):
                sent.wait_send()


def spread_tick(groups, tick):
    for stage in range(4):
        index = tick + 2 if stage == 0 else tick - stage + 1
        if 0 <= index < len(groups):
            for chunk in groups[index]:
                if stage:
                    chunk.arrived(stage - 1)
                chunk.start(stage)


def unpack_small(small, norm_out, offsets, ffn_out):
    iota = lambda shape, axis: lax.broadcasted_iota(jnp.int32, shape, axis)
    pick = ((iota((128, D), 1) % 24 == iota((128, D), 0))).astype(F32).astype(BF)
    pick_ffn = ((iota((128, FF), 1) % 96 == iota((128, FF), 0))).astype(F32).astype(BF)
    total = jnp.zeros((16, D), F32)
    ffn = jnp.zeros((1, FF), F32)
    line, col = iota((256, D), 0), iota((256, D), 1) // 24
    device, kind = line // 16, line % 16
    for core in range(2):
        block = small[core].reshape(256, 128).astype(BF)
        wide = dot(block, pick)
        right = jnp.where(kind < 6, 2 * device + core, 16 * core + device)
        wide = jnp.where((col == right) & (kind < 8), wide, 0.0)
        total = total + jnp.sum(wide.reshape(16, 16, D), axis=0)
        wide = dot(small[core, :, :, :, 8, :].reshape(16, 128).astype(BF), pick_ffn)
        right = iota((16, FF), 1) // 96 == iota((16, FF), 0) + 16 * core
        ffn = ffn + jnp.sum(jnp.where(right, wide, 0.0), axis=0, keepdims=True)
    norm_out[0:6, :] = total[0:6, :]
    norm_out[6:8, :] = jnp.zeros((2, D), F32)
    ffn_out[...] = ffn
    offsets[...] = jnp.zeros(offsets.shape, F32)
    for core in range(2):
        for pair in range(3):
            source = core * HALF + pair * 128
            for part, row in ((0, 6), (2, 7)):
                start = pair * PAIR + part * 128
                offsets[core, :, start:start + 128] = total[row:row + 1, source:source + 128]


def project_pair(tokens, weight, offsets, qkv, pair):
    cols = pl.ds(pl.multiple_of(pair * PAIR, PAIR), PAIR)
    scale = jnp.where(
        lax.broadcasted_iota(jnp.int32, (1, PAIR), 1) < 128, HD ** -0.5, 1.0).astype(BF)
    for core in range(2):
        piece = weight[core, :, :, :, :, cols].reshape(D, PAIR)
        out = dot(tokens[...], piece) + offsets[core, :, cols]
        qkv[core, :, cols] = out.astype(BF) * scale


def attend_pair(qkv, bias, context, logs_ref, core, row, pair):
    rows = pl.ds(pl.multiple_of(row * LEN, LEN), LEN)
    lane = lax.broadcasted_iota(jnp.int32, (LEN, 128), 1)
    item = core * 3 + pair
    queries, keys, values = (slab(qkv, core, row, part, pair) for part in range(3))
    wide = jnp.concatenate([values, jnp.ones_like(values)], axis=1)
    outs = []
    logs = logs_ref[row]
    for half, mask in enumerate(half_masks()):
        scores = dot_last(queries * mask, keys) + bias[row]
        peak = jnp.max(scores, axis=1, keepdims=True)
        raised = jnp.exp(scores - peak).astype(BF)
        both = dot(raised, wide)
        total = both[:, 128:]
        outs.append(both[:, :128] / total)
        logs = jnp.where(lane == item * 2 + half, peak + jnp.log(total), logs)
    logs_ref[row] = logs
    context[rows, pl.ds(pl.multiple_of(item * 128, 128), 128)] = jnp.where(
        lane < HD, outs[0], outs[1]).astype(BF)


def forward_gather_kernel(*refs):
    refs = list(refs)
    take = lambda number: [refs.pop(0) for _ in range(number)]
    w_qkv, w_out, w_up, w_down, head, ffn, norm, tokens, lengths = take(9)
    (sums, norm_out, ffn_out, lse, hidden_scale, out_full) = take(6)
    (qkv_full, up_full, down_full, qkv_out, context_flip, token_flip, hidden_flip, normed_out,
     context_out, act_out, act_flip, slope_out) = take(12)
    (g_small, g_qkv, g_out, g_up, cast_down, qkv, context, flip_context, flip_token, flip_hidden,
     hidden_b, normed_one, act, slope, flip_act, bias, logs, offsets) = take(18)
    send, recv, local = refs
    place = Place()
    here = (place.m, place.z, place.y, place.x)
    half = w_qkv.shape[2]
    place_small(g_small.at[here], norm[...], head[...], ffn[...], 0.0)
    for part in range(3):
        for pair in range(3):
            start = pair * PAIR + part * 128
            g_qkv[here + (EVERY, slice(start, start + 128))] = w_qkv[
                :, part, pair * 128:(pair + 1) * 128].astype(BF)
    value = w_out[...]
    spare = g_out.shape[4] - value.shape[0]
    g_out[here] = jnp.concatenate([value, jnp.zeros((spare, D), F32)], axis=0).astype(BF)
    g_up[here] = w_up[...].astype(BF)
    cast_down[...] = w_down[...].astype(BF)
    copies, used = [], [0]

    def keep(source, target):
        copy = pltpu.make_async_copy(source, target, local.at[used[0]])
        used[0] += 1
        copy.start()
        copies.append(copy)
        return copy

    down_own = keep(cast_down, down_full.at[here])
    sems, base = (send, recv), [0]

    def chunk(full, start, width, flip, shard=None):
        made = Spread(place, full, start, width, flip, sems, base[0], shard)
        base[0] += Spread.COUNT
        return made

    groups = [[chunk(g_small, 0, 128, False), chunk(g_qkv, 0, PAIR, False)]]
    groups += [[chunk(g_qkv, pair * PAIR, PAIR, pair == 1)] for pair in (1, 2)]
    groups += [[chunk(g_out, 0, D, False)]]
    groups += [[chunk(g_up, at, UP_CHUNK, False)] for at in range(0, FF // 2, UP_CHUNK)]
    groups += [[chunk(down_full, at, DOWN_CHUNK, False, cast_down)]
               for at in range(0, D, DOWN_CHUNK)]

    def ready(index):
        for made in groups[index]:
            made.arrived(3)

    greet(place)
    for index in (0, 1):
        for made in groups[index]:
            made.start(0)
    sums[...] = weight_sums_of([w_qkv, w_out, w_up, w_down], g_small[here])
    down_own.wait()
    spread_tick(groups, 0)
    for row in range(2):
        set_bias(bias.at[row], lengths, place.m * 2 + row)
    spread_tick(groups, 1)
    flip_token[...] = tokens[...].T
    keep(flip_token, token_flip)
    spread_tick(groups, 2)
    logs[...] = jnp.zeros(logs.shape, F32)
    ready(0)
    unpack_small(g_small, norm_out, offsets, ffn_out)

    @pl.loop(0, 12)
    def _(item):
        pair, row, core = item // 4, (item % 4) // 2, item % 2
        for number, at in enumerate((2, 4, 6, 8, 10)):
            @pl.when(item == at)
            def _():
                spread_tick(groups, 3 + number)
                if at in (4, 8):
                    ready(at // 4)

        @pl.when(item % 4 == 0)
        def _():
            project_pair(tokens, g_qkv, offsets, qkv, pair)

        attend_pair(qkv, bias, context, logs, core, row, pair)

    for core in range(2):
        keep(g_qkv.at[core], qkv_full.at[core])
    keep(qkv, qkv_out)
    keep(context, context_out)
    for row in range(2):
        lse[row] = logs[row].T[0:16, :]
    flip_context[...] = context[...].T
    keep(flip_context, context_flip)
    ready(3)
    rows_out = w_out.shape[0]
    for core in range(2):
        value = g_out[core].reshape(16, g_out.shape[4], D).astype(F32)[:, :rows_out]
        out_full[core * HALF:(core + 1) * HALF, :] = value.reshape(HALF, D).astype(BF)
    for row in range(2):
        rows = slice(row * LEN, (row + 1) * LEN)
        attended = dot(context[rows, :], out_full[...]) + norm_out[0:1, :]
        normed, scale = norm_parts(tokens[rows, :].astype(F32) + attended)
        normed_one[rows, :] = normed
        hidden_scale[rows, :] = jnp.broadcast_to(scale, (LEN, 128))
        hidden_b[rows, :] = (normed * norm_out[2:3, :] + norm_out[3:4, :]).astype(BF)
    keep(normed_one, normed_out)
    flip_hidden[...] = hidden_b[...].T
    keep(flip_hidden, hidden_flip)
    spread_tick(groups, 8)
    waiting = [[], []]
    for third in range(3):
        ready(4 + third)
        for core in range(2):
            for copy in waiting[core]:
                copy.wait()
            local_cols = slice(third * UP_CHUNK, (third + 1) * UP_CHUNK)
            start = core * (FF // 2) + third * UP_CHUNK
            cols = pl.ds(start, UP_CHUNK)
            up = g_up[core, :, :, :, :, local_cols].reshape(D, UP_CHUNK)

            @pl.loop(0, 2)
            def _(row):
                rows = pl.ds(pl.multiple_of(row * LEN, LEN), LEN)
                value, slope_value = gelu_both(
                    dot(hidden_b[rows, :], up) + ffn_out[:, start:start + UP_CHUNK])
                act[core, rows, :] = value.astype(BF)
                slope[core, rows, :] = slope_value.astype(BF)

            flip_act[core] = act[core].T
            slot = 16 + 3 * core
            waiting[core] = [
                pltpu.make_async_copy(act.at[core], act_out.at[:, cols], local.at[slot]),
                pltpu.make_async_copy(slope.at[core], slope_out.at[:, cols], local.at[slot + 1]),
                pltpu.make_async_copy(flip_act.at[core], act_flip.at[cols, :], local.at[slot + 2]),
            ]
            for copy in waiting[core]:
                copy.start()
        spread_tick(groups, 9 + third)
    for core in range(2):
        keep(g_up.at[core], up_full.at[core])
    for index in (7, 8, 9):
        ready(index)
    for copy in copies[1:] + waiting[0] + waiting[1]:
        copy.wait()
    for group in groups:
        for made in group:
            made.finish()


def forward_gather(weights, vectors, tokens, lengths):
    qkv, out, up, down = weights
    count = tokens.shape[0]
    shape = jax.ShapeDtypeStruct
    grid = (2, 4, 2, 2)
    held_out = 32
    flipped = shape((D, count), BF)
    small_outs = [
        shape((8, 128), F32), shape((8, D), F32), shape((1, FF), F32),
        shape((count // LEN, 16, LEN), F32), shape((count, 128), F32), shape((D, D), BF),
    ]
    large_outs = [
        shape(grid + (qkv.shape[0], QKV_HALF), BF), shape(grid + up.shape, BF),
        shape(grid + down.shape, BF), shape((2, count, QKV_HALF), BF), flipped, flipped, flipped,
        shape((count, D), F32), shape((count, D), BF), shape((count, FF), BF),
        shape((FF, count), BF), shape((count, FF), BF),
    ]
    slots = 11 * Spread.COUNT
    return pl.pallas_call(
        forward_gather_kernel,
        out_shape=small_outs + large_outs,
        in_specs=[VMEM] * 8 + [SMEM],
        out_specs=[VMEM] * len(small_outs) + [pl.BlockSpec(memory_space=pl.ANY)] * len(large_outs),
        scratch_shapes=[
            pltpu.VMEM(grid + (16, 128), F32),
            pltpu.VMEM(grid + (qkv.shape[0], QKV_HALF), BF),
            pltpu.VMEM(grid + (held_out, D), BF),
            pltpu.VMEM(grid + up.shape, BF),
            pltpu.VMEM(down.shape, BF),
            pltpu.VMEM((2, count, QKV_HALF), BF),
            pltpu.VMEM((count, D), BF),
            pltpu.VMEM((D, count), BF),
            pltpu.VMEM((D, count), BF),
            pltpu.VMEM((D, count), BF),
            pltpu.VMEM((count, D), BF),
            pltpu.VMEM((count, D), F32),
            pltpu.VMEM((2, count, UP_CHUNK), BF),
            pltpu.VMEM((2, count, UP_CHUNK), BF),
            pltpu.VMEM((2, UP_CHUNK, count), BF),
            pltpu.VMEM((2, LEN, LEN), F32),
            pltpu.VMEM((2, LEN, 128), F32),
            pltpu.VMEM((2, 1, QKV_HALF), F32),
            pltpu.SemaphoreType.DMA((slots,)),
            pltpu.SemaphoreType.DMA((slots,)),
            pltpu.SemaphoreType.DMA((24,)),
        ],
        compiler_params=pltpu.CompilerParams(
            collective_id=0, has_side_effects=True, vmem_limit_bytes=60 << 20),
        name="forward_gather",
    )(*weights, *vectors, tokens, lengths)


def finish_kernel(*refs):
    refs = list(refs)
    take = lambda number: [refs.pop(0) for _ in range(number)]
    lengths, norm, scale_one, w_out = take(4)
    (down_any, up_any, act_any, slope_any, normed_any, context_any, cotangent_any) = take(7)
    pooled, delta, norm_sums, ffn_sums = take(4)
    (layer_any, branch_any, inner_any, attended_any, grad_context_any, one_any) = take(6)
    (w_down, w_up, act, slope, normed_one, context, cotangent, layer_out, grad_branch,
     grad_attended, grad_context, hidden) = take(12)
    loads, stores = refs
    core = lax.axis_index("mp")
    started = []

    def load(source, target):
        copy = pltpu.make_async_copy(source, target, loads.at[len(started)])
        copy.start()
        started.append(copy)
        return copy

    halves = [pl.ds(row * LEN, LEN) for row in range(2)]
    pair = lambda source, target: [load(source.at[rows], target.at[rows]) for rows in halves]
    down_loaded = load(down_any, w_down)
    act_loaded, normed_loaded = [], []
    for rows in halves:
        act_loaded.append(load(act_any.at[rows], act.at[rows]))
        normed_loaded.append(load(normed_any.at[rows], normed_one.at[rows]))
    cotangent_loaded = pair(cotangent_any, cotangent)
    slope_loaded = pair(slope_any, slope)
    up_loaded = load(up_any, w_up)
    context_loaded = pair(context_any, context)
    norm_sums[...] = jnp.zeros(norm_sums.shape, F32)
    ffn_sums[...] = jnp.zeros(ffn_sums.shape, F32)
    kept = []

    def keep(source, target):
        copy = pltpu.make_async_copy(source, target, stores.at[len(kept)])
        copy.start()
        kept.append(copy)

    down_loaded.wait()
    for row, rows in enumerate(halves):
        act_loaded[row].wait()
        normed_loaded[row].wait()
        hidden[...] = normed_one[rows, :] * norm[2:3, :] + norm[3:4, :]
        branch = dot(act[rows, :], w_down[...])
        normed, scale = norm_parts(hidden[...] + branch + norm[1:2, :])
        output = normed * norm[4:5, :] + norm[5:6, :]
        high = output.astype(BF)
        layer_out[rows, :] = high
        keep(layer_out.at[rows], layer_any.at[rows])
        low = (output - high.astype(F32)).astype(BF)
        place = lax.broadcasted_iota(jnp.int32, (SEGS, LEN), 1)
        segment = lax.broadcasted_iota(jnp.int32, (SEGS, 1), 0)
        ids = ids_at(lengths, core * 2 + row, place)
        member = (ids == segment).astype(F32)
        sizes = jnp.sum(member, axis=1, keepdims=True)
        member = member.astype(BF)
        pooled[row] = (dot(member, high) + dot(member, low)) / sizes
        cotangent_loaded[row].wait()
        back, gain, shift = norm_back(cotangent[rows, :].astype(F32), normed, scale, norm[4:5, :])
        norm_sums[4:5, :] += gain
        norm_sums[5:6, :] += shift
        hidden[...] = back
        back = back.astype(BF)
        grad_branch[rows, :] = back
        keep(grad_branch.at[rows], branch_any.at[rows])
        norm_sums[1:2, :] += jnp.sum(back.astype(F32), axis=0, keepdims=True)
        slope_loaded[row].wait()
        for start in range(0, FF, FF // 4):
            cols = slice(start, start + FF // 4)
            value = dot_last(grad_branch[rows, :], w_down[cols, :])
            value = (value * slope[rows, cols].astype(F32)).astype(BF)
            slope[rows, cols] = value
            ffn_sums[:, cols] += jnp.sum(value.astype(F32), axis=0, keepdims=True)
        keep(slope.at[rows], inner_any.at[rows])
        if row == 0:
            up_loaded.wait()
        for half in range(2):
            cols = slice(half * FF // 2, (half + 1) * FF // 2)
            hidden[...] += dot_last(slope[rows, cols], w_up[half])
        normed = normed_one[rows, :]
        scale = scale_one[rows, 0:1]
        back, gain, shift = norm_back(hidden[...], normed, scale, norm[2:3, :])
        norm_sums[2:3, :] += gain
        norm_sums[3:4, :] += shift
        normed_one[rows, :] = back
        keep(normed_one.at[rows], one_any.at[rows])
        back = back.astype(BF)
        grad_attended[rows, :] = back
        keep(grad_attended.at[rows], attended_any.at[rows])
        norm_sums[0:1, :] += jnp.sum(back.astype(F32), axis=0, keepdims=True)
        back = dot_last(back, w_out[...]).astype(BF)
        grad_context[rows, :] = back
        keep(grad_context.at[rows], grad_context_any.at[rows])
        context_loaded[row].wait()
        product = back.astype(F32) * context[rows, :].astype(F32)
        high = product.astype(BF)
        low = (product - high.astype(F32)).astype(BF)
        head = lax.broadcasted_iota(jnp.int32, (16, D), 0)
        member = (lax.broadcasted_iota(jnp.int32, (16, D), 1) // HD == head).astype(F32).astype(BF)
        delta[row] = dot_last(member, high) + dot_last(member, low)
    for copy in kept:
        copy.wait()


def finish_forward(lengths, norm, scale_one, w_out, w_down, w_up, act, slope, normed, context,
                   cotangent):
    count = act.shape[0]
    shape = jax.ShapeDtypeStruct
    outs = [
        shape((count // LEN, SEGS, D), F32), shape((count // LEN, 16, LEN), F32),
        shape((8, D), F32), shape((1, FF), F32),
    ]
    large = [
        shape((count, D), BF), shape((count, D), BF), shape((count, FF), BF),
        shape((count, D), BF), shape((count, D), BF), shape((count, D), F32),
    ]
    some = pl.BlockSpec(memory_space=pl.ANY)
    return pl.pallas_call(
        finish_kernel,
        out_shape=outs + large,
        in_specs=[SMEM] + [VMEM] * 3 + [some] * 7,
        out_specs=[VMEM] * 4 + [some] * 6,
        scratch_shapes=[
            pltpu.VMEM((FF, D), BF),
            pltpu.VMEM((2, D, FF // 2), BF),
            pltpu.VMEM((count, FF), BF),
            pltpu.VMEM((count, FF), BF),
            pltpu.VMEM((count, D), F32),
            pltpu.VMEM((count, D), BF),
            pltpu.VMEM((count, D), BF),
            pltpu.VMEM((count, D), BF),
            pltpu.VMEM((count, D), BF),
            pltpu.VMEM((count, D), BF),
            pltpu.VMEM((count, D), BF),
            pltpu.VMEM((LEN, D), F32),
            pltpu.SemaphoreType.DMA((16,)),
            pltpu.SemaphoreType.DMA((16,)),
        ],
        compiler_params=pltpu.CompilerParams(vmem_limit_bytes=60 << 20),
        name="finish_forward",
    )(lengths, norm, scale_one, w_out, w_down, w_up, act, slope, normed, context, cotangent)


def small_block(norm, head, ffn):
    wide = lambda v: jnp.pad(v, [(0, 0)] * (v.ndim - 1) + [(0, 128 - v.shape[-1])])
    block = jnp.concatenate([wide(norm), wide(head), wide(ffn)], axis=-2)
    return jnp.pad(block, [(0, 0)] * (block.ndim - 2) + [(0, 16 - block.shape[-2]), (0, 0)])


def pair_major(weight):
    count = weight.shape[0]
    return weight.reshape(count, 3, 3, 128).transpose(0, 2, 1, 3).reshape(count, QKV_HALF)


def gather_plain(weights, vectors):
    head, ffn, norm = vectors
    qkv, out, up, down = (w.astype(BF) for w in weights)
    full = []
    for shard in (small_block(norm, head, ffn), pair_major(qkv), out, up, down):
        full.append(lax.all_gather(lax.all_gather(shard, "dp", axis=0), "mp", axis=0))
    return full


def scatter_plain(fulls):
    out = []
    for full in fulls:
        own = lax.psum_scatter(full.astype(F32), "mp", scatter_dimension=0)
        out.append(lax.psum_scatter(own, "dp", scatter_dimension=0))
    return out


def body(
    tokens, cotangent, seg_lengths, w_qkv, w_out, w_up, w_down, head_bias, ffn_bias, norm_bias,
    qkv_rows, qkv_cols, out_rows, out_cols, up_rows, up_cols, down_rows, down_cols,
    head_bias_sq, ffn_bias_sq, norm_sq,
):
    cores = lax.axis_size("mp")
    data = lax.axis_size("dp")
    rows_qkv = w_qkv.shape[0]
    fast = data == 16 and cores == 2
    weights = [w_qkv, w_out, w_up, w_down]
    vectors = [head_bias, ffn_bias.reshape(1, -1), norm_bias]
    rows_out = w_out.shape[0]
    held = 32 if fast else rows_out
    if fast:
        (weight_sums, norm_full, ffn_full, lse, scale_one, out_full, qkv_full, up_full, down_full,
         qkv, context_flip, token_flip, hidden_flip, normed_one, context, act, act_flip, slope
         ) = forward_gather(weights, vectors, tokens, seg_lengths)
        qkv_full = qkv_full.reshape(2, D, QKV_HALF)
        up_full = up_full.reshape(2, D, FF // 2)
        down_full = down_full.reshape(FF, D)
        (pooled, delta, norm_sums, ffn_sums, layer_out, grad_branch, grad_inner, grad_attended,
         grad_context, grad_one) = finish_forward(
            seg_lengths, norm_full, scale_one, out_full, down_full, up_full, act, slope,
            normed_one, context, cotangent)
        grad_out, grad_up, grad_down = weight_grads(
            context_flip, hidden_flip, act_flip, grad_branch, grad_inner, grad_attended,
            cores * data, held)
    else:
        small, qkv_g, out_g, up_g, down_g = gather_plain(weights, vectors)
        small = small.astype(BF).astype(F32)
        own_head, own_ffn, own_norm = head_bias.shape[1], ffn_bias.shape[0], norm_bias.shape[1]
        norm_full = small[:, :, 0:6, :own_norm].transpose(2, 1, 0, 3).reshape(6, D)
        head_full = small[:, :, 6:8, :own_head].transpose(2, 0, 1, 3).reshape(2, 2, 3, 1, 128)
        ffn_full = small[:, :, 8, :own_ffn].reshape(1, FF)
        offsets = jnp.concatenate([head_full[0], jnp.zeros_like(head_full[0]), head_full[1]], axis=2)
        offsets = offsets.reshape(2, 1, QKV_HALF)
        qkv_full = qkv_g.reshape(2, D, QKV_HALF)
        up_full = up_g.reshape(2, D, FF // 2)
        down_full = down_g.reshape(FF, D)
        out_full = out_g.reshape(D, D)
        norm_full = jnp.pad(norm_full, ((0, 2), (0, 0)))
        qkv, context, lse = forward(tokens, qkv_full, offsets, seg_lengths)
        (layer_out, pooled, hidden_b, act, grad_branch, grad_inner, grad_attended, grad_context,
         grad_one, delta, norm_sums, ffn_sums) = middle_call(
            tokens, context, cotangent, seg_lengths, out_full, up_full, down_full, ffn_full,
            norm_full)
        grad_out, grad_up, grad_down = weight_grads(
            context.T, hidden_b.T, act.T, grad_branch, grad_inner, grad_attended,
            cores * data, held)
        token_flip = tokens.T
    grad_qkv, input_grad, grad_head = backward(
        token_flip, qkv, grad_context, lse, delta, seg_lengths, qkv_full, grad_one)
    small_grads = small_block(
        norm_sums[:6].reshape(6, data, cores, -1).transpose(2, 1, 0, 3),
        grad_head.reshape(2, cores, data, -1).transpose(1, 2, 0, 3),
        ffn_sums.reshape(cores, data, 1, -1),
    )
    fulls = [
        small_grads,
        grad_qkv.reshape(cores, data, rows_qkv, QKV_HALF),
        grad_out.reshape(cores, data, held, D),
        grad_up.reshape(cores, data, rows_qkv, FF // 2),
        grad_down.reshape(cores, data, -1, D),
    ]
    if fast:
        fulls = [f.reshape(2, 4, 2, 2, *f.shape[-2:]) for f in fulls]
        rows_old = [v.reshape(1, -1) for v in (qkv_rows, out_rows, up_rows, down_rows)]
        cols_old = [qkv_cols] + [v.reshape(1, -1) for v in (out_cols, up_cols, down_cols)]
        old = [head_bias_sq, ffn_bias_sq.reshape(1, -1), norm_sq]
        *reduced, lines, totals = scatter(
            fulls, [16, rows_qkv, rows_out, rows_qkv, w_down.shape[0]],
            rows_old, cols_old, old, weight_sums)
        new = step(reduced, lines, totals, weights, rows_old, cols_old, vectors, old)
        grads, (g_head, g_ffn, g_norm) = new[:4], new[4:7]
        rows_new, cols_new = [r.reshape(-1) for r in new[7:11]], new[11:15]
        cols_new = [cols_new[0]] + [c.reshape(-1) for c in cols_new[1:]]
        (s_head, s_ffn, s_norm), mats = new[15:18], new[18:22]
        n_head, n_ffn, n_norm = new[22:25]
        stats = [v for pair in zip(rows_new, cols_new) for v in pair]
        return (
            layer_out, pooled, input_grad, *grads, g_head, g_ffn.reshape(-1), g_norm, *stats,
            s_head, s_ffn.reshape(-1), s_norm, *mats, n_head, n_ffn.reshape(-1), n_norm,
        )
    red_small, red_qkv, red_out, red_up, red_down = scatter_plain(fulls)
    norm_grad = red_small[0:6, :own_norm]
    red_qkv = pair_major(red_qkv)
    red_head = red_small[6:8, :own_head]
    red_ffn = red_small[8, :own_ffn]
    weights_flat = [w_qkv.reshape(rows_qkv, -1), w_out, w_up, w_down]
    grads_flat = [red_qkv, red_out, red_up, red_down]
    rows_old = [qkv_rows, out_rows, up_rows, down_rows]
    cols_old = [qkv_cols.reshape(-1), out_cols, up_cols, down_cols]
    col_count = [3 * D, D, FF, D]
    row_count = [D, D, D, FF]
    row_share = [cores, 1, cores, 1]
    squares = [grad * grad + EPS_SQUARE for grad in grads_flat]
    row_parts = [jnp.sum(square, axis=1) for square in squares]
    col_parts = [jnp.sum(square, axis=0) for square in squares]
    vec_weights = [head_bias, ffn_bias, norm_bias]
    vec_grads = [red_head, red_ffn, norm_grad]
    vec_old = [head_bias_sq, ffn_bias_sq, norm_sq]
    vec_counts = [2 * D, FF, 6 * D]
    vec_second = [
        DECAY * old + (1.0 - DECAY) * (grad * grad + EPS_SQUARE)
        for old, grad in zip(vec_old, vec_grads)
    ]
    vec_update = [grad * lax.rsqrt(second) for grad, second in zip(vec_grads, vec_second)]
    weight_parts = [jnp.sum(weight * weight) for weight in weights_flat + vec_weights]
    vec_parts = [jnp.sum(update * update) for update in vec_update]
    row_qkv, row_up = lax.psum((row_parts[0], row_parts[2]), "mp")
    col_qkv, col_up = lax.psum((col_parts[0], col_parts[2]), "dp")
    col_out, col_down = lax.psum((col_parts[1], col_parts[3]), ("dp", "mp"))
    row_sums = [row_qkv, row_parts[1], row_up, row_parts[3]]
    col_sums = [col_qkv, col_out, col_up, col_down]
    rows_new = [
        DECAY * rows_old[index] + (1.0 - DECAY) * row_sums[index] / col_count[index]
        for index in range(4)
    ]
    cols_new = [
        DECAY * cols_old[index] + (1.0 - DECAY) * col_sums[index] / row_count[index]
        for index in range(4)
    ]
    ratio_parts = [
        jnp.sum(
            grads_flat[index]
            * grads_flat[index]
            / (rows_new[index][:, None] * cols_new[index][None, :])
        )
        for index in range(4)
    ]
    extra_parts = (
        [jnp.sum(rows_new[index]) / row_share[index] for index in range(4)]
        + weight_parts
        + vec_parts
    )
    totals = lax.psum(jnp.stack(ratio_parts + extra_parts), ("dp", "mp"))
    row_means = [totals[4 + index] / row_count[index] for index in range(4)]
    weight_totals = [totals[8 + index] for index in range(7)]
    vec_totals = [totals[15 + index] for index in range(3)]
    new_mats = []
    for index in range(4):
        entries = row_count[index] * col_count[index]
        estimate = rows_new[index][:, None] * cols_new[index][None, :] / row_means[index]
        update = grads_flat[index] / jnp.sqrt(estimate)
        update_rms = jnp.sqrt(row_means[index] * totals[index] / entries)
        stride = (
            RATE * jnp.sqrt(weight_totals[index] / entries) / jnp.maximum(1.0, update_rms / CLIP)
        )
        new_mats.append(weights_flat[index] - stride * update)
    new_vecs = []
    for index in range(3):
        update_rms = jnp.sqrt(vec_totals[index] / vec_counts[index])
        stride = (
            RATE
            * jnp.sqrt(weight_totals[4 + index] / vec_counts[index])
            / jnp.maximum(1.0, update_rms / CLIP)
        )
        new_vecs.append(vec_weights[index] - stride * vec_update[index])
    return (
        layer_out,
        pooled,
        input_grad,
        red_qkv.reshape(w_qkv.shape),
        red_out,
        red_up,
        red_down,
        red_head,
        red_ffn,
        norm_grad,
        rows_new[0],
        cols_new[0].reshape(qkv_cols.shape),
        rows_new[1],
        cols_new[1],
        rows_new[2],
        cols_new[2],
        rows_new[3],
        cols_new[3],
        vec_second[0],
        vec_second[1],
        vec_second[2],
        new_mats[0].reshape(w_qkv.shape),
        new_mats[1],
        new_mats[2],
        new_mats[3],
        new_vecs[0],
        new_vecs[1],
        new_vecs[2],
    )


def solution(mesh):
    return jax.shard_map(
        body,
        mesh=mesh,
        in_specs=(
            P(("dp", "mp"), None),
            P(("dp", "mp"), None),
            P("dp", None),
            P("dp", None, "mp"),
            P(("mp", "dp"), None),
            P("dp", "mp"),
            P(("mp", "dp"), None),
            P(None, ("mp", "dp")),
            P(("mp", "dp")),
            P(None, ("dp", "mp")),
            P("dp"),
            P(None, "mp"),
            P(("mp", "dp")),
            P(),
            P("dp"),
            P("mp"),
            P(("mp", "dp")),
            P(),
            P(None, ("mp", "dp")),
            P(("mp", "dp")),
            P(None, ("dp", "mp")),
        ),
        out_specs=(
            P(("dp", "mp"), None),
            P(("dp", "mp"), None, None),
            P(("dp", "mp"), None),
            P("dp", None, "mp"),
            P(("mp", "dp"), None),
            P("dp", "mp"),
            P(("mp", "dp"), None),
            P(None, ("mp", "dp")),
            P(("mp", "dp")),
            P(None, ("dp", "mp")),
            P("dp"),
            P(None, "mp"),
            P(("mp", "dp")),
            P(),
            P("dp"),
            P("mp"),
            P(("mp", "dp")),
            P(),
            P(None, ("mp", "dp")),
            P(("mp", "dp")),
            P(None, ("dp", "mp")),
            P("dp", None, "mp"),
            P(("mp", "dp"), None),
            P("dp", "mp"),
            P(("mp", "dp"), None),
            P(None, ("mp", "dp")),
            P(("mp", "dp")),
            P(None, ("dp", "mp")),
        ),
        check_vma=False,
    )
```

```python
import functools

import jax
import jax.numpy as jnp
from jax import lax
from jax.experimental import pallas as pl
from jax.experimental.pallas import tpu as pltpu
from jax.sharding import PartitionSpec as P

D = 768
HD = 64
FF = 3072
LEN = 512
SEGS = 8

EPS_NORM = 1e-12
EPS_SQUARE = 1e-30
DECAY = 0.5
RATE = 3.0
CLIP = 0.3

MESH = pl.DeviceIdType.MESH
BF = jnp.bfloat16
F32 = jnp.float32
EVERY = slice(None)


class Place:
    def __init__(self):
        d = lax.axis_index("dp")
        self.m = lax.axis_index("mp")
        self.z, self.y, self.x = d // 4, (d // 2) % 2, d % 2

    def at(self, axis, step):
        size = 4 if axis == "z" else 2
        spot = {"z": self.z, "y": self.y, "x": self.x, "m": self.m}
        spot[axis] = (spot[axis] + step) % size
        return spot

    @staticmethod
    def device(spot):
        return (spot["z"] * 4 + spot["y"] * 2 + spot["x"], spot["m"])


def steps_of(axis):
    return (1, 2, 3) if axis == "z" else (1,)


def greet(place):
    barrier = pltpu.get_barrier_semaphore()
    count = 0
    for axis in "zyxm":
        for step in steps_of(axis):
            pl.semaphore_signal(
                barrier, inc=1, device_id=place.device(place.at(axis, step)), device_id_type=MESH
            )
            count += 1
    pl.semaphore_wait(barrier, count)


def weight_sums_of(weights, small):
    parts = []
    for weight in weights:
        value = weight[...]
        if value.ndim == 3:
            parts.append(sum(all_sum(value[:, part] * value[:, part]) for part in range(3)))
        else:
            parts.append(all_sum(value * value))
    return scalars([jnp.zeros((1, 1), F32)] * 11 + parts + small_sums(small))


def to_column(row):
    count = row.shape[1]
    here = lax.broadcasted_iota(jnp.int32, (count, count), 0)
    there = lax.broadcasted_iota(jnp.int32, (count, count), 1)
    return jnp.sum(jnp.where(here == there, row, 0.0), axis=1, keepdims=True)


def to_row(column):
    count = column.shape[0]
    here = lax.broadcasted_iota(jnp.int32, (count, count), 0)
    there = lax.broadcasted_iota(jnp.int32, (count, count), 1)
    return jnp.sum(jnp.where(here == there, column, 0.0), axis=0, keepdims=True)


def put_line(ref, line, row):
    for tile in range(row.shape[1] // 128):
        ref[line + tile:line + tile + 1, :] = row[:, tile * 128:(tile + 1) * 128]


def get_line(ref, line, width):
    tiles = width // 128
    return jnp.concatenate([ref[line + t:line + t + 1, :] for t in range(tiles)], axis=1)


def scalars(values):
    lane = lax.broadcasted_iota(jnp.int32, (8, 128), 1)
    out = jnp.zeros((8, 128), F32)
    for index, value in enumerate(values):
        out = jnp.where(lane == index, value, out)
    return out


def all_sum(values):
    return jnp.sum(jnp.sum(values, axis=1, keepdims=True), axis=0, keepdims=True)


class Exchange:
    def __init__(self, place, mine, land, sems, base):
        self.place, self.mine, self.land = place, mine, land
        self.sems, self.base = sems, base
        self.sent = []

    def swap(self, stage, axis):
        place = self.place
        send, recv = self.sems
        own = place.z if axis == "z" else 0
        for step in steps_of(axis):
            slot = self.base + 4 * stage + step
            copy = pltpu.make_async_remote_copy(
                self.mine.at[stage], self.land.at[stage, own], send.at[slot], recv.at[slot],
                device_id=place.device(place.at(axis, step)), device_id_type=MESH)
            copy.start()
            self.sent.append(copy)
        if axis == "z":
            self.land[stage, place.z] = self.mine[stage]
        for step in steps_of(axis):
            slot = self.base + 4 * stage + step
            spot = (place.z - step) % 4 if axis == "z" else 0
            pltpu.make_async_remote_copy(
                self.mine.at[stage], self.land.at[stage, spot], send.at[slot], recv.at[slot],
                device_id=place.device(place.at(axis, step)), device_id_type=MESH).wait_recv()
        if axis == "z":
            land = self.land
            return (land[stage, 0] + land[stage, 1]) + (land[stage, 2] + land[stage, 3])
        return self.mine[stage] + self.land[stage, 0]

    def finish(self):
        for copy in self.sent:
            copy.wait_send()


def add_up(exchange, value, picked=None):
    exchange.mine[0] = value
    total = exchange.swap(0, "m")
    if picked is not None:
        total = jnp.where(picked, total, value)
    for stage, axis in ((1, "x"), (2, "y"), (3, "z")):
        exchange.mine[stage] = total
        total = exchange.swap(stage, axis)
    return total


QKV_LINE, UP_LINE, OUT_LINE, DOWN_LINE, ROW_LINE = 0, 9, 21, 27, 33
LINES = 40
WIDTHS = (3 * D // 2, D, FF // 2, D)
COL_LINES = (QKV_LINE, OUT_LINE, UP_LINE, DOWN_LINE)
COL_COUNT = (3 * D, D, FF, D)
ROW_COUNT = (D, D, D, FF)


def pair_cuts():
    out = []
    for pair in range(3):
        for part in range(3):
            start = (pair * 3 + part) * 128
            out.append(((slice(part, part + 1), slice(pair * 128, (pair + 1) * 128)),
                        slice(start, start + 128)))
    return out


def new_rows_cols(grads, rows_old, cols_old, lines):
    rows_new, cols_new = [], []
    for index in range(4):
        if index in (0, 2):
            line = ROW_LINE + index // 2
            count = rows_old[index].shape[1]
            row_sum = to_column(lines[line:line + 1, :count])
        else:
            grad = grads[index][...]
            row_sum = jnp.sum(grad * grad + EPS_SQUARE, axis=1, keepdims=True)
        rows_new.append(
            DECAY * to_column(rows_old[index][...]) + (1.0 - DECAY) * row_sum / COL_COUNT[index])
        col_sum = get_line(lines, COL_LINES[index], WIDTHS[index])
        if index == 0:
            old = jnp.concatenate([cols_old[0][at] for at, _ in pair_cuts()], axis=1)
        else:
            old = cols_old[index][...]
        cols_new.append(DECAY * old + (1.0 - DECAY) * col_sum / ROW_COUNT[index])
    return rows_new, cols_new


def place_small(ref, norm, head, ffn, fill):
    ref[...] = jnp.full(ref.shape, fill, F32)
    ref[0:6, 0:norm.shape[1]] = norm
    ref[6:8, 0:head.shape[1]] = head
    ref[8:9, 0:ffn.shape[1]] = ffn


def small_update(grad, old):
    second = DECAY * old + (1.0 - DECAY) * (grad * grad + EPS_SQUARE)
    return second, grad * lax.rsqrt(second)


def small_sums(values):
    line = lax.broadcasted_iota(jnp.int32, values.shape, 0)
    square = values * values
    return [
        all_sum(jnp.where((line >= 6) & (line < 8), square, 0.0)),
        all_sum(jnp.where(line == 8, square, 0.0)),
        all_sum(jnp.where(line < 6, square, 0.0)),
    ]


def step_kernel(*refs):
    refs = list(refs)
    take = lambda number: [refs.pop(0) for _ in range(number)]
    grads = take(4)
    small, lines, totals = take(3)
    weights, rows_old, cols_old = take(4), take(4), take(4)
    head, ffn, norm, head_sq, ffn_sq, norm_sq = take(6)
    grads_out = take(4)
    head_grad, ffn_grad, norm_grad = take(3)
    rows_out, cols_out = take(4), take(4)
    head_second, ffn_second, norm_second = take(3)
    weights_out = take(4)
    head_new, ffn_new, norm_new = take(3)
    old_small, weight_small = refs
    rows_new, cols_new = new_rows_cols(grads, rows_old, cols_old, lines)
    total = lambda lane: totals[0:1, lane:lane + 1]
    for index in range(4):
        rows_out[index][...] = to_row(rows_new[index])
        if index == 0:
            for at, cut in pair_cuts():
                cols_out[0][at] = cols_new[0][:, cut]
        else:
            cols_out[index][...] = cols_new[index]
        entries = ROW_COUNT[index] * COL_COUNT[index]
        row_mean = total(4 + index) / ROW_COUNT[index]
        update_rms = jnp.sqrt(row_mean * total(index) / entries)
        stride = (
            RATE * jnp.sqrt(total(11 + index) / entries) / jnp.maximum(1.0, update_rms / CLIP))
        scale_rows = lax.rsqrt(rows_new[index] / row_mean) * stride
        scale_cols = lax.rsqrt(cols_new[index])
        if index == 0:
            for (part, cols), cut in pair_cuts():
                at = (EVERY, part.start, cols)
                grad = grads[0][:, cut]
                grads_out[0][at] = grad
                weights_out[0][at] = weights[0][at] - grad * scale_rows * scale_cols[:, cut]
        else:
            grad = grads[index][...]
            grads_out[index][...] = grad
            weights_out[index][...] = weights[index][...] - grad * scale_rows * scale_cols
    place_small(old_small, norm_sq[...], head_sq[...], ffn_sq[...], 1.0)
    place_small(weight_small, norm[...], head[...], ffn[...], 0.0)
    grad = small[...]
    second, update = small_update(grad, old_small[...])
    line = lax.broadcasted_iota(jnp.int32, grad.shape, 0)
    counts = (2 * D, FF, 6 * D)
    strides = []
    for index in range(3):
        update_rms = jnp.sqrt(total(8 + index) / counts[index])
        strides.append(
            RATE * jnp.sqrt(total(15 + index) / counts[index])
            / jnp.maximum(1.0, update_rms / CLIP))
    stride = jnp.where(line < 6, strides[2], jnp.where(line < 8, strides[0], strides[1]))
    fresh = weight_small[...] - stride * update
    for values, (norm_ref, head_ref, ffn_ref) in (
        (grad, (norm_grad, head_grad, ffn_grad)),
        (second, (norm_second, head_second, ffn_second)),
        (fresh, (norm_new, head_new, ffn_new)),
    ):
        norm_ref[...] = values[0:6, 0:norm_ref.shape[1]]
        head_ref[...] = values[6:8, 0:head_ref.shape[1]]
        ffn_ref[...] = values[8:9, 0:ffn_ref.shape[1]]


def step(reduced, lines, totals, weights, rows_old, cols_old, vectors, squares):
    vmem = pl.BlockSpec(memory_space=pltpu.VMEM)
    small, grads = reduced[0], reduced[1:]
    shapes = [w.shape for w in weights] + [v.shape for v in vectors]
    shapes += [r.shape for r in rows_old] + [c.shape for c in cols_old]
    shapes += [v.shape for v in vectors] + [w.shape for w in weights] + [v.shape for v in vectors]
    operands = [*grads, small, lines, totals, *weights, *rows_old, *cols_old, *vectors, *squares]
    return pl.pallas_call(
        step_kernel,
        out_shape=[jax.ShapeDtypeStruct(s, F32) for s in shapes],
        in_specs=[vmem] * len(operands),
        out_specs=[vmem] * len(shapes),
        scratch_shapes=[pltpu.VMEM((16, 128), F32), pltpu.VMEM((16, 128), F32)],
        compiler_params=pltpu.CompilerParams(vmem_limit_bytes=32 << 20),
        name="adafactor_step",
    )(*operands)


HALF = D // 2
QKV_HALF = 3 * HALF
VMEM = pl.BlockSpec(memory_space=pltpu.VMEM)
SMEM = pl.BlockSpec(memory_space=pltpu.SMEM)


def dot(a, b):
    return jnp.dot(a, b, preferred_element_type=F32)


def dot_last(a, b):
    return lax.dot_general(a, b, (((1,), (1,)), ((), ())), preferred_element_type=F32)


def dot_first(a, b):
    return lax.dot_general(a, b, (((0,), (0,)), ((), ())), preferred_element_type=F32)


def ids_at(lengths, row, places):
    bound = jnp.int32(0)
    ids = jnp.zeros(places.shape, jnp.int32)
    for segment in range(SEGS):
        bound = bound + lengths[row, segment]
        ids = ids + (places >= bound).astype(jnp.int32)
    return ids


def set_bias(bias, lengths, row):
    down = ids_at(lengths, row, lax.broadcasted_iota(jnp.int32, (LEN, 1), 0))
    across = ids_at(lengths, row, lax.broadcasted_iota(jnp.int32, (1, LEN), 1))
    bias[...] = jnp.where(down == across, 0.0, -1e30)


def half_masks():
    lane = lax.broadcasted_iota(jnp.int32, (1, 128), 1)
    return [((lane // HD) == half).astype(F32).astype(BF) for half in range(2)]


PAIR = 3 * 128


def slab(ref, core, row, part, pair):
    return ref[core, pl.ds(pl.multiple_of(row * LEN, LEN), LEN),
               pl.ds(pl.multiple_of(pair * PAIR + part * 128, 128), 128)]


def project(tokens, weight, offsets, qkv, row):
    rows = pl.ds(pl.multiple_of(row * LEN, LEN), LEN)
    values = tokens[rows, :]
    for core in range(2):
        for pair in range(3):
            cut = slice(pair * PAIR, (pair + 1) * PAIR)
            out = (dot(values, weight[core, :, cut]) + offsets[core, :, cut]).astype(BF)
            scale = jnp.where(
                lax.broadcasted_iota(jnp.int32, (1, PAIR), 1) < 128, HD ** -0.5, 1.0).astype(BF)
            qkv[core, rows, cut] = out * scale


def attend(qkv, bias, context, lse, held, row):
    rows = pl.ds(pl.multiple_of(row * LEN, LEN), LEN)
    lane = lax.broadcasted_iota(jnp.int32, (LEN, 128), 1)
    held[...] = jnp.zeros(held.shape, F32)

    @pl.loop(0, 6)
    def _(item):
        core, pair = item // 3, item % 3
        queries, keys, values = (slab(qkv, core, row, part, pair) for part in range(3))
        wide = jnp.concatenate([values, jnp.ones_like(values)], axis=1)
        outs = []
        logs = held[...]
        for half, mask in enumerate(half_masks()):
            scores = dot_last(queries * mask, keys) + bias[...]
            peak = jnp.max(scores, axis=1, keepdims=True)
            raised = jnp.exp(scores - peak).astype(BF)
            both = dot(raised, wide)
            total = both[:, 128:]
            outs.append(both[:, :128] / total)
            logs = jnp.where(lane == item * 2 + half, peak + jnp.log(total), logs)
        held[...] = logs
        context[rows, pl.ds(pl.multiple_of(item * 128, 128), 128)] = jnp.where(
            lane < HD, outs[0], outs[1]).astype(BF)

    lse[row] = held[...].T[0:16, :]


def forward_kernel(tokens, weight, offsets, lengths, qkv, context, lse, bias, held):
    core = lax.axis_index("mp")

    @pl.loop(0, 2)
    def _(row):
        set_bias(bias, lengths, core * 2 + row)
        project(tokens, weight, offsets, qkv, row)
        attend(qkv, bias, context, lse, held, row)


def forward(tokens, weight, offsets, lengths):
    count = tokens.shape[0]
    return pl.pallas_call(
        forward_kernel,
        out_shape=[
            jax.ShapeDtypeStruct((2, count, QKV_HALF), BF),
            jax.ShapeDtypeStruct((count, D), BF),
            jax.ShapeDtypeStruct((count // LEN, 16, LEN), F32),
        ],
        in_specs=[VMEM, VMEM, VMEM, SMEM],
        out_specs=[VMEM] * 3,
        scratch_shapes=[pltpu.VMEM((LEN, LEN), F32), pltpu.VMEM((LEN, 128), F32)],
        compiler_params=pltpu.CompilerParams(vmem_limit_bytes=56 << 20),
        name="project_attend",
    )(tokens, weight, offsets, lengths)


def gelu_both(inner):
    cdf = 0.5 * (1.0 + lax.erf(inner * 0.7071067811865476))
    density = 0.3989422804014327 * jnp.exp(-0.5 * inner * inner)
    return inner * cdf, cdf + inner * density


def norm_parts(values):
    center = values - jnp.mean(values, axis=-1, keepdims=True)
    scale = lax.rsqrt(jnp.mean(center * center, axis=-1, keepdims=True) + EPS_NORM)
    return center * scale, scale


def norm_back(grad, normed, scale, gain):
    scaled = grad * gain
    mean = jnp.mean(scaled, axis=-1, keepdims=True)
    along = jnp.mean(scaled * normed, axis=-1, keepdims=True)
    return (
        (scaled - mean - normed * along) * scale,
        jnp.sum(grad * normed, axis=0, keepdims=True),
        jnp.sum(grad, axis=0, keepdims=True),
    )


CHUNK = 512


def middle(row, core, tokens, context, cotangent, lengths, w_out, w_up, w_down, ffn, norm, layer_out,
           pooled, hidden_b, act, grad_branch, grad_inner, grad_attended, grad_context,
           grad_one, delta, norm_sums, ffn_sums, slope, branch, hidden, normed_one, grad_two):
    rows = pl.ds(pl.multiple_of(row * LEN, LEN), LEN)
    attended = dot(context[rows, :], w_out[...]) + norm[0:1, :]
    normed, scale_one = norm_parts(tokens[rows, :].astype(F32) + attended)
    normed_one[...] = normed
    value = normed * norm[2:3, :] + norm[3:4, :]
    hidden[...] = value
    hidden_b[rows, :] = value.astype(BF)
    branch[...] = jnp.zeros(branch.shape, F32)
    for chunk in range(FF // CHUNK):
        core_of, start = chunk * CHUNK // (FF // 2), chunk * CHUNK % (FF // 2)
        cols = slice(chunk * CHUNK, (chunk + 1) * CHUNK)
        up = w_up[core_of, :, start:start + CHUNK]
        value, slope_value = gelu_both(dot(hidden_b[rows, :], up) + ffn[:, cols])
        value = value.astype(BF)
        act[rows, cols] = value
        slope[:, cols] = slope_value.astype(BF)
        branch[...] += dot(value, w_down[cols, :])
    normed, scale = norm_parts(hidden[...] + branch[...] + norm[1:2, :])
    output = normed * norm[4:5, :] + norm[5:6, :]
    high = output.astype(BF)
    layer_out[rows, :] = high
    low = (output - high.astype(F32)).astype(BF)
    place = lax.broadcasted_iota(jnp.int32, (SEGS, LEN), 1)
    segment = lax.broadcasted_iota(jnp.int32, (SEGS, 1), 0)
    ids = ids_at(lengths, core * 2 + row, place)
    member = (ids == segment).astype(F32)
    sizes = jnp.sum(member, axis=1, keepdims=True)
    member = member.astype(BF)
    pooled[row] = (dot(member, high) + dot(member, low)) / sizes
    back, gain, shift = norm_back(cotangent[rows, :].astype(F32), normed, scale, norm[4:5, :])
    norm_sums[4:5, :] += gain
    norm_sums[5:6, :] += shift
    grad_two[...] = back
    back = back.astype(BF)
    grad_branch[rows, :] = back
    norm_sums[1:2, :] += jnp.sum(back.astype(F32), axis=0, keepdims=True)
    for chunk in range(FF // CHUNK):
        core_of, start = chunk * CHUNK // (FF // 2), chunk * CHUNK % (FF // 2)
        cols = slice(chunk * CHUNK, (chunk + 1) * CHUNK)
        value = dot_last(grad_branch[rows, :], w_down[cols, :])
        value = (value * slope[:, cols].astype(F32)).astype(BF)
        grad_inner[rows, cols] = value
        ffn_sums[:, cols] += jnp.sum(value.astype(F32), axis=0, keepdims=True)
        grad_two[...] += dot_last(value, w_up[core_of, :, start:start + CHUNK])
    back, gain, shift = norm_back(grad_two[...], normed_one[...], scale_one, norm[2:3, :])
    norm_sums[2:3, :] += gain
    norm_sums[3:4, :] += shift
    grad_one[rows, :] = back
    back = back.astype(BF)
    grad_attended[rows, :] = back
    norm_sums[0:1, :] += jnp.sum(back.astype(F32), axis=0, keepdims=True)
    back = dot_last(back, w_out[...]).astype(BF)
    grad_context[rows, :] = back
    product = back.astype(F32) * context[rows, :].astype(F32)
    high = product.astype(BF)
    low = (product - high.astype(F32)).astype(BF)
    head = lax.broadcasted_iota(jnp.int32, (16, D), 0)
    member = (lax.broadcasted_iota(jnp.int32, (16, D), 1) // HD == head).astype(F32).astype(BF)
    delta[row] = dot_last(member, high) + dot_last(member, low)


def middle_kernel(*refs):
    core = lax.axis_index("mp")
    norm_sums, ffn_sums = refs[19], refs[20]
    norm_sums[...] = jnp.zeros(norm_sums.shape, F32)
    ffn_sums[...] = jnp.zeros(ffn_sums.shape, F32)

    @pl.loop(0, 2)
    def _(row):
        middle(row, core, *refs)


def middle_call(tokens, context, cotangent, lengths, w_out, w_up, w_down, ffn, norm):
    count = tokens.shape[0]
    shape = jax.ShapeDtypeStruct
    return pl.pallas_call(
        middle_kernel,
        out_shape=[
            shape((count, D), BF),
            shape((count // LEN, SEGS, D), F32),
            shape((count, D), BF),
            shape((count, FF), BF),
            shape((count, D), BF),
            shape((count, FF), BF),
            shape((count, D), BF),
            shape((count, D), BF),
            shape((count, D), F32),
            shape((count // LEN, 16, LEN), F32),
            shape((8, D), F32),
            shape((1, FF), F32),
        ],
        in_specs=[VMEM] * 3 + [SMEM] + [VMEM] * 5,
        out_specs=[VMEM] * 12,
        scratch_shapes=[
            pltpu.VMEM((LEN, FF), BF),
            pltpu.VMEM((LEN, D), F32),
            pltpu.VMEM((LEN, D), F32),
            pltpu.VMEM((LEN, D), F32),
            pltpu.VMEM((LEN, D), F32),
        ],
        compiler_params=pltpu.CompilerParams(vmem_limit_bytes=60 << 20),
        name="feed_forward",
    )(tokens, context, cotangent, lengths, w_out, w_up, w_down, ffn, norm)


def weight_grads_kernel(context, hidden_b, act, grad_branch, grad_inner, grad_attended,
                        out_grad, up_grad, down_grad):

    @pl.loop(0, FF // CHUNK)
    def _(chunk):
        half_chunks = FF // 2 // CHUNK
        cols = pl.ds(pl.multiple_of(chunk * CHUNK, CHUNK), CHUNK)
        local = pl.ds(pl.multiple_of((chunk % half_chunks) * CHUNK, CHUNK), CHUNK)
        up_grad[chunk // half_chunks, :, local] = dot(hidden_b[...], grad_inner[:, cols]).astype(BF)
        down_grad[cols, :] = dot(act[cols, :], grad_branch[...]).astype(BF)

    value = dot(context[...], grad_attended[...])
    rows, held = D // out_grad.shape[0], out_grad.shape[1]
    for block in range(out_grad.shape[0]):
        piece = value[block * rows:(block + 1) * rows, :]
        if held > rows:
            piece = jnp.concatenate([piece, jnp.zeros((held - rows, D), F32)], axis=0)
        out_grad[block] = piece.astype(BF)


def weight_grads(context, hidden_b, act, grad_branch, grad_inner, grad_attended, blocks, held):
    shape = jax.ShapeDtypeStruct
    return pl.pallas_call(
        weight_grads_kernel,
        out_shape=[shape((blocks, held, D), BF), shape((2, D, FF // 2), BF), shape((FF, D), BF)],
        in_specs=[VMEM] * 6,
        out_specs=[VMEM] * 3,
        compiler_params=pltpu.CompilerParams(vmem_limit_bytes=60 << 20),
        name="weight_grads",
    )(context, hidden_b, act, grad_branch, grad_inner, grad_attended)


def attend_back(qkv, grad_context, lse, delta, bias, grad_qkv, grad_head, row):
    rows = pl.ds(pl.multiple_of(row * LEN, LEN), LEN)
    lane = lax.broadcasted_iota(jnp.int32, (LEN, 128), 1)

    @pl.loop(0, 6)
    def _(item):
        core, pair = item // 3, item % 3
        queries, keys, values = (slab(qkv, core, row, part, pair) for part in range(3))
        wide = pl.ds(pl.multiple_of(item * 128, 128), 128)
        grad = grad_context[rows, wide]
        flipped = keys.T
        grads_k, grads_v, grads_q = [], [], []
        for half, mask in enumerate(half_masks()):
            head = item * 2 + half
            scores = dot_last(keys * mask, queries) + bias[...] - lse[row, pl.ds(head, 1), :]
            probs = jnp.exp(scores)
            grad_probs = dot_last(values * mask, grad)
            grad_scores = (probs * (grad_probs - delta[row, pl.ds(head, 1), :])).astype(BF)
            grads_v.append(dot(probs.astype(BF), grad))
            grads_k.append(dot(grad_scores, queries))
            grads_q.append(dot(flipped[half * HD:(half + 1) * HD, :], grad_scores))
        grad_q = (jnp.concatenate(grads_q, axis=0).T * HD ** -0.5).astype(BF)
        grad_k = jnp.where(lane < HD, grads_k[0], grads_k[1]).astype(BF)
        grad_v = jnp.where(lane < HD, grads_v[0], grads_v[1]).astype(BF)
        for part, value in enumerate((grad_q, grad_k, grad_v)):
            grad_qkv[core, rows, pl.ds(pl.multiple_of(pair * PAIR + part * 128, 128), 128)] = value
        grad_head[0:1, wide] += jnp.sum(grad_q.astype(F32), axis=0, keepdims=True)
        grad_head[1:2, wide] += jnp.sum(grad_v.astype(F32), axis=0, keepdims=True)


def backward_kernel(tokens, qkv, grad_context, lse, delta, lengths, weight, grad_one,
                    qkv_grad, input_grad, grad_head, grad_qkv, bias):
    core = lax.axis_index("mp")
    grad_head[...] = jnp.zeros(grad_head.shape, F32)

    @pl.loop(0, 2)
    def _(row):
        set_bias(bias, lengths, core * 2 + row)
        attend_back(qkv, grad_context, lse, delta, bias, grad_qkv, grad_head, row)
        rows = pl.ds(pl.multiple_of(row * LEN, LEN), LEN)
        input_grad[rows, :] = (
            grad_one[rows, :]
            + dot_last(grad_qkv[0, rows, :], weight[0])
            + dot_last(grad_qkv[1, rows, :], weight[1])
        )

    for core_of in range(2):
        for part in range(3):
            cut = slice(part * HALF, (part + 1) * HALF)
            qkv_grad[core_of, :, cut] = dot(tokens[...], grad_qkv[core_of, :, cut]).astype(BF)


def backward(tokens, qkv, grad_context, lse, delta, lengths, weight, grad_one):
    count = tokens.shape[1]
    shape = jax.ShapeDtypeStruct
    return pl.pallas_call(
        backward_kernel,
        out_shape=[shape((2, D, QKV_HALF), BF), shape((count, D), F32), shape((2, D), F32)],
        in_specs=[VMEM] * 5 + [SMEM] + [VMEM] * 2,
        out_specs=[VMEM] * 3,
        scratch_shapes=[
            pltpu.VMEM((2, count, QKV_HALF), BF),
            pltpu.VMEM((LEN, LEN), F32),
        ],
        compiler_params=pltpu.CompilerParams(vmem_limit_bytes=60 << 20),
        name="attend_back",
    )(tokens, qkv, grad_context, lse, delta, lengths, weight, grad_one)


UP_CHUNK = 512
DOWN_CHUNK = 256


class Spread:
    COUNT = 8

    def __init__(self, place, full, start, width, flip, sems, base, shard=None):
        self.place, self.full, self.shard = place, full, shard
        self.cols = pl.ds(start, width)
        tiles = width // 128
        cut = (tiles // 2 if flip else tiles - tiles // 2) * 128
        self.halves = [("xy", pl.ds(start, cut))]
        if cut < width:
            self.halves.append(("yx", pl.ds(start + cut, width - cut)))
        self.sems, self.base = sems, base

    def view(self, spot, cols):
        return self.full.at[spot["m"], spot["z"], spot["y"], spot["x"], :, cols]

    def copy(self, slot, axis, step, spot, cols, source=None):
        place = self.place
        send, recv = self.sems
        send, recv = send.at[self.base + slot], recv.at[self.base + slot]
        device = place.device(place.at(axis, step))
        view = self.view(spot, cols)
        sent = pltpu.make_async_remote_copy(
            view if source is None else source, view, send, recv,
            device_id=device, device_id_type=MESH)
        land = dict(spot)
        land[axis] = place.at(axis, -step)[axis]
        land = self.view(land, cols)
        arrives = pltpu.make_async_remote_copy(
            land, land, send, recv, device_id=device, device_id_type=MESH)
        return sent, arrives

    def copies(self, stage):
        place = self.place
        here = {"z": place.z, "y": place.y, "x": place.x, "m": place.m}
        if stage == 0:
            source = None if self.shard is None else self.shard.at[:, self.cols]
            return [self.copy(step - 1, "z", step, here, self.cols, source) for step in (1, 2, 3)]
        here["z"] = EVERY
        if stage == 3:
            here["y"] = here["x"] = EVERY
            return [self.copy(7, "m", 1, here, self.cols)]
        out = []
        for number, (order, cols) in enumerate(self.halves):
            spot = dict(here)
            if stage == 2:
                spot[order[0]] = EVERY
            out.append(self.copy(1 + 2 * stage + number, order[stage - 1], 1, spot, cols))
        return out

    def start(self, stage):
        for sent, _ in self.copies(stage):
            sent.start()

    def arrived(self, stage):
        for _, arrives in self.copies(stage):
            arrives.wait_recv()

    def finish(self):
        for stage in range(4):
            for sent, _ in self.copies(stage):
                sent.wait_send()


def spread_tick(groups, tick):
    for stage in range(4):
        index = tick + 2 if stage == 0 else tick - stage + 1
        if 0 <= index < len(groups):
            for chunk in groups[index]:
                if stage:
                    chunk.arrived(stage - 1)
                chunk.start(stage)


def unpack_small(small, norm_out, offsets, ffn_out):
    iota = lambda shape, axis: lax.broadcasted_iota(jnp.int32, shape, axis)
    pick = ((iota((128, D), 1) % 24 == iota((128, D), 0))).astype(F32).astype(BF)
    pick_ffn = ((iota((128, FF), 1) % 96 == iota((128, FF), 0))).astype(F32).astype(BF)
    total = jnp.zeros((16, D), F32)
    ffn = jnp.zeros((1, FF), F32)
    line, col = iota((256, D), 0), iota((256, D), 1) // 24
    device, kind = line // 16, line % 16
    for core in range(2):
        block = small[core].reshape(256, 128).astype(BF)
        wide = dot(block, pick)
        right = jnp.where(kind < 6, 2 * device + core, 16 * core + device)
        wide = jnp.where((col == right) & (kind < 8), wide, 0.0)
        total = total + jnp.sum(wide.reshape(16, 16, D), axis=0)
        wide = dot(small[core, :, :, :, 8, :].reshape(16, 128).astype(BF), pick_ffn)
        right = iota((16, FF), 1) // 96 == iota((16, FF), 0) + 16 * core
        ffn = ffn + jnp.sum(jnp.where(right, wide, 0.0), axis=0, keepdims=True)
    norm_out[0:6, :] = total[0:6, :]
    norm_out[6:8, :] = jnp.zeros((2, D), F32)
    ffn_out[...] = ffn
    offsets[...] = jnp.zeros(offsets.shape, F32)
    for core in range(2):
        for pair in range(3):
            source = core * HALF + pair * 128
            for part, row in ((0, 6), (2, 7)):
                start = pair * PAIR + part * 128
                offsets[core, :, start:start + 128] = total[row:row + 1, source:source + 128]


def project_pair(tokens, weight, offsets, qkv, pair):
    cols = pl.ds(pl.multiple_of(pair * PAIR, PAIR), PAIR)
    scale = jnp.where(
        lax.broadcasted_iota(jnp.int32, (1, PAIR), 1) < 128, HD ** -0.5, 1.0).astype(BF)
    for core in range(2):
        piece = weight[core, :, :, :, :, cols].reshape(D, PAIR)
        out = dot(tokens[...], piece) + offsets[core, :, cols]
        qkv[core, :, cols] = out.astype(BF) * scale


def attend_pair(qkv, bias, context, logs_ref, core, row, pair):
    rows = pl.ds(pl.multiple_of(row * LEN, LEN), LEN)
    lane = lax.broadcasted_iota(jnp.int32, (LEN, 128), 1)
    item = core * 3 + pair
    queries, keys, values = (slab(qkv, core, row, part, pair) for part in range(3))
    wide = jnp.concatenate([values, jnp.ones_like(values)], axis=1)
    outs = []
    logs = logs_ref[row]
    for half, mask in enumerate(half_masks()):
        scores = dot_last(queries * mask, keys) + bias[row]
        peak = jnp.max(scores, axis=1, keepdims=True)
        raised = jnp.exp(scores - peak).astype(BF)
        both = dot(raised, wide)
        total = both[:, 128:]
        outs.append(both[:, :128] / total)
        logs = jnp.where(lane == item * 2 + half, peak + jnp.log(total), logs)
    logs_ref[row] = logs
    context[rows, pl.ds(pl.multiple_of(item * 128, 128), 128)] = jnp.where(
        lane < HD, outs[0], outs[1]).astype(BF)


def forward_gather_kernel(*refs):
    refs = list(refs)
    take = lambda number: [refs.pop(0) for _ in range(number)]
    w_qkv, w_out, w_up, w_down, head, ffn, norm, tokens, lengths = take(9)
    (sums, norm_out, ffn_out, lse, hidden_scale, out_full) = take(6)
    (qkv_full, up_full, down_full, qkv_out, context_flip, token_flip, hidden_flip, normed_out,
     context_out, act_out, act_flip, slope_out) = take(12)
    (g_small, g_qkv, g_out, g_up, cast_down, qkv, context, flip_context, flip_token, flip_hidden,
     hidden_b, normed_one, act, slope, flip_act, bias, logs, offsets) = take(18)
    send, recv, local = refs
    place = Place()
    here = (place.m, place.z, place.y, place.x)
    half = w_qkv.shape[2]
    place_small(g_small.at[here], norm[...], head[...], ffn[...], 0.0)
    for part in range(3):
        for pair in range(3):
            start = pair * PAIR + part * 128
            g_qkv[here + (EVERY, slice(start, start + 128))] = w_qkv[
                :, part, pair * 128:(pair + 1) * 128].astype(BF)
    value = w_out[...]
    spare = g_out.shape[4] - value.shape[0]
    g_out[here] = jnp.concatenate([value, jnp.zeros((spare, D), F32)], axis=0).astype(BF)
    g_up[here] = w_up[...].astype(BF)
    cast_down[...] = w_down[...].astype(BF)
    copies, used = [], [0]

    def keep(source, target):
        copy = pltpu.make_async_copy(source, target, local.at[used[0]])
        used[0] += 1
        copy.start()
        copies.append(copy)
        return copy

    down_own = keep(cast_down, down_full.at[here])
    sems, base = (send, recv), [0]

    def chunk(full, start, width, flip, shard=None):
        made = Spread(place, full, start, width, flip, sems, base[0], shard)
        base[0] += Spread.COUNT
        return made

    groups = [[chunk(g_small, 0, 128, False), chunk(g_qkv, 0, PAIR, False)]]
    groups += [[chunk(g_qkv, pair * PAIR, PAIR, pair == 1)] for pair in (1, 2)]
    groups += [[chunk(g_out, 0, D, False)]]
    groups += [[chunk(g_up, at, UP_CHUNK, False)] for at in range(0, FF // 2, UP_CHUNK)]
    groups += [[chunk(down_full, at, DOWN_CHUNK, False, cast_down)]
               for at in range(0, D, DOWN_CHUNK)]

    def ready(index):
        for made in groups[index]:
            made.arrived(3)

    greet(place)
    for index in (0, 1):
        for made in groups[index]:
            made.start(0)
    sums[...] = weight_sums_of([w_qkv, w_out, w_up, w_down], g_small[here])
    down_own.wait()
    spread_tick(groups, 0)
    for row in range(2):
        set_bias(bias.at[row], lengths, place.m * 2 + row)
    spread_tick(groups, 1)
    flip_token[...] = tokens[...].T
    keep(flip_token, token_flip)
    spread_tick(groups, 2)
    logs[...] = jnp.zeros(logs.shape, F32)
    ready(0)
    unpack_small(g_small, norm_out, offsets, ffn_out)

    @pl.loop(0, 12)
    def _(item):
        pair, row, core = item // 4, (item % 4) // 2, item % 2
        for number, at in enumerate((2, 4, 6, 8, 10)):
            @pl.when(item == at)
            def _():
                spread_tick(groups, 3 + number)
                if at in (4, 8):
                    ready(at // 4)

        @pl.when(item % 4 == 0)
        def _():
            project_pair(tokens, g_qkv, offsets, qkv, pair)

        attend_pair(qkv, bias, context, logs, core, row, pair)

    for core in range(2):
        keep(g_qkv.at[core], qkv_full.at[core])
    keep(qkv, qkv_out)
    keep(context, context_out)
    for row in range(2):
        lse[row] = logs[row].T[0:16, :]
    flip_context[...] = context[...].T
    keep(flip_context, context_flip)
    ready(3)
    rows_out = w_out.shape[0]
    for core in range(2):
        value = g_out[core].reshape(16, g_out.shape[4], D).astype(F32)[:, :rows_out]
        out_full[core * HALF:(core + 1) * HALF, :] = value.reshape(HALF, D).astype(BF)
    for row in range(2):
        rows = slice(row * LEN, (row + 1) * LEN)
        attended = dot(context[rows, :], out_full[...]) + norm_out[0:1, :]
        normed, scale = norm_parts(tokens[rows, :].astype(F32) + attended)
        normed_one[rows, :] = normed
        hidden_scale[rows, :] = jnp.broadcast_to(scale, (LEN, 128))
        hidden_b[rows, :] = (normed * norm_out[2:3, :] + norm_out[3:4, :]).astype(BF)
    keep(normed_one, normed_out)
    flip_hidden[...] = hidden_b[...].T
    keep(flip_hidden, hidden_flip)
    spread_tick(groups, 8)
    waiting = [[], []]
    for third in range(3):
        ready(4 + third)
        for core in range(2):
            for copy in waiting[core]:
                copy.wait()
            local_cols = slice(third * UP_CHUNK, (third + 1) * UP_CHUNK)
            start = core * (FF // 2) + third * UP_CHUNK
            cols = pl.ds(start, UP_CHUNK)
            up = g_up[core, :, :, :, :, local_cols].reshape(D, UP_CHUNK)

            @pl.loop(0, 2)
            def _(row):
                rows = pl.ds(pl.multiple_of(row * LEN, LEN), LEN)
                value, slope_value = gelu_both(
                    dot(hidden_b[rows, :], up) + ffn_out[:, start:start + UP_CHUNK])
                act[core, rows, :] = value.astype(BF)
                slope[core, rows, :] = slope_value.astype(BF)

            flip_act[core] = act[core].T
            slot = 16 + 3 * core
            waiting[core] = [
                pltpu.make_async_copy(act.at[core], act_out.at[:, cols], local.at[slot]),
                pltpu.make_async_copy(slope.at[core], slope_out.at[:, cols], local.at[slot + 1]),
                pltpu.make_async_copy(flip_act.at[core], act_flip.at[cols, :], local.at[slot + 2]),
            ]
            for copy in waiting[core]:
                copy.start()
        spread_tick(groups, 9 + third)
    for core in range(2):
        keep(g_up.at[core], up_full.at[core])
    for index in (7, 8, 9):
        ready(index)
    for copy in copies[1:] + waiting[0] + waiting[1]:
        copy.wait()
    for group in groups:
        for made in group:
            made.finish()


def forward_gather(weights, vectors, tokens, lengths):
    qkv, out, up, down = weights
    count = tokens.shape[0]
    shape = jax.ShapeDtypeStruct
    grid = (2, 4, 2, 2)
    held_out = 32
    flipped = shape((D, count), BF)
    small_outs = [
        shape((8, 128), F32), shape((8, D), F32), shape((1, FF), F32),
        shape((count // LEN, 16, LEN), F32), shape((count, 128), F32), shape((D, D), BF),
    ]
    large_outs = [
        shape(grid + (qkv.shape[0], QKV_HALF), BF), shape(grid + up.shape, BF),
        shape(grid + down.shape, BF), shape((2, count, QKV_HALF), BF), flipped, flipped, flipped,
        shape((count, D), F32), shape((count, D), BF), shape((count, FF), BF),
        shape((FF, count), BF), shape((count, FF), BF),
    ]
    slots = 11 * Spread.COUNT
    return pl.pallas_call(
        forward_gather_kernel,
        out_shape=small_outs + large_outs,
        in_specs=[VMEM] * 8 + [SMEM],
        out_specs=[VMEM] * len(small_outs) + [pl.BlockSpec(memory_space=pl.ANY)] * len(large_outs),
        scratch_shapes=[
            pltpu.VMEM(grid + (16, 128), F32),
            pltpu.VMEM(grid + (qkv.shape[0], QKV_HALF), BF),
            pltpu.VMEM(grid + (held_out, D), BF),
            pltpu.VMEM(grid + up.shape, BF),
            pltpu.VMEM(down.shape, BF),
            pltpu.VMEM((2, count, QKV_HALF), BF),
            pltpu.VMEM((count, D), BF),
            pltpu.VMEM((D, count), BF),
            pltpu.VMEM((D, count), BF),
            pltpu.VMEM((D, count), BF),
            pltpu.VMEM((count, D), BF),
            pltpu.VMEM((count, D), F32),
            pltpu.VMEM((2, count, UP_CHUNK), BF),
            pltpu.VMEM((2, count, UP_CHUNK), BF),
            pltpu.VMEM((2, UP_CHUNK, count), BF),
            pltpu.VMEM((2, LEN, LEN), F32),
            pltpu.VMEM((2, LEN, 128), F32),
            pltpu.VMEM((2, 1, QKV_HALF), F32),
            pltpu.SemaphoreType.DMA((slots,)),
            pltpu.SemaphoreType.DMA((slots,)),
            pltpu.SemaphoreType.DMA((24,)),
        ],
        compiler_params=pltpu.CompilerParams(
            collective_id=0, has_side_effects=True, vmem_limit_bytes=60 << 20),
        name="forward_gather",
    )(*weights, *vectors, tokens, lengths)


def finish_kernel(*refs):
    refs = list(refs)
    take = lambda number: [refs.pop(0) for _ in range(number)]
    lengths, norm, scale_one, w_out = take(4)
    (down_any, up_any, act_any, slope_any, normed_any, context_any, cotangent_any) = take(7)
    pooled, delta, norm_sums, ffn_sums = take(4)
    (layer_any, branch_any, inner_any, attended_any, grad_context_any, one_any) = take(6)
    (w_down, w_up, act, slope, normed_one, context, cotangent, layer_out, grad_branch,
     grad_attended, grad_context, hidden) = take(12)
    loads, stores = refs
    core = lax.axis_index("mp")
    started = []

    def load(source, target):
        copy = pltpu.make_async_copy(source, target, loads.at[len(started)])
        copy.start()
        started.append(copy)
        return copy

    halves = [pl.ds(row * LEN, LEN) for row in range(2)]
    pair = lambda source, target: [load(source.at[rows], target.at[rows]) for rows in halves]
    down_loaded = load(down_any, w_down)
    act_loaded, normed_loaded = [], []
    for rows in halves:
        act_loaded.append(load(act_any.at[rows], act.at[rows]))
        normed_loaded.append(load(normed_any.at[rows], normed_one.at[rows]))
    cotangent_loaded = pair(cotangent_any, cotangent)
    slope_loaded = pair(slope_any, slope)
    up_loaded = load(up_any, w_up)
    context_loaded = pair(context_any, context)
    norm_sums[...] = jnp.zeros(norm_sums.shape, F32)
    ffn_sums[...] = jnp.zeros(ffn_sums.shape, F32)
    kept = []

    def keep(source, target):
        copy = pltpu.make_async_copy(source, target, stores.at[len(kept)])
        copy.start()
        kept.append(copy)

    down_loaded.wait()
    for row, rows in enumerate(halves):
        act_loaded[row].wait()
        normed_loaded[row].wait()
        hidden[...] = normed_one[rows, :] * norm[2:3, :] + norm[3:4, :]
        branch = dot(act[rows, :], w_down[...])
        normed, scale = norm_parts(hidden[...] + branch + norm[1:2, :])
        output = normed * norm[4:5, :] + norm[5:6, :]
        high = output.astype(BF)
        layer_out[rows, :] = high
        keep(layer_out.at[rows], layer_any.at[rows])
        low = (output - high.astype(F32)).astype(BF)
        place = lax.broadcasted_iota(jnp.int32, (SEGS, LEN), 1)
        segment = lax.broadcasted_iota(jnp.int32, (SEGS, 1), 0)
        ids = ids_at(lengths, core * 2 + row, place)
        member = (ids == segment).astype(F32)
        sizes = jnp.sum(member, axis=1, keepdims=True)
        member = member.astype(BF)
        pooled[row] = (dot(member, high) + dot(member, low)) / sizes
        cotangent_loaded[row].wait()
        back, gain, shift = norm_back(cotangent[rows, :].astype(F32), normed, scale, norm[4:5, :])
        norm_sums[4:5, :] += gain
        norm_sums[5:6, :] += shift
        hidden[...] = back
        back = back.astype(BF)
        grad_branch[rows, :] = back
        keep(grad_branch.at[rows], branch_any.at[rows])
        norm_sums[1:2, :] += jnp.sum(back.astype(F32), axis=0, keepdims=True)
        slope_loaded[row].wait()
        for start in range(0, FF, FF // 4):
            cols = slice(start, start + FF // 4)
            value = dot_last(grad_branch[rows, :], w_down[cols, :])
            value = (value * slope[rows, cols].astype(F32)).astype(BF)
            slope[rows, cols] = value
            ffn_sums[:, cols] += jnp.sum(value.astype(F32), axis=0, keepdims=True)
        keep(slope.at[rows], inner_any.at[rows])
        if row == 0:
            up_loaded.wait()
        for half in range(2):
            cols = slice(half * FF // 2, (half + 1) * FF // 2)
            hidden[...] += dot_last(slope[rows, cols], w_up[half])
        normed = normed_one[rows, :]
        scale = scale_one[rows, 0:1]
        back, gain, shift = norm_back(hidden[...], normed, scale, norm[2:3, :])
        norm_sums[2:3, :] += gain
        norm_sums[3:4, :] += shift
        normed_one[rows, :] = back
        keep(normed_one.at[rows], one_any.at[rows])
        back = back.astype(BF)
        grad_attended[rows, :] = back
        keep(grad_attended.at[rows], attended_any.at[rows])
        norm_sums[0:1, :] += jnp.sum(back.astype(F32), axis=0, keepdims=True)
        back = dot_last(back, w_out[...]).astype(BF)
        grad_context[rows, :] = back
        keep(grad_context.at[rows], grad_context_any.at[rows])
        context_loaded[row].wait()
        product = back.astype(F32) * context[rows, :].astype(F32)
        high = product.astype(BF)
        low = (product - high.astype(F32)).astype(BF)
        head = lax.broadcasted_iota(jnp.int32, (16, D), 0)
        member = (lax.broadcasted_iota(jnp.int32, (16, D), 1) // HD == head).astype(F32).astype(BF)
        delta[row] = dot_last(member, high) + dot_last(member, low)
    for copy in kept:
        copy.wait()


def finish_forward(lengths, norm, scale_one, w_out, w_down, w_up, act, slope, normed, context,
                   cotangent):
    count = act.shape[0]
    shape = jax.ShapeDtypeStruct
    outs = [
        shape((count // LEN, SEGS, D), F32), shape((count // LEN, 16, LEN), F32),
        shape((8, D), F32), shape((1, FF), F32),
    ]
    large = [
        shape((count, D), BF), shape((count, D), BF), shape((count, FF), BF),
        shape((count, D), BF), shape((count, D), BF), shape((count, D), F32),
    ]
    some = pl.BlockSpec(memory_space=pl.ANY)
    return pl.pallas_call(
        finish_kernel,
        out_shape=outs + large,
        in_specs=[SMEM] + [VMEM] * 3 + [some] * 7,
        out_specs=[VMEM] * 4 + [some] * 6,
        scratch_shapes=[
            pltpu.VMEM((FF, D), BF),
            pltpu.VMEM((2, D, FF // 2), BF),
            pltpu.VMEM((count, FF), BF),
            pltpu.VMEM((count, FF), BF),
            pltpu.VMEM((count, D), F32),
            pltpu.VMEM((count, D), BF),
            pltpu.VMEM((count, D), BF),
            pltpu.VMEM((count, D), BF),
            pltpu.VMEM((count, D), BF),
            pltpu.VMEM((count, D), BF),
            pltpu.VMEM((count, D), BF),
            pltpu.VMEM((LEN, D), F32),
            pltpu.SemaphoreType.DMA((16,)),
            pltpu.SemaphoreType.DMA((16,)),
        ],
        compiler_params=pltpu.CompilerParams(vmem_limit_bytes=60 << 20),
        name="finish_forward",
    )(lengths, norm, scale_one, w_out, w_down, w_up, act, slope, normed, context, cotangent)


class Collect:
    COUNT = 8

    def __init__(self, place, held, slots, result, start, width, flip, sems, base):
        self.place, self.held, self.slots, self.result = place, held, slots, result
        self.cols = pl.ds(start, width)
        tiles = width // 128
        cut = (tiles // 2 if flip else tiles - tiles // 2) * 128
        self.halves = [("xy", pl.ds(start, cut))]
        if cut < width:
            self.halves.append(("yx", pl.ds(start + cut, width - cut)))
        self.sems, self.base = sems, base

    def copy(self, slot, axis, step, source, target):
        send, recv = self.sems
        return pltpu.make_async_remote_copy(
            source, target, send.at[self.base + slot], recv.at[self.base + slot],
            device_id=self.place.device(self.place.at(axis, step)), device_id_type=MESH)

    def copies(self, stage):
        place = self.place
        if stage == 2:
            out = []
            for step in (1, 2, 3):
                source = self.held.at[place.at("z", step)["z"], place.y, place.x, :, self.cols]
                out.append(self.copy(
                    step - 1, "z", step, source, self.slots[2].at[step - 1, :, self.cols]))
            return out
        out = []
        for number, (order, cols) in enumerate(self.halves):
            axis = order[stage]
            spot = {"y": EVERY, "x": EVERY}
            if stage == 1:
                spot[order[0]] = getattr(place, order[0])
            spot[axis] = place.at(axis, 1)[axis]
            land = (EVERY,) * (2 - stage) + (EVERY, cols)
            out.append(self.copy(
                3 + 2 * stage + number, axis, 1, self.held.at[:, spot["y"], spot["x"], :, cols],
                self.slots[stage].at[land]))
        return out

    def start(self, stage):
        for sent in self.copies(stage):
            sent.start()

    def add(self, stage):
        place, held, slots = self.place, self.held, self.slots[stage]
        for sent in self.copies(stage):
            sent.wait_recv()
        if stage == 2:
            value = held[place.z, place.y, place.x, :, self.cols].astype(F32)
            for step in range(3):
                value = value + slots[step, :, self.cols].astype(F32)
            self.result[:, self.cols] = value[:self.result.shape[0]]
            return
        for order, cols in self.halves:

            @pl.loop(0, 8 if stage == 0 else 4)
            def _(index):
                spot = {"y": place.y, "x": place.x}
                if stage == 0:
                    layer = index // 2
                    spot[order[1]] = index % 2
                    arrived = slots[layer, index % 2, :, cols]
                else:
                    layer = index
                    arrived = slots[layer, :, cols]
                at = (layer, spot["y"], spot["x"], EVERY, cols)
                held[at] = (held[at].astype(F32) + arrived.astype(F32)).astype(held.dtype)

    def finish(self):
        for stage in range(3):
            for sent in self.copies(stage):
                sent.wait_send()


def collect_tick(groups, tick):
    for stage in range(4):
        if 0 <= tick - stage < len(groups):
            for chunk in groups[tick - stage]:
                if stage:
                    chunk.add(stage - 1)
                if stage < 3:
                    chunk.start(stage)


def pack_small(target, core, norm_sums, grad_head, ffn_sums):
    iota = lambda shape, axis: lax.broadcasted_iota(jnp.int32, shape, axis)
    pick = (iota((D, 128), 0) % 24 == iota((D, 128), 1)).astype(F32).astype(BF)
    pick_ffn = (iota((FF, 128), 0) % 96 == iota((FF, 128), 1)).astype(F32).astype(BF)

    def split_dot(value, other):
        high = value.astype(BF)
        return dot(high, other) + dot((value - high.astype(F32)).astype(BF), other)

    rows = jnp.concatenate(
        [norm_sums[0:6, :], grad_head[0:2, :], jnp.zeros((8, D), F32)], axis=0)
    rows = jnp.broadcast_to(rows[None], (16, 16, D)).reshape(256, D)
    line = iota((256, D), 0)
    device, kind = line // 16, line % 16
    right = jnp.where(kind < 6, 2 * device + core, 16 * core + device)
    rows = jnp.where(iota((256, D), 1) // 24 == right, rows, 0.0)
    target[...] = split_dot(rows, pick).reshape(4, 2, 2, 16, 128)
    right = iota((16, FF), 1) // 96 == iota((16, FF), 0) + 16 * core
    ffn = split_dot(jnp.where(right, ffn_sums[...], 0.0), pick_ffn)
    target[:, :, :, 8, :] = ffn.reshape(4, 2, 2, 128)


def attend_back_pair(qkv, grad_context, lse, delta, bias, grad_head, core, row, pair):
    lane = lax.broadcasted_iota(jnp.int32, (LEN, 128), 1)
    item = core * 3 + pair
    queries, keys, values = (slab(qkv, core, row, part, pair) for part in range(3))
    rows = pl.ds(pl.multiple_of(row * LEN, LEN), LEN)
    wide = pl.ds(pl.multiple_of(item * 128, 128), 128)
    grad = grad_context[rows, wide]
    flipped = keys.T
    grads_k, grads_v, grads_q = [], [], []
    for half, mask in enumerate(half_masks()):
        head = item * 2 + half
        scores = dot_last(keys * mask, queries) + bias[row] - lse[row, pl.ds(head, 1), :]
        probs = jnp.exp(scores)
        grad_probs = dot_last(values * mask, grad)
        grad_scores = (probs * (grad_probs - delta[row, pl.ds(head, 1), :])).astype(BF)
        grads_v.append(dot(probs.astype(BF), grad))
        grads_k.append(dot(grad_scores, queries))
        grads_q.append(dot(flipped[half * HD:(half + 1) * HD, :], grad_scores))
    grad_q = (jnp.concatenate(grads_q, axis=0).T * HD ** -0.5).astype(BF)
    grad_k = jnp.where(lane < HD, grads_k[0], grads_k[1]).astype(BF)
    grad_v = jnp.where(lane < HD, grads_v[0], grads_v[1]).astype(BF)
    for part, value in enumerate((grad_q, grad_k, grad_v)):
        qkv[core, rows, pl.ds(pl.multiple_of(pair * PAIR + part * 128, 128), 128)] = value
    grad_head[0:1, wide] += jnp.sum(grad_q.astype(F32), axis=0, keepdims=True)
    grad_head[1:2, wide] += jnp.sum(grad_v.astype(F32), axis=0, keepdims=True)


def backward_scatter_kernel(*refs):
    refs = list(refs)
    take = lambda number: [refs.pop(0) for _ in range(number)]
    lengths, lse, delta, norm_sums, ffn_sums = take(5)
    rows_old, cols_old = take(4), take(4)
    head_sq, ffn_sq, norm_sq, weight_sums = take(4)
    (act_any, inner_any, branch_any, hidden_any, context_any, attended_any, token_any, qkv_any,
     grad_context_any, weight_any, one_any) = take(11)
    results = take(5)
    lines, totals, input_any = take(3)
    held, other = take(5), take(5)
    slots = [take(3) for _ in range(5)]
    (wide, flip, flip_context, attended, qkv, weight, one, act, inner, bias, grad_head) = take(11)
    mine_one, land_one, mine_two, land_two, old_small = take(5)
    send, recv, local = refs
    place = Place()
    sems = (send, recv)
    partner = place.device(place.at("m", 1))
    mine, theirs = place.m, 1 - place.m
    loaded = {}

    def load(name, source, target):
        copy = pltpu.make_async_copy(source, target, local.at[len(loaded)])
        copy.start()
        loaded[name] = copy

    tile_rows = FF // 2 // 4
    act_slots, inner_slots = 12, 14

    def act_load(index):
        core = jnp.where(index < 4, theirs, mine)
        start = pl.multiple_of(core * (FF // 2) + (index % 4) * tile_rows, tile_rows)
        return pltpu.make_async_copy(
            act_any.at[pl.ds(start, tile_rows)], act.at[index % 2], local.at[act_slots + index % 2])

    def inner_load(index):
        core = jnp.where(index < 3, theirs, mine)
        start = pl.multiple_of(core * (FF // 2) + (index % 3) * UP_CHUNK, UP_CHUNK)
        return pltpu.make_async_copy(
            inner_any.at[:, pl.ds(start, UP_CHUNK)], inner.at[index % 2],
            local.at[inner_slots + index % 2])

    load("branch", branch_any, wide)
    for index in range(2):
        act_load(index).start()
    load("hidden", hidden_any, flip)
    for index in range(2):
        inner_load(index).start()
    load("attended", attended_any, attended)
    load("context", context_any, flip_context)
    load("qkv", qkv_any, qkv)
    load("weight", weight_any, weight)
    load("one", one_any, one)

    small, qkv_held, out_held, up_held, down_held = held
    small_other, qkv_other, out_other, up_other, down_other = other
    base = 12

    def swap(slot, source, target):
        return pltpu.make_async_remote_copy(
            source, target, send.at[slot], recv.at[slot],
            device_id=partner, device_id_type=MESH)

    def down_swap(layer):
        return swap(layer, down_held.at[layer], down_other.at[layer])

    def up_swap(third):
        cols = pl.ds(pl.multiple_of(third * UP_CHUNK, UP_CHUNK), UP_CHUNK)
        at = (EVERY, EVERY, EVERY, EVERY, cols)
        return swap(4 + third, up_held.at[at], up_other.at[at])

    def qkv_swap(pair):
        at = (EVERY, EVERY, EVERY, EVERY, pl.ds(pl.multiple_of(pair * PAIR, PAIR), PAIR))
        return swap(8 + pair, qkv_held.at[at], qkv_other.at[at])

    out_swap = swap(7, out_held, out_other)
    small_swap = swap(11, small, small_other)
    widths = (128, PAIR, D, UP_CHUNK, DOWN_CHUNK)
    chunks = [[] for _ in range(5)]
    for index in (4, 3, 2, 1, 0):
        for start in range(0, held[index].shape[4], widths[index]):
            chunks[index].append(Collect(
                place, held[index], slots[index], results[index], start, widths[index],
                index == 1 and start == PAIR, sems, base))
            base += Collect.COUNT
    groups = [[c] for index in (4, 3, 2, 1) for c in chunks[index]]
    groups[-1] += chunks[0]

    greet(place)
    loaded["branch"].wait()

    @pl.loop(0, 4)
    def _(layer):
        act_load(layer).wait()
        value = dot(act[layer % 2], wide[...])
        down_held[layer] = value.reshape(2, 2, tile_rows // 4, D).astype(BF)
        down_swap(layer).start()
        act_load(layer + 2).start()

    @pl.loop(0, 4)
    def _(layer):
        act_load(layer + 4).wait()
        value = dot(act[layer % 2], wide[...]).reshape(2, 2, tile_rows // 4, D)
        down_swap(layer).wait()
        down_held[layer] = (value + down_other[layer].astype(F32)).astype(BF)

        @pl.when(layer < 2)
        def _():
            act_load(layer + 6).start()

    load("grad_context", grad_context_any, wide)
    collect_tick(groups, 0)
    loaded["hidden"].wait()

    @pl.loop(0, 3)
    def _(third):
        inner_load(third).wait()
        cols = pl.ds(pl.multiple_of(third * UP_CHUNK, UP_CHUNK), UP_CHUNK)
        value = dot(flip[...], inner[third % 2])
        up_held[:, :, :, :, cols] = value.reshape(4, 2, 2, D // 16, UP_CHUNK).astype(BF)
        up_swap(third).start()
        inner_load(third + 2).start()

    @pl.loop(0, 3)
    def _(third):
        inner_load(third + 3).wait()
        at = (EVERY, EVERY, EVERY, EVERY,
              pl.ds(pl.multiple_of(third * UP_CHUNK, UP_CHUNK), UP_CHUNK))
        value = dot(flip[...], inner[(third + 3) % 2]).reshape(4, 2, 2, D // 16, UP_CHUNK)
        up_swap(third).wait()
        up_held[at] = (value + up_other[at].astype(F32)).astype(BF)

        @pl.when(third == 0)
        def _():
            inner_load(5).start()
            collect_tick(groups, 1)

    load("token", token_any, flip)
    loaded["attended"].wait()
    loaded["context"].wait()
    spare = out_held.shape[3] - D // 32

    def out_half(core):
        rows = pl.ds(pl.multiple_of(core * HALF, HALF), HALF)
        value = dot(flip_context[rows, :], attended[...]).reshape(16, D // 32, D)
        value = jnp.concatenate([value, jnp.zeros((16, spare, D), F32)], axis=1)
        return value.reshape(4, 2, 2, D // 32 + spare, D)

    out_held[...] = out_half(theirs).astype(BF)
    out_swap.start()
    value = out_half(mine)
    out_swap.wait()
    out_held[...] = (value + out_other[...].astype(F32)).astype(BF)
    collect_tick(groups, 2)
    for row in range(2):
        set_bias(bias.at[row], lengths, place.m * 2 + row)
    grad_head[...] = jnp.zeros(grad_head.shape, F32)
    for name in ("qkv", "grad_context", "token"):
        loaded[name].wait()

    def qkv_theirs(pair):
        cols = pl.ds(pl.multiple_of(pair * PAIR, PAIR), PAIR)
        value = dot(flip[...], qkv[theirs, :, cols])
        qkv_held[:, :, :, :, cols] = value.reshape(4, 2, 2, D // 16, PAIR).astype(BF)
        qkv_swap(pair).start()

    def qkv_mine(pair):
        cols = pl.ds(pl.multiple_of(pair * PAIR, PAIR), PAIR)
        at = (EVERY, EVERY, EVERY, EVERY, cols)
        value = dot(flip[...], qkv[mine, :, cols]).reshape(4, 2, 2, D // 16, PAIR)
        qkv_swap(pair).wait()
        qkv_held[at] = (value + qkv_other[at].astype(F32)).astype(BF)

    @pl.loop(0, 12)
    def _(item):
        pair, row, core = item // 4, (item % 4) // 2, item % 2

        @pl.when((item == 4) | (item == 8))
        def _():
            qkv_theirs(pair - 1)

        @pl.when((item == 5) | (item == 9))
        def _():
            qkv_mine(pair - 1)

        for number, at in enumerate((1, 3, 5, 7, 9, 11)):
            @pl.when(item == at)
            def _():
                collect_tick(groups, 3 + number)

        attend_back_pair(qkv, wide, lse, delta, bias, grad_head, core, row, pair)

    qkv_theirs(2)
    pack_small(small, theirs, norm_sums, grad_head, ffn_sums)
    small_swap.start()
    loaded["weight"].wait()
    loaded["one"].wait()

    def input_rows(row):
        rows = pl.ds(pl.multiple_of(row * LEN, LEN), LEN)
        one[rows, :] += dot_last(qkv[0, rows, :], weight[0]) + dot_last(qkv[1, rows, :], weight[1])

    qkv_mine(2)
    small_swap.wait()
    pack_small(small, mine, norm_sums, grad_head, ffn_sums)
    small[...] += small_other[...]
    collect_tick(groups, 9)
    input_rows(0)
    collect_tick(groups, 10)
    input_rows(1)
    input_done = pltpu.make_async_copy(one, input_any, local.at[16])
    input_done.start()
    collect_tick(groups, 11)
    collect_tick(groups, 12)
    small_sum, grads = results[0], results[1:]
    lines[...] = jnp.zeros(lines.shape, F32)
    for index in range(4):
        grad = grads[index][...]
        square = grad * grad + EPS_SQUARE
        put_line(lines, COL_LINES[index], jnp.sum(square, axis=0, keepdims=True))
        if index in (0, 2):
            line = ROW_LINE + index // 2
            lines[line:line + 1, 0:grad.shape[0]] = to_row(jnp.sum(square, axis=1, keepdims=True))
    first = Exchange(place, mine_one, land_one, sems, base)
    line = lax.broadcasted_iota(jnp.int32, lines.shape, 0)
    value = lines[...]
    first.mine[0] = value
    paired = jnp.where(line >= OUT_LINE, first.swap(0, "m"), value)
    total = paired
    for stage, axis in ((1, "x"), (2, "y"), (3, "z")):
        first.mine[stage] = total
        total = first.swap(stage, axis)
    lines[...] = jnp.where(line >= ROW_LINE, paired, total)
    rows_new, cols_new = new_rows_cols(grads, rows_old, cols_old, lines)
    ratios, row_totals = [], []
    for index in range(4):
        grad = grads[index][...]
        scaled = jnp.sum(grad * grad * (1.0 / cols_new[index]), axis=1, keepdims=True)
        ratios.append(jnp.sum(scaled / rows_new[index], axis=0, keepdims=True))
        share = 0.5 if index in (0, 2) else 1.0
        row_totals.append(jnp.sum(rows_new[index], axis=0, keepdims=True) * share)
    place_small(old_small, norm_sq[...], head_sq[...], ffn_sq[...], 1.0)
    _, update = small_update(small_sum[...], old_small[...])
    second = Exchange(place, mine_two, land_two, sems, base + 16)
    totals[...] = add_up(
        second, scalars(ratios + row_totals + small_sums(update)) + weight_sums[...])
    input_done.wait()
    for group in groups:
        for chunk in group:
            chunk.finish()
    first.finish()
    second.finish()


def backward_scatter(lengths, lse, delta, norm_sums, ffn_sums, rows_old, cols_old, squares,
                     weight_sums, large, rows, widths):
    count = large[2].shape[0]
    shape = jax.ShapeDtypeStruct
    some = pl.BlockSpec(memory_space=pl.ANY)
    kinds = [F32, BF, BF, BF, BF]
    padded = [16, rows[1], 32, rows[3], rows[4]]
    held = [pltpu.VMEM((4, 2, 2, r, w), k) for r, w, k in zip(padded, widths, kinds)]
    slots = []
    for r, w, k in zip(padded, widths, kinds):
        slots += [pltpu.VMEM((4, 2, r, w), k), pltpu.VMEM((4, r, w), k), pltpu.VMEM((3, r, w), k)]
    sems = 12 + 11 * Collect.COUNT + 32
    outs = [shape((r, w), F32) for r, w in zip(rows, widths)]
    outs += [shape((LINES, 128), F32), shape((8, 128), F32), shape((count, D), F32)]
    small = [lse, delta, norm_sums, ffn_sums, *rows_old, *cols_old, *squares, weight_sums]
    return pl.pallas_call(
        backward_scatter_kernel,
        out_shape=outs,
        in_specs=[SMEM] + [VMEM] * len(small) + [some] * len(large),
        out_specs=[VMEM] * 7 + [some],
        scratch_shapes=held + held + slots + [
            pltpu.VMEM((count, D), BF),
            pltpu.VMEM((D, count), BF),
            pltpu.VMEM((D, count), BF),
            pltpu.VMEM((count, D), BF),
            pltpu.VMEM((2, count, QKV_HALF), BF),
            pltpu.VMEM((2, D, QKV_HALF), BF),
            pltpu.VMEM((count, D), F32),
            pltpu.VMEM((2, FF // 8, count), BF),
            pltpu.VMEM((2, count, UP_CHUNK), BF),
            pltpu.VMEM((2, LEN, LEN), F32),
            pltpu.VMEM((8, D), F32),
            pltpu.VMEM((4, LINES, 128), F32),
            pltpu.VMEM((4, 4, LINES, 128), F32),
            pltpu.VMEM((4, 8, 128), F32),
            pltpu.VMEM((4, 4, 8, 128), F32),
            pltpu.VMEM((16, 128), F32),
            pltpu.SemaphoreType.DMA((sems,)),
            pltpu.SemaphoreType.DMA((sems,)),
            pltpu.SemaphoreType.DMA((18,)),
        ],
        compiler_params=pltpu.CompilerParams(
            collective_id=1, has_side_effects=True, vmem_limit_bytes=62 << 20),
        name="backward_scatter",
    )(lengths, *small, *large)


def small_block(norm, head, ffn):
    wide = lambda v: jnp.pad(v, [(0, 0)] * (v.ndim - 1) + [(0, 128 - v.shape[-1])])
    block = jnp.concatenate([wide(norm), wide(head), wide(ffn)], axis=-2)
    return jnp.pad(block, [(0, 0)] * (block.ndim - 2) + [(0, 16 - block.shape[-2]), (0, 0)])


def pair_major(weight):
    count = weight.shape[0]
    return weight.reshape(count, 3, 3, 128).transpose(0, 2, 1, 3).reshape(count, QKV_HALF)


def gather_plain(weights, vectors):
    head, ffn, norm = vectors
    qkv, out, up, down = (w.astype(BF) for w in weights)
    full = []
    for shard in (small_block(norm, head, ffn), pair_major(qkv), out, up, down):
        full.append(lax.all_gather(lax.all_gather(shard, "dp", axis=0), "mp", axis=0))
    return full


def scatter_plain(fulls):
    out = []
    for full in fulls:
        own = lax.psum_scatter(full.astype(F32), "mp", scatter_dimension=0)
        out.append(lax.psum_scatter(own, "dp", scatter_dimension=0))
    return out


def body(
    tokens, cotangent, seg_lengths, w_qkv, w_out, w_up, w_down, head_bias, ffn_bias, norm_bias,
    qkv_rows, qkv_cols, out_rows, out_cols, up_rows, up_cols, down_rows, down_cols,
    head_bias_sq, ffn_bias_sq, norm_sq,
):
    cores = lax.axis_size("mp")
    data = lax.axis_size("dp")
    rows_qkv = w_qkv.shape[0]
    fast = data == 16 and cores == 2
    weights = [w_qkv, w_out, w_up, w_down]
    vectors = [head_bias, ffn_bias.reshape(1, -1), norm_bias]
    rows_out = w_out.shape[0]
    if fast:
        (weight_sums, norm_full, ffn_full, lse, scale_one, out_full, qkv_full, up_full, down_full,
         qkv, context_flip, token_flip, hidden_flip, normed_one, context, act, act_flip, slope
         ) = forward_gather(weights, vectors, tokens, seg_lengths)
        qkv_full = qkv_full.reshape(2, D, QKV_HALF)
        up_full = up_full.reshape(2, D, FF // 2)
        down_full = down_full.reshape(FF, D)
        (pooled, delta, norm_sums, ffn_sums, layer_out, grad_branch, grad_inner, grad_attended,
         grad_context, grad_one) = finish_forward(
            seg_lengths, norm_full, scale_one, out_full, down_full, up_full, act, slope,
            normed_one, context, cotangent)
        rows_old = [v.reshape(1, -1) for v in (qkv_rows, out_rows, up_rows, down_rows)]
        cols_old = [qkv_cols] + [v.reshape(1, -1) for v in (out_cols, up_cols, down_cols)]
        old = [head_bias_sq, ffn_bias_sq.reshape(1, -1), norm_sq]
        *reduced, lines, totals, input_grad = backward_scatter(
            seg_lengths, lse, delta, norm_sums, ffn_sums, rows_old, cols_old, old, weight_sums,
            [act_flip, grad_inner, grad_branch, hidden_flip, context_flip, grad_attended,
             token_flip, qkv, grad_context, qkv_full, grad_one],
            [16, rows_qkv, rows_out, rows_qkv, w_down.shape[0]],
            [128, QKV_HALF, D, w_up.shape[1], D])
        new = step(reduced, lines, totals, weights, rows_old, cols_old, vectors, old)
        grads, (g_head, g_ffn, g_norm) = new[:4], new[4:7]
        rows_new, cols_new = [r.reshape(-1) for r in new[7:11]], new[11:15]
        cols_new = [cols_new[0]] + [c.reshape(-1) for c in cols_new[1:]]
        (s_head, s_ffn, s_norm), mats = new[15:18], new[18:22]
        n_head, n_ffn, n_norm = new[22:25]
        stats = [v for pair in zip(rows_new, cols_new) for v in pair]
        return (
            layer_out, pooled, input_grad, *grads, g_head, g_ffn.reshape(-1), g_norm, *stats,
            s_head, s_ffn.reshape(-1), s_norm, *mats, n_head, n_ffn.reshape(-1), n_norm,
        )
    small, qkv_g, out_g, up_g, down_g = gather_plain(weights, vectors)
    small = small.astype(BF).astype(F32)
    own_head, own_ffn, own_norm = head_bias.shape[1], ffn_bias.shape[0], norm_bias.shape[1]
    norm_full = small[:, :, 0:6, :own_norm].transpose(2, 1, 0, 3).reshape(6, D)
    head_full = small[:, :, 6:8, :own_head].transpose(2, 0, 1, 3).reshape(2, 2, 3, 1, 128)
    ffn_full = small[:, :, 8, :own_ffn].reshape(1, FF)
    offsets = jnp.concatenate([head_full[0], jnp.zeros_like(head_full[0]), head_full[1]], axis=2)
    offsets = offsets.reshape(2, 1, QKV_HALF)
    qkv_full = qkv_g.reshape(2, D, QKV_HALF)
    up_full = up_g.reshape(2, D, FF // 2)
    down_full = down_g.reshape(FF, D)
    out_full = out_g.reshape(D, D)
    norm_full = jnp.pad(norm_full, ((0, 2), (0, 0)))
    qkv, context, lse = forward(tokens, qkv_full, offsets, seg_lengths)
    (layer_out, pooled, hidden_b, act, grad_branch, grad_inner, grad_attended, grad_context,
     grad_one, delta, norm_sums, ffn_sums) = middle_call(
        tokens, context, cotangent, seg_lengths, out_full, up_full, down_full, ffn_full,
        norm_full)
    grad_out, grad_up, grad_down = weight_grads(
        context.T, hidden_b.T, act.T, grad_branch, grad_inner, grad_attended,
        cores * data, rows_out)
    token_flip = tokens.T
    grad_qkv, input_grad, grad_head = backward(
        token_flip, qkv, grad_context, lse, delta, seg_lengths, qkv_full, grad_one)
    small_grads = small_block(
        norm_sums[:6].reshape(6, data, cores, -1).transpose(2, 1, 0, 3),
        grad_head.reshape(2, cores, data, -1).transpose(1, 2, 0, 3),
        ffn_sums.reshape(cores, data, 1, -1),
    )
    fulls = [
        small_grads,
        grad_qkv.reshape(cores, data, rows_qkv, QKV_HALF),
        grad_out.reshape(cores, data, rows_out, D),
        grad_up.reshape(cores, data, rows_qkv, FF // 2),
        grad_down.reshape(cores, data, -1, D),
    ]
    red_small, red_qkv, red_out, red_up, red_down = scatter_plain(fulls)
    norm_grad = red_small[0:6, :own_norm]
    red_qkv = pair_major(red_qkv)
    red_head = red_small[6:8, :own_head]
    red_ffn = red_small[8, :own_ffn]
    weights_flat = [w_qkv.reshape(rows_qkv, -1), w_out, w_up, w_down]
    grads_flat = [red_qkv, red_out, red_up, red_down]
    rows_old = [qkv_rows, out_rows, up_rows, down_rows]
    cols_old = [qkv_cols.reshape(-1), out_cols, up_cols, down_cols]
    col_count = [3 * D, D, FF, D]
    row_count = [D, D, D, FF]
    row_share = [cores, 1, cores, 1]
    squares = [grad * grad + EPS_SQUARE for grad in grads_flat]
    row_parts = [jnp.sum(square, axis=1) for square in squares]
    col_parts = [jnp.sum(square, axis=0) for square in squares]
    vec_weights = [head_bias, ffn_bias, norm_bias]
    vec_grads = [red_head, red_ffn, norm_grad]
    vec_old = [head_bias_sq, ffn_bias_sq, norm_sq]
    vec_counts = [2 * D, FF, 6 * D]
    vec_second = [
        DECAY * old + (1.0 - DECAY) * (grad * grad + EPS_SQUARE)
        for old, grad in zip(vec_old, vec_grads)
    ]
    vec_update = [grad * lax.rsqrt(second) for grad, second in zip(vec_grads, vec_second)]
    weight_parts = [jnp.sum(weight * weight) for weight in weights_flat + vec_weights]
    vec_parts = [jnp.sum(update * update) for update in vec_update]
    row_qkv, row_up = lax.psum((row_parts[0], row_parts[2]), "mp")
    col_qkv, col_up = lax.psum((col_parts[0], col_parts[2]), "dp")
    col_out, col_down = lax.psum((col_parts[1], col_parts[3]), ("dp", "mp"))
    row_sums = [row_qkv, row_parts[1], row_up, row_parts[3]]
    col_sums = [col_qkv, col_out, col_up, col_down]
    rows_new = [
        DECAY * rows_old[index] + (1.0 - DECAY) * row_sums[index] / col_count[index]
        for index in range(4)
    ]
    cols_new = [
        DECAY * cols_old[index] + (1.0 - DECAY) * col_sums[index] / row_count[index]
        for index in range(4)
    ]
    ratio_parts = [
        jnp.sum(
            grads_flat[index]
            * grads_flat[index]
            / (rows_new[index][:, None] * cols_new[index][None, :])
        )
        for index in range(4)
    ]
    extra_parts = (
        [jnp.sum(rows_new[index]) / row_share[index] for index in range(4)]
        + weight_parts
        + vec_parts
    )
    totals = lax.psum(jnp.stack(ratio_parts + extra_parts), ("dp", "mp"))
    row_means = [totals[4 + index] / row_count[index] for index in range(4)]
    weight_totals = [totals[8 + index] for index in range(7)]
    vec_totals = [totals[15 + index] for index in range(3)]
    new_mats = []
    for index in range(4):
        entries = row_count[index] * col_count[index]
        estimate = rows_new[index][:, None] * cols_new[index][None, :] / row_means[index]
        update = grads_flat[index] / jnp.sqrt(estimate)
        update_rms = jnp.sqrt(row_means[index] * totals[index] / entries)
        stride = (
            RATE * jnp.sqrt(weight_totals[index] / entries) / jnp.maximum(1.0, update_rms / CLIP)
        )
        new_mats.append(weights_flat[index] - stride * update)
    new_vecs = []
    for index in range(3):
        update_rms = jnp.sqrt(vec_totals[index] / vec_counts[index])
        stride = (
            RATE
            * jnp.sqrt(weight_totals[4 + index] / vec_counts[index])
            / jnp.maximum(1.0, update_rms / CLIP)
        )
        new_vecs.append(vec_weights[index] - stride * vec_update[index])
    return (
        layer_out,
        pooled,
        input_grad,
        red_qkv.reshape(w_qkv.shape),
        red_out,
        red_up,
        red_down,
        red_head,
        red_ffn,
        norm_grad,
        rows_new[0],
        cols_new[0].reshape(qkv_cols.shape),
        rows_new[1],
        cols_new[1],
        rows_new[2],
        cols_new[2],
        rows_new[3],
        cols_new[3],
        vec_second[0],
        vec_second[1],
        vec_second[2],
        new_mats[0].reshape(w_qkv.shape),
        new_mats[1],
        new_mats[2],
        new_mats[3],
        new_vecs[0],
        new_vecs[1],
        new_vecs[2],
    )


def solution(mesh):
    return jax.shard_map(
        body,
        mesh=mesh,
        in_specs=(
            P(("dp", "mp"), None),
            P(("dp", "mp"), None),
            P("dp", None),
            P("dp", None, "mp"),
            P(("mp", "dp"), None),
            P("dp", "mp"),
            P(("mp", "dp"), None),
            P(None, ("mp", "dp")),
            P(("mp", "dp")),
            P(None, ("dp", "mp")),
            P("dp"),
            P(None, "mp"),
            P(("mp", "dp")),
            P(),
            P("dp"),
            P("mp"),
            P(("mp", "dp")),
            P(),
            P(None, ("mp", "dp")),
            P(("mp", "dp")),
            P(None, ("dp", "mp")),
        ),
        out_specs=(
            P(("dp", "mp"), None),
            P(("dp", "mp"), None, None),
            P(("dp", "mp"), None),
            P("dp", None, "mp"),
            P(("mp", "dp"), None),
            P("dp", "mp"),
            P(("mp", "dp"), None),
            P(None, ("mp", "dp")),
            P(("mp", "dp")),
            P(None, ("dp", "mp")),
            P("dp"),
            P(None, "mp"),
            P(("mp", "dp")),
            P(),
            P("dp"),
            P("mp"),
            P(("mp", "dp")),
            P(),
            P(None, ("mp", "dp")),
            P(("mp", "dp")),
            P(None, ("dp", "mp")),
            P("dp", None, "mp"),
            P(("mp", "dp"), None),
            P("dp", "mp"),
            P(("mp", "dp"), None),
            P(None, ("mp", "dp")),
            P(("mp", "dp")),
            P(None, ("dp", "mp")),
        ),
        check_vma=False,
    )
```

```python
import functools

import jax
import jax.numpy as jnp
from jax import lax
from jax.experimental import pallas as pl
from jax.experimental.pallas import tpu as pltpu
from jax.sharding import PartitionSpec as P

D = 768
HD = 64
FF = 3072
LEN = 512
SEGS = 8

EPS_NORM = 1e-12
EPS_SQUARE = 1e-30
DECAY = 0.5
RATE = 3.0
CLIP = 0.3

MESH = pl.DeviceIdType.MESH
BF = jnp.bfloat16
F32 = jnp.float32
EVERY = slice(None)


class Place:
    def __init__(self):
        d = lax.axis_index("dp")
        self.m = lax.axis_index("mp")
        self.z, self.y, self.x = d // 4, (d // 2) % 2, d % 2

    def at(self, axis, step):
        size = 4 if axis == "z" else 2
        spot = {"z": self.z, "y": self.y, "x": self.x, "m": self.m}
        spot[axis] = (spot[axis] + step) % size
        return spot

    @staticmethod
    def device(spot):
        return (spot["z"] * 4 + spot["y"] * 2 + spot["x"], spot["m"])


def steps_of(axis):
    return (1, 2, 3) if axis == "z" else (1,)


def greet(place):
    barrier = pltpu.get_barrier_semaphore()
    count = 0
    for axis in "zyxm":
        for step in steps_of(axis):
            pl.semaphore_signal(
                barrier, inc=1, device_id=place.device(place.at(axis, step)), device_id_type=MESH
            )
            count += 1
    pl.semaphore_wait(barrier, count)


def weight_sums_of(weights, small):
    parts = []
    for weight in weights:
        value = weight[...]
        if value.ndim == 3:
            parts.append(sum(all_sum(value[part] * value[part]) for part in range(3)))
        else:
            parts.append(all_sum(value * value))
    return scalars([jnp.zeros((1, 1), F32)] * 11 + parts + small_sums(small))


def as_row(ref):
    value = ref[...]
    return value.reshape(1, value.shape[0]) if value.ndim == 1 else value


def to_column(row):
    count = row.shape[1]
    here = lax.broadcasted_iota(jnp.int32, (count, count), 0)
    there = lax.broadcasted_iota(jnp.int32, (count, count), 1)
    return jnp.sum(jnp.where(here == there, row, 0.0), axis=1, keepdims=True)


def to_row(column):
    count = column.shape[0]
    here = lax.broadcasted_iota(jnp.int32, (count, count), 0)
    there = lax.broadcasted_iota(jnp.int32, (count, count), 1)
    return jnp.sum(jnp.where(here == there, column, 0.0), axis=0, keepdims=True)


def put_line(ref, line, row):
    for tile in range(row.shape[1] // 128):
        ref[line + tile:line + tile + 1, :] = row[:, tile * 128:(tile + 1) * 128]


def get_line(ref, line, width):
    tiles = width // 128
    return jnp.concatenate([ref[line + t:line + t + 1, :] for t in range(tiles)], axis=1)


def scalars(values):
    lane = lax.broadcasted_iota(jnp.int32, (8, 128), 1)
    out = jnp.zeros((8, 128), F32)
    for index, value in enumerate(values):
        out = jnp.where(lane == index, value, out)
    return out


def all_sum(values):
    return jnp.sum(jnp.sum(values, axis=1, keepdims=True), axis=0, keepdims=True)


class Exchange:
    def __init__(self, place, mine, land, sems, base):
        self.place, self.mine, self.land = place, mine, land
        self.sems, self.base = sems, base
        self.sent = []

    def swap(self, stage, axis):
        place = self.place
        send, recv = self.sems
        own = place.z if axis == "z" else 0
        for step in steps_of(axis):
            slot = self.base + 4 * stage + step
            copy = pltpu.make_async_remote_copy(
                self.mine.at[stage], self.land.at[stage, own], send.at[slot], recv.at[slot],
                device_id=place.device(place.at(axis, step)), device_id_type=MESH)
            copy.start()
            self.sent.append(copy)
        if axis == "z":
            self.land[stage, place.z] = self.mine[stage]
        for step in steps_of(axis):
            slot = self.base + 4 * stage + step
            spot = (place.z - step) % 4 if axis == "z" else 0
            pltpu.make_async_remote_copy(
                self.mine.at[stage], self.land.at[stage, spot], send.at[slot], recv.at[slot],
                device_id=place.device(place.at(axis, step)), device_id_type=MESH).wait_recv()
        if axis == "z":
            land = self.land
            return (land[stage, 0] + land[stage, 1]) + (land[stage, 2] + land[stage, 3])
        return self.mine[stage] + self.land[stage, 0]

    def finish(self):
        for copy in self.sent:
            copy.wait_send()


def add_up(exchange, value, picked=None):
    exchange.mine[0] = value
    total = exchange.swap(0, "m")
    if picked is not None:
        total = jnp.where(picked, total, value)
    for stage, axis in ((1, "x"), (2, "y"), (3, "z")):
        exchange.mine[stage] = total
        total = exchange.swap(stage, axis)
    return total


QKV_LINE, UP_LINE, OUT_LINE, DOWN_LINE, ROW_LINE = 0, 9, 21, 27, 33
LINES = 40
WIDTHS = (3 * D // 2, D, FF // 2, D)
COL_LINES = (QKV_LINE, OUT_LINE, UP_LINE, DOWN_LINE)
COL_COUNT = (3 * D, D, FF, D)
ROW_COUNT = (D, D, D, FF)


def pair_cuts():
    out = []
    for pair in range(3):
        for part in range(3):
            start = (pair * 3 + part) * 128
            out.append(((slice(part, part + 1), slice(pair * 128, (pair + 1) * 128)),
                        slice(start, start + 128)))
    return out


def new_rows_cols(grads, rows_old, cols_old, lines):
    rows_new, cols_new = [], []
    for index in range(4):
        if index in (0, 2):
            line = ROW_LINE + index // 2
            count = rows_old[index].shape[0]
            row_sum = to_column(lines[line:line + 1, :count])
        else:
            grad = grads[index][...]
            row_sum = jnp.sum(grad * grad + EPS_SQUARE, axis=1, keepdims=True)
        rows_new.append(
            DECAY * to_column(as_row(rows_old[index])) + (1.0 - DECAY) * row_sum / COL_COUNT[index])
        col_sum = get_line(lines, COL_LINES[index], WIDTHS[index])
        if index == 0:
            old = jnp.concatenate([cols_old[0][at] for at, _ in pair_cuts()], axis=1)
        else:
            old = as_row(cols_old[index])
        cols_new.append(DECAY * old + (1.0 - DECAY) * col_sum / ROW_COUNT[index])
    return rows_new, cols_new


def place_small(ref, norm, head, ffn, fill):
    ref[...] = jnp.full(ref.shape, fill, F32)
    ref[0:6, 0:norm.shape[1]] = norm
    ref[6:8, 0:head.shape[1]] = head
    ref[8:9, 0:ffn.shape[1]] = ffn


def small_update(grad, old):
    second = DECAY * old + (1.0 - DECAY) * (grad * grad + EPS_SQUARE)
    return second, grad * lax.rsqrt(second)


def small_sums(values):
    line = lax.broadcasted_iota(jnp.int32, values.shape, 0)
    square = values * values
    return [
        all_sum(jnp.where((line >= 6) & (line < 8), square, 0.0)),
        all_sum(jnp.where(line == 8, square, 0.0)),
        all_sum(jnp.where(line < 6, square, 0.0)),
    ]


def step_kernel(*refs):
    refs = list(refs)
    take = lambda number: [refs.pop(0) for _ in range(number)]
    grads_any, weights_any = take(4), take(4)
    passed = take(3)
    small, lines, totals = take(3)
    rows_old, cols_old = take(4), take(4)
    head, ffn, norm, head_sq, ffn_sq, norm_sq = take(6)
    grads_out = take(4)
    head_grad, ffn_grad, norm_grad = take(3)
    rows_out, cols_out = take(4), take(4)
    head_second, ffn_second, norm_second = take(3)
    weights_out = take(4)
    head_new, ffn_new, norm_new = take(3)
    passed_out = take(3)
    grads, weights = take(4), take(4)
    old_small, weight_small, sems = refs
    loads = []
    for number, (source, target) in enumerate(
            zip(grads_any + weights_any + passed, grads + weights + passed_out)):
        copy = pltpu.make_async_copy(source, target, sems.at[number])
        copy.start()
        loads.append(copy)
    place_small(old_small, norm_sq[...], head_sq[...], as_row(ffn_sq), 1.0)
    place_small(weight_small, norm[...], head[...], as_row(ffn), 0.0)
    for copy in loads[:4]:
        copy.wait()
    rows_new, cols_new = new_rows_cols(grads, rows_old, cols_old, lines)
    total = lambda lane: totals[0:1, lane:lane + 1]
    for index in range(4):
        rows_out[index][...] = to_row(rows_new[index]).reshape(rows_out[index].shape)
        if index == 0:
            for at, cut in pair_cuts():
                cols_out[0][at] = cols_new[0][:, cut]
        else:
            cols_out[index][...] = cols_new[index].reshape(cols_out[index].shape)
        entries = ROW_COUNT[index] * COL_COUNT[index]
        row_mean = total(4 + index) / ROW_COUNT[index]
        update_rms = jnp.sqrt(row_mean * total(index) / entries)
        stride = (
            RATE * jnp.sqrt(total(11 + index) / entries) / jnp.maximum(1.0, update_rms / CLIP))
        scale_rows = lax.rsqrt(rows_new[index] / row_mean) * stride
        scale_cols = lax.rsqrt(cols_new[index])
        loads[4 + index].wait()
        if index == 0:
            for (part, cols), cut in pair_cuts():
                at = (part.start, EVERY, cols)
                grad = grads[0][:, cut]
                grads_out[0][at] = grad
                weights_out[0][at] = weights[0][at] - grad * scale_rows * scale_cols[:, cut]
        else:
            grad = grads[index][...]
            grads_out[index][...] = grad
            weights_out[index][...] = weights[index][...] - grad * scale_rows * scale_cols
    grad = small[...]
    second, update = small_update(grad, old_small[...])
    line = lax.broadcasted_iota(jnp.int32, grad.shape, 0)
    counts = (2 * D, FF, 6 * D)
    strides = []
    for index in range(3):
        update_rms = jnp.sqrt(total(8 + index) / counts[index])
        strides.append(
            RATE * jnp.sqrt(total(15 + index) / counts[index])
            / jnp.maximum(1.0, update_rms / CLIP))
    stride = jnp.where(line < 6, strides[2], jnp.where(line < 8, strides[0], strides[1]))
    fresh = weight_small[...] - stride * update
    for values, (norm_ref, head_ref, ffn_ref) in (
        (grad, (norm_grad, head_grad, ffn_grad)),
        (second, (norm_second, head_second, ffn_second)),
        (fresh, (norm_new, head_new, ffn_new)),
    ):
        norm_ref[...] = values[0:6, 0:norm_ref.shape[1]]
        head_ref[...] = values[6:8, 0:head_ref.shape[1]]
        ffn_ref[...] = values[8:9, 0:ffn_ref.shape[0]].reshape(ffn_ref.shape)
    for copy in loads[8:]:
        copy.wait()


def step(reduced, lines, totals, weights, rows_old, cols_old, vectors, squares, passed):
    vmem, some = pl.BlockSpec(memory_space=pltpu.VMEM), pl.BlockSpec(memory_space=pl.ANY)
    small, grads = reduced[0], reduced[1:]
    shapes = [w.shape for w in weights] + [v.shape for v in vectors]
    shapes += [r.shape for r in rows_old] + [c.shape for c in cols_old]
    shapes += [v.shape for v in vectors] + [w.shape for w in weights] + [v.shape for v in vectors]
    outs = [jax.ShapeDtypeStruct(s, F32) for s in shapes]
    large = [*grads, *weights, *passed]
    operands = [small, lines, totals, *rows_old, *cols_old, *vectors, *squares]
    return pl.pallas_call(
        step_kernel,
        out_shape=outs + [jax.ShapeDtypeStruct(v.shape, v.dtype) for v in passed],
        in_specs=[some] * len(large) + [vmem] * len(operands),
        out_specs=[vmem] * (len(shapes) + len(passed)),
        scratch_shapes=[pltpu.VMEM(v.shape, F32) for v in [*grads, *weights]] + [
            pltpu.VMEM((16, 128), F32), pltpu.VMEM((16, 128), F32),
            pltpu.SemaphoreType.DMA((11,)),
        ],
        compiler_params=pltpu.CompilerParams(vmem_limit_bytes=60 << 20),
        name="adafactor_step",
    )(*large, *operands)


HALF = D // 2
QKV_HALF = 3 * HALF
VMEM = pl.BlockSpec(memory_space=pltpu.VMEM)
SMEM = pl.BlockSpec(memory_space=pltpu.SMEM)


def dot(a, b):
    return jnp.dot(a, b, preferred_element_type=F32)


def dot_last(a, b):
    return lax.dot_general(a, b, (((1,), (1,)), ((), ())), preferred_element_type=F32)


def dot_first(a, b):
    return lax.dot_general(a, b, (((0,), (0,)), ((), ())), preferred_element_type=F32)


def ids_at(lengths, row, places):
    bound = jnp.int32(0)
    ids = jnp.zeros(places.shape, jnp.int32)
    for segment in range(SEGS):
        bound = bound + lengths[row, segment]
        ids = ids + (places >= bound).astype(jnp.int32)
    return ids


def set_bias(bias, lengths, row):
    down = ids_at(lengths, row, lax.broadcasted_iota(jnp.int32, (LEN, 1), 0))
    across = ids_at(lengths, row, lax.broadcasted_iota(jnp.int32, (1, LEN), 1))
    bias[...] = jnp.where(down == across, 0.0, -1e30)


def half_masks():
    lane = lax.broadcasted_iota(jnp.int32, (1, 128), 1)
    return [((lane // HD) == half).astype(F32).astype(BF) for half in range(2)]


PAIR = 3 * 128


def slab(ref, core, row, part, pair):
    return ref[core, pl.ds(pl.multiple_of(row * LEN, LEN), LEN),
               pl.ds(pl.multiple_of(pair * PAIR + part * 128, 128), 128)]


def project(tokens, weight, offsets, qkv, row):
    rows = pl.ds(pl.multiple_of(row * LEN, LEN), LEN)
    values = tokens[rows, :]
    for core in range(2):
        for pair in range(3):
            cut = slice(pair * PAIR, (pair + 1) * PAIR)
            out = (dot(values, weight[core, :, cut]) + offsets[core, :, cut]).astype(BF)
            scale = jnp.where(
                lax.broadcasted_iota(jnp.int32, (1, PAIR), 1) < 128, HD ** -0.5, 1.0).astype(BF)
            qkv[core, rows, cut] = out * scale


def attend(qkv, bias, context, lse, held, row):
    rows = pl.ds(pl.multiple_of(row * LEN, LEN), LEN)
    lane = lax.broadcasted_iota(jnp.int32, (LEN, 128), 1)
    held[...] = jnp.zeros(held.shape, F32)

    @pl.loop(0, 6)
    def _(item):
        core, pair = item // 3, item % 3
        queries, keys, values = (slab(qkv, core, row, part, pair) for part in range(3))
        wide = jnp.concatenate([values, jnp.ones_like(values)], axis=1)
        outs = []
        logs = held[...]
        for half, mask in enumerate(half_masks()):
            scores = dot_last(queries * mask, keys) + bias[...]
            peak = jnp.max(scores, axis=1, keepdims=True)
            raised = jnp.exp(scores - peak).astype(BF)
            both = dot(raised, wide)
            total = both[:, 128:]
            outs.append(both[:, :128] / total)
            logs = jnp.where(lane == item * 2 + half, peak + jnp.log(total), logs)
        held[...] = logs
        context[rows, pl.ds(pl.multiple_of(item * 128, 128), 128)] = jnp.where(
            lane < HD, outs[0], outs[1]).astype(BF)

    lse[row] = held[...].T[0:16, :]


def forward_kernel(tokens, weight, offsets, lengths, qkv, context, lse, bias, held):
    core = lax.axis_index("mp")

    @pl.loop(0, 2)
    def _(row):
        set_bias(bias, lengths, core * 2 + row)
        project(tokens, weight, offsets, qkv, row)
        attend(qkv, bias, context, lse, held, row)


def forward(tokens, weight, offsets, lengths):
    count = tokens.shape[0]
    return pl.pallas_call(
        forward_kernel,
        out_shape=[
            jax.ShapeDtypeStruct((2, count, QKV_HALF), BF),
            jax.ShapeDtypeStruct((count, D), BF),
            jax.ShapeDtypeStruct((count // LEN, 16, LEN), F32),
        ],
        in_specs=[VMEM, VMEM, VMEM, SMEM],
        out_specs=[VMEM] * 3,
        scratch_shapes=[pltpu.VMEM((LEN, LEN), F32), pltpu.VMEM((LEN, 128), F32)],
        compiler_params=pltpu.CompilerParams(vmem_limit_bytes=56 << 20),
        name="project_attend",
    )(tokens, weight, offsets, lengths)


def gelu_both(inner):
    cdf = 0.5 * (1.0 + lax.erf(inner * 0.7071067811865476))
    density = 0.3989422804014327 * jnp.exp(-0.5 * inner * inner)
    return inner * cdf, cdf + inner * density


def norm_parts(values):
    center = values - jnp.mean(values, axis=-1, keepdims=True)
    scale = lax.rsqrt(jnp.mean(center * center, axis=-1, keepdims=True) + EPS_NORM)
    return center * scale, scale


def norm_back(grad, normed, scale, gain):
    scaled = grad * gain
    mean = jnp.mean(scaled, axis=-1, keepdims=True)
    along = jnp.mean(scaled * normed, axis=-1, keepdims=True)
    return (
        (scaled - mean - normed * along) * scale,
        jnp.sum(grad * normed, axis=0, keepdims=True),
        jnp.sum(grad, axis=0, keepdims=True),
    )


CHUNK = 512


def middle(row, core, tokens, context, cotangent, lengths, w_out, w_up, w_down, ffn, norm, layer_out,
           pooled, hidden_b, act, grad_branch, grad_inner, grad_attended, grad_context,
           grad_one, delta, norm_sums, ffn_sums, slope, branch, hidden, normed_one, grad_two):
    rows = pl.ds(pl.multiple_of(row * LEN, LEN), LEN)
    attended = dot(context[rows, :], w_out[...]) + norm[0:1, :]
    normed, scale_one = norm_parts(tokens[rows, :].astype(F32) + attended)
    normed_one[...] = normed
    value = normed * norm[2:3, :] + norm[3:4, :]
    hidden[...] = value
    hidden_b[rows, :] = value.astype(BF)
    branch[...] = jnp.zeros(branch.shape, F32)
    for chunk in range(FF // CHUNK):
        core_of, start = chunk * CHUNK // (FF // 2), chunk * CHUNK % (FF // 2)
        cols = slice(chunk * CHUNK, (chunk + 1) * CHUNK)
        up = w_up[core_of, :, start:start + CHUNK]
        value, slope_value = gelu_both(dot(hidden_b[rows, :], up) + ffn[:, cols])
        value = value.astype(BF)
        act[rows, cols] = value
        slope[:, cols] = slope_value.astype(BF)
        branch[...] += dot(value, w_down[cols, :])
    normed, scale = norm_parts(hidden[...] + branch[...] + norm[1:2, :])
    output = normed * norm[4:5, :] + norm[5:6, :]
    high = output.astype(BF)
    layer_out[rows, :] = high
    low = (output - high.astype(F32)).astype(BF)
    place = lax.broadcasted_iota(jnp.int32, (SEGS, LEN), 1)
    segment = lax.broadcasted_iota(jnp.int32, (SEGS, 1), 0)
    ids = ids_at(lengths, core * 2 + row, place)
    member = (ids == segment).astype(F32)
    sizes = jnp.sum(member, axis=1, keepdims=True)
    member = member.astype(BF)
    pooled[row] = (dot(member, high) + dot(member, low)) / sizes
    back, gain, shift = norm_back(cotangent[rows, :].astype(F32), normed, scale, norm[4:5, :])
    norm_sums[4:5, :] += gain
    norm_sums[5:6, :] += shift
    grad_two[...] = back
    back = back.astype(BF)
    grad_branch[rows, :] = back
    norm_sums[1:2, :] += jnp.sum(back.astype(F32), axis=0, keepdims=True)
    for chunk in range(FF // CHUNK):
        core_of, start = chunk * CHUNK // (FF // 2), chunk * CHUNK % (FF // 2)
        cols = slice(chunk * CHUNK, (chunk + 1) * CHUNK)
        value = dot_last(grad_branch[rows, :], w_down[cols, :])
        value = (value * slope[:, cols].astype(F32)).astype(BF)
        grad_inner[rows, cols] = value
        ffn_sums[:, cols] += jnp.sum(value.astype(F32), axis=0, keepdims=True)
        grad_two[...] += dot_last(value, w_up[core_of, :, start:start + CHUNK])
    back, gain, shift = norm_back(grad_two[...], normed_one[...], scale_one, norm[2:3, :])
    norm_sums[2:3, :] += gain
    norm_sums[3:4, :] += shift
    grad_one[rows, :] = back
    back = back.astype(BF)
    grad_attended[rows, :] = back
    norm_sums[0:1, :] += jnp.sum(back.astype(F32), axis=0, keepdims=True)
    back = dot_last(back, w_out[...]).astype(BF)
    grad_context[rows, :] = back
    product = back.astype(F32) * context[rows, :].astype(F32)
    high = product.astype(BF)
    low = (product - high.astype(F32)).astype(BF)
    head = lax.broadcasted_iota(jnp.int32, (16, D), 0)
    member = (lax.broadcasted_iota(jnp.int32, (16, D), 1) // HD == head).astype(F32).astype(BF)
    delta[row] = dot_last(member, high) + dot_last(member, low)


def middle_kernel(*refs):
    core = lax.axis_index("mp")
    norm_sums, ffn_sums = refs[19], refs[20]
    norm_sums[...] = jnp.zeros(norm_sums.shape, F32)
    ffn_sums[...] = jnp.zeros(ffn_sums.shape, F32)

    @pl.loop(0, 2)
    def _(row):
        middle(row, core, *refs)


def middle_call(tokens, context, cotangent, lengths, w_out, w_up, w_down, ffn, norm):
    count = tokens.shape[0]
    shape = jax.ShapeDtypeStruct
    return pl.pallas_call(
        middle_kernel,
        out_shape=[
            shape((count, D), BF),
            shape((count // LEN, SEGS, D), F32),
            shape((count, D), BF),
            shape((count, FF), BF),
            shape((count, D), BF),
            shape((count, FF), BF),
            shape((count, D), BF),
            shape((count, D), BF),
            shape((count, D), F32),
            shape((count // LEN, 16, LEN), F32),
            shape((8, D), F32),
            shape((1, FF), F32),
        ],
        in_specs=[VMEM] * 3 + [SMEM] + [VMEM] * 5,
        out_specs=[VMEM] * 12,
        scratch_shapes=[
            pltpu.VMEM((LEN, FF), BF),
            pltpu.VMEM((LEN, D), F32),
            pltpu.VMEM((LEN, D), F32),
            pltpu.VMEM((LEN, D), F32),
            pltpu.VMEM((LEN, D), F32),
        ],
        compiler_params=pltpu.CompilerParams(vmem_limit_bytes=60 << 20),
        name="feed_forward",
    )(tokens, context, cotangent, lengths, w_out, w_up, w_down, ffn, norm)


def weight_grads_kernel(context, hidden_b, act, grad_branch, grad_inner, grad_attended,
                        out_grad, up_grad, down_grad):

    @pl.loop(0, FF // CHUNK)
    def _(chunk):
        half_chunks = FF // 2 // CHUNK
        cols = pl.ds(pl.multiple_of(chunk * CHUNK, CHUNK), CHUNK)
        local = pl.ds(pl.multiple_of((chunk % half_chunks) * CHUNK, CHUNK), CHUNK)
        up_grad[chunk // half_chunks, :, local] = dot(hidden_b[...], grad_inner[:, cols]).astype(BF)
        down_grad[cols, :] = dot(act[cols, :], grad_branch[...]).astype(BF)

    value = dot(context[...], grad_attended[...])
    rows, held = D // out_grad.shape[0], out_grad.shape[1]
    for block in range(out_grad.shape[0]):
        piece = value[block * rows:(block + 1) * rows, :]
        if held > rows:
            piece = jnp.concatenate([piece, jnp.zeros((held - rows, D), F32)], axis=0)
        out_grad[block] = piece.astype(BF)


def weight_grads(context, hidden_b, act, grad_branch, grad_inner, grad_attended, blocks, held):
    shape = jax.ShapeDtypeStruct
    return pl.pallas_call(
        weight_grads_kernel,
        out_shape=[shape((blocks, held, D), BF), shape((2, D, FF // 2), BF), shape((FF, D), BF)],
        in_specs=[VMEM] * 6,
        out_specs=[VMEM] * 3,
        compiler_params=pltpu.CompilerParams(vmem_limit_bytes=60 << 20),
        name="weight_grads",
    )(context, hidden_b, act, grad_branch, grad_inner, grad_attended)


def attend_back(qkv, grad_context, lse, delta, bias, grad_qkv, grad_head, row):
    rows = pl.ds(pl.multiple_of(row * LEN, LEN), LEN)
    lane = lax.broadcasted_iota(jnp.int32, (LEN, 128), 1)

    @pl.loop(0, 6)
    def _(item):
        core, pair = item // 3, item % 3
        queries, keys, values = (slab(qkv, core, row, part, pair) for part in range(3))
        wide = pl.ds(pl.multiple_of(item * 128, 128), 128)
        grad = grad_context[rows, wide]
        flipped = keys.T
        grads_k, grads_v, grads_q = [], [], []
        for half, mask in enumerate(half_masks()):
            head = item * 2 + half
            scores = dot_last(keys * mask, queries) + bias[...] - lse[row, pl.ds(head, 1), :]
            probs = jnp.exp(scores)
            grad_probs = dot_last(values * mask, grad)
            grad_scores = (probs * (grad_probs - delta[row, pl.ds(head, 1), :])).astype(BF)
            grads_v.append(dot(probs.astype(BF), grad))
            grads_k.append(dot(grad_scores, queries))
            grads_q.append(dot(flipped[half * HD:(half + 1) * HD, :], grad_scores))
        grad_q = (jnp.concatenate(grads_q, axis=0).T * HD ** -0.5).astype(BF)
        grad_k = jnp.where(lane < HD, grads_k[0], grads_k[1]).astype(BF)
        grad_v = jnp.where(lane < HD, grads_v[0], grads_v[1]).astype(BF)
        for part, value in enumerate((grad_q, grad_k, grad_v)):
            grad_qkv[core, rows, pl.ds(pl.multiple_of(pair * PAIR + part * 128, 128), 128)] = value
        grad_head[0:1, wide] += jnp.sum(grad_q.astype(F32), axis=0, keepdims=True)
        grad_head[1:2, wide] += jnp.sum(grad_v.astype(F32), axis=0, keepdims=True)


def backward_kernel(tokens, qkv, grad_context, lse, delta, lengths, weight, grad_one,
                    qkv_grad, input_grad, grad_head, grad_qkv, bias):
    core = lax.axis_index("mp")
    grad_head[...] = jnp.zeros(grad_head.shape, F32)

    @pl.loop(0, 2)
    def _(row):
        set_bias(bias, lengths, core * 2 + row)
        attend_back(qkv, grad_context, lse, delta, bias, grad_qkv, grad_head, row)
        rows = pl.ds(pl.multiple_of(row * LEN, LEN), LEN)
        input_grad[rows, :] = (
            grad_one[rows, :]
            + dot_last(grad_qkv[0, rows, :], weight[0])
            + dot_last(grad_qkv[1, rows, :], weight[1])
        )

    for core_of in range(2):
        for part in range(3):
            cut = slice(part * HALF, (part + 1) * HALF)
            qkv_grad[core_of, :, cut] = dot(tokens[...], grad_qkv[core_of, :, cut]).astype(BF)


def backward(tokens, qkv, grad_context, lse, delta, lengths, weight, grad_one):
    count = tokens.shape[1]
    shape = jax.ShapeDtypeStruct
    return pl.pallas_call(
        backward_kernel,
        out_shape=[shape((2, D, QKV_HALF), BF), shape((count, D), F32), shape((2, D), F32)],
        in_specs=[VMEM] * 5 + [SMEM] + [VMEM] * 2,
        out_specs=[VMEM] * 3,
        scratch_shapes=[
            pltpu.VMEM((2, count, QKV_HALF), BF),
            pltpu.VMEM((LEN, LEN), F32),
        ],
        compiler_params=pltpu.CompilerParams(vmem_limit_bytes=60 << 20),
        name="attend_back",
    )(tokens, qkv, grad_context, lse, delta, lengths, weight, grad_one)


UP_CHUNK = 512
DOWN_CHUNK = 256


class Spread:
    COUNT = 8

    def __init__(self, place, full, start, width, flip, sems, base, shard=None):
        self.place, self.full, self.shard = place, full, shard
        self.cols = pl.ds(start, width)
        tiles = width // 128
        cut = (tiles // 2 if flip else tiles - tiles // 2) * 128
        self.halves = [("xy", pl.ds(start, cut))]
        if cut < width:
            self.halves.append(("yx", pl.ds(start + cut, width - cut)))
        self.sems, self.base = sems, base

    def view(self, spot, cols):
        return self.full.at[spot["m"], spot["z"], spot["y"], spot["x"], :, cols]

    def copy(self, slot, axis, step, spot, cols, source=None):
        place = self.place
        send, recv = self.sems
        send, recv = send.at[self.base + slot], recv.at[self.base + slot]
        device = place.device(place.at(axis, step))
        view = self.view(spot, cols)
        sent = pltpu.make_async_remote_copy(
            view if source is None else source, view, send, recv,
            device_id=device, device_id_type=MESH)
        land = dict(spot)
        land[axis] = place.at(axis, -step)[axis]
        land = self.view(land, cols)
        arrives = pltpu.make_async_remote_copy(
            land, land, send, recv, device_id=device, device_id_type=MESH)
        return sent, arrives

    def copies(self, stage):
        place = self.place
        here = {"z": place.z, "y": place.y, "x": place.x, "m": place.m}
        if stage == 0:
            source = None if self.shard is None else self.shard.at[:, self.cols]
            return [self.copy(step - 1, "z", step, here, self.cols, source) for step in (1, 2, 3)]
        here["z"] = EVERY
        if stage == 3:
            here["y"] = here["x"] = EVERY
            return [self.copy(7, "m", 1, here, self.cols)]
        out = []
        for number, (order, cols) in enumerate(self.halves):
            spot = dict(here)
            if stage == 2:
                spot[order[0]] = EVERY
            out.append(self.copy(1 + 2 * stage + number, order[stage - 1], 1, spot, cols))
        return out

    def start(self, stage):
        for sent, _ in self.copies(stage):
            sent.start()

    def arrived(self, stage):
        for _, arrives in self.copies(stage):
            arrives.wait_recv()

    def finish(self):
        for stage in range(4):
            for sent, _ in self.copies(stage):
                sent.wait_send()


def spread_tick(groups, tick):
    for stage in range(4):
        index = tick + 2 if stage == 0 else tick - stage + 1
        if 0 <= index < len(groups):
            for chunk in groups[index]:
                if stage:
                    chunk.arrived(stage - 1)
                chunk.start(stage)


def unpack_small(small, norm_out, offsets, ffn_out):
    iota = lambda shape, axis: lax.broadcasted_iota(jnp.int32, shape, axis)
    pick = ((iota((128, D), 1) % 24 == iota((128, D), 0))).astype(F32).astype(BF)
    pick_ffn = ((iota((128, FF), 1) % 96 == iota((128, FF), 0))).astype(F32).astype(BF)
    total = jnp.zeros((16, D), F32)
    ffn = jnp.zeros((1, FF), F32)
    line, col = iota((256, D), 0), iota((256, D), 1) // 24
    device, kind = line // 16, line % 16
    for core in range(2):
        block = small[core].reshape(256, 128).astype(BF)
        wide = dot(block, pick)
        right = jnp.where(kind < 6, 2 * device + core, 16 * core + device)
        wide = jnp.where((col == right) & (kind < 8), wide, 0.0)
        total = total + jnp.sum(wide.reshape(16, 16, D), axis=0)
        wide = dot(small[core, :, :, :, 8, :].reshape(16, 128).astype(BF), pick_ffn)
        right = iota((16, FF), 1) // 96 == iota((16, FF), 0) + 16 * core
        ffn = ffn + jnp.sum(jnp.where(right, wide, 0.0), axis=0, keepdims=True)
    norm_out[0:6, :] = total[0:6, :]
    norm_out[6:8, :] = jnp.zeros((2, D), F32)
    ffn_out[...] = ffn
    offsets[...] = jnp.zeros(offsets.shape, F32)
    for core in range(2):
        for pair in range(3):
            source = core * HALF + pair * 128
            for part, row in ((0, 6), (2, 7)):
                start = pair * PAIR + part * 128
                offsets[core, :, start:start + 128] = total[row:row + 1, source:source + 128]


def place_of(core, part, width):
    return pl.ds(pl.multiple_of(core * PAIR + part * 128, 128), width)


def trio(ref, core, row, part, pair):
    return ref[pair, pl.ds(pl.multiple_of(row * LEN, LEN), LEN), place_of(core, part, 128)]


def project_pair(tokens, weight, offsets, qkv, pair):
    cols = pl.ds(pl.multiple_of(pair * PAIR, PAIR), PAIR)
    scale = jnp.where(
        lax.broadcasted_iota(jnp.int32, (1, PAIR), 1) < 128, HD ** -0.5, 1.0).astype(BF)
    for core in range(2):
        piece = weight[core, :, :, :, :, cols].reshape(D, PAIR)
        out = dot(tokens[...], piece) + offsets[core, :, cols]
        qkv[pair, :, place_of(core, 0, PAIR)] = out.astype(BF) * scale


def attend_pair(qkv, bias, context, logs_ref, core, row, pair):
    rows = pl.ds(pl.multiple_of(row * LEN, LEN), LEN)
    lane = lax.broadcasted_iota(jnp.int32, (LEN, 128), 1)
    item = core * 3 + pair
    queries, keys, values = (trio(qkv, core, row, part, pair) for part in range(3))
    wide = jnp.concatenate([values, jnp.ones_like(values)], axis=1)
    outs = []
    logs = logs_ref[row]
    for half, mask in enumerate(half_masks()):
        scores = dot_last(queries * mask, keys) + bias[row]
        peak = jnp.max(scores, axis=1, keepdims=True)
        raised = jnp.exp(scores - peak).astype(BF)
        both = dot(raised, wide)
        total = both[:, 128:]
        outs.append(both[:, :128] / total)
        logs = jnp.where(lane == item * 2 + half, peak + jnp.log(total), logs)
    logs_ref[row] = logs
    context[rows, pl.ds(pl.multiple_of(item * 128, 128), 128)] = jnp.where(
        lane < HD, outs[0], outs[1]).astype(BF)


def forward_gather_kernel(*refs):
    refs = list(refs)
    take = lambda number: [refs.pop(0) for _ in range(number)]
    w_qkv, w_out, w_up, w_down, head, ffn, norm, lengths = take(8)
    tokens_any, cotangent_any = take(2)
    (sums, norm_out, ffn_out, lse, hidden_scale, out_full, pooled, norm_sums) = take(8)
    (qkv_full, up_full, down_full, qkv_out, context_flip, token_flip, hidden_flip, normed_out,
     context_out, act_flip, slope_out, layer_out, branch_out, grad_two_out) = take(14)
    (g_small, g_qkv, g_out, g_up, g_down, tokens, qkv, context, flip,
     hidden_b, normed_one, act, slope, flip_act, bias, logs, offsets, branch) = take(18)
    send, recv, local = refs
    place = Place()
    here = (place.m, place.z, place.y, place.x)
    used = [0]
    unwaited = []

    def keep(source, target):
        copy = pltpu.make_async_copy(source, target, local.at[used[0]])
        used[0] += 1
        copy.start()
        unwaited.append(copy)
        return copy

    def done(copy):
        copy.wait()
        unwaited[:] = [other for other in unwaited if other is not copy]

    tokens_loaded = keep(tokens_any, tokens)
    place_small(g_small.at[here], norm[...], head[...], as_row(ffn), 0.0)
    for part in range(3):
        for pair in range(3):
            start = pair * PAIR + part * 128
            g_qkv[here + (EVERY, slice(start, start + 128))] = w_qkv[
                part, :, pair * 128:(pair + 1) * 128].astype(BF)
    value = w_out[...]
    spare = g_out.shape[4] - value.shape[0]
    g_out[here] = jnp.concatenate([value, jnp.zeros((spare, D), F32)], axis=0).astype(BF)
    g_up[here] = w_up[...].astype(BF)
    g_down[here] = w_down[...].astype(BF)
    sems, base = (send, recv), [0]

    def chunk(full, start, width, flip=False):
        made = Spread(place, full, start, width, flip, sems, base[0])
        base[0] += Spread.COUNT
        return made

    groups = [[chunk(g_small, 0, 128), chunk(g_qkv, 0, PAIR)]]
    groups += [[chunk(g_qkv, pair * PAIR, PAIR, pair == 1)] for pair in (1, 2)]
    groups += [[chunk(g_out, 0, D)]]
    groups += [[chunk(g_up, at, UP_CHUNK)] for at in range(0, FF // 2, UP_CHUNK)]
    groups += [[chunk(g_down, at, DOWN_CHUNK)] for at in range(0, D, DOWN_CHUNK)]

    def ready(index):
        for made in groups[index]:
            made.arrived(3)

    greet(place)
    for index in (0, 1):
        for made in groups[index]:
            made.start(0)
    sums[...] = weight_sums_of([w_qkv, w_out, w_up, w_down], g_small[here])
    spread_tick(groups, 0)
    for row in range(2):
        set_bias(bias.at[row], lengths, place.m * 2 + row)
    spread_tick(groups, 1)
    done(tokens_loaded)
    flip[...] = tokens[...].T
    flip_kept = keep(flip, token_flip)
    spread_tick(groups, 2)
    logs[...] = jnp.zeros(logs.shape, F32)
    ready(0)
    unpack_small(g_small, norm_out, offsets, ffn_out)

    @pl.loop(0, 12)
    def _(item):
        pair, row, core = item // 4, (item % 4) // 2, item % 2
        for number, at in enumerate((2, 4, 6, 8, 10)):
            @pl.when(item == at)
            def _():
                spread_tick(groups, 3 + number)
                if at in (4, 8):
                    ready(at // 4)

        @pl.when(item % 4 == 0)
        def _():
            project_pair(tokens, g_qkv, offsets, qkv, pair)

        attend_pair(qkv, bias, context, logs, core, row, pair)

    for core in range(2):
        for pair in range(3):
            cols = slice(pair * PAIR, (pair + 1) * PAIR)
            keep(g_qkv.at[core, :, :, :, :, cols],
                 qkv_full.at[pair, :, :, :, :, core * PAIR:(core + 1) * PAIR])
    keep(qkv, qkv_out)
    context_kept = keep(context, context_out)
    for row in range(2):
        lse[row] = logs[row].T[0:16, :]
    done(flip_kept)
    flip[...] = context[...].T
    flip_kept = keep(flip, context_flip)
    ready(3)
    rows_out = w_out.shape[0]
    for core in range(2):
        value = g_out[core].reshape(16, g_out.shape[4], D).astype(F32)[:, :rows_out]
        out_full[core * HALF:(core + 1) * HALF, :] = value.reshape(HALF, D).astype(BF)
    halves = [slice(row * LEN, (row + 1) * LEN) for row in range(2)]
    for rows in halves:
        attended = dot(context[rows, :], out_full[...]) + norm_out[0:1, :]
        normed, scale = norm_parts(tokens[rows, :].astype(F32) + attended)
        normed_one[rows, :] = normed
        hidden_scale[rows, :] = jnp.broadcast_to(scale, (LEN, 128))
        hidden_b[rows, :] = (normed * norm_out[2:3, :] + norm_out[3:4, :]).astype(BF)
    cotangent_loaded = keep(cotangent_any, tokens)
    keep(normed_one, normed_out)
    spread_tick(groups, 8)
    waiting = [[], []]
    for third in range(3):
        ready(4 + third)
        for core in range(2):
            for copy in waiting[core]:
                copy.wait()
            local_cols = slice(third * UP_CHUNK, (third + 1) * UP_CHUNK)
            start = core * (FF // 2) + third * UP_CHUNK
            cols = pl.ds(start, UP_CHUNK)
            up = g_up[core, :, :, :, :, local_cols].reshape(D, UP_CHUNK)

            @pl.loop(0, 2)
            def _(row):
                rows = pl.ds(pl.multiple_of(row * LEN, LEN), LEN)
                value, slope_value = gelu_both(
                    dot(hidden_b[rows, :], up) + ffn_out[:, start:start + UP_CHUNK])
                act[rows, cols] = value.astype(BF)
                slope[core, rows, :] = slope_value.astype(BF)

            flip_act[core] = act[:, cols].T
            slot = 24 + 2 * core
            waiting[core] = [
                pltpu.make_async_copy(slope.at[core], slope_out.at[:, cols], local.at[slot]),
                pltpu.make_async_copy(flip_act.at[core], act_flip.at[cols, :], local.at[slot + 1]),
            ]
            for copy in waiting[core]:
                copy.start()
        spread_tick(groups, 9 + third)
    done(flip_kept)
    flip[...] = hidden_b[...].T
    keep(flip, hidden_flip)
    for core in range(2):
        keep(g_up.at[core], up_full.at[core])
    for third in range(3):
        ready(7 + third)
        cols = slice(third * DOWN_CHUNK, (third + 1) * DOWN_CHUNK)
        down = g_down[:, :, :, :, :, cols].reshape(FF, DOWN_CHUNK)
        for rows in halves:
            branch[rows, cols] = dot(act[rows, :], down)
    for core in range(2):
        keep(g_down.at[core], down_full.at[core])
    norm_sums[...] = jnp.zeros(norm_sums.shape, F32)
    done(cotangent_loaded)
    done(context_kept)
    for row, rows in enumerate(halves):
        hidden = normed_one[rows, :] * norm_out[2:3, :] + norm_out[3:4, :]
        normed, scale = norm_parts(hidden + branch[rows, :] + norm_out[1:2, :])
        output = normed * norm_out[4:5, :] + norm_out[5:6, :]
        high = output.astype(BF)
        context[rows, :] = high
        keep(context.at[rows], layer_out.at[rows])
        low = (output - high.astype(F32)).astype(BF)
        spots = lax.broadcasted_iota(jnp.int32, (SEGS, LEN), 1)
        segment = lax.broadcasted_iota(jnp.int32, (SEGS, 1), 0)
        member = (ids_at(lengths, place.m * 2 + row, spots) == segment).astype(F32)
        sizes = jnp.sum(member, axis=1, keepdims=True)
        member = member.astype(BF)
        pooled[row] = (dot(member, high) + dot(member, low)) / sizes
        back, gain, shift = norm_back(tokens[rows, :].astype(F32), normed, scale, norm_out[4:5, :])
        norm_sums[4:5, :] += gain
        norm_sums[5:6, :] += shift
        branch[rows, :] = back
        keep(branch.at[rows], grad_two_out.at[rows])
        back = back.astype(BF)
        hidden_b[rows, :] = back
        keep(hidden_b.at[rows], branch_out.at[rows])
        norm_sums[1:2, :] += jnp.sum(back.astype(F32), axis=0, keepdims=True)
    for copy in unwaited + waiting[0] + waiting[1]:
        copy.wait()
    for group in groups:
        for made in group:
            made.finish()


def forward_gather(weights, vectors, lengths, tokens, cotangent):
    qkv, out, up, down = weights
    count = tokens.shape[0]
    shape = jax.ShapeDtypeStruct
    grid = (2, 4, 2, 2)
    rows = count // LEN
    flipped = shape((D, count), BF)
    small_outs = [
        shape((8, 128), F32), shape((8, D), F32), shape((1, FF), F32), shape((rows, 16, LEN), F32),
        shape((count, 128), F32), shape((D, D), BF), shape((rows, SEGS, D), F32), shape((8, D), F32),
    ]
    large_outs = [
        shape((3,) + grid[1:] + (qkv.shape[1], D), BF), shape(grid + up.shape, BF),
        shape(grid + down.shape, BF), shape((3, count, D), BF), flipped, flipped, flipped,
        shape((count, D), F32), shape((count, D), BF), shape((FF, count), BF),
        shape((count, FF), BF), shape((count, D), BF), shape((count, D), BF), shape((count, D), F32),
    ]
    slots = 11 * Spread.COUNT
    some = pl.BlockSpec(memory_space=pl.ANY)
    return pl.pallas_call(
        forward_gather_kernel,
        out_shape=small_outs + large_outs,
        in_specs=[VMEM] * 7 + [SMEM] + [some] * 2,
        out_specs=[VMEM] * len(small_outs) + [some] * len(large_outs),
        scratch_shapes=[
            pltpu.VMEM(grid + (16, 128), F32),
            pltpu.VMEM(grid + (qkv.shape[1], QKV_HALF), BF),
            pltpu.VMEM(grid + (32, D), BF),
            pltpu.VMEM(grid + up.shape, BF),
            pltpu.VMEM(grid + down.shape, BF),
            pltpu.VMEM((count, D), BF),
            pltpu.VMEM((3, count, D), BF),
            pltpu.VMEM((count, D), BF),
            pltpu.VMEM((D, count), BF),
            pltpu.VMEM((count, D), BF),
            pltpu.VMEM((count, D), F32),
            pltpu.VMEM((count, FF), BF),
            pltpu.VMEM((2, count, UP_CHUNK), BF),
            pltpu.VMEM((2, UP_CHUNK, count), BF),
            pltpu.VMEM((2, LEN, LEN), F32),
            pltpu.VMEM((2, LEN, 128), F32),
            pltpu.VMEM((2, 1, QKV_HALF), F32),
            pltpu.VMEM((count, D), F32),
            pltpu.SemaphoreType.DMA((slots,)),
            pltpu.SemaphoreType.DMA((slots,)),
            pltpu.SemaphoreType.DMA((30,)),
        ],
        compiler_params=pltpu.CompilerParams(
            collective_id=0, has_side_effects=True, vmem_limit_bytes=61 << 20),
        name="forward_gather",
    )(*weights, *vectors, lengths, tokens, cotangent)


class Collect:
    COUNT = 8

    def __init__(self, place, held, slots, result, start, width, flip, sems, base):
        self.place, self.held, self.slots, self.result = place, held, slots, result
        self.cols = pl.ds(start, width)
        tiles = width // 128
        cut = (tiles // 2 if flip else tiles - tiles // 2) * 128
        self.halves = [("xy", pl.ds(start, cut))]
        if cut < width:
            self.halves.append(("yx", pl.ds(start + cut, width - cut)))
        self.sems, self.base = sems, base

    def copy(self, slot, axis, step, source, target):
        send, recv = self.sems
        return pltpu.make_async_remote_copy(
            source, target, send.at[self.base + slot], recv.at[self.base + slot],
            device_id=self.place.device(self.place.at(axis, step)), device_id_type=MESH)

    def copies(self, stage):
        place = self.place
        if stage == 2:
            out = []
            for step in (1, 2, 3):
                source = self.held.at[place.at("z", step)["z"], place.y, place.x, :, self.cols]
                out.append(self.copy(
                    step - 1, "z", step, source, self.slots[2].at[step - 1, :, self.cols]))
            return out
        out = []
        for number, (order, cols) in enumerate(self.halves):
            axis = order[stage]
            spot = {"y": EVERY, "x": EVERY}
            if stage == 1:
                spot[order[0]] = getattr(place, order[0])
            spot[axis] = place.at(axis, 1)[axis]
            land = (EVERY,) * (2 - stage) + (EVERY, cols)
            out.append(self.copy(
                3 + 2 * stage + number, axis, 1, self.held.at[:, spot["y"], spot["x"], :, cols],
                self.slots[stage].at[land]))
        return out

    def start(self, stage):
        for sent in self.copies(stage):
            sent.start()

    def add(self, stage):
        place, held, slots = self.place, self.held, self.slots[stage]
        for sent in self.copies(stage):
            sent.wait_recv()
        if stage == 2:
            value = held[place.z, place.y, place.x, :, self.cols].astype(F32)
            for step in range(3):
                value = value + slots[step, :, self.cols].astype(F32)
            self.result[:, self.cols] = value[:self.result.shape[0]]
            return
        for order, cols in self.halves:

            @pl.loop(0, 8 if stage == 0 else 4)
            def _(index):
                spot = {"y": place.y, "x": place.x}
                if stage == 0:
                    layer = index // 2
                    spot[order[1]] = index % 2
                    arrived = slots[layer, index % 2, :, cols]
                else:
                    layer = index
                    arrived = slots[layer, :, cols]
                at = (layer, spot["y"], spot["x"], EVERY, cols)
                held[at] = (held[at].astype(F32) + arrived.astype(F32)).astype(held.dtype)

    def finish(self):
        for stage in range(3):
            for sent in self.copies(stage):
                sent.wait_send()


def collect_tick(groups, tick):
    for stage in range(4):
        if 0 <= tick - stage < len(groups):
            for chunk in groups[tick - stage]:
                if stage:
                    chunk.add(stage - 1)
                if stage < 3:
                    chunk.start(stage)


def pack_small(target, core, norm_sums, grad_head, ffn_sums):
    iota = lambda shape, axis: lax.broadcasted_iota(jnp.int32, shape, axis)
    pick = (iota((D, 128), 0) % 24 == iota((D, 128), 1)).astype(F32).astype(BF)
    pick_ffn = (iota((FF, 128), 0) % 96 == iota((FF, 128), 1)).astype(F32).astype(BF)

    def split_dot(value, other):
        high = value.astype(BF)
        return dot(high, other) + dot((value - high.astype(F32)).astype(BF), other)

    rows = jnp.concatenate(
        [norm_sums[0:6, :], grad_head[0:2, :], jnp.zeros((8, D), F32)], axis=0)
    rows = jnp.broadcast_to(rows[None], (16, 16, D)).reshape(256, D)
    line = iota((256, D), 0)
    device, kind = line // 16, line % 16
    right = jnp.where(kind < 6, 2 * device + core, 16 * core + device)
    rows = jnp.where(iota((256, D), 1) // 24 == right, rows, 0.0)
    target[...] = split_dot(rows, pick).reshape(4, 2, 2, 16, 128)
    right = iota((16, FF), 1) // 96 == iota((16, FF), 0) + 16 * core
    ffn = split_dot(jnp.where(right, ffn_sums[...], 0.0), pick_ffn)
    target[:, :, :, 8, :] = ffn.reshape(4, 2, 2, 128)


def attend_back_pair(qkv, grad_context, lse, delta, bias, grad_head, core, row, pair):
    lane = lax.broadcasted_iota(jnp.int32, (LEN, 128), 1)
    item = core * 3 + pair
    queries, keys, values = (trio(qkv, core, row, part, pair) for part in range(3))
    rows = pl.ds(pl.multiple_of(row * LEN, LEN), LEN)
    wide = pl.ds(pl.multiple_of(item * 128, 128), 128)
    grad = grad_context[rows, wide]
    flipped = keys.T
    grads_k, grads_v, grads_q = [], [], []
    for half, mask in enumerate(half_masks()):
        head = item * 2 + half
        scores = dot_last(keys * mask, queries) + bias[row] - lse[row, pl.ds(head, 1), :]
        probs = jnp.exp(scores)
        grad_probs = dot_last(values * mask, grad)
        grad_scores = (probs * (grad_probs - delta[row, pl.ds(head, 1), :])).astype(BF)
        grads_v.append(dot(probs.astype(BF), grad))
        grads_k.append(dot(grad_scores, queries))
        grads_q.append(dot(flipped[half * HD:(half + 1) * HD, :], grad_scores))
    grad_q = (jnp.concatenate(grads_q, axis=0).T * HD ** -0.5).astype(BF)
    grad_k = jnp.where(lane < HD, grads_k[0], grads_k[1]).astype(BF)
    grad_v = jnp.where(lane < HD, grads_v[0], grads_v[1]).astype(BF)
    for part, value in enumerate((grad_q, grad_k, grad_v)):
        qkv[pair, rows, place_of(core, part, 128)] = value
    grad_head[0:1, wide] += jnp.sum(grad_q.astype(F32), axis=0, keepdims=True)
    grad_head[1:2, wide] += jnp.sum(grad_v.astype(F32), axis=0, keepdims=True)


def backward_scatter_kernel(*refs):
    refs = list(refs)
    take = lambda number: [refs.pop(0) for _ in range(number)]
    lengths, lse, norm_given, norm, scale_one, w_out = take(6)
    rows_old, cols_old = take(4), take(4)
    head_sq, ffn_sq, norm_sq, weight_sums = take(4)
    (act_any, branch_any, down_any, slope_any, up_any, two_any, normed_any, hidden_any, context_any,
     flip_any, token_any, qkv_any, weight_any) = take(13)
    results = take(5)
    lines, totals, input_any = take(3)
    held, other = take(5), take(5)
    slots = [take(3) for _ in range(5)]
    (wide, flip, flip_context, context, attended, qkv, weight, one, two, act, inner, bias, delta,
     grad_head, norm_sums, ffn_sums) = take(16)
    mine_one, land_one, mine_two, land_two, old_small = take(5)
    send, recv, local = refs
    place = Place()
    sems = (send, recv)
    partner = place.device(place.at("m", 1))
    mine, theirs = place.m, 1 - place.m
    loaded = {}

    def load(name, source, target):
        copy = pltpu.make_async_copy(source, target, local.at[len(loaded)])
        copy.start()
        loaded[name] = copy

    tile_rows = FF // 2 // 4
    act_slots, chunk_slots = 16, 18

    def act_load(index):
        core = jnp.where(index < 4, theirs, mine)
        start = pl.multiple_of(core * (FF // 2) + (index % 4) * tile_rows, tile_rows)
        return pltpu.make_async_copy(
            act_any.at[pl.ds(start, tile_rows)], act.at[index % 2], local.at[act_slots + index % 2])

    def down_tile(index):
        return qkv.at[0, pl.ds(pl.multiple_of(index % 2 * UP_CHUNK, UP_CHUNK), UP_CHUNK)]

    def slope_tile(index):
        return qkv.at[1 + index % 2, :, pl.ds(0, UP_CHUNK)]

    def up_tile(index):
        return weight.at[index % 2, :, pl.ds(0, UP_CHUNK)]

    def chunk_loads(index):
        core = jnp.where(index < 3, theirs, mine)
        inside = pl.ds(pl.multiple_of(index % 3 * UP_CHUNK, UP_CHUNK), UP_CHUNK)
        whole = pl.ds(
            pl.multiple_of(core * (FF // 2) + index % 3 * UP_CHUNK, UP_CHUNK), UP_CHUNK)
        slot = chunk_slots + 3 * (index % 2)
        return [
            pltpu.make_async_copy(down_any.at[whole], down_tile(index), local.at[slot]),
            pltpu.make_async_copy(slope_any.at[:, whole], slope_tile(index), local.at[slot + 1]),
            pltpu.make_async_copy(up_any.at[core, :, inside], up_tile(index), local.at[slot + 2]),
        ]

    load("branch", branch_any, wide)
    for index in range(2):
        act_load(index).start()
    load("hidden", hidden_any, flip)
    load("two", two_any, two)
    for index in range(2):
        for copy in chunk_loads(index):
            copy.start()
    load("normed", normed_any, one)
    load("context", context_any, context)
    load("flip", flip_any, flip_context)

    small, qkv_held, out_held, up_held, down_held = held
    small_other, qkv_other, out_other, up_other, down_other = other
    base = 12

    def swap(slot, source, target):
        return pltpu.make_async_remote_copy(
            source, target, send.at[slot], recv.at[slot],
            device_id=partner, device_id_type=MESH)

    def down_swap(layer):
        return swap(layer, down_held.at[layer], down_other.at[layer])

    def up_swap(third):
        cols = pl.ds(pl.multiple_of(third * UP_CHUNK, UP_CHUNK), UP_CHUNK)
        at = (EVERY, EVERY, EVERY, EVERY, cols)
        return swap(4 + third, up_held.at[at], up_other.at[at])

    def qkv_swap(pair):
        at = (EVERY, EVERY, EVERY, EVERY, pl.ds(pl.multiple_of(pair * PAIR, PAIR), PAIR))
        return swap(8 + pair, qkv_held.at[at], qkv_other.at[at])

    out_swap = swap(7, out_held, out_other)
    small_swap = swap(11, small, small_other)
    widths = (128, PAIR, D, UP_CHUNK, DOWN_CHUNK)
    chunks = [[] for _ in range(5)]
    for index in (4, 3, 2, 1, 0):
        for start in range(0, held[index].shape[4], widths[index]):
            chunks[index].append(Collect(
                place, held[index], slots[index], results[index], start, widths[index],
                index == 1 and start == PAIR, sems, base))
            base += Collect.COUNT
    groups = [[c] for index in (4, 3, 2, 1) for c in chunks[index]]
    groups[-1] += chunks[0]

    greet(place)
    norm_sums[...] = norm_given[...]
    loaded["branch"].wait()

    @pl.loop(0, 4)
    def _(layer):
        act_load(layer).wait()
        value = dot(act[layer % 2], wide[...])
        down_held[layer] = value.reshape(2, 2, tile_rows // 4, D).astype(BF)
        down_swap(layer).start()
        act_load(layer + 2).start()

    @pl.loop(0, 4)
    def _(layer):
        act_load(layer + 4).wait()
        value = dot(act[layer % 2], wide[...]).reshape(2, 2, tile_rows // 4, D)
        down_swap(layer).wait()
        down_held[layer] = (value + down_other[layer].astype(F32)).astype(BF)

        @pl.when(layer < 2)
        def _():
            act_load(layer + 6).start()

    collect_tick(groups, 0)
    loaded["hidden"].wait()
    loaded["two"].wait()

    def feed_back(index):
        for copy in chunk_loads(index):
            copy.wait()
        core = jnp.where(index < 3, theirs, mine)
        whole = pl.ds(
            pl.multiple_of(core * (FF // 2) + index % 3 * UP_CHUNK, UP_CHUNK), UP_CHUNK)
        value = dot_last(wide[...], down_tile(index)[...])
        value = (value * slope_tile(index)[...].astype(F32)).astype(BF)
        inner[...] = value
        ffn_sums[:, whole] = jnp.sum(value.astype(F32), axis=0, keepdims=True)
        two[...] += dot_last(inner[...], up_tile(index)[...])
        return dot(flip[...], inner[...]).reshape(4, 2, 2, D // 16, UP_CHUNK)

    @pl.loop(0, 3)
    def _(third):
        cols = pl.ds(pl.multiple_of(third * UP_CHUNK, UP_CHUNK), UP_CHUNK)
        up_held[:, :, :, :, cols] = feed_back(third).astype(BF)
        up_swap(third).start()
        for copy in chunk_loads(third + 2):
            copy.start()

        @pl.when(third == 1)
        def _():
            collect_tick(groups, 1)

    @pl.loop(0, 3)
    def _(third):
        at = (EVERY, EVERY, EVERY, EVERY,
              pl.ds(pl.multiple_of(third * UP_CHUNK, UP_CHUNK), UP_CHUNK))
        value = feed_back(third + 3)
        up_swap(third).wait()
        up_held[at] = (value + up_other[at].astype(F32)).astype(BF)

        @pl.when(third == 0)
        def _():
            for copy in chunk_loads(5):
                copy.start()
            collect_tick(groups, 2)

    load("token", token_any, flip)
    load("qkv", qkv_any, qkv)
    load("weight", weight_any, weight)
    loaded["normed"].wait()
    loaded["context"].wait()
    collect_tick(groups, 3)
    for row in range(2):
        rows = slice(row * LEN, (row + 1) * LEN)
        back, gain, shift = norm_back(
            two[rows, :], one[rows, :], scale_one[rows, 0:1], norm[2:3, :])
        norm_sums[2:3, :] += gain
        norm_sums[3:4, :] += shift
        one[rows, :] = back
        back = back.astype(BF)
        attended[rows, :] = back
        norm_sums[0:1, :] += jnp.sum(back.astype(F32), axis=0, keepdims=True)
        back = dot_last(back, w_out[...]).astype(BF)
        wide[rows, :] = back
        product = back.astype(F32) * context[rows, :].astype(F32)
        high = product.astype(BF)
        low = (product - high.astype(F32)).astype(BF)
        head = lax.broadcasted_iota(jnp.int32, (16, D), 0)
        member = (lax.broadcasted_iota(jnp.int32, (16, D), 1) // HD == head).astype(F32).astype(BF)
        delta[row] = dot_last(member, high) + dot_last(member, low)
    loaded["flip"].wait()
    spare = out_held.shape[3] - D // 32

    def out_half(core):
        rows = pl.ds(pl.multiple_of(core * HALF, HALF), HALF)
        value = dot(flip_context[rows, :], attended[...]).reshape(16, D // 32, D)
        value = jnp.concatenate([value, jnp.zeros((16, spare, D), F32)], axis=1)
        return value.reshape(4, 2, 2, D // 32 + spare, D)

    out_held[...] = out_half(theirs).astype(BF)
    out_swap.start()
    value = out_half(mine)
    out_swap.wait()
    out_held[...] = (value + out_other[...].astype(F32)).astype(BF)
    collect_tick(groups, 4)
    for row in range(2):
        set_bias(bias.at[row], lengths, place.m * 2 + row)
    grad_head[...] = jnp.zeros(grad_head.shape, F32)
    for name in ("qkv", "token"):
        loaded[name].wait()

    def qkv_theirs(pair):
        cols = pl.ds(pl.multiple_of(pair * PAIR, PAIR), PAIR)
        value = dot(flip[...], qkv[pair, :, place_of(theirs, 0, PAIR)])
        qkv_held[:, :, :, :, cols] = value.reshape(4, 2, 2, D // 16, PAIR).astype(BF)
        qkv_swap(pair).start()

    def qkv_mine(pair):
        cols = pl.ds(pl.multiple_of(pair * PAIR, PAIR), PAIR)
        at = (EVERY, EVERY, EVERY, EVERY, cols)
        value = dot(flip[...], qkv[pair, :, place_of(mine, 0, PAIR)]).reshape(4, 2, 2, D // 16, PAIR)
        qkv_swap(pair).wait()
        qkv_held[at] = (value + qkv_other[at].astype(F32)).astype(BF)

    @pl.loop(0, 12)
    def _(item):
        pair, row, core = item // 4, (item % 4) // 2, item % 2

        @pl.when((item == 4) | (item == 8))
        def _():
            qkv_theirs(pair - 1)

        @pl.when((item == 5) | (item == 9))
        def _():
            qkv_mine(pair - 1)

        for number, at in enumerate((1, 4, 7, 10)):
            @pl.when(item == at)
            def _():
                collect_tick(groups, 5 + number)

        attend_back_pair(qkv, wide, lse, delta, bias, grad_head, core, row, pair)

    qkv_theirs(2)
    pack_small(small, theirs, norm_sums, grad_head, ffn_sums)
    small_swap.start()
    loaded["weight"].wait()

    def input_rows(row):
        rows = pl.ds(pl.multiple_of(row * LEN, LEN), LEN)
        one[rows, :] += (dot_last(qkv[0, rows, :], weight[0]) + dot_last(qkv[1, rows, :], weight[1])
                         + dot_last(qkv[2, rows, :], weight[2]))

    qkv_mine(2)
    small_swap.wait()
    pack_small(small, mine, norm_sums, grad_head, ffn_sums)
    small[...] += small_other[...]
    collect_tick(groups, 9)
    input_rows(0)
    collect_tick(groups, 10)
    input_rows(1)
    input_done = pltpu.make_async_copy(one, input_any, local.at[12])
    input_done.start()
    collect_tick(groups, 11)
    collect_tick(groups, 12)
    small_sum, grads = results[0], results[1:]
    lines[...] = jnp.zeros(lines.shape, F32)
    for index in range(4):
        grad = grads[index][...]
        square = grad * grad + EPS_SQUARE
        put_line(lines, COL_LINES[index], jnp.sum(square, axis=0, keepdims=True))
        if index in (0, 2):
            line = ROW_LINE + index // 2
            lines[line:line + 1, 0:grad.shape[0]] = to_row(jnp.sum(square, axis=1, keepdims=True))
    first = Exchange(place, mine_one, land_one, sems, base)
    line = lax.broadcasted_iota(jnp.int32, lines.shape, 0)
    value = lines[...]
    first.mine[0] = value
    paired = jnp.where(line >= OUT_LINE, first.swap(0, "m"), value)
    total = paired
    for stage, axis in ((1, "x"), (2, "y"), (3, "z")):
        first.mine[stage] = total
        total = first.swap(stage, axis)
    lines[...] = jnp.where(line >= ROW_LINE, paired, total)
    rows_new, cols_new = new_rows_cols(grads, rows_old, cols_old, lines)
    ratios, row_totals = [], []
    for index in range(4):
        grad = grads[index][...]
        scaled = jnp.sum(grad * grad * (1.0 / cols_new[index]), axis=1, keepdims=True)
        ratios.append(jnp.sum(scaled / rows_new[index], axis=0, keepdims=True))
        share = 0.5 if index in (0, 2) else 1.0
        row_totals.append(jnp.sum(rows_new[index], axis=0, keepdims=True) * share)
    place_small(old_small, norm_sq[...], head_sq[...], as_row(ffn_sq), 1.0)
    _, update = small_update(small_sum[...], old_small[...])
    second = Exchange(place, mine_two, land_two, sems, base + 16)
    totals[...] = add_up(
        second, scalars(ratios + row_totals + small_sums(update)) + weight_sums[...])
    input_done.wait()
    for group in groups:
        for chunk in group:
            chunk.finish()
    first.finish()
    second.finish()


def backward_scatter(lengths, lse, norm_sums, norm, scale_one, w_out, rows_old, cols_old, squares,
                     weight_sums, large, rows, widths):
    count = scale_one.shape[0]
    shape = jax.ShapeDtypeStruct
    some = pl.BlockSpec(memory_space=pl.ANY)
    kinds = [F32, BF, BF, BF, BF]
    padded = [16, rows[1], 32, rows[3], rows[4]]
    held = [pltpu.VMEM((4, 2, 2, r, w), k) for r, w, k in zip(padded, widths, kinds)]
    slots = []
    for r, w, k in zip(padded, widths, kinds):
        slots += [pltpu.VMEM((4, 2, r, w), k), pltpu.VMEM((4, r, w), k), pltpu.VMEM((3, r, w), k)]
    sems = 12 + 11 * Collect.COUNT + 32
    outs = [shape((r, w), F32) for r, w in zip(rows, widths)]
    outs += [shape((LINES, 128), F32), shape((8, 128), F32), shape((count, D), F32)]
    small = [lse, norm_sums, norm, scale_one, w_out, *rows_old, *cols_old, *squares, weight_sums]
    return pl.pallas_call(
        backward_scatter_kernel,
        out_shape=outs,
        in_specs=[SMEM] + [VMEM] * len(small) + [some] * len(large),
        out_specs=[VMEM] * 7 + [some],
        scratch_shapes=held + held + slots + [
            pltpu.VMEM((count, D), BF),
            pltpu.VMEM((D, count), BF),
            pltpu.VMEM((D, count), BF),
            pltpu.VMEM((count, D), BF),
            pltpu.VMEM((count, D), BF),
            pltpu.VMEM((3, count, D), BF),
            pltpu.VMEM((3, D, D), BF),
            pltpu.VMEM((count, D), F32),
            pltpu.VMEM((count, D), F32),
            pltpu.VMEM((2, FF // 8, count), BF),
            pltpu.VMEM((count, UP_CHUNK), BF),
            pltpu.VMEM((2, LEN, LEN), F32),
            pltpu.VMEM((2, 16, LEN), F32),
            pltpu.VMEM((8, D), F32),
            pltpu.VMEM((8, D), F32),
            pltpu.VMEM((1, FF), F32),
            pltpu.VMEM((4, LINES, 128), F32),
            pltpu.VMEM((4, 4, LINES, 128), F32),
            pltpu.VMEM((4, 8, 128), F32),
            pltpu.VMEM((4, 4, 8, 128), F32),
            pltpu.VMEM((16, 128), F32),
            pltpu.SemaphoreType.DMA((sems,)),
            pltpu.SemaphoreType.DMA((sems,)),
            pltpu.SemaphoreType.DMA((24,)),
        ],
        compiler_params=pltpu.CompilerParams(
            collective_id=1, has_side_effects=True, vmem_limit_bytes=62 << 20),
        name="backward_scatter",
    )(lengths, *small, *large)


def small_block(norm, head, ffn):
    wide = lambda v: jnp.pad(v, [(0, 0)] * (v.ndim - 1) + [(0, 128 - v.shape[-1])])
    block = jnp.concatenate([wide(norm), wide(head), wide(ffn)], axis=-2)
    return jnp.pad(block, [(0, 0)] * (block.ndim - 2) + [(0, 16 - block.shape[-2]), (0, 0)])


def pair_major(weight):
    count = weight.shape[0]
    return weight.reshape(count, 3, 3, 128).transpose(0, 2, 1, 3).reshape(count, QKV_HALF)


def gather_plain(weights, vectors):
    head, ffn, norm = vectors
    qkv, out, up, down = (w.astype(BF) for w in weights)
    full = []
    for shard in (small_block(norm, head, ffn), pair_major(qkv), out, up, down):
        full.append(lax.all_gather(lax.all_gather(shard, "dp", axis=0), "mp", axis=0))
    return full


def scatter_plain(fulls):
    out = []
    for full in fulls:
        own = lax.psum_scatter(full.astype(F32), "mp", scatter_dimension=0)
        out.append(lax.psum_scatter(own, "dp", scatter_dimension=0))
    return out


def body(
    tokens, cotangent, seg_lengths, w_qkv, w_out, w_up, w_down, head_bias, ffn_bias, norm_bias,
    qkv_rows, qkv_cols, out_rows, out_cols, up_rows, up_cols, down_rows, down_cols,
    head_bias_sq, ffn_bias_sq, norm_sq,
):
    cores = lax.axis_size("mp")
    data = lax.axis_size("dp")
    rows_qkv = w_qkv.shape[0]
    fast = data == 16 and cores == 2
    weights = [w_qkv.transpose(1, 0, 2) if fast else w_qkv, w_out, w_up, w_down]
    vectors = [head_bias, ffn_bias if fast else ffn_bias.reshape(1, -1), norm_bias]
    rows_out = w_out.shape[0]
    if fast:
        (weight_sums, norm_full, ffn_full, lse, scale_one, out_full, pooled, norm_sums, qkv_full,
         up_full, down_full, qkv, context_flip, token_flip, hidden_flip, normed_one, context,
         act_flip, slope, layer_out, grad_branch, grad_two
         ) = forward_gather(weights, vectors, seg_lengths, tokens, cotangent)
        rows_old = [qkv_rows, out_rows, up_rows, down_rows]
        cols_old = [qkv_cols, out_cols, up_cols, down_cols]
        old = [head_bias_sq, ffn_bias_sq, norm_sq]
        *reduced, lines, totals, input_grad = backward_scatter(
            seg_lengths, lse, norm_sums, norm_full, scale_one, out_full, rows_old, cols_old, old,
            weight_sums,
            [act_flip, grad_branch, down_full.reshape(FF, D), slope,
             up_full.reshape(2, D, FF // 2), grad_two, normed_one, hidden_flip, context,
             context_flip, token_flip, qkv, qkv_full.reshape(3, D, D)],
            [16, rows_qkv, rows_out, rows_qkv, w_down.shape[0]],
            [128, QKV_HALF, D, w_up.shape[1], D])
        new = step(reduced, lines, totals, weights, rows_old, cols_old, vectors, old,
                   [layer_out, pooled, input_grad])
        new = list(new)
        grads, small_grads, rows_new, cols_new = new[:4], new[4:7], new[7:11], new[11:15]
        seconds, mats, fresh, passed = new[15:18], new[18:22], new[22:25], new[25:]
        grads[0], mats[0] = grads[0].transpose(1, 0, 2), mats[0].transpose(1, 0, 2)
        stats = [v for pair in zip(rows_new, cols_new) for v in pair]
        return (*passed, *grads, *small_grads, *stats, *seconds, *mats, *fresh)
    small, qkv_g, out_g, up_g, down_g = gather_plain(weights, vectors)
    small = small.astype(BF).astype(F32)
    own_head, own_ffn, own_norm = head_bias.shape[1], ffn_bias.shape[0], norm_bias.shape[1]
    norm_full = small[:, :, 0:6, :own_norm].transpose(2, 1, 0, 3).reshape(6, D)
    head_full = small[:, :, 6:8, :own_head].transpose(2, 0, 1, 3).reshape(2, 2, 3, 1, 128)
    ffn_full = small[:, :, 8, :own_ffn].reshape(1, FF)
    offsets = jnp.concatenate([head_full[0], jnp.zeros_like(head_full[0]), head_full[1]], axis=2)
    offsets = offsets.reshape(2, 1, QKV_HALF)
    qkv_full = qkv_g.reshape(2, D, QKV_HALF)
    up_full = up_g.reshape(2, D, FF // 2)
    down_full = down_g.reshape(FF, D)
    out_full = out_g.reshape(D, D)
    norm_full = jnp.pad(norm_full, ((0, 2), (0, 0)))
    qkv, context, lse = forward(tokens, qkv_full, offsets, seg_lengths)
    (layer_out, pooled, hidden_b, act, grad_branch, grad_inner, grad_attended, grad_context,
     grad_one, delta, norm_sums, ffn_sums) = middle_call(
        tokens, context, cotangent, seg_lengths, out_full, up_full, down_full, ffn_full,
        norm_full)
    grad_out, grad_up, grad_down = weight_grads(
        context.T, hidden_b.T, act.T, grad_branch, grad_inner, grad_attended,
        cores * data, rows_out)
    token_flip = tokens.T
    grad_qkv, input_grad, grad_head = backward(
        token_flip, qkv, grad_context, lse, delta, seg_lengths, qkv_full, grad_one)
    small_grads = small_block(
        norm_sums[:6].reshape(6, data, cores, -1).transpose(2, 1, 0, 3),
        grad_head.reshape(2, cores, data, -1).transpose(1, 2, 0, 3),
        ffn_sums.reshape(cores, data, 1, -1),
    )
    fulls = [
        small_grads,
        grad_qkv.reshape(cores, data, rows_qkv, QKV_HALF),
        grad_out.reshape(cores, data, rows_out, D),
        grad_up.reshape(cores, data, rows_qkv, FF // 2),
        grad_down.reshape(cores, data, -1, D),
    ]
    red_small, red_qkv, red_out, red_up, red_down = scatter_plain(fulls)
    norm_grad = red_small[0:6, :own_norm]
    red_qkv = pair_major(red_qkv)
    red_head = red_small[6:8, :own_head]
    red_ffn = red_small[8, :own_ffn]
    weights_flat = [w_qkv.reshape(rows_qkv, -1), w_out, w_up, w_down]
    grads_flat = [red_qkv, red_out, red_up, red_down]
    rows_old = [qkv_rows, out_rows, up_rows, down_rows]
    cols_old = [qkv_cols.reshape(-1), out_cols, up_cols, down_cols]
    col_count = [3 * D, D, FF, D]
    row_count = [D, D, D, FF]
    row_share = [cores, 1, cores, 1]
    squares = [grad * grad + EPS_SQUARE for grad in grads_flat]
    row_parts = [jnp.sum(square, axis=1) for square in squares]
    col_parts = [jnp.sum(square, axis=0) for square in squares]
    vec_weights = [head_bias, ffn_bias, norm_bias]
    vec_grads = [red_head, red_ffn, norm_grad]
    vec_old = [head_bias_sq, ffn_bias_sq, norm_sq]
    vec_counts = [2 * D, FF, 6 * D]
    vec_second = [
        DECAY * old + (1.0 - DECAY) * (grad * grad + EPS_SQUARE)
        for old, grad in zip(vec_old, vec_grads)
    ]
    vec_update = [grad * lax.rsqrt(second) for grad, second in zip(vec_grads, vec_second)]
    weight_parts = [jnp.sum(weight * weight) for weight in weights_flat + vec_weights]
    vec_parts = [jnp.sum(update * update) for update in vec_update]
    row_qkv, row_up = lax.psum((row_parts[0], row_parts[2]), "mp")
    col_qkv, col_up = lax.psum((col_parts[0], col_parts[2]), "dp")
    col_out, col_down = lax.psum((col_parts[1], col_parts[3]), ("dp", "mp"))
    row_sums = [row_qkv, row_parts[1], row_up, row_parts[3]]
    col_sums = [col_qkv, col_out, col_up, col_down]
    rows_new = [
        DECAY * rows_old[index] + (1.0 - DECAY) * row_sums[index] / col_count[index]
        for index in range(4)
    ]
    cols_new = [
        DECAY * cols_old[index] + (1.0 - DECAY) * col_sums[index] / row_count[index]
        for index in range(4)
    ]
    ratio_parts = [
        jnp.sum(
            grads_flat[index]
            * grads_flat[index]
            / (rows_new[index][:, None] * cols_new[index][None, :])
        )
        for index in range(4)
    ]
    extra_parts = (
        [jnp.sum(rows_new[index]) / row_share[index] for index in range(4)]
        + weight_parts
        + vec_parts
    )
    totals = lax.psum(jnp.stack(ratio_parts + extra_parts), ("dp", "mp"))
    row_means = [totals[4 + index] / row_count[index] for index in range(4)]
    weight_totals = [totals[8 + index] for index in range(7)]
    vec_totals = [totals[15 + index] for index in range(3)]
    new_mats = []
    for index in range(4):
        entries = row_count[index] * col_count[index]
        estimate = rows_new[index][:, None] * cols_new[index][None, :] / row_means[index]
        update = grads_flat[index] / jnp.sqrt(estimate)
        update_rms = jnp.sqrt(row_means[index] * totals[index] / entries)
        stride = (
            RATE * jnp.sqrt(weight_totals[index] / entries) / jnp.maximum(1.0, update_rms / CLIP)
        )
        new_mats.append(weights_flat[index] - stride * update)
    new_vecs = []
    for index in range(3):
        update_rms = jnp.sqrt(vec_totals[index] / vec_counts[index])
        stride = (
            RATE
            * jnp.sqrt(weight_totals[4 + index] / vec_counts[index])
            / jnp.maximum(1.0, update_rms / CLIP)
        )
        new_vecs.append(vec_weights[index] - stride * vec_update[index])
    return (
        layer_out,
        pooled,
        input_grad,
        red_qkv.reshape(w_qkv.shape),
        red_out,
        red_up,
        red_down,
        red_head,
        red_ffn,
        norm_grad,
        rows_new[0],
        cols_new[0].reshape(qkv_cols.shape),
        rows_new[1],
        cols_new[1],
        rows_new[2],
        cols_new[2],
        rows_new[3],
        cols_new[3],
        vec_second[0],
        vec_second[1],
        vec_second[2],
        new_mats[0].reshape(w_qkv.shape),
        new_mats[1],
        new_mats[2],
        new_mats[3],
        new_vecs[0],
        new_vecs[1],
        new_vecs[2],
    )


def solution(mesh):
    return jax.shard_map(
        body,
        mesh=mesh,
        in_specs=(
            P(("dp", "mp"), None),
            P(("dp", "mp"), None),
            P("dp", None),
            P("dp", None, "mp"),
            P(("mp", "dp"), None),
            P("dp", "mp"),
            P(("mp", "dp"), None),
            P(None, ("mp", "dp")),
            P(("mp", "dp")),
            P(None, ("dp", "mp")),
            P("dp"),
            P(None, "mp"),
            P(("mp", "dp")),
            P(),
            P("dp"),
            P("mp"),
            P(("mp", "dp")),
            P(),
            P(None, ("mp", "dp")),
            P(("mp", "dp")),
            P(None, ("dp", "mp")),
        ),
        out_specs=(
            P(("dp", "mp"), None),
            P(("dp", "mp"), None, None),
            P(("dp", "mp"), None),
            P("dp", None, "mp"),
            P(("mp", "dp"), None),
            P("dp", "mp"),
            P(("mp", "dp"), None),
            P(None, ("mp", "dp")),
            P(("mp", "dp")),
            P(None, ("dp", "mp")),
            P("dp"),
            P(None, "mp"),
            P(("mp", "dp")),
            P(),
            P("dp"),
            P("mp"),
            P(("mp", "dp")),
            P(),
            P(None, ("mp", "dp")),
            P(("mp", "dp")),
            P(None, ("dp", "mp")),
            P("dp", None, "mp"),
            P(("mp", "dp"), None),
            P("dp", "mp"),
            P(("mp", "dp"), None),
            P(None, ("mp", "dp")),
            P(("mp", "dp")),
            P(None, ("dp", "mp")),
        ),
        check_vma=False,
    )
```

```python
import functools

import jax
import jax.numpy as jnp
from jax import lax
from jax.experimental import pallas as pl
from jax.experimental.pallas import tpu as pltpu
from jax.sharding import PartitionSpec as P

D = 768
HD = 64
FF = 3072
LEN = 512
SEGS = 8

EPS_NORM = 1e-12
EPS_SQUARE = 1e-30
DECAY = 0.5
RATE = 3.0
CLIP = 0.3

MESH = pl.DeviceIdType.MESH
BF = jnp.bfloat16
F32 = jnp.float32
EVERY = slice(None)


PLANE = [(m, y, x) for m in range(2) for y in range(2) for x in range(2)][1:]


class Place:
    def __init__(self):
        d = lax.axis_index("dp")
        self.m = lax.axis_index("mp")
        self.z, self.y, self.x = d // 4, (d // 2) % 2, d % 2

    def at(self, axis, step):
        size = 4 if axis == "z" else 2
        spot = {"z": self.z, "y": self.y, "x": self.x, "m": self.m}
        spot[axis] = (spot[axis] + step) % size
        return spot

    def across(self, steps):
        m, y, x = steps
        return {"z": self.z, "m": (self.m + m) % 2, "y": (self.y + y) % 2, "x": (self.x + x) % 2}

    @staticmethod
    def device(spot):
        return (spot["z"] * 4 + spot["y"] * 2 + spot["x"], spot["m"])


def steps_of(axis):
    return (1, 2, 3) if axis == "z" else (1,)


def near(place, wide):
    spots = [place.at("z", step) for step in (1, 2, 3)]
    for steps in PLANE:
        if wide or sum(steps) == 1:
            spots.append(place.across(steps))
    return [place.device(spot) for spot in spots]


def greet(place, wide=False):
    barrier = pltpu.get_barrier_semaphore()
    for device in near(place, wide):
        pl.semaphore_signal(barrier, inc=1, device_id=device, device_id_type=MESH)


def meet(place, wide=False):
    pl.semaphore_wait(pltpu.get_barrier_semaphore(), len(near(place, wide)))


def weight_sums_of(weights, small):
    parts = []
    for weight in weights:
        value = weight[...]
        if value.ndim == 3:
            parts.append(sum(all_sum(value[part] * value[part]) for part in range(3)))
        else:
            parts.append(all_sum(value * value))
    return scalars([jnp.zeros((1, 1), F32)] * 11 + parts + small_sums(small))


def as_row(ref):
    value = ref[...]
    return value.reshape(1, value.shape[0]) if value.ndim == 1 else value


def to_column(row):
    count = row.shape[1]
    here = lax.broadcasted_iota(jnp.int32, (count, count), 0)
    there = lax.broadcasted_iota(jnp.int32, (count, count), 1)
    return jnp.sum(jnp.where(here == there, row, 0.0), axis=1, keepdims=True)


def to_row(column):
    count = column.shape[0]
    here = lax.broadcasted_iota(jnp.int32, (count, count), 0)
    there = lax.broadcasted_iota(jnp.int32, (count, count), 1)
    return jnp.sum(jnp.where(here == there, column, 0.0), axis=0, keepdims=True)


def put_line(ref, line, row):
    for tile in range(row.shape[1] // 128):
        ref[line + tile:line + tile + 1, :] = row[:, tile * 128:(tile + 1) * 128]


def get_line(ref, line, width):
    tiles = width // 128
    return jnp.concatenate([ref[line + t:line + t + 1, :] for t in range(tiles)], axis=1)


def scalars(values):
    lane = lax.broadcasted_iota(jnp.int32, (8, 128), 1)
    out = jnp.zeros((8, 128), F32)
    for index, value in enumerate(values):
        out = jnp.where(lane == index, value, out)
    return out


def all_sum(values):
    return jnp.sum(jnp.sum(values, axis=1, keepdims=True), axis=0, keepdims=True)


class Exchange:
    COUNT = 10

    def __init__(self, place, mine, plane, line, sems, base):
        self.place, self.mine, self.plane, self.line = place, mine, plane, line
        self.sems, self.base = sems, base

    def plane_copies(self):
        place = self.place
        send, recv = self.sems
        out = []
        for number, steps in enumerate(PLANE):
            spot = place.across(steps)
            slot = self.base + number
            device = place.device(spot)
            sent, arrives = (
                pltpu.make_async_remote_copy(
                    self.mine.at[0], self.plane.at[at["m"], at["y"], at["x"]],
                    send.at[slot], recv.at[slot], device_id=device, device_id_type=MESH)
                for at in ({"m": place.m, "y": place.y, "x": place.x}, spot))
            out.append((sent, arrives))
        return out

    def line_copies(self):
        place = self.place
        send, recv = self.sems
        out = []
        for step in (1, 2, 3):
            slot = self.base + 6 + step
            device = place.device(place.at("z", step))
            sent, arrives = (
                pltpu.make_async_remote_copy(
                    self.mine.at[1], self.line.at[layer], send.at[slot], recv.at[slot],
                    device_id=device, device_id_type=MESH)
                for layer in (place.z, place.at("z", -step)["z"]))
            out.append((sent, arrives))
        return out

    def start_plane(self, value):
        place = self.place
        self.mine[0] = value
        for sent, _ in self.plane_copies():
            sent.start()
        self.plane[place.m, place.y, place.x] = value

    def end_plane(self):
        plane, core = self.plane, self.place.m
        for _, arrives in self.plane_copies():
            arrives.wait_recv()
        return [(plane[c, 0, 0] + plane[c, 0, 1]) + (plane[c, 1, 0] + plane[c, 1, 1])
                for c in (core, 1 - core)]

    def start_line(self, value):
        self.mine[1] = value
        for sent, _ in self.line_copies():
            sent.start()
        self.line[self.place.z] = value

    def end_line(self):
        line = self.line
        for _, arrives in self.line_copies():
            arrives.wait_recv()
        return (line[0] + line[1]) + (line[2] + line[3])

    def finish(self):
        for sent, _ in self.plane_copies() + self.line_copies():
            sent.wait_send()


QKV_LINE, QKV_ROWS, UP_LINE, OUT_LINE, DOWN_LINE, UP_ROWS = 0, 9, 16, 28, 34, 40
LATE, LINES = 16, 48
WIDTHS = (3 * D // 2, D, FF // 2, D)
COL_LINES = (QKV_LINE, OUT_LINE, UP_LINE, DOWN_LINE)
COL_COUNT = (3 * D, D, FF, D)
ROW_COUNT = (D, D, D, FF)


def pair_cuts():
    out = []
    for pair in range(3):
        for part in range(3):
            start = (pair * 3 + part) * 128
            out.append(((slice(part, part + 1), slice(pair * 128, (pair + 1) * 128)),
                        slice(start, start + 128)))
    return out


def new_rows_cols(grads, rows_old, cols_old, lines, which=range(4)):
    rows_new, cols_new = [], []
    for index in which:
        if index in (0, 2):
            line = UP_ROWS if index else QKV_ROWS
            count = rows_old[index].shape[0]
            row_sum = to_column(lines[line:line + 1, :count])
        else:
            grad = grads[index][...]
            row_sum = jnp.sum(grad * grad + EPS_SQUARE, axis=1, keepdims=True)
        rows_new.append(
            DECAY * to_column(as_row(rows_old[index])) + (1.0 - DECAY) * row_sum / COL_COUNT[index])
        col_sum = get_line(lines, COL_LINES[index], WIDTHS[index])
        if index == 0:
            old = jnp.concatenate([cols_old[0][at] for at, _ in pair_cuts()], axis=1)
        else:
            old = as_row(cols_old[index])
        cols_new.append(DECAY * old + (1.0 - DECAY) * col_sum / ROW_COUNT[index])
    return rows_new, cols_new


def place_small(ref, norm, head, ffn, fill):
    ref[...] = jnp.full(ref.shape, fill, F32)
    ref[0:6, 0:norm.shape[1]] = norm
    ref[6:8, 0:head.shape[1]] = head
    ref[8:9, 0:ffn.shape[1]] = ffn


def small_update(grad, old):
    second = DECAY * old + (1.0 - DECAY) * (grad * grad + EPS_SQUARE)
    return second, grad * lax.rsqrt(second)


def small_sums(values):
    line = lax.broadcasted_iota(jnp.int32, values.shape, 0)
    square = values * values
    return [
        all_sum(jnp.where((line >= 6) & (line < 8), square, 0.0)),
        all_sum(jnp.where(line == 8, square, 0.0)),
        all_sum(jnp.where(line < 6, square, 0.0)),
    ]


def step_kernel(*refs):
    refs = list(refs)
    take = lambda number: [refs.pop(0) for _ in range(number)]
    grads_any, weights_any = take(4), take(4)
    passed = take(3)
    small, lines, totals = take(3)
    rows_old, cols_old = take(4), take(4)
    head, ffn, norm, head_sq, ffn_sq, norm_sq = take(6)
    grads_out = take(4)
    head_grad, ffn_grad, norm_grad = take(3)
    rows_out, cols_out = take(4), take(4)
    head_second, ffn_second, norm_second = take(3)
    weights_out = take(4)
    head_new, ffn_new, norm_new = take(3)
    passed_out = take(3)
    grads, weights = take(4), take(4)
    old_small, weight_small, sems = refs
    loads = []
    for number, (source, target) in enumerate(
            zip(grads_any + weights_any + passed, grads + weights + passed_out)):
        copy = pltpu.make_async_copy(source, target, sems.at[number])
        copy.start()
        loads.append(copy)
    place_small(old_small, norm_sq[...], head_sq[...], as_row(ffn_sq), 1.0)
    place_small(weight_small, norm[...], head[...], as_row(ffn), 0.0)
    for copy in loads[:4]:
        copy.wait()
    rows_new, cols_new = new_rows_cols(grads, rows_old, cols_old, lines)
    total = lambda lane: totals[0:1, lane:lane + 1]
    for index in range(4):
        rows_out[index][...] = to_row(rows_new[index]).reshape(rows_out[index].shape)
        if index == 0:
            for at, cut in pair_cuts():
                cols_out[0][at] = cols_new[0][:, cut]
        else:
            cols_out[index][...] = cols_new[index].reshape(cols_out[index].shape)
        entries = ROW_COUNT[index] * COL_COUNT[index]
        row_mean = total(4 + index) / ROW_COUNT[index]
        update_rms = jnp.sqrt(row_mean * total(index) / entries)
        stride = (
            RATE * jnp.sqrt(total(11 + index) / entries) / jnp.maximum(1.0, update_rms / CLIP))
        scale_rows = lax.rsqrt(rows_new[index] / row_mean) * stride
        scale_cols = lax.rsqrt(cols_new[index])
        loads[4 + index].wait()
        if index == 0:
            for (part, cols), cut in pair_cuts():
                at = (part.start, EVERY, cols)
                grad = grads[0][:, cut]
                grads_out[0][at] = grad
                weights_out[0][at] = weights[0][at] - grad * scale_rows * scale_cols[:, cut]
        else:
            grad = grads[index][...]
            grads_out[index][...] = grad
            weights_out[index][...] = weights[index][...] - grad * scale_rows * scale_cols
    grad = small[...]
    second, update = small_update(grad, old_small[...])
    line = lax.broadcasted_iota(jnp.int32, grad.shape, 0)
    counts = (2 * D, FF, 6 * D)
    strides = []
    for index in range(3):
        update_rms = jnp.sqrt(total(8 + index) / counts[index])
        strides.append(
            RATE * jnp.sqrt(total(15 + index) / counts[index])
            / jnp.maximum(1.0, update_rms / CLIP))
    stride = jnp.where(line < 6, strides[2], jnp.where(line < 8, strides[0], strides[1]))
    fresh = weight_small[...] - stride * update
    for values, (norm_ref, head_ref, ffn_ref) in (
        (grad, (norm_grad, head_grad, ffn_grad)),
        (second, (norm_second, head_second, ffn_second)),
        (fresh, (norm_new, head_new, ffn_new)),
    ):
        norm_ref[...] = values[0:6, 0:norm_ref.shape[1]]
        head_ref[...] = values[6:8, 0:head_ref.shape[1]]
        ffn_ref[...] = values[8:9, 0:ffn_ref.shape[0]].reshape(ffn_ref.shape)
    for copy in loads[8:]:
        copy.wait()


def step(reduced, lines, totals, weights, rows_old, cols_old, vectors, squares, passed):
    vmem, some = pl.BlockSpec(memory_space=pltpu.VMEM), pl.BlockSpec(memory_space=pl.ANY)
    small, grads = reduced[0], reduced[1:]
    shapes = [w.shape for w in weights] + [v.shape for v in vectors]
    shapes += [r.shape for r in rows_old] + [c.shape for c in cols_old]
    shapes += [v.shape for v in vectors] + [w.shape for w in weights] + [v.shape for v in vectors]
    outs = [jax.ShapeDtypeStruct(s, F32) for s in shapes]
    large = [*grads, *weights, *passed]
    operands = [small, lines, totals, *rows_old, *cols_old, *vectors, *squares]
    return pl.pallas_call(
        step_kernel,
        out_shape=outs + [jax.ShapeDtypeStruct(v.shape, v.dtype) for v in passed],
        in_specs=[some] * len(large) + [vmem] * len(operands),
        out_specs=[vmem] * (len(shapes) + len(passed)),
        scratch_shapes=[pltpu.VMEM(v.shape, F32) for v in [*grads, *weights]] + [
            pltpu.VMEM((16, 128), F32), pltpu.VMEM((16, 128), F32),
            pltpu.SemaphoreType.DMA((11,)),
        ],
        compiler_params=pltpu.CompilerParams(vmem_limit_bytes=60 << 20),
        name="adafactor_step",
    )(*large, *operands)


HALF = D // 2
QKV_HALF = 3 * HALF
VMEM = pl.BlockSpec(memory_space=pltpu.VMEM)
SMEM = pl.BlockSpec(memory_space=pltpu.SMEM)


def dot(a, b):
    return jnp.dot(a, b, preferred_element_type=F32)


def dot_last(a, b):
    return lax.dot_general(a, b, (((1,), (1,)), ((), ())), preferred_element_type=F32)


def dot_first(a, b):
    return lax.dot_general(a, b, (((0,), (0,)), ((), ())), preferred_element_type=F32)


def ids_at(lengths, row, places):
    bound = jnp.int32(0)
    ids = jnp.zeros(places.shape, jnp.int32)
    for segment in range(SEGS):
        bound = bound + lengths[row, segment]
        ids = ids + (places >= bound).astype(jnp.int32)
    return ids


def set_bias(bias, lengths, row):
    down = ids_at(lengths, row, lax.broadcasted_iota(jnp.int32, (LEN, 1), 0))
    across = ids_at(lengths, row, lax.broadcasted_iota(jnp.int32, (1, LEN), 1))
    bias[...] = jnp.where(down == across, 0.0, -1e30)


def half_masks():
    lane = lax.broadcasted_iota(jnp.int32, (1, 128), 1)
    return [((lane // HD) == half).astype(F32).astype(BF) for half in range(2)]


PAIR = 3 * 128


def slab(ref, core, row, part, pair):
    return ref[core, pl.ds(pl.multiple_of(row * LEN, LEN), LEN),
               pl.ds(pl.multiple_of(pair * PAIR + part * 128, 128), 128)]


def project(tokens, weight, offsets, qkv, row):
    rows = pl.ds(pl.multiple_of(row * LEN, LEN), LEN)
    values = tokens[rows, :]
    for core in range(2):
        for pair in range(3):
            cut = slice(pair * PAIR, (pair + 1) * PAIR)
            out = (dot(values, weight[core, :, cut]) + offsets[core, :, cut]).astype(BF)
            scale = jnp.where(
                lax.broadcasted_iota(jnp.int32, (1, PAIR), 1) < 128, HD ** -0.5, 1.0).astype(BF)
            qkv[core, rows, cut] = out * scale


def attend(qkv, bias, context, lse, held, row):
    rows = pl.ds(pl.multiple_of(row * LEN, LEN), LEN)
    lane = lax.broadcasted_iota(jnp.int32, (LEN, 128), 1)
    held[...] = jnp.zeros(held.shape, F32)

    @pl.loop(0, 6)
    def _(item):
        core, pair = item // 3, item % 3
        queries, keys, values = (slab(qkv, core, row, part, pair) for part in range(3))
        wide = jnp.concatenate([values, jnp.ones_like(values)], axis=1)
        outs = []
        logs = held[...]
        for half, mask in enumerate(half_masks()):
            scores = dot_last(queries * mask, keys) + bias[...]
            peak = jnp.max(scores, axis=1, keepdims=True)
            raised = jnp.exp(scores - peak).astype(BF)
            both = dot(raised, wide)
            total = both[:, 128:]
            outs.append(both[:, :128] / total)
            logs = jnp.where(lane == item * 2 + half, peak + jnp.log(total), logs)
        held[...] = logs
        context[rows, pl.ds(pl.multiple_of(item * 128, 128), 128)] = jnp.where(
            lane < HD, outs[0], outs[1]).astype(BF)

    lse[row] = held[...].T[0:16, :]


def forward_kernel(tokens, weight, offsets, lengths, qkv, context, lse, bias, held):
    core = lax.axis_index("mp")

    @pl.loop(0, 2)
    def _(row):
        set_bias(bias, lengths, core * 2 + row)
        project(tokens, weight, offsets, qkv, row)
        attend(qkv, bias, context, lse, held, row)


def forward(tokens, weight, offsets, lengths):
    count = tokens.shape[0]
    return pl.pallas_call(
        forward_kernel,
        out_shape=[
            jax.ShapeDtypeStruct((2, count, QKV_HALF), BF),
            jax.ShapeDtypeStruct((count, D), BF),
            jax.ShapeDtypeStruct((count // LEN, 16, LEN), F32),
        ],
        in_specs=[VMEM, VMEM, VMEM, SMEM],
        out_specs=[VMEM] * 3,
        scratch_shapes=[pltpu.VMEM((LEN, LEN), F32), pltpu.VMEM((LEN, 128), F32)],
        compiler_params=pltpu.CompilerParams(vmem_limit_bytes=56 << 20),
        name="project_attend",
    )(tokens, weight, offsets, lengths)


def gelu_both(inner):
    cdf = 0.5 * (1.0 + lax.erf(inner * 0.7071067811865476))
    density = 0.3989422804014327 * jnp.exp(-0.5 * inner * inner)
    return inner * cdf, cdf + inner * density


def norm_parts(values):
    center = values - jnp.mean(values, axis=-1, keepdims=True)
    scale = lax.rsqrt(jnp.mean(center * center, axis=-1, keepdims=True) + EPS_NORM)
    return center * scale, scale


def norm_back(grad, normed, scale, gain):
    scaled = grad * gain
    mean = jnp.mean(scaled, axis=-1, keepdims=True)
    along = jnp.mean(scaled * normed, axis=-1, keepdims=True)
    return (
        (scaled - mean - normed * along) * scale,
        jnp.sum(grad * normed, axis=0, keepdims=True),
        jnp.sum(grad, axis=0, keepdims=True),
    )


CHUNK = 512


def middle(row, core, tokens, context, cotangent, lengths, w_out, w_up, w_down, ffn, norm, layer_out,
           pooled, hidden_b, act, grad_branch, grad_inner, grad_attended, grad_context,
           grad_one, delta, norm_sums, ffn_sums, slope, branch, hidden, normed_one, grad_two):
    rows = pl.ds(pl.multiple_of(row * LEN, LEN), LEN)
    attended = dot(context[rows, :], w_out[...]) + norm[0:1, :]
    normed, scale_one = norm_parts(tokens[rows, :].astype(F32) + attended)
    normed_one[...] = normed
    value = normed * norm[2:3, :] + norm[3:4, :]
    hidden[...] = value
    hidden_b[rows, :] = value.astype(BF)
    branch[...] = jnp.zeros(branch.shape, F32)
    for chunk in range(FF // CHUNK):
        core_of, start = chunk * CHUNK // (FF // 2), chunk * CHUNK % (FF // 2)
        cols = slice(chunk * CHUNK, (chunk + 1) * CHUNK)
        up = w_up[core_of, :, start:start + CHUNK]
        value, slope_value = gelu_both(dot(hidden_b[rows, :], up) + ffn[:, cols])
        value = value.astype(BF)
        act[rows, cols] = value
        slope[:, cols] = slope_value.astype(BF)
        branch[...] += dot(value, w_down[cols, :])
    normed, scale = norm_parts(hidden[...] + branch[...] + norm[1:2, :])
    output = normed * norm[4:5, :] + norm[5:6, :]
    high = output.astype(BF)
    layer_out[rows, :] = high
    low = (output - high.astype(F32)).astype(BF)
    place = lax.broadcasted_iota(jnp.int32, (SEGS, LEN), 1)
    segment = lax.broadcasted_iota(jnp.int32, (SEGS, 1), 0)
    ids = ids_at(lengths, core * 2 + row, place)
    member = (ids == segment).astype(F32)
    sizes = jnp.sum(member, axis=1, keepdims=True)
    member = member.astype(BF)
    pooled[row] = (dot(member, high) + dot(member, low)) / sizes
    back, gain, shift = norm_back(cotangent[rows, :].astype(F32), normed, scale, norm[4:5, :])
    norm_sums[4:5, :] += gain
    norm_sums[5:6, :] += shift
    grad_two[...] = back
    back = back.astype(BF)
    grad_branch[rows, :] = back
    norm_sums[1:2, :] += jnp.sum(back.astype(F32), axis=0, keepdims=True)
    for chunk in range(FF // CHUNK):
        core_of, start = chunk * CHUNK // (FF // 2), chunk * CHUNK % (FF // 2)
        cols = slice(chunk * CHUNK, (chunk + 1) * CHUNK)
        value = dot_last(grad_branch[rows, :], w_down[cols, :])
        value = (value * slope[:, cols].astype(F32)).astype(BF)
        grad_inner[rows, cols] = value
        ffn_sums[:, cols] += jnp.sum(value.astype(F32), axis=0, keepdims=True)
        grad_two[...] += dot_last(value, w_up[core_of, :, start:start + CHUNK])
    back, gain, shift = norm_back(grad_two[...], normed_one[...], scale_one, norm[2:3, :])
    norm_sums[2:3, :] += gain
    norm_sums[3:4, :] += shift
    grad_one[rows, :] = back
    back = back.astype(BF)
    grad_attended[rows, :] = back
    norm_sums[0:1, :] += jnp.sum(back.astype(F32), axis=0, keepdims=True)
    back = dot_last(back, w_out[...]).astype(BF)
    grad_context[rows, :] = back
    product = back.astype(F32) * context[rows, :].astype(F32)
    high = product.astype(BF)
    low = (product - high.astype(F32)).astype(BF)
    head = lax.broadcasted_iota(jnp.int32, (16, D), 0)
    member = (lax.broadcasted_iota(jnp.int32, (16, D), 1) // HD == head).astype(F32).astype(BF)
    delta[row] = dot_last(member, high) + dot_last(member, low)


def middle_kernel(*refs):
    core = lax.axis_index("mp")
    norm_sums, ffn_sums = refs[19], refs[20]
    norm_sums[...] = jnp.zeros(norm_sums.shape, F32)
    ffn_sums[...] = jnp.zeros(ffn_sums.shape, F32)

    @pl.loop(0, 2)
    def _(row):
        middle(row, core, *refs)


def middle_call(tokens, context, cotangent, lengths, w_out, w_up, w_down, ffn, norm):
    count = tokens.shape[0]
    shape = jax.ShapeDtypeStruct
    return pl.pallas_call(
        middle_kernel,
        out_shape=[
            shape((count, D), BF),
            shape((count // LEN, SEGS, D), F32),
            shape((count, D), BF),
            shape((count, FF), BF),
            shape((count, D), BF),
            shape((count, FF), BF),
            shape((count, D), BF),
            shape((count, D), BF),
            shape((count, D), F32),
            shape((count // LEN, 16, LEN), F32),
            shape((8, D), F32),
            shape((1, FF), F32),
        ],
        in_specs=[VMEM] * 3 + [SMEM] + [VMEM] * 5,
        out_specs=[VMEM] * 12,
        scratch_shapes=[
            pltpu.VMEM((LEN, FF), BF),
            pltpu.VMEM((LEN, D), F32),
            pltpu.VMEM((LEN, D), F32),
            pltpu.VMEM((LEN, D), F32),
            pltpu.VMEM((LEN, D), F32),
        ],
        compiler_params=pltpu.CompilerParams(vmem_limit_bytes=60 << 20),
        name="feed_forward",
    )(tokens, context, cotangent, lengths, w_out, w_up, w_down, ffn, norm)


def weight_grads_kernel(context, hidden_b, act, grad_branch, grad_inner, grad_attended,
                        out_grad, up_grad, down_grad):

    @pl.loop(0, FF // CHUNK)
    def _(chunk):
        half_chunks = FF // 2 // CHUNK
        cols = pl.ds(pl.multiple_of(chunk * CHUNK, CHUNK), CHUNK)
        local = pl.ds(pl.multiple_of((chunk % half_chunks) * CHUNK, CHUNK), CHUNK)
        up_grad[chunk // half_chunks, :, local] = dot(hidden_b[...], grad_inner[:, cols]).astype(BF)
        down_grad[cols, :] = dot(act[cols, :], grad_branch[...]).astype(BF)

    value = dot(context[...], grad_attended[...])
    rows, held = D // out_grad.shape[0], out_grad.shape[1]
    for block in range(out_grad.shape[0]):
        piece = value[block * rows:(block + 1) * rows, :]
        if held > rows:
            piece = jnp.concatenate([piece, jnp.zeros((held - rows, D), F32)], axis=0)
        out_grad[block] = piece.astype(BF)


def weight_grads(context, hidden_b, act, grad_branch, grad_inner, grad_attended, blocks, held):
    shape = jax.ShapeDtypeStruct
    return pl.pallas_call(
        weight_grads_kernel,
        out_shape=[shape((blocks, held, D), BF), shape((2, D, FF // 2), BF), shape((FF, D), BF)],
        in_specs=[VMEM] * 6,
        out_specs=[VMEM] * 3,
        compiler_params=pltpu.CompilerParams(vmem_limit_bytes=60 << 20),
        name="weight_grads",
    )(context, hidden_b, act, grad_branch, grad_inner, grad_attended)


def attend_back(qkv, grad_context, lse, delta, bias, grad_qkv, grad_head, row):
    rows = pl.ds(pl.multiple_of(row * LEN, LEN), LEN)
    lane = lax.broadcasted_iota(jnp.int32, (LEN, 128), 1)

    @pl.loop(0, 6)
    def _(item):
        core, pair = item // 3, item % 3
        queries, keys, values = (slab(qkv, core, row, part, pair) for part in range(3))
        wide = pl.ds(pl.multiple_of(item * 128, 128), 128)
        grad = grad_context[rows, wide]
        flipped = keys.T
        grads_k, grads_v, grads_q = [], [], []
        for half, mask in enumerate(half_masks()):
            head = item * 2 + half
            scores = dot_last(keys * mask, queries) + bias[...] - lse[row, pl.ds(head, 1), :]
            probs = jnp.exp(scores)
            grad_probs = dot_last(values * mask, grad)
            grad_scores = (probs * (grad_probs - delta[row, pl.ds(head, 1), :])).astype(BF)
            grads_v.append(dot(probs.astype(BF), grad))
            grads_k.append(dot(grad_scores, queries))
            grads_q.append(dot(flipped[half * HD:(half + 1) * HD, :], grad_scores))
        grad_q = (jnp.concatenate(grads_q, axis=0).T * HD ** -0.5).astype(BF)
        grad_k = jnp.where(lane < HD, grads_k[0], grads_k[1]).astype(BF)
        grad_v = jnp.where(lane < HD, grads_v[0], grads_v[1]).astype(BF)
        for part, value in enumerate((grad_q, grad_k, grad_v)):
            grad_qkv[core, rows, pl.ds(pl.multiple_of(pair * PAIR + part * 128, 128), 128)] = value
        grad_head[0:1, wide] += jnp.sum(grad_q.astype(F32), axis=0, keepdims=True)
        grad_head[1:2, wide] += jnp.sum(grad_v.astype(F32), axis=0, keepdims=True)


def backward_kernel(tokens, qkv, grad_context, lse, delta, lengths, weight, grad_one,
                    qkv_grad, input_grad, grad_head, grad_qkv, bias):
    core = lax.axis_index("mp")
    grad_head[...] = jnp.zeros(grad_head.shape, F32)

    @pl.loop(0, 2)
    def _(row):
        set_bias(bias, lengths, core * 2 + row)
        attend_back(qkv, grad_context, lse, delta, bias, grad_qkv, grad_head, row)
        rows = pl.ds(pl.multiple_of(row * LEN, LEN), LEN)
        input_grad[rows, :] = (
            grad_one[rows, :]
            + dot_last(grad_qkv[0, rows, :], weight[0])
            + dot_last(grad_qkv[1, rows, :], weight[1])
        )

    for core_of in range(2):
        for part in range(3):
            cut = slice(part * HALF, (part + 1) * HALF)
            qkv_grad[core_of, :, cut] = dot(tokens[...], grad_qkv[core_of, :, cut]).astype(BF)


def backward(tokens, qkv, grad_context, lse, delta, lengths, weight, grad_one):
    count = tokens.shape[1]
    shape = jax.ShapeDtypeStruct
    return pl.pallas_call(
        backward_kernel,
        out_shape=[shape((2, D, QKV_HALF), BF), shape((count, D), F32), shape((2, D), F32)],
        in_specs=[VMEM] * 5 + [SMEM] + [VMEM] * 2,
        out_specs=[VMEM] * 3,
        scratch_shapes=[
            pltpu.VMEM((2, count, QKV_HALF), BF),
            pltpu.VMEM((LEN, LEN), F32),
        ],
        compiler_params=pltpu.CompilerParams(vmem_limit_bytes=60 << 20),
        name="attend_back",
    )(tokens, qkv, grad_context, lse, delta, lengths, weight, grad_one)


UP_CHUNK = 512
DOWN_CHUNK = 256


class Spread:
    def __init__(self, place, full, start, width, flip, orders, sems, base):
        self.place, self.full = place, full
        self.cols = pl.ds(start, width)
        tiles = width // 128
        cut = (tiles // 2 if flip else tiles - tiles // 2) * 128
        self.halves = [(orders[0], pl.ds(start, cut))]
        if cut < width:
            self.halves.append((orders[1], pl.ds(start + cut, width - cut)))
        self.sems, self.base, self.slots = sems, base, {}
        self.count = sum(len(self.copies(stage)) for stage in range(4))

    def view(self, spot, cols):
        return self.full.at[spot["m"], spot["z"], spot["y"], spot["x"], :, cols]

    def copy(self, key, axis, step, spot, cols):
        place = self.place
        slot = self.base + self.slots.setdefault(key, len(self.slots))
        send, recv = self.sems
        send, recv = send.at[slot], recv.at[slot]
        device = place.device(place.at(axis, step))
        view = self.view(spot, cols)
        sent = pltpu.make_async_remote_copy(
            view, view, send, recv, device_id=device, device_id_type=MESH)
        land = dict(spot)
        land[axis] = place.at(axis, -step)[axis]
        land = self.view(land, cols)
        arrives = pltpu.make_async_remote_copy(
            land, land, send, recv, device_id=device, device_id_type=MESH)
        return sent, arrives

    def copies(self, stage):
        place = self.place
        here = {"z": place.z, "y": place.y, "x": place.x, "m": place.m}
        if stage == 3:
            here["z"] = here["y"] = here["x"] = EVERY
            return [self.copy((3, 0, 1), "m", 1, here, self.cols)]
        halves = self.halves
        if stage == 0 and halves[0][0][0] == "z":
            halves = [(halves[0][0], self.cols)]
        out = []
        for number, (order, cols) in enumerate(halves):
            spot = dict(here)
            for axis in order[:stage]:
                spot[axis] = EVERY
            for step in steps_of(order[stage]):
                out.append(self.copy((stage, number, step), order[stage], step, spot, cols))
        return out

    def start(self, stage):
        for sent, _ in self.copies(stage):
            sent.start()

    def arrived(self, stage):
        for _, arrives in self.copies(stage):
            arrives.wait_recv()

    def finish(self):
        for stage in range(4):
            for sent, _ in self.copies(stage):
                sent.wait_send()


def spread(groups, *moves):
    for group, stage in moves:
        for chunk in groups[group]:
            if stage:
                chunk.arrived(stage - 1)
            chunk.start(stage)


def unpack_small(small, norm_out, offsets, ffn_out):
    iota = lambda shape, axis: lax.broadcasted_iota(jnp.int32, shape, axis)
    pick = ((iota((128, D), 1) % 24 == iota((128, D), 0))).astype(F32).astype(BF)
    pick_ffn = ((iota((128, FF), 1) % 96 == iota((128, FF), 0))).astype(F32).astype(BF)
    total = jnp.zeros((16, D), F32)
    ffn = jnp.zeros((1, FF), F32)
    line, col = iota((256, D), 0), iota((256, D), 1) // 24
    device, kind = line // 16, line % 16
    for core in range(2):
        block = small[core].reshape(256, 128).astype(BF)
        wide = dot(block, pick)
        right = jnp.where(kind < 6, 2 * device + core, 16 * core + device)
        wide = jnp.where((col == right) & (kind < 8), wide, 0.0)
        total = total + jnp.sum(wide.reshape(16, 16, D), axis=0)
        wide = dot(small[core, :, :, :, 8, :].reshape(16, 128).astype(BF), pick_ffn)
        right = iota((16, FF), 1) // 96 == iota((16, FF), 0) + 16 * core
        ffn = ffn + jnp.sum(jnp.where(right, wide, 0.0), axis=0, keepdims=True)
    norm_out[0:6, :] = total[0:6, :]
    norm_out[6:8, :] = jnp.zeros((2, D), F32)
    ffn_out[...] = ffn
    offsets[...] = jnp.zeros(offsets.shape, F32)
    for core in range(2):
        for pair in range(3):
            source = core * HALF + pair * 128
            for part, row in ((0, 6), (2, 7)):
                start = pair * PAIR + part * 128
                offsets[core, :, start:start + 128] = total[row:row + 1, source:source + 128]


def place_of(core, part, width):
    return pl.ds(pl.multiple_of(core * PAIR + part * 128, 128), width)


def trio(ref, core, row, part, pair):
    return ref[pair, pl.ds(pl.multiple_of(row * LEN, LEN), LEN), place_of(core, part, 128)]


def project_pair(tokens, weight, offsets, qkv, pair):
    cols = pl.ds(pl.multiple_of(pair * PAIR, PAIR), PAIR)
    scale = jnp.where(
        lax.broadcasted_iota(jnp.int32, (1, PAIR), 1) < 128, HD ** -0.5, 1.0).astype(BF)
    for core in range(2):
        piece = weight[core, :, :, :, :, cols].reshape(D, PAIR)
        out = dot(tokens[...], piece) + offsets[core, :, cols]
        qkv[pair, :, place_of(core, 0, PAIR)] = out.astype(BF) * scale


def attend_pair(qkv, bias, probs, flip, core, row, pair):
    item = core * 3 + pair
    queries, keys, values = (trio(qkv, core, row, part, pair) for part in range(3))
    flipped = values.T
    cols = pl.ds(pl.multiple_of(row * LEN, LEN), LEN)
    for half, mask in enumerate(half_masks()):
        scores = dot_last(keys * mask, queries) + bias[row]
        raised = jnp.exp(scores - jnp.max(scores, axis=0, keepdims=True))
        share = (raised * (1.0 / jnp.sum(raised, axis=0, keepdims=True))).astype(BF)
        probs[half] = share
        lines = pl.ds(pl.multiple_of(item * 128 + half * HD, HD), HD)
        flip[lines, cols] = dot(flipped[half * HD:(half + 1) * HD, :], share).astype(BF)


FEED_MOVES = (
    ((8, 2),), ((9, 2),), (), ((6, 3),), ((7, 3),), ((8, 3),),
)


def forward_gather_kernel(*refs):
    refs = list(refs)
    take = lambda number: [refs.pop(0) for _ in range(number)]
    w_qkv, w_out, w_up, w_down, head, ffn, norm, lengths = take(8)
    tokens_any, cotangent_any = take(2)
    (sums, norm_out, ffn_out, hidden_scale, out_full, pooled, norm_sums) = take(7)
    (qkv_full, up_full, down_full, qkv_out, context_flip, token_flip, hidden_flip, normed_out,
     context_out, act_flip, slope_out, layer_out, branch_out, grad_two_out, probs_out) = take(15)
    (g_small, g_qkv, g_out, g_up, g_down, tokens, qkv, context, flip,
     hidden_b, normed_one, act, slope, flip_act, bias, probs, offsets, branch, flip_context) = take(19)
    send, recv, local = refs
    place = Place()
    greet(place)
    here = (place.m, place.z, place.y, place.x)
    used = [0]
    unwaited = []

    def keep(source, target):
        copy = pltpu.make_async_copy(source, target, local.at[used[0]])
        used[0] += 1
        copy.start()
        unwaited.append(copy)
        return copy

    def done(copy):
        copy.wait()
        unwaited[:] = [other for other in unwaited if other is not copy]

    tokens_loaded = keep(tokens_any, tokens)
    place_small(g_small.at[here], norm[...], head[...], as_row(ffn), 0.0)
    for part in range(3):
        for pair in range(3):
            start = pair * PAIR + part * 128
            g_qkv[here + (EVERY, slice(start, start + 128))] = w_qkv[
                part, :, pair * 128:(pair + 1) * 128].astype(BF)
    value = w_out[...]
    spare = g_out.shape[4] - value.shape[0]
    g_out[here] = jnp.concatenate([value, jnp.zeros((spare, D), F32)], axis=0).astype(BF)
    g_up[here] = w_up[...].astype(BF)
    g_down[here] = w_down[...].astype(BF)
    sems, base = (send, recv), [0]

    def chunk(full, start, width, flip=False, orders=("zxy", "zyx")):
        made = Spread(place, full, start, width, flip, orders, sems, base[0])
        base[0] += made.count
        return made

    groups = [[chunk(g_small, 0, 128), chunk(g_qkv, 0, PAIR)]]
    groups += [[chunk(g_qkv, pair * PAIR, PAIR, pair == 1)] for pair in (1, 2)]
    groups += [[chunk(g_out, 0, D)]]
    groups += [[chunk(g_up, at, UP_CHUNK)] for at in range(0, FF // 2, UP_CHUNK)]
    groups += [[chunk(g_down, at, DOWN_CHUNK)] for at in range(0, D, DOWN_CHUNK)]

    def ready(index):
        for made in groups[index]:
            made.arrived(3)

    meet(place)
    spread(groups, (0, 0), (1, 0))
    sums[...] = weight_sums_of([w_qkv, w_out, w_up, w_down], g_small[here])
    for row in range(2):
        set_bias(bias.at[row], lengths, place.m * 2 + row)
    done(tokens_loaded)
    flip[...] = tokens[...].T
    flip_kept = keep(flip, token_flip)
    spread(groups, (0, 1), (2, 0))
    spread(groups, (1, 1), (3, 0))
    spread(groups, (0, 2))
    spread(groups, (2, 1), (4, 0))
    spread(groups, (1, 2))
    spread(groups, (0, 3), (3, 1), (5, 0))
    ready(0)
    unpack_small(g_small, norm_out, offsets, ffn_out)

    @pl.loop(0, 12)
    def _(item):
        pair, row, core = item // 4, (item % 4) // 2, item % 2
        for at, moves in (
            (1, ((3, 2), (5, 1), (7, 0))),
            (4, ((2, 3),)),
            (6, ((7, 1), (9, 0))),
            (7, ((3, 3),)),
            (10, ((4, 3), (9, 1))),
            (11, ((6, 2),)),
        ):
            @pl.when(item == at)
            def _():
                spread(groups, *moves)

        for at in (4, 8):
            @pl.when(item == at)
            def _():
                ready(at // 4)

        @pl.when(item % 4 == 0)
        def _():
            project_pair(tokens, g_qkv, offsets, qkv, pair)

        for at, moves in (
            (0, ((1, 3), (2, 2), (4, 1), (6, 0))),
            (4, ((4, 2), (6, 1), (8, 0))),
            (8, ((5, 2), (8, 1))),
        ):
            @pl.when(item == at)
            def _():
                spread(groups, *moves)

        def probs_copy(number):
            return pltpu.make_async_copy(
                probs.at[number % 2], probs_out.at[number], local.at[28 + number % 2])

        @pl.when(item >= 2)
        def _():
            probs_copy(item - 2).wait()

        attend_pair(qkv, bias, probs.at[item % 2], flip_context, core, row, pair)
        probs_copy(item).start()

    spread(groups, (7, 2))
    for core in range(2):
        for pair in range(3):
            cols = slice(pair * PAIR, (pair + 1) * PAIR)
            keep(g_qkv.at[core, :, :, :, :, cols],
                 qkv_full.at[pair, :, :, :, :, core * PAIR:(core + 1) * PAIR])
    keep(qkv, qkv_out)
    keep(flip_context, context_flip)
    context[...] = flip_context[...].T
    context_kept = keep(context, context_out)
    for slot in range(2):
        unwaited.append(
            pltpu.make_async_copy(probs.at[slot], probs_out.at[10 + slot], local.at[28 + slot]))
    ready(3)
    rows_out = w_out.shape[0]
    for core in range(2):
        value = g_out[core].reshape(16, g_out.shape[4], D).astype(F32)[:, :rows_out]
        out_full[core * HALF:(core + 1) * HALF, :] = value.reshape(HALF, D).astype(BF)
    halves = [slice(row * LEN, (row + 1) * LEN) for row in range(2)]
    for number, rows in enumerate(halves):
        attended = dot(context[rows, :], out_full[...]) + norm_out[0:1, :]
        normed, scale = norm_parts(tokens[rows, :].astype(F32) + attended)
        normed_one[rows, :] = normed
        hidden_scale[rows, :] = jnp.broadcast_to(scale, (LEN, 128))
        hidden_b[rows, :] = (normed * norm_out[2:3, :] + norm_out[3:4, :]).astype(BF)
        spread(groups, *(((), ((5, 3),)))[number])
    cotangent_loaded = keep(cotangent_any, tokens)
    keep(normed_one, normed_out)
    waiting = [[], []]
    for third in range(3):
        ready(4 + third)
        for core in range(2):
            for copy in waiting[core]:
                copy.wait()
            local_cols = slice(third * UP_CHUNK, (third + 1) * UP_CHUNK)
            start = core * (FF // 2) + third * UP_CHUNK
            cols = pl.ds(start, UP_CHUNK)
            up = g_up[core, :, :, :, :, local_cols].reshape(D, UP_CHUNK)

            @pl.loop(0, 2)
            def _(row):
                rows = pl.ds(pl.multiple_of(row * LEN, LEN), LEN)
                value, slope_value = gelu_both(
                    dot(hidden_b[rows, :], up) + ffn_out[:, start:start + UP_CHUNK])
                act[rows, cols] = value.astype(BF)
                slope[core, rows, :] = slope_value.astype(BF)

            flip_act[core] = act[:, cols].T
            slot = 24 + 2 * core
            waiting[core] = [
                pltpu.make_async_copy(slope.at[core], slope_out.at[:, cols], local.at[slot]),
                pltpu.make_async_copy(flip_act.at[core], act_flip.at[cols, :], local.at[slot + 1]),
            ]
            for copy in waiting[core]:
                copy.start()
            spread(groups, *FEED_MOVES[2 * third + core])
    done(flip_kept)
    flip[...] = hidden_b[...].T
    keep(flip, hidden_flip)
    for core in range(2):
        keep(g_up.at[core], up_full.at[core])
    for third in range(3):
        ready(7 + third)
        cols = slice(third * DOWN_CHUNK, (third + 1) * DOWN_CHUNK)
        down = g_down[:, :, :, :, :, cols].reshape(FF, DOWN_CHUNK)
        for rows in halves:
            branch[rows, cols] = dot(act[rows, :], down)
        spread(groups, *(((), ((9, 3),), ()))[third])
    for core in range(2):
        keep(g_down.at[core], down_full.at[core])
    norm_sums[...] = jnp.zeros(norm_sums.shape, F32)
    done(cotangent_loaded)
    done(context_kept)
    for row, rows in enumerate(halves):
        hidden = normed_one[rows, :] * norm_out[2:3, :] + norm_out[3:4, :]
        normed, scale = norm_parts(hidden + branch[rows, :] + norm_out[1:2, :])
        output = normed * norm_out[4:5, :] + norm_out[5:6, :]
        high = output.astype(BF)
        context[rows, :] = high
        keep(context.at[rows], layer_out.at[rows])
        low = (output - high.astype(F32)).astype(BF)
        spots = lax.broadcasted_iota(jnp.int32, (SEGS, LEN), 1)
        segment = lax.broadcasted_iota(jnp.int32, (SEGS, 1), 0)
        member = (ids_at(lengths, place.m * 2 + row, spots) == segment).astype(F32)
        sizes = jnp.sum(member, axis=1, keepdims=True)
        member = member.astype(BF)
        pooled[row] = (dot(member, high) + dot(member, low)) / sizes
        back, gain, shift = norm_back(tokens[rows, :].astype(F32), normed, scale, norm_out[4:5, :])
        norm_sums[4:5, :] += gain
        norm_sums[5:6, :] += shift
        branch[rows, :] = back
        keep(branch.at[rows], grad_two_out.at[rows])
        back = back.astype(BF)
        hidden_b[rows, :] = back
        keep(hidden_b.at[rows], branch_out.at[rows])
        norm_sums[1:2, :] += jnp.sum(back.astype(F32), axis=0, keepdims=True)
    for copy in unwaited + waiting[0] + waiting[1]:
        copy.wait()
    for group in groups:
        for made in group:
            made.finish()


def forward_gather(weights, vectors, lengths, tokens, cotangent):
    qkv, out, up, down = weights
    count = tokens.shape[0]
    shape = jax.ShapeDtypeStruct
    grid = (2, 4, 2, 2)
    rows = count // LEN
    flipped = shape((D, count), BF)
    small_outs = [
        shape((8, 128), F32), shape((8, D), F32), shape((1, FF), F32),
        shape((count, 128), F32), shape((D, D), BF), shape((rows, SEGS, D), F32), shape((8, D), F32),
    ]
    large_outs = [
        shape((3,) + grid[1:] + (qkv.shape[1], D), BF), shape(grid + up.shape, BF),
        shape(grid + down.shape, BF), shape((3, count, D), BF), flipped, flipped, flipped,
        shape((count, D), F32), shape((count, D), BF), shape((FF, count), BF),
        shape((count, FF), BF), shape((count, D), BF), shape((count, D), BF), shape((count, D), F32),
        shape((6 * rows, 2, LEN, LEN), BF),
    ]
    slots = 88
    some = pl.BlockSpec(memory_space=pl.ANY)
    return pl.pallas_call(
        forward_gather_kernel,
        out_shape=small_outs + large_outs,
        in_specs=[VMEM] * 7 + [SMEM] + [some] * 2,
        out_specs=[VMEM] * len(small_outs) + [some] * len(large_outs),
        scratch_shapes=[
            pltpu.VMEM(grid + (16, 128), F32),
            pltpu.VMEM(grid + (qkv.shape[1], QKV_HALF), BF),
            pltpu.VMEM(grid + (32, D), BF),
            pltpu.VMEM(grid + up.shape, BF),
            pltpu.VMEM(grid + down.shape, BF),
            pltpu.VMEM((count, D), BF),
            pltpu.VMEM((3, count, D), BF),
            pltpu.VMEM((count, D), BF),
            pltpu.VMEM((D, count), BF),
            pltpu.VMEM((count, D), BF),
            pltpu.VMEM((count, D), F32),
            pltpu.VMEM((count, FF), BF),
            pltpu.VMEM((2, count, UP_CHUNK), BF),
            pltpu.VMEM((2, UP_CHUNK, count), BF),
            pltpu.VMEM((2, LEN, LEN), F32),
            pltpu.VMEM((2, 2, LEN, LEN), BF),
            pltpu.VMEM((2, 1, QKV_HALF), F32),
            pltpu.VMEM((count, D), F32),
            pltpu.VMEM((D, count), BF),
            pltpu.SemaphoreType.DMA((slots,)),
            pltpu.SemaphoreType.DMA((slots,)),
            pltpu.SemaphoreType.DMA((30,)),
        ],
        compiler_params=pltpu.CompilerParams(
            collective_id=0, has_side_effects=True, vmem_limit_bytes=61 << 20),
        name="forward_gather",
    )(*weights, *vectors, lengths, tokens, cotangent)


class Collect:
    COUNT = 7

    def __init__(self, place, held, slots, result, start, width, flip, sems, base, layer=None,
                 stages=(0, 2)):
        self.place, self.held, self.slots, self.result = place, held, slots, result
        self.layer, self.stages = layer, stages
        self.cols = pl.ds(start, width)
        tiles = width // 128
        cut = (tiles // 2 if flip else tiles - tiles // 2) * 128
        self.halves = [("xy", pl.ds(start, cut))]
        if cut < width:
            self.halves.append(("yx", pl.ds(start + cut, width - cut)))
        self.sems, self.base = sems, base

    def copy(self, slot, axis, step, source, target):
        send, recv = self.sems
        return pltpu.make_async_remote_copy(
            source, target, send.at[self.base + slot], recv.at[self.base + slot],
            device_id=self.place.device(self.place.at(axis, step)), device_id_type=MESH)

    def copies(self, stage):
        place = self.place
        if stage == 2:
            out = []
            for step in (1, 2, 3):
                source = self.held.at[place.at("z", step)["z"], place.y, place.x, :, self.cols]
                out.append(self.copy(
                    step - 1, "z", step, source, self.slots[2].at[step - 1, :, self.cols]))
            return out
        out = []
        for number, (order, cols) in enumerate(self.halves):
            axis = order[stage]
            spot = {"y": EVERY, "x": EVERY}
            if stage == 1:
                spot[order[0]] = getattr(place, order[0])
            spot[axis] = place.at(axis, 1)[axis]
            layer = EVERY if self.layer is None else self.layer
            land = (layer,) + (EVERY,) * (1 - stage) + (EVERY, cols)
            out.append(self.copy(
                2 * stage + number + (0 if self.layer is not None else 3), axis, 1,
                self.held.at[layer, spot["y"], spot["x"], :, cols], self.slots[stage].at[land]))
        return out

    def start(self, stage):
        for sent in self.copies(stage):
            sent.start()

    def add(self, stage):
        place, held, slots = self.place, self.held, self.slots[stage]
        for sent in self.copies(stage):
            sent.wait_recv()
        if stage == 2:
            value = held[place.z, place.y, place.x, :, self.cols].astype(F32)
            for step in range(3):
                value = value + slots[step, :, self.cols].astype(F32)
            self.result[:, self.cols] = value[:self.result.shape[0]]
            return
        for order, cols in self.halves:

            layers = 4 if self.layer is None else 1

            @pl.loop(0, layers * (2 - stage))
            def _(index):
                spot = {"y": place.y, "x": place.x}
                if stage == 0:
                    layer = index // 2 if self.layer is None else self.layer
                    spot[order[1]] = index % 2
                    arrived = slots[layer, index % 2, :, cols]
                else:
                    layer = index if self.layer is None else self.layer
                    arrived = slots[layer, :, cols]
                at = (layer, spot["y"], spot["x"], EVERY, cols)
                held[at] = (held[at].astype(F32) + arrived.astype(F32)).astype(held.dtype)

    def finish(self):
        for stage in range(self.stages[0], self.stages[1] + 1):
            for sent in self.copies(stage):
                sent.wait_send()


def advance(groups, *moves):
    for group, stage in moves:
        for chunk in groups[group]:
            if stage > chunk.stages[0]:
                chunk.add(stage - 1)
            if stage <= chunk.stages[1]:
                chunk.start(stage)


def split_dot(value, other):
    high = value.astype(BF)
    return dot(high, other) + dot((value - high.astype(F32)).astype(BF), other)


def picks(count, width):
    shape = (count, 128)
    lane = lax.broadcasted_iota(jnp.int32, shape, 0) % width
    return (lane == lax.broadcasted_iota(jnp.int32, shape, 1)).astype(F32).astype(BF)


def pack_rows(rows, right):
    rows = jnp.broadcast_to(rows[None], (16, 8, D)).reshape(128, D)
    iota = lambda axis: lax.broadcasted_iota(jnp.int32, (128, D), axis)
    rows = jnp.where(iota(1) // 24 == right(iota(0) // 8), rows, 0.0)
    return split_dot(rows, picks(D, 24)).reshape(4, 2, 2, 8, 128)


def pack_small(target, core, norm_sums, ffn_sums):
    target[:, :, :, 0:8, :] = pack_rows(norm_sums[...], lambda device: 2 * device + core)
    iota = lambda axis: lax.broadcasted_iota(jnp.int32, (16, FF), axis)
    ffn = jnp.where(iota(1) // 96 == iota(0) + 16 * core, ffn_sums[...], 0.0)
    target[:, :, :, 8:16, :] = jnp.zeros((4, 2, 2, 8, 128), F32)
    target[:, :, :, 8, :] = split_dot(ffn, picks(FF, 96)).reshape(4, 2, 2, 128)


def pack_heads(core, grad_head):
    return pack_rows(grad_head[...], lambda device: 16 * core + device)


def attend_back_pair(qkv, grad_context, probs, delta, grad_head, core, row, pair):
    lane = lax.broadcasted_iota(jnp.int32, (LEN, 128), 1)
    item = core * 3 + pair
    queries, keys, values = (trio(qkv, core, row, part, pair) for part in range(3))
    rows = pl.ds(pl.multiple_of(row * LEN, LEN), LEN)
    wide = pl.ds(pl.multiple_of(item * 128, 128), 128)
    grad = grad_context[rows, wide]
    flipped = keys.T
    grads_k, grads_v, grads_q = [], [], []
    for half, mask in enumerate(half_masks()):
        share = probs[half]
        grad_probs = dot_last(values * mask, grad) - delta[row, pl.ds(item * 2 + half, 1), :]
        grad_scores = (share.astype(F32) * grad_probs).astype(BF)
        grads_v.append(dot(share, grad))
        grads_k.append(dot(grad_scores, queries))
        grads_q.append(dot(flipped[half * HD:(half + 1) * HD, :], grad_scores))
    grad_q = (jnp.concatenate(grads_q, axis=0).T * HD ** -0.5).astype(BF)
    grad_k = jnp.where(lane < HD, grads_k[0], grads_k[1]).astype(BF)
    grad_v = jnp.where(lane < HD, grads_v[0], grads_v[1]).astype(BF)
    for part, value in enumerate((grad_q, grad_k, grad_v)):
        qkv[pair, rows, place_of(core, part, 128)] = value
    grad_head[0:1, wide] += jnp.sum(grad_q.astype(F32), axis=0, keepdims=True)
    grad_head[1:2, wide] += jnp.sum(grad_v.astype(F32), axis=0, keepdims=True)


def backward_scatter_kernel(*refs):
    refs = list(refs)
    take = lambda number: [refs.pop(0) for _ in range(number)]
    norm_given, norm, scale_one, w_out = take(4)
    rows_old, cols_old = take(4), take(4)
    head_sq, ffn_sq, norm_sq, weight_sums = take(4)
    (act_any, branch_any, down_any, slope_any, up_any, two_any, normed_any, hidden_any, context_any,
     flip_any, token_any, qkv_any, weight_any, probs_any) = take(14)
    results = take(5)
    lines, totals, input_any = take(3)
    held, other = take(6), take(6)
    slots = [take(3) for _ in range(6)]
    heads_sum = refs.pop(0)
    (wide, flip, flip_context, context, attended, qkv, weight, one, two, act, inner, probs, delta,
     grad_head, norm_sums, ffn_sums) = take(16)
    (mine_early, plane_early, line_early, mine_one, plane_one, line_one, mine_two, plane_two,
     line_two, old_small) = take(10)
    send, recv, local = refs
    place = Place()
    greet(place, True)
    sems = (send, recv)
    partner = place.device(place.at("m", 1))
    mine, theirs = place.m, 1 - place.m
    loaded = {}

    def load(name, source, target):
        copy = pltpu.make_async_copy(source, target, local.at[len(loaded)])
        copy.start()
        loaded[name] = copy

    tile_rows = FF // 2 // 4
    act_slots, chunk_slots = 16, 18

    def act_load(index):
        core = jnp.where(index % 2 == 0, theirs, mine)
        start = pl.multiple_of(core * (FF // 2) + (index // 2) * tile_rows, tile_rows)
        return pltpu.make_async_copy(
            act_any.at[pl.ds(start, tile_rows)], act.at[index % 2], local.at[act_slots + index % 2])

    def down_tile(index):
        return qkv.at[0, pl.ds(pl.multiple_of(index % 2 * UP_CHUNK, UP_CHUNK), UP_CHUNK)]

    def slope_tile(index):
        return qkv.at[1 + index % 2, :, pl.ds(0, UP_CHUNK)]

    def up_tile(index):
        return weight.at[index % 2, :, pl.ds(0, UP_CHUNK)]

    def chunk_loads(index):
        core = jnp.where(index < 3, theirs, mine)
        inside = pl.ds(pl.multiple_of(index % 3 * UP_CHUNK, UP_CHUNK), UP_CHUNK)
        whole = pl.ds(
            pl.multiple_of(core * (FF // 2) + index % 3 * UP_CHUNK, UP_CHUNK), UP_CHUNK)
        slot = chunk_slots + 3 * (index % 2)
        return [
            pltpu.make_async_copy(down_any.at[whole], down_tile(index), local.at[slot]),
            pltpu.make_async_copy(slope_any.at[:, whole], slope_tile(index), local.at[slot + 1]),
            pltpu.make_async_copy(up_any.at[core, :, inside], up_tile(index), local.at[slot + 2]),
        ]

    load("branch", branch_any, wide)
    for index in range(2):
        act_load(index).start()

    small, qkv_held, out_held, up_held, down_held, heads = held
    small_other, qkv_other, out_other, up_other, down_other, heads_other = other
    base = 13

    def swap(slot, source, target):
        return pltpu.make_async_remote_copy(
            source, target, send.at[slot], recv.at[slot],
            device_id=partner, device_id_type=MESH)

    def down_swap(layer):
        return swap(layer, down_held.at[layer], down_other.at[layer])

    def up_swap(third):
        cols = pl.ds(pl.multiple_of(third * UP_CHUNK, UP_CHUNK), UP_CHUNK)
        at = (EVERY, EVERY, EVERY, EVERY, cols)
        return swap(4 + third, up_held.at[at], up_other.at[at])

    def qkv_swap(pair):
        at = (EVERY, EVERY, EVERY, EVERY, pl.ds(pl.multiple_of(pair * PAIR, PAIR), PAIR))
        return swap(8 + pair, qkv_held.at[at], qkv_other.at[at])

    out_swap = swap(7, out_held, out_other)
    small_swap = swap(11, small, small_other)
    heads_swap = swap(12, heads, heads_other)
    widths = (128, PAIR, D, UP_CHUNK, DOWN_CHUNK, 128)
    chunks = [[] for _ in range(6)]
    targets = results + [heads_sum]

    def collect(index, start, width, flip=False, layer=None, stages=(0, 2), count=Collect.COUNT):
        nonlocal base
        made = Collect(place, held[index], slots[index], targets[index], start, width, flip, sems,
                       base, layer, stages)
        base += count
        return made

    groups = [[collect(4, 0, D, layer=z, stages=(0, 1), count=4)] for z in range(4)]
    groups += [[collect(4, 0, D, stages=(2, 2), count=3)]]
    for index in (3, 2, 1):
        for start in range(0, held[index].shape[4], widths[index]):
            groups.append([collect(index, start, widths[index], index == 1 and start == PAIR)])
    groups[8].append(collect(0, 0, 128))
    groups[11].append(collect(5, 0, 128))
    norm_sums[...] = norm_given[...]
    loaded["branch"].wait()
    meet(place, True)

    def down_tile_of(index):
        act_load(index).wait()
        value = dot(act[index % 2], wide[...]).reshape(2, 2, tile_rows // 4, D)

        @pl.when(index < 6)
        def _():
            act_load(index + 2).start()

        return value

    def down_theirs(layer):
        down_held[layer] = down_tile_of(2 * layer).astype(BF)
        down_swap(layer).start()

    down_theirs(0)
    load("hidden", hidden_any, flip)
    for index in range(2):
        for copy in chunk_loads(index):
            copy.start()
    load("two", two_any, two)
    load("normed", normed_any, one)
    load("context", context_any, context)
    load("flip", flip_any, flip_context)

    @pl.loop(0, 4)
    def _(layer):
        value = down_tile_of(2 * layer + 1)

        @pl.when(layer < 3)
        def _():
            down_theirs(layer + 1)

        down_swap(layer).wait()
        down_held[layer] = (value + down_other[layer].astype(F32)).astype(BF)
        for z in range(4):
            @pl.when(layer == z)
            def _():
                advance(groups, (z, 0))

    loaded["hidden"].wait()
    loaded["two"].wait()

    def feed_back(index):
        for copy in chunk_loads(index):
            copy.wait()
        core = jnp.where(index < 3, theirs, mine)
        whole = pl.ds(
            pl.multiple_of(core * (FF // 2) + index % 3 * UP_CHUNK, UP_CHUNK), UP_CHUNK)
        value = dot_last(wide[...], down_tile(index)[...])
        value = (value * slope_tile(index)[...].astype(F32)).astype(BF)
        inner[...] = value
        ffn_sums[:, whole] = jnp.sum(value.astype(F32), axis=0, keepdims=True)
        two[...] += dot_last(inner[...], up_tile(index)[...])
        return dot(flip[...], inner[...]).reshape(4, 2, 2, D // 16, UP_CHUNK)

    @pl.loop(0, 3)
    def _(third):
        cols = pl.ds(pl.multiple_of(third * UP_CHUNK, UP_CHUNK), UP_CHUNK)
        up_held[:, :, :, :, cols] = feed_back(third).astype(BF)
        up_swap(third).start()
        for copy in chunk_loads(third + 2):
            copy.start()

        for at, moves in (
            (0, ((0, 1),)),
            (1, ((1, 1),)),
            (2, ((2, 1),)),
        ):
            @pl.when(third == at)
            def _():
                advance(groups, *moves)

    @pl.loop(0, 3)
    def _(third):
        at = (EVERY, EVERY, EVERY, EVERY,
              pl.ds(pl.multiple_of(third * UP_CHUNK, UP_CHUNK), UP_CHUNK))
        value = feed_back(third + 3)
        up_swap(third).wait()
        up_held[at] = (value + up_other[at].astype(F32)).astype(BF)

        @pl.when(third == 0)
        def _():
            for copy in chunk_loads(5):
                copy.start()

        for spot, moves in (
            (0, ((3, 1), (5, 0))),
            (1, ((0, 2), (1, 2), (6, 0))),
            (2, ((2, 2), (3, 2), (4, 2), (7, 0))),
        ):
            @pl.when(third == spot)
            def _():
                advance(groups, *moves)

    def probs_load(item):
        pair, row = item // 4, item % 2
        core = jnp.where(item % 4 < 2, theirs, mine)
        return pltpu.make_async_copy(
            probs_any.at[pair * 4 + row * 2 + core], probs.at[item % 2], local.at[24 + item % 2])

    for item in range(2):
        probs_load(item).start()
    load("token", token_any, flip)
    load("qkv", qkv_any, qkv)
    load("weight", weight_any, weight)
    loaded["normed"].wait()
    loaded["context"].wait()
    for row in range(2):
        rows = slice(row * LEN, (row + 1) * LEN)
        back, gain, shift = norm_back(
            two[rows, :], one[rows, :], scale_one[rows, 0:1], norm[2:3, :])
        norm_sums[2:3, :] += gain
        norm_sums[3:4, :] += shift
        one[rows, :] = back
        back = back.astype(BF)
        attended[rows, :] = back
        norm_sums[0:1, :] += jnp.sum(back.astype(F32), axis=0, keepdims=True)
        back = dot_last(back, w_out[...]).astype(BF)
        wide[rows, :] = back
        product = back.astype(F32) * context[rows, :].astype(F32)
        high = product.astype(BF)
        low = (product - high.astype(F32)).astype(BF)
        head = lax.broadcasted_iota(jnp.int32, (16, D), 0)
        member = (lax.broadcasted_iota(jnp.int32, (16, D), 1) // HD == head).astype(F32).astype(BF)
        delta[row] = dot_last(member, high) + dot_last(member, low)
    loaded["flip"].wait()
    advance(groups, (5, 1))
    spare = out_held.shape[3] - D // 32

    def out_half(core):
        rows = pl.ds(pl.multiple_of(core * HALF, HALF), HALF)
        value = dot(flip_context[rows, :], attended[...]).reshape(16, D // 32, D)
        value = jnp.concatenate([value, jnp.zeros((16, spare, D), F32)], axis=1)
        return value.reshape(4, 2, 2, D // 32 + spare, D)

    out_held[...] = out_half(theirs).astype(BF)
    out_swap.start()
    pack_small(small, theirs, norm_sums, ffn_sums)
    small_swap.start()
    value = out_half(mine)
    out_swap.wait()
    out_held[...] = (value + out_other[...].astype(F32)).astype(BF)
    small_swap.wait()
    pack_small(small, mine, norm_sums, ffn_sums)
    small[...] += small_other[...]
    advance(groups, (8, 0))
    grad_head[...] = jnp.zeros(grad_head.shape, F32)
    for name in ("qkv", "token"):
        loaded[name].wait()

    def qkv_theirs(pair):
        cols = pl.ds(pl.multiple_of(pair * PAIR, PAIR), PAIR)
        value = dot(flip[...], qkv[pair, :, place_of(theirs, 0, PAIR)])
        qkv_held[:, :, :, :, cols] = value.reshape(4, 2, 2, D // 16, PAIR).astype(BF)
        qkv_swap(pair).start()

    def qkv_mine(pair):
        cols = pl.ds(pl.multiple_of(pair * PAIR, PAIR), PAIR)
        at = (EVERY, EVERY, EVERY, EVERY, cols)
        value = dot(flip[...], qkv[pair, :, place_of(mine, 0, PAIR)]).reshape(4, 2, 2, D // 16, PAIR)
        qkv_swap(pair).wait()
        qkv_held[at] = (value + qkv_other[at].astype(F32)).astype(BF)

    @pl.loop(0, 12)
    def _(item):
        pair, row = item // 4, item % 2
        core = jnp.where(item % 4 < 2, theirs, mine)

        @pl.when(item % 4 == 2)
        def _():
            qkv_theirs(pair)

        @pl.when((item == 4) | (item == 8))
        def _():
            qkv_mine(pair - 1)

        for at, moves in (
            (1, ((6, 1),)),
            (3, ((7, 1),)),
            (4, ((5, 2), (9, 0))),
            (6, ((4, 3),)),
            (7, ((8, 1),)),
            (8, ((5, 3), (6, 2), (10, 0))),
            (9, ((7, 2),)),
            (10, ((9, 1),)),
        ):
            @pl.when(item == at)
            def _():
                advance(groups, *moves)

        probs_load(item).wait()
        attend_back_pair(qkv, wide, probs.at[item % 2], delta, grad_head, core, row, pair)

        @pl.when(item < 10)
        def _():
            probs_load(item + 2).start()

    heads[...] = pack_heads(theirs, grad_head)
    heads_swap.start()
    loaded["weight"].wait()

    def input_rows(row):
        rows = pl.ds(pl.multiple_of(row * LEN, LEN), LEN)
        one[rows, :] += (dot_last(qkv[0, rows, :], weight[0]) + dot_last(qkv[1, rows, :], weight[1])
                         + dot_last(qkv[2, rows, :], weight[2]))

    qkv_mine(2)
    heads_swap.wait()
    heads[...] = pack_heads(mine, grad_head) + heads_other[...]
    advance(groups, (6, 3), (8, 2), (11, 0))
    input_rows(0)
    advance(groups, (10, 1))
    input_rows(1)
    input_done = pltpu.make_async_copy(one, input_any, local.at[12])
    input_done.start()
    advance(groups, (7, 3), (9, 2), (11, 1), (10, 2), (8, 3))
    small_sum, grads = results[0], results[1:]
    lines[...] = jnp.zeros(lines.shape, F32)

    def put_sums(index):
        grad = grads[index][...]
        square = grad * grad + EPS_SQUARE
        put_line(lines, COL_LINES[index], jnp.sum(square, axis=0, keepdims=True))
        if index in (0, 2):
            line = UP_ROWS if index else QKV_ROWS
            lines[line:line + 1, 0:grad.shape[0]] = to_row(jnp.sum(square, axis=1, keepdims=True))

    def ratio_of(index):
        (row,), (col,) = new_rows_cols(grads, rows_old, cols_old, lines, (index,))
        grad = grads[index][...]
        scaled = jnp.sum(grad * grad * (1.0 / col), axis=1, keepdims=True)
        share = 0.5 if index in (0, 2) else 1.0
        return (jnp.sum(scaled / row, axis=0, keepdims=True),
                jnp.sum(row, axis=0, keepdims=True) * share)

    for index in (1, 2, 3):
        put_sums(index)
    early = Exchange(place, mine_early, plane_early, line_early, sems, base)
    late = Exchange(place, mine_one, plane_one, line_one, sems, base + Exchange.COUNT)
    second = Exchange(place, mine_two, plane_two, line_two, sems, base + 2 * Exchange.COUNT)
    value = lines[LATE:, :]
    early.start_plane(value)
    advance(groups, (9, 3), (11, 2))
    line = lax.broadcasted_iota(jnp.int32, value.shape, 0) + LATE
    same, cross = early.end_plane()
    paired = value + plane_early[theirs, place.y, place.x]
    early.start_line(jnp.where((line >= OUT_LINE) & (line < UP_ROWS), same + cross, same))
    advance(groups, (10, 3))
    lines[LATE:, :] = jnp.where(line >= UP_ROWS, paired, early.end_line())
    sums = {index: ratio_of(index) for index in (1, 2, 3)}
    place_small(old_small, norm_sq[...], head_sq[...], as_row(ffn_sq), 1.0)
    advance(groups, (11, 3))
    put_sums(0)
    value = lines[0:LATE, :]
    late.start_plane(value)
    small_sum[6:8, :] = heads_sum[0:2, :]
    _, update = small_update(small_sum[...], old_small[...])
    others = small_sums(update)
    line = lax.broadcasted_iota(jnp.int32, value.shape, 0)
    same, _ = late.end_plane()
    paired = value + plane_one[theirs, place.y, place.x]
    late.start_line(same)
    lines[0:LATE, :] = jnp.where(line >= QKV_ROWS, paired, late.end_line())
    sums[0] = ratio_of(0)
    second.start_plane(
        scalars([sums[index][0] for index in range(4)] + [sums[index][1] for index in range(4)]
                + others) + weight_sums[...])
    same, cross = second.end_plane()
    second.start_line(same + cross)
    totals[...] = second.end_line()
    input_done.wait()
    for group in groups:
        for chunk in group:
            chunk.finish()
    for exchange in (early, late, second):
        exchange.finish()


def backward_scatter(norm_sums, norm, scale_one, w_out, rows_old, cols_old, squares,
                     weight_sums, large, rows, widths):
    count = scale_one.shape[0]
    shape = jax.ShapeDtypeStruct
    some = pl.BlockSpec(memory_space=pl.ANY)
    kinds = [F32, BF, BF, BF, BF, F32]
    padded = [16, rows[1], 32, rows[3], rows[4], 8]
    wide = widths + [128]
    held = [pltpu.VMEM((4, 2, 2, r, w), k) for r, w, k in zip(padded, wide, kinds)]
    slots = []
    for r, w, k in zip(padded, wide, kinds):
        slots += [pltpu.VMEM((4, 2, r, w), k), pltpu.VMEM((4, r, w), k), pltpu.VMEM((3, r, w), k)]
    sems = 13 + 19 + 9 * Collect.COUNT + 3 * Exchange.COUNT
    outs = [shape((r, w), F32) for r, w in zip(rows, widths)]
    outs += [shape((LINES, 128), F32), shape((8, 128), F32), shape((count, D), F32)]
    small = [norm_sums, norm, scale_one, w_out, *rows_old, *cols_old, *squares, weight_sums]
    return pl.pallas_call(
        backward_scatter_kernel,
        out_shape=outs,
        in_specs=[VMEM] * len(small) + [some] * len(large),
        out_specs=[VMEM] * 7 + [some],
        scratch_shapes=held + held + slots + [
            pltpu.VMEM((8, 128), F32),
            pltpu.VMEM((count, D), BF),
            pltpu.VMEM((D, count), BF),
            pltpu.VMEM((D, count), BF),
            pltpu.VMEM((count, D), BF),
            pltpu.VMEM((count, D), BF),
            pltpu.VMEM((3, count, D), BF),
            pltpu.VMEM((3, D, D), BF),
            pltpu.VMEM((count, D), F32),
            pltpu.VMEM((count, D), F32),
            pltpu.VMEM((2, FF // 8, count), BF),
            pltpu.VMEM((count, UP_CHUNK), BF),
            pltpu.VMEM((2, 2, LEN, LEN), BF),
            pltpu.VMEM((2, 16, LEN), F32),
            pltpu.VMEM((8, D), F32),
            pltpu.VMEM((8, D), F32),
            pltpu.VMEM((1, FF), F32),
        ] + [
            pltpu.VMEM(lead + (count, 128), F32)
            for count in (LINES - LATE, LATE, 8) for lead in ((2,), (2, 2, 2), (4,))
        ] + [
            pltpu.VMEM((16, 128), F32),
            pltpu.SemaphoreType.DMA((sems,)),
            pltpu.SemaphoreType.DMA((sems,)),
            pltpu.SemaphoreType.DMA((26,)),
        ],
        compiler_params=pltpu.CompilerParams(
            collective_id=1, has_side_effects=True, vmem_limit_bytes=62 << 20),
        name="backward_scatter",
    )(*small, *large)


def small_block(norm, head, ffn):
    wide = lambda v: jnp.pad(v, [(0, 0)] * (v.ndim - 1) + [(0, 128 - v.shape[-1])])
    block = jnp.concatenate([wide(norm), wide(head), wide(ffn)], axis=-2)
    return jnp.pad(block, [(0, 0)] * (block.ndim - 2) + [(0, 16 - block.shape[-2]), (0, 0)])


def pair_major(weight):
    count = weight.shape[0]
    return weight.reshape(count, 3, 3, 128).transpose(0, 2, 1, 3).reshape(count, QKV_HALF)


def gather_plain(weights, vectors):
    head, ffn, norm = vectors
    qkv, out, up, down = (w.astype(BF) for w in weights)
    full = []
    for shard in (small_block(norm, head, ffn), pair_major(qkv), out, up, down):
        full.append(lax.all_gather(lax.all_gather(shard, "dp", axis=0), "mp", axis=0))
    return full


def scatter_plain(fulls):
    out = []
    for full in fulls:
        own = lax.psum_scatter(full.astype(F32), "mp", scatter_dimension=0)
        out.append(lax.psum_scatter(own, "dp", scatter_dimension=0))
    return out


def body(
    tokens, cotangent, seg_lengths, w_qkv, w_out, w_up, w_down, head_bias, ffn_bias, norm_bias,
    qkv_rows, qkv_cols, out_rows, out_cols, up_rows, up_cols, down_rows, down_cols,
    head_bias_sq, ffn_bias_sq, norm_sq,
):
    cores = lax.axis_size("mp")
    data = lax.axis_size("dp")
    rows_qkv = w_qkv.shape[0]
    fast = data == 16 and cores == 2
    weights = [w_qkv.transpose(1, 0, 2) if fast else w_qkv, w_out, w_up, w_down]
    vectors = [head_bias, ffn_bias if fast else ffn_bias.reshape(1, -1), norm_bias]
    rows_out = w_out.shape[0]
    if fast:
        (weight_sums, norm_full, ffn_full, scale_one, out_full, pooled, norm_sums, qkv_full,
         up_full, down_full, qkv, context_flip, token_flip, hidden_flip, normed_one, context,
         act_flip, slope, layer_out, grad_branch, grad_two, probs
         ) = forward_gather(weights, vectors, seg_lengths, tokens, cotangent)
        rows_old = [qkv_rows, out_rows, up_rows, down_rows]
        cols_old = [qkv_cols, out_cols, up_cols, down_cols]
        old = [head_bias_sq, ffn_bias_sq, norm_sq]
        *reduced, lines, totals, input_grad = backward_scatter(
            norm_sums, norm_full, scale_one, out_full, rows_old, cols_old, old, weight_sums,
            [act_flip, grad_branch, down_full.reshape(FF, D), slope,
             up_full.reshape(2, D, FF // 2), grad_two, normed_one, hidden_flip, context,
             context_flip, token_flip, qkv, qkv_full.reshape(3, D, D), probs],
            [16, rows_qkv, rows_out, rows_qkv, w_down.shape[0]],
            [128, QKV_HALF, D, w_up.shape[1], D])
        new = step(reduced, lines, totals, weights, rows_old, cols_old, vectors, old,
                   [layer_out, pooled, input_grad])
        new = list(new)
        grads, small_grads, rows_new, cols_new = new[:4], new[4:7], new[7:11], new[11:15]
        seconds, mats, fresh, passed = new[15:18], new[18:22], new[22:25], new[25:]
        grads[0], mats[0] = grads[0].transpose(1, 0, 2), mats[0].transpose(1, 0, 2)
        stats = [v for pair in zip(rows_new, cols_new) for v in pair]
        return (*passed, *grads, *small_grads, *stats, *seconds, *mats, *fresh)
    small, qkv_g, out_g, up_g, down_g = gather_plain(weights, vectors)
    small = small.astype(BF).astype(F32)
    own_head, own_ffn, own_norm = head_bias.shape[1], ffn_bias.shape[0], norm_bias.shape[1]
    norm_full = small[:, :, 0:6, :own_norm].transpose(2, 1, 0, 3).reshape(6, D)
    head_full = small[:, :, 6:8, :own_head].transpose(2, 0, 1, 3).reshape(2, 2, 3, 1, 128)
    ffn_full = small[:, :, 8, :own_ffn].reshape(1, FF)
    offsets = jnp.concatenate([head_full[0], jnp.zeros_like(head_full[0]), head_full[1]], axis=2)
    offsets = offsets.reshape(2, 1, QKV_HALF)
    qkv_full = qkv_g.reshape(2, D, QKV_HALF)
    up_full = up_g.reshape(2, D, FF // 2)
    down_full = down_g.reshape(FF, D)
    out_full = out_g.reshape(D, D)
    norm_full = jnp.pad(norm_full, ((0, 2), (0, 0)))
    qkv, context, lse = forward(tokens, qkv_full, offsets, seg_lengths)
    (layer_out, pooled, hidden_b, act, grad_branch, grad_inner, grad_attended, grad_context,
     grad_one, delta, norm_sums, ffn_sums) = middle_call(
        tokens, context, cotangent, seg_lengths, out_full, up_full, down_full, ffn_full,
        norm_full)
    grad_out, grad_up, grad_down = weight_grads(
        context.T, hidden_b.T, act.T, grad_branch, grad_inner, grad_attended,
        cores * data, rows_out)
    token_flip = tokens.T
    grad_qkv, input_grad, grad_head = backward(
        token_flip, qkv, grad_context, lse, delta, seg_lengths, qkv_full, grad_one)
    small_grads = small_block(
        norm_sums[:6].reshape(6, data, cores, -1).transpose(2, 1, 0, 3),
        grad_head.reshape(2, cores, data, -1).transpose(1, 2, 0, 3),
        ffn_sums.reshape(cores, data, 1, -1),
    )
    fulls = [
        small_grads,
        grad_qkv.reshape(cores, data, rows_qkv, QKV_HALF),
        grad_out.reshape(cores, data, rows_out, D),
        grad_up.reshape(cores, data, rows_qkv, FF // 2),
        grad_down.reshape(cores, data, -1, D),
    ]
    red_small, red_qkv, red_out, red_up, red_down = scatter_plain(fulls)
    norm_grad = red_small[0:6, :own_norm]
    red_qkv = pair_major(red_qkv)
    red_head = red_small[6:8, :own_head]
    red_ffn = red_small[8, :own_ffn]
    weights_flat = [w_qkv.reshape(rows_qkv, -1), w_out, w_up, w_down]
    grads_flat = [red_qkv, red_out, red_up, red_down]
    rows_old = [qkv_rows, out_rows, up_rows, down_rows]
    cols_old = [qkv_cols.reshape(-1), out_cols, up_cols, down_cols]
    col_count = [3 * D, D, FF, D]
    row_count = [D, D, D, FF]
    row_share = [cores, 1, cores, 1]
    squares = [grad * grad + EPS_SQUARE for grad in grads_flat]
    row_parts = [jnp.sum(square, axis=1) for square in squares]
    col_parts = [jnp.sum(square, axis=0) for square in squares]
    vec_weights = [head_bias, ffn_bias, norm_bias]
    vec_grads = [red_head, red_ffn, norm_grad]
    vec_old = [head_bias_sq, ffn_bias_sq, norm_sq]
    vec_counts = [2 * D, FF, 6 * D]
    vec_second = [
        DECAY * old + (1.0 - DECAY) * (grad * grad + EPS_SQUARE)
        for old, grad in zip(vec_old, vec_grads)
    ]
    vec_update = [grad * lax.rsqrt(second) for grad, second in zip(vec_grads, vec_second)]
    weight_parts = [jnp.sum(weight * weight) for weight in weights_flat + vec_weights]
    vec_parts = [jnp.sum(update * update) for update in vec_update]
    row_qkv, row_up = lax.psum((row_parts[0], row_parts[2]), "mp")
    col_qkv, col_up = lax.psum((col_parts[0], col_parts[2]), "dp")
    col_out, col_down = lax.psum((col_parts[1], col_parts[3]), ("dp", "mp"))
    row_sums = [row_qkv, row_parts[1], row_up, row_parts[3]]
    col_sums = [col_qkv, col_out, col_up, col_down]
    rows_new = [
        DECAY * rows_old[index] + (1.0 - DECAY) * row_sums[index] / col_count[index]
        for index in range(4)
    ]
    cols_new = [
        DECAY * cols_old[index] + (1.0 - DECAY) * col_sums[index] / row_count[index]
        for index in range(4)
    ]
    ratio_parts = [
        jnp.sum(
            grads_flat[index]
            * grads_flat[index]
            / (rows_new[index][:, None] * cols_new[index][None, :])
        )
        for index in range(4)
    ]
    extra_parts = (
        [jnp.sum(rows_new[index]) / row_share[index] for index in range(4)]
        + weight_parts
        + vec_parts
    )
    totals = lax.psum(jnp.stack(ratio_parts + extra_parts), ("dp", "mp"))
    row_means = [totals[4 + index] / row_count[index] for index in range(4)]
    weight_totals = [totals[8 + index] for index in range(7)]
    vec_totals = [totals[15 + index] for index in range(3)]
    new_mats = []
    for index in range(4):
        entries = row_count[index] * col_count[index]
        estimate = rows_new[index][:, None] * cols_new[index][None, :] / row_means[index]
        update = grads_flat[index] / jnp.sqrt(estimate)
        update_rms = jnp.sqrt(row_means[index] * totals[index] / entries)
        stride = (
            RATE * jnp.sqrt(weight_totals[index] / entries) / jnp.maximum(1.0, update_rms / CLIP)
        )
        new_mats.append(weights_flat[index] - stride * update)
    new_vecs = []
    for index in range(3):
        update_rms = jnp.sqrt(vec_totals[index] / vec_counts[index])
        stride = (
            RATE
            * jnp.sqrt(weight_totals[4 + index] / vec_counts[index])
            / jnp.maximum(1.0, update_rms / CLIP)
        )
        new_vecs.append(vec_weights[index] - stride * vec_update[index])
    return (
        layer_out,
        pooled,
        input_grad,
        red_qkv.reshape(w_qkv.shape),
        red_out,
        red_up,
        red_down,
        red_head,
        red_ffn,
        norm_grad,
        rows_new[0],
        cols_new[0].reshape(qkv_cols.shape),
        rows_new[1],
        cols_new[1],
        rows_new[2],
        cols_new[2],
        rows_new[3],
        cols_new[3],
        vec_second[0],
        vec_second[1],
        vec_second[2],
        new_mats[0].reshape(w_qkv.shape),
        new_mats[1],
        new_mats[2],
        new_mats[3],
        new_vecs[0],
        new_vecs[1],
        new_vecs[2],
    )


def solution(mesh):
    return jax.shard_map(
        body,
        mesh=mesh,
        in_specs=(
            P(("dp", "mp"), None),
            P(("dp", "mp"), None),
            P("dp", None),
            P("dp", None, "mp"),
            P(("mp", "dp"), None),
            P("dp", "mp"),
            P(("mp", "dp"), None),
            P(None, ("mp", "dp")),
            P(("mp", "dp")),
            P(None, ("dp", "mp")),
            P("dp"),
            P(None, "mp"),
            P(("mp", "dp")),
            P(),
            P("dp"),
            P("mp"),
            P(("mp", "dp")),
            P(),
            P(None, ("mp", "dp")),
            P(("mp", "dp")),
            P(None, ("dp", "mp")),
        ),
        out_specs=(
            P(("dp", "mp"), None),
            P(("dp", "mp"), None, None),
            P(("dp", "mp"), None),
            P("dp", None, "mp"),
            P(("mp", "dp"), None),
            P("dp", "mp"),
            P(("mp", "dp"), None),
            P(None, ("mp", "dp")),
            P(("mp", "dp")),
            P(None, ("dp", "mp")),
            P("dp"),
            P(None, "mp"),
            P(("mp", "dp")),
            P(),
            P("dp"),
            P("mp"),
            P(("mp", "dp")),
            P(),
            P(None, ("mp", "dp")),
            P(("mp", "dp")),
            P(None, ("dp", "mp")),
            P("dp", None, "mp"),
            P(("mp", "dp"), None),
            P("dp", "mp"),
            P(("mp", "dp"), None),
            P(None, ("mp", "dp")),
            P(("mp", "dp")),
            P(None, ("dp", "mp")),
        ),
        check_vma=False,
    )
```

```python
import functools

import jax
import jax.numpy as jnp
from jax import lax
from jax.experimental import pallas as pl
from jax.experimental.pallas import tpu as pltpu
from jax.sharding import PartitionSpec as P

D = 768
HD = 64
FF = 3072
LEN = 512
SEGS = 8

EPS_NORM = 1e-12
EPS_SQUARE = 1e-30
DECAY = 0.5
RATE = 3.0
CLIP = 0.3

MESH = pl.DeviceIdType.MESH
BF = jnp.bfloat16
F32 = jnp.float32
EVERY = slice(None)


PLANE = [(m, y, x) for m in range(2) for y in range(2) for x in range(2)][1:]


class Place:
    def __init__(self):
        d = lax.axis_index("dp")
        self.m = lax.axis_index("mp")
        self.z, self.y, self.x = d // 4, (d // 2) % 2, d % 2

    def at(self, axis, step):
        size = 4 if axis == "z" else 2
        spot = {"z": self.z, "y": self.y, "x": self.x, "m": self.m}
        spot[axis] = (spot[axis] + step) % size
        return spot

    def across(self, steps):
        m, y, x = steps
        return {"z": self.z, "m": (self.m + m) % 2, "y": (self.y + y) % 2, "x": (self.x + x) % 2}

    @staticmethod
    def device(spot):
        return (spot["z"] * 4 + spot["y"] * 2 + spot["x"], spot["m"])


def steps_of(axis):
    return (1, 2, 3) if axis == "z" else (1,)


def other_device(step):
    count = lax.axis_size("dp") * lax.axis_size("mp")
    number = (lax.axis_index("dp") * 2 + lax.axis_index("mp") + step) % count
    return (number // 2, number % 2)


def greet(place):
    barrier = pltpu.get_barrier_semaphore()
    for axis in "zyxm":
        for step in steps_of(axis):
            pl.semaphore_signal(
                barrier, inc=1, device_id=place.device(place.at(axis, step)), device_id_type=MESH)


def meet():
    pl.semaphore_wait(pltpu.get_barrier_semaphore(), 6)


def greet_all():
    barrier = pltpu.get_barrier_semaphore()

    @pl.loop(1, 32)
    def _(step):
        pl.semaphore_signal(
            barrier, inc=1, device_id=other_device(step), device_id_type=MESH)


def meet_all():
    pl.semaphore_wait(pltpu.get_barrier_semaphore(), 31)


def weight_sums_of(weights, small):
    parts = []
    for weight in weights:
        value = weight[...]
        if value.ndim == 3:
            parts.append(sum(all_sum(value[part] * value[part]) for part in range(3)))
        else:
            parts.append(all_sum(value * value))
    return scalars([jnp.zeros((1, 1), F32)] * 11 + parts + small_sums(small))


def as_row(ref):
    value = ref[...]
    return value.reshape(1, value.shape[0]) if value.ndim == 1 else value


def to_column(row):
    count = row.shape[1]
    here = lax.broadcasted_iota(jnp.int32, (count, count), 0)
    there = lax.broadcasted_iota(jnp.int32, (count, count), 1)
    return jnp.sum(jnp.where(here == there, row, 0.0), axis=1, keepdims=True)


def to_row(column):
    count = column.shape[0]
    here = lax.broadcasted_iota(jnp.int32, (count, count), 0)
    there = lax.broadcasted_iota(jnp.int32, (count, count), 1)
    return jnp.sum(jnp.where(here == there, column, 0.0), axis=0, keepdims=True)


def put_line(ref, line, row):
    for tile in range(row.shape[1] // 128):
        ref[line + tile:line + tile + 1, :] = row[:, tile * 128:(tile + 1) * 128]


def get_line(ref, line, width):
    tiles = width // 128
    return jnp.concatenate([ref[line + t:line + t + 1, :] for t in range(tiles)], axis=1)


def scalars(values):
    lane = lax.broadcasted_iota(jnp.int32, (8, 128), 1)
    out = jnp.zeros((8, 128), F32)
    for index, value in enumerate(values):
        out = jnp.where(lane == index, value, out)
    return out


def all_sum(values):
    return jnp.sum(jnp.sum(values, axis=1, keepdims=True), axis=0, keepdims=True)


class Exchange:
    COUNT = 10

    def __init__(self, place, mine, plane, line, sems, base, peers=PLANE):
        self.place, self.mine, self.plane, self.line = place, mine, plane, line
        self.peers = peers
        self.sems, self.base = sems, base

    def plane_copies(self):
        place = self.place
        send, recv = self.sems
        out = []
        for number, steps in enumerate(self.peers):
            spot = place.across(steps)
            slot = self.base + number
            device = place.device(spot)
            sent, arrives = (
                pltpu.make_async_remote_copy(
                    self.mine.at[0], self.plane.at[at["m"], at["y"], at["x"]],
                    send.at[slot], recv.at[slot], device_id=device, device_id_type=MESH)
                for at in ({"m": place.m, "y": place.y, "x": place.x}, spot))
            out.append((sent, arrives))
        return out

    def line_copies(self):
        place = self.place
        send, recv = self.sems
        out = []
        for step in (1, 2, 3):
            slot = self.base + 6 + step
            device = place.device(place.at("z", step))
            sent, arrives = (
                pltpu.make_async_remote_copy(
                    self.mine.at[1], self.line.at[layer], send.at[slot], recv.at[slot],
                    device_id=device, device_id_type=MESH)
                for layer in (place.z, place.at("z", -step)["z"]))
            out.append((sent, arrives))
        return out

    def start_plane(self, value):
        place = self.place
        self.mine[0] = value
        for sent, _ in self.plane_copies():
            sent.start()
        self.plane[place.m, place.y, place.x] = value

    def end_plane(self):
        plane, core = self.plane, self.place.m
        for _, arrives in self.plane_copies():
            arrives.wait_recv()
        cores = (core, 1 - core) if self.peers is PLANE else (core,)
        return [(plane[c, 0, 0] + plane[c, 0, 1]) + (plane[c, 1, 0] + plane[c, 1, 1])
                for c in cores]

    def start_line(self, value):
        self.mine[1] = value
        for sent, _ in self.line_copies():
            sent.start()
        self.line[self.place.z] = value

    def end_line(self):
        line = self.line
        for _, arrives in self.line_copies():
            arrives.wait_recv()
        return (line[0] + line[1]) + (line[2] + line[3])

    def finish(self):
        for sent, _ in self.plane_copies() + self.line_copies():
            sent.wait_send()


class Broadcast:
    def __init__(self, mine, land, sems, slot, core_only):
        self.mine, self.land, self.core_only = mine, land, core_only
        self.send, self.recv = (sem.at[slot] for sem in sems)
        self.number = lax.axis_index("dp") * 2 + lax.axis_index("mp")

    def copy(self, device):
        return pltpu.make_async_remote_copy(
            self.mine, self.land.at[self.number], self.send, self.recv,
            device_id=device, device_id_type=MESH)

    def start(self, value):
        self.mine[...] = value
        if self.core_only:
            @pl.loop(2, 32, step=2)
            def _(step):
                self.copy(other_device(step)).start()

            self.copy((self.number // 2, 1 - self.number % 2)).start()
        else:
            @pl.loop(1, 32)
            def _(step):
                self.copy(other_device(step)).start()

        self.land[self.number] = value

    def all_of_it(self):
        ref = self.land.at[pl.ds(0, 16 if self.core_only else 31)]
        return pltpu.make_async_remote_copy(
            ref, ref, self.send, self.recv, device_id=(0, 0), device_id_type=MESH)

    def end(self):
        self.all_of_it().wait_recv()

    def finish(self):
        self.all_of_it().wait_send()


QKV_LINE, QKV_ROWS, UP_LINE, OUT_LINE, DOWN_LINE, UP_ROWS = 0, 9, 16, 28, 34, 40
LATE, LINES = 16, 48
WIDTHS = (3 * D // 2, D, FF // 2, D)
COL_LINES = (QKV_LINE, OUT_LINE, UP_LINE, DOWN_LINE)
COL_COUNT = (3 * D, D, FF, D)
ROW_COUNT = (D, D, D, FF)


def pair_cuts():
    out = []
    for pair in range(3):
        for part in range(3):
            start = (pair * 3 + part) * 128
            out.append(((slice(part, part + 1), slice(pair * 128, (pair + 1) * 128)),
                        slice(start, start + 128)))
    return out


def new_rows_cols(grads, rows_old, cols_old, lines, which=range(4)):
    rows_new, cols_new = [], []
    for index in which:
        if index in (0, 2):
            line = UP_ROWS if index else QKV_ROWS
            count = rows_old[index].shape[0]
            row_sum = to_column(lines[line:line + 1, :count])
        else:
            grad = grads[index][...]
            row_sum = jnp.sum(grad * grad + EPS_SQUARE, axis=1, keepdims=True)
        rows_new.append(
            DECAY * to_column(as_row(rows_old[index])) + (1.0 - DECAY) * row_sum / COL_COUNT[index])
        col_sum = get_line(lines, COL_LINES[index], WIDTHS[index])
        if index == 0:
            old = jnp.concatenate([cols_old[0][at] for at, _ in pair_cuts()], axis=1)
        else:
            old = as_row(cols_old[index])
        cols_new.append(DECAY * old + (1.0 - DECAY) * col_sum / ROW_COUNT[index])
    return rows_new, cols_new


def place_small(ref, norm, head, ffn, fill):
    ref[...] = jnp.full(ref.shape, fill, F32)
    ref[0:6, 0:norm.shape[1]] = norm
    ref[6:8, 0:head.shape[1]] = head
    ref[8:9, 0:ffn.shape[1]] = ffn


def small_update(grad, old):
    second = DECAY * old + (1.0 - DECAY) * (grad * grad + EPS_SQUARE)
    return second, grad * lax.rsqrt(second)


def small_sums(values):
    line = lax.broadcasted_iota(jnp.int32, values.shape, 0)
    square = values * values
    return [
        all_sum(jnp.where((line >= 6) & (line < 8), square, 0.0)),
        all_sum(jnp.where(line == 8, square, 0.0)),
        all_sum(jnp.where(line < 6, square, 0.0)),
    ]


def step_kernel(*refs):
    refs = list(refs)
    take = lambda number: [refs.pop(0) for _ in range(number)]
    grads_any, weights_any = take(4), take(4)
    passed = take(3)
    small, lines, totals = take(3)
    rows_old, cols_old = take(4), take(4)
    head, ffn, norm, head_sq, ffn_sq, norm_sq = take(6)
    grads_out = take(4)
    head_grad, ffn_grad, norm_grad = take(3)
    rows_out, cols_out = take(4), take(4)
    head_second, ffn_second, norm_second = take(3)
    weights_out = take(4)
    head_new, ffn_new, norm_new = take(3)
    passed_out = take(3)
    grads, weights = take(4), take(4)
    old_small, weight_small, sems = refs
    loads = []
    for number, (source, target) in enumerate(
            zip(grads_any + weights_any + passed, grads + weights + passed_out)):
        copy = pltpu.make_async_copy(source, target, sems.at[number])
        copy.start()
        loads.append(copy)
    place_small(old_small, norm_sq[...], head_sq[...], as_row(ffn_sq), 1.0)
    place_small(weight_small, norm[...], head[...], as_row(ffn), 0.0)
    for copy in loads[:4]:
        copy.wait()
    rows_new, cols_new = new_rows_cols(grads, rows_old, cols_old, lines)
    total = lambda lane: totals[0:1, lane:lane + 1]
    for index in range(4):
        rows_out[index][...] = to_row(rows_new[index]).reshape(rows_out[index].shape)
        if index == 0:
            for at, cut in pair_cuts():
                cols_out[0][at] = cols_new[0][:, cut]
        else:
            cols_out[index][...] = cols_new[index].reshape(cols_out[index].shape)
        entries = ROW_COUNT[index] * COL_COUNT[index]
        row_mean = total(4 + index) / ROW_COUNT[index]
        update_rms = jnp.sqrt(row_mean * total(index) / entries)
        stride = (
            RATE * jnp.sqrt(total(11 + index) / entries) / jnp.maximum(1.0, update_rms / CLIP))
        scale_rows = lax.rsqrt(rows_new[index] / row_mean) * stride
        scale_cols = lax.rsqrt(cols_new[index])
        loads[4 + index].wait()
        if index == 0:
            for (part, cols), cut in pair_cuts():
                at = (part.start, EVERY, cols)
                grad = grads[0][:, cut]
                grads_out[0][at] = grad
                weights_out[0][at] = weights[0][at] - grad * scale_rows * scale_cols[:, cut]
        else:
            grad = grads[index][...]
            grads_out[index][...] = grad
            weights_out[index][...] = weights[index][...] - grad * scale_rows * scale_cols
    grad = small[...]
    second, update = small_update(grad, old_small[...])
    line = lax.broadcasted_iota(jnp.int32, grad.shape, 0)
    counts = (2 * D, FF, 6 * D)
    strides = []
    for index in range(3):
        update_rms = jnp.sqrt(total(8 + index) / counts[index])
        strides.append(
            RATE * jnp.sqrt(total(15 + index) / counts[index])
            / jnp.maximum(1.0, update_rms / CLIP))
    stride = jnp.where(line < 6, strides[2], jnp.where(line < 8, strides[0], strides[1]))
    fresh = weight_small[...] - stride * update
    for values, (norm_ref, head_ref, ffn_ref) in (
        (grad, (norm_grad, head_grad, ffn_grad)),
        (second, (norm_second, head_second, ffn_second)),
        (fresh, (norm_new, head_new, ffn_new)),
    ):
        norm_ref[...] = values[0:6, 0:norm_ref.shape[1]]
        head_ref[...] = values[6:8, 0:head_ref.shape[1]]
        ffn_ref[...] = values[8:9, 0:ffn_ref.shape[0]].reshape(ffn_ref.shape)
    for copy in loads[8:]:
        copy.wait()


def step(reduced, lines, totals, weights, rows_old, cols_old, vectors, squares, passed):
    vmem, some = pl.BlockSpec(memory_space=pltpu.VMEM), pl.BlockSpec(memory_space=pl.ANY)
    small, grads = reduced[0], reduced[1:]
    shapes = [w.shape for w in weights] + [v.shape for v in vectors]
    shapes += [r.shape for r in rows_old] + [c.shape for c in cols_old]
    shapes += [v.shape for v in vectors] + [w.shape for w in weights] + [v.shape for v in vectors]
    outs = [jax.ShapeDtypeStruct(s, F32) for s in shapes]
    large = [*grads, *weights, *passed]
    operands = [small, lines, totals, *rows_old, *cols_old, *vectors, *squares]
    return pl.pallas_call(
        step_kernel,
        out_shape=outs + [jax.ShapeDtypeStruct(v.shape, v.dtype) for v in passed],
        in_specs=[some] * len(large) + [vmem] * len(operands),
        out_specs=[vmem] * (len(shapes) + len(passed)),
        scratch_shapes=[pltpu.VMEM(v.shape, F32) for v in [*grads, *weights]] + [
            pltpu.VMEM((16, 128), F32), pltpu.VMEM((16, 128), F32),
            pltpu.SemaphoreType.DMA((11,)),
        ],
        compiler_params=pltpu.CompilerParams(vmem_limit_bytes=60 << 20),
        name="adafactor_step",
    )(*large, *operands)


HALF = D // 2
QKV_HALF = 3 * HALF
VMEM = pl.BlockSpec(memory_space=pltpu.VMEM)
SMEM = pl.BlockSpec(memory_space=pltpu.SMEM)


def dot(a, b):
    return jnp.dot(a, b, preferred_element_type=F32)


def dot_last(a, b):
    return lax.dot_general(a, b, (((1,), (1,)), ((), ())), preferred_element_type=F32)


def dot_first(a, b):
    return lax.dot_general(a, b, (((0,), (0,)), ((), ())), preferred_element_type=F32)


def ids_at(lengths, row, places):
    bound = jnp.int32(0)
    ids = jnp.zeros(places.shape, jnp.int32)
    for segment in range(SEGS):
        bound = bound + lengths[row, segment]
        ids = ids + (places >= bound).astype(jnp.int32)
    return ids


def set_bias(bias, lengths, row):
    down = ids_at(lengths, row, lax.broadcasted_iota(jnp.int32, (LEN, 1), 0))
    across = ids_at(lengths, row, lax.broadcasted_iota(jnp.int32, (1, LEN), 1))
    bias[...] = jnp.where(down == across, 0.0, -1e30)


def half_masks():
    lane = lax.broadcasted_iota(jnp.int32, (1, 128), 1)
    return [((lane // HD) == half).astype(F32).astype(BF) for half in range(2)]


PAIR = 3 * 128


def slab(ref, core, row, part, pair):
    return ref[core, pl.ds(pl.multiple_of(row * LEN, LEN), LEN),
               pl.ds(pl.multiple_of(pair * PAIR + part * 128, 128), 128)]


def project(tokens, weight, offsets, qkv, row):
    rows = pl.ds(pl.multiple_of(row * LEN, LEN), LEN)
    values = tokens[rows, :]
    for core in range(2):
        for pair in range(3):
            cut = slice(pair * PAIR, (pair + 1) * PAIR)
            out = (dot(values, weight[core, :, cut]) + offsets[core, :, cut]).astype(BF)
            scale = jnp.where(
                lax.broadcasted_iota(jnp.int32, (1, PAIR), 1) < 128, HD ** -0.5, 1.0).astype(BF)
            qkv[core, rows, cut] = out * scale


def attend(qkv, bias, context, lse, held, row):
    rows = pl.ds(pl.multiple_of(row * LEN, LEN), LEN)
    lane = lax.broadcasted_iota(jnp.int32, (LEN, 128), 1)
    held[...] = jnp.zeros(held.shape, F32)

    @pl.loop(0, 6)
    def _(item):
        core, pair = item // 3, item % 3
        queries, keys, values = (slab(qkv, core, row, part, pair) for part in range(3))
        wide = jnp.concatenate([values, jnp.ones_like(values)], axis=1)
        outs = []
        logs = held[...]
        for half, mask in enumerate(half_masks()):
            scores = dot_last(queries * mask, keys) + bias[...]
            peak = jnp.max(scores, axis=1, keepdims=True)
            raised = jnp.exp(scores - peak).astype(BF)
            both = dot(raised, wide)
            total = both[:, 128:]
            outs.append(both[:, :128] / total)
            logs = jnp.where(lane == item * 2 + half, peak + jnp.log(total), logs)
        held[...] = logs
        context[rows, pl.ds(pl.multiple_of(item * 128, 128), 128)] = jnp.where(
            lane < HD, outs[0], outs[1]).astype(BF)

    lse[row] = held[...].T[0:16, :]


def forward_kernel(tokens, weight, offsets, lengths, qkv, context, lse, bias, held):
    core = lax.axis_index("mp")

    @pl.loop(0, 2)
    def _(row):
        set_bias(bias, lengths, core * 2 + row)
        project(tokens, weight, offsets, qkv, row)
        attend(qkv, bias, context, lse, held, row)


def forward(tokens, weight, offsets, lengths):
    count = tokens.shape[0]
    return pl.pallas_call(
        forward_kernel,
        out_shape=[
            jax.ShapeDtypeStruct((2, count, QKV_HALF), BF),
            jax.ShapeDtypeStruct((count, D), BF),
            jax.ShapeDtypeStruct((count // LEN, 16, LEN), F32),
        ],
        in_specs=[VMEM, VMEM, VMEM, SMEM],
        out_specs=[VMEM] * 3,
        scratch_shapes=[pltpu.VMEM((LEN, LEN), F32), pltpu.VMEM((LEN, 128), F32)],
        compiler_params=pltpu.CompilerParams(vmem_limit_bytes=56 << 20),
        name="project_attend",
    )(tokens, weight, offsets, lengths)


def gelu_both(inner):
    cdf = 0.5 * (1.0 + lax.erf(inner * 0.7071067811865476))
    density = 0.3989422804014327 * jnp.exp(-0.5 * inner * inner)
    return inner * cdf, cdf + inner * density


def norm_parts(values):
    center = values - jnp.mean(values, axis=-1, keepdims=True)
    scale = lax.rsqrt(jnp.mean(center * center, axis=-1, keepdims=True) + EPS_NORM)
    return center * scale, scale


def norm_back(grad, normed, scale, gain):
    scaled = grad * gain
    mean = jnp.mean(scaled, axis=-1, keepdims=True)
    along = jnp.mean(scaled * normed, axis=-1, keepdims=True)
    return (
        (scaled - mean - normed * along) * scale,
        jnp.sum(grad * normed, axis=0, keepdims=True),
        jnp.sum(grad, axis=0, keepdims=True),
    )


CHUNK = 512


def middle(row, core, tokens, context, cotangent, lengths, w_out, w_up, w_down, ffn, norm, layer_out,
           pooled, hidden_b, act, grad_branch, grad_inner, grad_attended, grad_context,
           grad_one, delta, norm_sums, ffn_sums, slope, branch, hidden, normed_one, grad_two):
    rows = pl.ds(pl.multiple_of(row * LEN, LEN), LEN)
    attended = dot(context[rows, :], w_out[...]) + norm[0:1, :]
    normed, scale_one = norm_parts(tokens[rows, :].astype(F32) + attended)
    normed_one[...] = normed
    value = normed * norm[2:3, :] + norm[3:4, :]
    hidden[...] = value
    hidden_b[rows, :] = value.astype(BF)
    branch[...] = jnp.zeros(branch.shape, F32)
    for chunk in range(FF // CHUNK):
        core_of, start = chunk * CHUNK // (FF // 2), chunk * CHUNK % (FF // 2)
        cols = slice(chunk * CHUNK, (chunk + 1) * CHUNK)
        up = w_up[core_of, :, start:start + CHUNK]
        value, slope_value = gelu_both(dot(hidden_b[rows, :], up) + ffn[:, cols])
        value = value.astype(BF)
        act[rows, cols] = value
        slope[:, cols] = slope_value.astype(BF)
        branch[...] += dot(value, w_down[cols, :])
    normed, scale = norm_parts(hidden[...] + branch[...] + norm[1:2, :])
    output = normed * norm[4:5, :] + norm[5:6, :]
    high = output.astype(BF)
    layer_out[rows, :] = high
    low = (output - high.astype(F32)).astype(BF)
    place = lax.broadcasted_iota(jnp.int32, (SEGS, LEN), 1)
    segment = lax.broadcasted_iota(jnp.int32, (SEGS, 1), 0)
    ids = ids_at(lengths, core * 2 + row, place)
    member = (ids == segment).astype(F32)
    sizes = jnp.sum(member, axis=1, keepdims=True)
    member = member.astype(BF)
    pooled[row] = (dot(member, high) + dot(member, low)) / sizes
    back, gain, shift = norm_back(cotangent[rows, :].astype(F32), normed, scale, norm[4:5, :])
    norm_sums[4:5, :] += gain
    norm_sums[5:6, :] += shift
    grad_two[...] = back
    back = back.astype(BF)
    grad_branch[rows, :] = back
    norm_sums[1:2, :] += jnp.sum(back.astype(F32), axis=0, keepdims=True)
    for chunk in range(FF // CHUNK):
        core_of, start = chunk * CHUNK // (FF // 2), chunk * CHUNK % (FF // 2)
        cols = slice(chunk * CHUNK, (chunk + 1) * CHUNK)
        value = dot_last(grad_branch[rows, :], w_down[cols, :])
        value = (value * slope[:, cols].astype(F32)).astype(BF)
        grad_inner[rows, cols] = value
        ffn_sums[:, cols] += jnp.sum(value.astype(F32), axis=0, keepdims=True)
        grad_two[...] += dot_last(value, w_up[core_of, :, start:start + CHUNK])
    back, gain, shift = norm_back(grad_two[...], normed_one[...], scale_one, norm[2:3, :])
    norm_sums[2:3, :] += gain
    norm_sums[3:4, :] += shift
    grad_one[rows, :] = back
    back = back.astype(BF)
    grad_attended[rows, :] = back
    norm_sums[0:1, :] += jnp.sum(back.astype(F32), axis=0, keepdims=True)
    back = dot_last(back, w_out[...]).astype(BF)
    grad_context[rows, :] = back
    product = back.astype(F32) * context[rows, :].astype(F32)
    high = product.astype(BF)
    low = (product - high.astype(F32)).astype(BF)
    head = lax.broadcasted_iota(jnp.int32, (16, D), 0)
    member = (lax.broadcasted_iota(jnp.int32, (16, D), 1) // HD == head).astype(F32).astype(BF)
    delta[row] = dot_last(member, high) + dot_last(member, low)


def middle_kernel(*refs):
    core = lax.axis_index("mp")
    norm_sums, ffn_sums = refs[19], refs[20]
    norm_sums[...] = jnp.zeros(norm_sums.shape, F32)
    ffn_sums[...] = jnp.zeros(ffn_sums.shape, F32)

    @pl.loop(0, 2)
    def _(row):
        middle(row, core, *refs)


def middle_call(tokens, context, cotangent, lengths, w_out, w_up, w_down, ffn, norm):
    count = tokens.shape[0]
    shape = jax.ShapeDtypeStruct
    return pl.pallas_call(
        middle_kernel,
        out_shape=[
            shape((count, D), BF),
            shape((count // LEN, SEGS, D), F32),
            shape((count, D), BF),
            shape((count, FF), BF),
            shape((count, D), BF),
            shape((count, FF), BF),
            shape((count, D), BF),
            shape((count, D), BF),
            shape((count, D), F32),
            shape((count // LEN, 16, LEN), F32),
            shape((8, D), F32),
            shape((1, FF), F32),
        ],
        in_specs=[VMEM] * 3 + [SMEM] + [VMEM] * 5,
        out_specs=[VMEM] * 12,
        scratch_shapes=[
            pltpu.VMEM((LEN, FF), BF),
            pltpu.VMEM((LEN, D), F32),
            pltpu.VMEM((LEN, D), F32),
            pltpu.VMEM((LEN, D), F32),
            pltpu.VMEM((LEN, D), F32),
        ],
        compiler_params=pltpu.CompilerParams(vmem_limit_bytes=60 << 20),
        name="feed_forward",
    )(tokens, context, cotangent, lengths, w_out, w_up, w_down, ffn, norm)


def weight_grads_kernel(context, hidden_b, act, grad_branch, grad_inner, grad_attended,
                        out_grad, up_grad, down_grad):

    @pl.loop(0, FF // CHUNK)
    def _(chunk):
        half_chunks = FF // 2 // CHUNK
        cols = pl.ds(pl.multiple_of(chunk * CHUNK, CHUNK), CHUNK)
        local = pl.ds(pl.multiple_of((chunk % half_chunks) * CHUNK, CHUNK), CHUNK)
        up_grad[chunk // half_chunks, :, local] = dot(hidden_b[...], grad_inner[:, cols]).astype(BF)
        down_grad[cols, :] = dot(act[cols, :], grad_branch[...]).astype(BF)

    value = dot(context[...], grad_attended[...])
    rows, held = D // out_grad.shape[0], out_grad.shape[1]
    for block in range(out_grad.shape[0]):
        piece = value[block * rows:(block + 1) * rows, :]
        if held > rows:
            piece = jnp.concatenate([piece, jnp.zeros((held - rows, D), F32)], axis=0)
        out_grad[block] = piece.astype(BF)


def weight_grads(context, hidden_b, act, grad_branch, grad_inner, grad_attended, blocks, held):
    shape = jax.ShapeDtypeStruct
    return pl.pallas_call(
        weight_grads_kernel,
        out_shape=[shape((blocks, held, D), BF), shape((2, D, FF // 2), BF), shape((FF, D), BF)],
        in_specs=[VMEM] * 6,
        out_specs=[VMEM] * 3,
        compiler_params=pltpu.CompilerParams(vmem_limit_bytes=60 << 20),
        name="weight_grads",
    )(context, hidden_b, act, grad_branch, grad_inner, grad_attended)


def attend_back(qkv, grad_context, lse, delta, bias, grad_qkv, grad_head, row):
    rows = pl.ds(pl.multiple_of(row * LEN, LEN), LEN)
    lane = lax.broadcasted_iota(jnp.int32, (LEN, 128), 1)

    @pl.loop(0, 6)
    def _(item):
        core, pair = item // 3, item % 3
        queries, keys, values = (slab(qkv, core, row, part, pair) for part in range(3))
        wide = pl.ds(pl.multiple_of(item * 128, 128), 128)
        grad = grad_context[rows, wide]
        flipped = keys.T
        grads_k, grads_v, grads_q = [], [], []
        for half, mask in enumerate(half_masks()):
            head = item * 2 + half
            scores = dot_last(keys * mask, queries) + bias[...] - lse[row, pl.ds(head, 1), :]
            probs = jnp.exp(scores)
            grad_probs = dot_last(values * mask, grad)
            grad_scores = (probs * (grad_probs - delta[row, pl.ds(head, 1), :])).astype(BF)
            grads_v.append(dot(probs.astype(BF), grad))
            grads_k.append(dot(grad_scores, queries))
            grads_q.append(dot(flipped[half * HD:(half + 1) * HD, :], grad_scores))
        grad_q = (jnp.concatenate(grads_q, axis=0).T * HD ** -0.5).astype(BF)
        grad_k = jnp.where(lane < HD, grads_k[0], grads_k[1]).astype(BF)
        grad_v = jnp.where(lane < HD, grads_v[0], grads_v[1]).astype(BF)
        for part, value in enumerate((grad_q, grad_k, grad_v)):
            grad_qkv[core, rows, pl.ds(pl.multiple_of(pair * PAIR + part * 128, 128), 128)] = value
        grad_head[0:1, wide] += jnp.sum(grad_q.astype(F32), axis=0, keepdims=True)
        grad_head[1:2, wide] += jnp.sum(grad_v.astype(F32), axis=0, keepdims=True)


def backward_kernel(tokens, qkv, grad_context, lse, delta, lengths, weight, grad_one,
                    qkv_grad, input_grad, grad_head, grad_qkv, bias):
    core = lax.axis_index("mp")
    grad_head[...] = jnp.zeros(grad_head.shape, F32)

    @pl.loop(0, 2)
    def _(row):
        set_bias(bias, lengths, core * 2 + row)
        attend_back(qkv, grad_context, lse, delta, bias, grad_qkv, grad_head, row)
        rows = pl.ds(pl.multiple_of(row * LEN, LEN), LEN)
        input_grad[rows, :] = (
            grad_one[rows, :]
            + dot_last(grad_qkv[0, rows, :], weight[0])
            + dot_last(grad_qkv[1, rows, :], weight[1])
        )

    for core_of in range(2):
        for part in range(3):
            cut = slice(part * HALF, (part + 1) * HALF)
            qkv_grad[core_of, :, cut] = dot(tokens[...], grad_qkv[core_of, :, cut]).astype(BF)


def backward(tokens, qkv, grad_context, lse, delta, lengths, weight, grad_one):
    count = tokens.shape[1]
    shape = jax.ShapeDtypeStruct
    return pl.pallas_call(
        backward_kernel,
        out_shape=[shape((2, D, QKV_HALF), BF), shape((count, D), F32), shape((2, D), F32)],
        in_specs=[VMEM] * 5 + [SMEM] + [VMEM] * 2,
        out_specs=[VMEM] * 3,
        scratch_shapes=[
            pltpu.VMEM((2, count, QKV_HALF), BF),
            pltpu.VMEM((LEN, LEN), F32),
        ],
        compiler_params=pltpu.CompilerParams(vmem_limit_bytes=60 << 20),
        name="attend_back",
    )(tokens, qkv, grad_context, lse, delta, lengths, weight, grad_one)


UP_CHUNK = 512
DOWN_CHUNK = 256


class Spread:
    def __init__(self, place, full, start, width, flip, orders, sems, base):
        self.place, self.full = place, full
        self.cols = pl.ds(start, width)
        tiles = width // 128
        cut = (tiles // 2 if flip else tiles - tiles // 2) * 128
        self.halves = [(orders[0], pl.ds(start, cut))]
        if cut < width:
            self.halves.append((orders[1], pl.ds(start + cut, width - cut)))
        self.sems, self.base, self.slots = sems, base, {}
        self.count = sum(len(self.copies(stage)) for stage in range(4))

    def view(self, spot, cols):
        return self.full.at[spot["m"], spot["z"], spot["y"], spot["x"], :, cols]

    def copy(self, key, axis, step, spot, cols):
        place = self.place
        slot = self.base + self.slots.setdefault(key, len(self.slots))
        send, recv = self.sems
        send, recv = send.at[slot], recv.at[slot]
        device = place.device(place.at(axis, step))
        view = self.view(spot, cols)
        sent = pltpu.make_async_remote_copy(
            view, view, send, recv, device_id=device, device_id_type=MESH)
        land = dict(spot)
        land[axis] = place.at(axis, -step)[axis]
        land = self.view(land, cols)
        arrives = pltpu.make_async_remote_copy(
            land, land, send, recv, device_id=device, device_id_type=MESH)
        return sent, arrives

    def copies(self, stage):
        place = self.place
        here = {"z": place.z, "y": place.y, "x": place.x, "m": place.m}
        if stage == 3:
            here["z"] = here["y"] = here["x"] = EVERY
            return [self.copy((3, 0, 1), "m", 1, here, self.cols)]
        halves = self.halves
        if stage == 0 and halves[0][0][0] == "z":
            halves = [(halves[0][0], self.cols)]
        out = []
        for number, (order, cols) in enumerate(halves):
            spot = dict(here)
            for axis in order[:stage]:
                spot[axis] = EVERY
            for step in steps_of(order[stage]):
                out.append(self.copy((stage, number, step), order[stage], step, spot, cols))
        return out

    def start(self, stage):
        for sent, _ in self.copies(stage):
            sent.start()

    def arrived(self, stage):
        for _, arrives in self.copies(stage):
            arrives.wait_recv()

    def finish(self):
        for stage in range(4):
            for sent, _ in self.copies(stage):
                sent.wait_send()


def spread(groups, *moves):
    for group, stage in moves:
        for chunk in groups[group]:
            if stage:
                chunk.arrived(stage - 1)
            chunk.start(stage)


def unpack_small(small, norm_out, offsets, ffn_out):
    iota = lambda shape, axis: lax.broadcasted_iota(jnp.int32, shape, axis)
    pick = ((iota((128, D), 1) % 24 == iota((128, D), 0))).astype(F32).astype(BF)
    pick_ffn = ((iota((128, FF), 1) % 96 == iota((128, FF), 0))).astype(F32).astype(BF)
    total = jnp.zeros((16, D), F32)
    ffn = jnp.zeros((1, FF), F32)
    line, col = iota((256, D), 0), iota((256, D), 1) // 24
    device, kind = line // 16, line % 16
    for core in range(2):
        block = small[core].reshape(256, 128).astype(BF)
        wide = dot(block, pick)
        right = jnp.where(kind < 6, 2 * device + core, 16 * core + device)
        wide = jnp.where((col == right) & (kind < 8), wide, 0.0)
        total = total + jnp.sum(wide.reshape(16, 16, D), axis=0)
        wide = dot(small[core, :, :, :, 8, :].reshape(16, 128).astype(BF), pick_ffn)
        right = iota((16, FF), 1) // 96 == iota((16, FF), 0) + 16 * core
        ffn = ffn + jnp.sum(jnp.where(right, wide, 0.0), axis=0, keepdims=True)
    norm_out[0:6, :] = total[0:6, :]
    norm_out[6:8, :] = jnp.zeros((2, D), F32)
    ffn_out[...] = ffn
    offsets[...] = jnp.zeros(offsets.shape, F32)
    for core in range(2):
        for pair in range(3):
            source = core * HALF + pair * 128
            for part, row in ((0, 6), (2, 7)):
                start = pair * PAIR + part * 128
                offsets[core, :, start:start + 128] = total[row:row + 1, source:source + 128]


def place_of(core, part, width):
    return pl.ds(pl.multiple_of(core * PAIR + part * 128, 128), width)


def trio(ref, core, row, part, pair):
    return ref[pair, pl.ds(pl.multiple_of(row * LEN, LEN), LEN), place_of(core, part, 128)]


def project_pair(tokens, weight, offsets, qkv, pair):
    cols = pl.ds(pl.multiple_of(pair * PAIR, PAIR), PAIR)
    scale = jnp.where(
        lax.broadcasted_iota(jnp.int32, (1, PAIR), 1) < 128, HD ** -0.5, 1.0).astype(BF)
    for core in range(2):
        piece = weight[core, :, :, :, :, cols].reshape(D, PAIR)
        out = dot(tokens[...], piece) + offsets[core, :, cols]
        qkv[pair, :, place_of(core, 0, PAIR)] = out.astype(BF) * scale


def attend_pair(qkv, bias, probs, flip, core, row, pair):
    item = core * 3 + pair
    queries, keys, values = (trio(qkv, core, row, part, pair) for part in range(3))
    flipped = values.T
    cols = pl.ds(pl.multiple_of(row * LEN, LEN), LEN)
    for half, mask in enumerate(half_masks()):
        scores = dot_last(keys * mask, queries) + bias[row]
        raised = jnp.exp(scores - jnp.max(scores, axis=0, keepdims=True))
        share = (raised * (1.0 / jnp.sum(raised, axis=0, keepdims=True))).astype(BF)
        probs[half] = share
        lines = pl.ds(pl.multiple_of(item * 128 + half * HD, HD), HD)
        flip[lines, cols] = dot(flipped[half * HD:(half + 1) * HD, :], share).astype(BF)


FEED_MOVES = (
    ((8, 2),), ((9, 2),), (), ((6, 3),), ((7, 3),), ((8, 3),),
)


def forward_gather_kernel(*refs):
    refs = list(refs)
    take = lambda number: [refs.pop(0) for _ in range(number)]
    w_qkv, w_out, w_up, w_down, head, ffn, norm, lengths = take(8)
    tokens_any, cotangent_any = take(2)
    (sums, norm_out, ffn_out, hidden_scale, out_full, pooled, norm_sums) = take(7)
    (qkv_full, up_full, down_full, qkv_out, context_flip, token_flip, hidden_flip, normed_out,
     context_out, act_flip, slope_out, layer_out, branch_out, grad_two_out, probs_out) = take(15)
    (g_small, g_qkv, g_out, g_up, g_down, tokens, qkv, context, flip,
     hidden_b, normed_one, act, slope, flip_act, bias, probs, offsets, branch, flip_context) = take(19)
    send, recv, local = refs
    place = Place()
    greet(place)
    here = (place.m, place.z, place.y, place.x)
    used = [0]
    unwaited = []

    def keep(source, target):
        copy = pltpu.make_async_copy(source, target, local.at[used[0]])
        used[0] += 1
        copy.start()
        unwaited.append(copy)
        return copy

    def done(copy):
        copy.wait()
        unwaited[:] = [other for other in unwaited if other is not copy]

    tokens_loaded = keep(tokens_any, tokens)
    place_small(g_small.at[here], norm[...], head[...], as_row(ffn), 0.0)
    for part in range(3):
        for pair in range(3):
            start = pair * PAIR + part * 128
            g_qkv[here + (EVERY, slice(start, start + 128))] = w_qkv[
                part, :, pair * 128:(pair + 1) * 128].astype(BF)
    value = w_out[...]
    spare = g_out.shape[4] - value.shape[0]
    g_out[here] = jnp.concatenate([value, jnp.zeros((spare, D), F32)], axis=0).astype(BF)
    g_up[here] = w_up[...].astype(BF)
    g_down[here] = w_down[...].astype(BF)
    sems, base = (send, recv), [0]

    def chunk(full, start, width, flip=False, orders=("zxy", "zyx")):
        made = Spread(place, full, start, width, flip, orders, sems, base[0])
        base[0] += made.count
        return made

    groups = [[chunk(g_small, 0, 128), chunk(g_qkv, 0, PAIR)]]
    groups += [[chunk(g_qkv, pair * PAIR, PAIR, pair == 1)] for pair in (1, 2)]
    groups += [[chunk(g_out, 0, D)]]
    groups += [[chunk(g_up, at, UP_CHUNK)] for at in range(0, FF // 2, UP_CHUNK)]
    groups += [[chunk(g_down, at, DOWN_CHUNK)] for at in range(0, D, DOWN_CHUNK)]

    def ready(index):
        for made in groups[index]:
            made.arrived(3)

    meet()
    spread(groups, (0, 0), (1, 0))
    sums[...] = weight_sums_of([w_qkv, w_out, w_up, w_down], g_small[here])
    for row in range(2):
        set_bias(bias.at[row], lengths, place.m * 2 + row)
    done(tokens_loaded)
    flip[...] = tokens[...].T
    flip_kept = keep(flip, token_flip)
    spread(groups, (0, 1), (2, 0))
    spread(groups, (1, 1), (3, 0))
    spread(groups, (0, 2))
    spread(groups, (2, 1), (4, 0))
    spread(groups, (1, 2))
    spread(groups, (0, 3), (3, 1), (5, 0))
    ready(0)
    unpack_small(g_small, norm_out, offsets, ffn_out)

    @pl.loop(0, 12)
    def _(item):
        pair, row, core = item // 4, (item % 4) // 2, item % 2
        for at, moves in (
            (1, ((3, 2), (5, 1), (7, 0))),
            (4, ((2, 3),)),
            (6, ((7, 1), (9, 0))),
            (7, ((3, 3),)),
            (9, ((9, 1),)),
            (10, ((4, 3),)),
            (11, ((6, 2),)),
        ):
            @pl.when(item == at)
            def _():
                spread(groups, *moves)

        for at in (4, 8):
            @pl.when(item == at)
            def _():
                ready(at // 4)

        @pl.when(item % 4 == 0)
        def _():
            project_pair(tokens, g_qkv, offsets, qkv, pair)

        for at, moves in (
            (0, ((1, 3), (2, 2), (4, 1), (6, 0))),
            (4, ((4, 2), (6, 1), (8, 0))),
            (8, ((5, 2), (8, 1))),
        ):
            @pl.when(item == at)
            def _():
                spread(groups, *moves)

        def probs_copy(number):
            return pltpu.make_async_copy(
                probs.at[number % 2], probs_out.at[number], local.at[28 + number % 2])

        @pl.when(item >= 2)
        def _():
            probs_copy(item - 2).wait()

        attend_pair(qkv, bias, probs.at[item % 2], flip_context, core, row, pair)
        probs_copy(item).start()

    spread(groups, (7, 2))
    for core in range(2):
        for pair in range(3):
            cols = slice(pair * PAIR, (pair + 1) * PAIR)
            keep(g_qkv.at[core, :, :, :, :, cols],
                 qkv_full.at[pair, :, :, :, :, core * PAIR:(core + 1) * PAIR])
    keep(qkv, qkv_out)
    keep(flip_context, context_flip)
    context[...] = flip_context[...].T
    context_kept = keep(context, context_out)
    for slot in range(2):
        unwaited.append(
            pltpu.make_async_copy(probs.at[slot], probs_out.at[10 + slot], local.at[28 + slot]))
    ready(3)
    rows_out = w_out.shape[0]
    for core in range(2):
        value = g_out[core].reshape(16, g_out.shape[4], D).astype(F32)[:, :rows_out]
        out_full[core * HALF:(core + 1) * HALF, :] = value.reshape(HALF, D).astype(BF)
    halves = [slice(row * LEN, (row + 1) * LEN) for row in range(2)]
    for number, rows in enumerate(halves):
        attended = dot(context[rows, :], out_full[...]) + norm_out[0:1, :]
        normed, scale = norm_parts(tokens[rows, :].astype(F32) + attended)
        normed_one[rows, :] = normed
        hidden_scale[rows, :] = jnp.broadcast_to(scale, (LEN, 128))
        hidden_b[rows, :] = (normed * norm_out[2:3, :] + norm_out[3:4, :]).astype(BF)
        spread(groups, *(((), ((5, 3),)))[number])
    cotangent_loaded = keep(cotangent_any, tokens)
    keep(normed_one, normed_out)
    waiting = [[], []]
    for third in range(3):
        ready(4 + third)
        for core in range(2):
            for copy in waiting[core]:
                copy.wait()
            local_cols = slice(third * UP_CHUNK, (third + 1) * UP_CHUNK)
            start = core * (FF // 2) + third * UP_CHUNK
            cols = pl.ds(start, UP_CHUNK)
            up = g_up[core, :, :, :, :, local_cols].reshape(D, UP_CHUNK)

            @pl.loop(0, 2)
            def _(row):
                rows = pl.ds(pl.multiple_of(row * LEN, LEN), LEN)
                value, slope_value = gelu_both(
                    dot(hidden_b[rows, :], up) + ffn_out[:, start:start + UP_CHUNK])
                act[rows, cols] = value.astype(BF)
                slope[core, rows, :] = slope_value.astype(BF)

            flip_act[core] = act[:, cols].T
            slot = 24 + 2 * core
            waiting[core] = [
                pltpu.make_async_copy(slope.at[core], slope_out.at[:, cols], local.at[slot]),
                pltpu.make_async_copy(flip_act.at[core], act_flip.at[cols, :], local.at[slot + 1]),
            ]
            for copy in waiting[core]:
                copy.start()
            spread(groups, *FEED_MOVES[2 * third + core])
    done(flip_kept)
    flip[...] = hidden_b[...].T
    keep(flip, hidden_flip)
    for core in range(2):
        keep(g_up.at[core], up_full.at[core])
    for third in range(3):
        if third == 1:
            spread(groups, (9, 3))
        ready(7 + third)
        cols = slice(third * DOWN_CHUNK, (third + 1) * DOWN_CHUNK)
        down = g_down[:, :, :, :, :, cols].reshape(FF, DOWN_CHUNK)
        for rows in halves:
            branch[rows, cols] = dot(act[rows, :], down)
    for core in range(2):
        keep(g_down.at[core], down_full.at[core])
    norm_sums[...] = jnp.zeros(norm_sums.shape, F32)
    done(cotangent_loaded)
    done(context_kept)
    for row, rows in enumerate(halves):
        hidden = normed_one[rows, :] * norm_out[2:3, :] + norm_out[3:4, :]
        normed, scale = norm_parts(hidden + branch[rows, :] + norm_out[1:2, :])
        output = normed * norm_out[4:5, :] + norm_out[5:6, :]
        high = output.astype(BF)
        context[rows, :] = high
        keep(context.at[rows], layer_out.at[rows])
        low = (output - high.astype(F32)).astype(BF)
        spots = lax.broadcasted_iota(jnp.int32, (SEGS, LEN), 1)
        segment = lax.broadcasted_iota(jnp.int32, (SEGS, 1), 0)
        member = (ids_at(lengths, place.m * 2 + row, spots) == segment).astype(F32)
        sizes = jnp.sum(member, axis=1, keepdims=True)
        member = member.astype(BF)
        pooled[row] = (dot(member, high) + dot(member, low)) / sizes
        back, gain, shift = norm_back(tokens[rows, :].astype(F32), normed, scale, norm_out[4:5, :])
        norm_sums[4:5, :] += gain
        norm_sums[5:6, :] += shift
        branch[rows, :] = back
        keep(branch.at[rows], grad_two_out.at[rows])
        back = back.astype(BF)
        hidden_b[rows, :] = back
        keep(hidden_b.at[rows], branch_out.at[rows])
        norm_sums[1:2, :] += jnp.sum(back.astype(F32), axis=0, keepdims=True)
    for copy in unwaited + waiting[0] + waiting[1]:
        copy.wait()
    for group in groups:
        for made in group:
            made.finish()


def forward_gather(weights, vectors, lengths, tokens, cotangent):
    qkv, out, up, down = weights
    count = tokens.shape[0]
    shape = jax.ShapeDtypeStruct
    grid = (2, 4, 2, 2)
    rows = count // LEN
    flipped = shape((D, count), BF)
    small_outs = [
        shape((8, 128), F32), shape((8, D), F32), shape((1, FF), F32),
        shape((count, 128), F32), shape((D, D), BF), shape((rows, SEGS, D), F32), shape((8, D), F32),
    ]
    large_outs = [
        shape((3,) + grid[1:] + (qkv.shape[1], D), BF), shape(grid + up.shape, BF),
        shape(grid + down.shape, BF), shape((3, count, D), BF), flipped, flipped, flipped,
        shape((count, D), F32), shape((count, D), BF), shape((FF, count), BF),
        shape((count, FF), BF), shape((count, D), BF), shape((count, D), BF), shape((count, D), F32),
        shape((6 * rows, 2, LEN, LEN), BF),
    ]
    slots = 88
    some = pl.BlockSpec(memory_space=pl.ANY)
    return pl.pallas_call(
        forward_gather_kernel,
        out_shape=small_outs + large_outs,
        in_specs=[VMEM] * 7 + [SMEM] + [some] * 2,
        out_specs=[VMEM] * len(small_outs) + [some] * len(large_outs),
        scratch_shapes=[
            pltpu.VMEM(grid + (16, 128), F32),
            pltpu.VMEM(grid + (qkv.shape[1], QKV_HALF), BF),
            pltpu.VMEM(grid + (32, D), BF),
            pltpu.VMEM(grid + up.shape, BF),
            pltpu.VMEM(grid + down.shape, BF),
            pltpu.VMEM((count, D), BF),
            pltpu.VMEM((3, count, D), BF),
            pltpu.VMEM((count, D), BF),
            pltpu.VMEM((D, count), BF),
            pltpu.VMEM((count, D), BF),
            pltpu.VMEM((count, D), F32),
            pltpu.VMEM((count, FF), BF),
            pltpu.VMEM((2, count, UP_CHUNK), BF),
            pltpu.VMEM((2, UP_CHUNK, count), BF),
            pltpu.VMEM((2, LEN, LEN), F32),
            pltpu.VMEM((2, 2, LEN, LEN), BF),
            pltpu.VMEM((2, 1, QKV_HALF), F32),
            pltpu.VMEM((count, D), F32),
            pltpu.VMEM((D, count), BF),
            pltpu.SemaphoreType.DMA((slots,)),
            pltpu.SemaphoreType.DMA((slots,)),
            pltpu.SemaphoreType.DMA((30,)),
        ],
        compiler_params=pltpu.CompilerParams(
            collective_id=0, has_side_effects=True, vmem_limit_bytes=61 << 20),
        name="forward_gather",
    )(*weights, *vectors, lengths, tokens, cotangent)


class Collect:
    COUNT = 7

    def __init__(self, place, held, slots, result, start, width, flip, sems, base, layer=None,
                 stages=(0, 2)):
        self.place, self.held, self.slots, self.result = place, held, slots, result
        self.layer, self.stages = layer, stages
        self.cols = pl.ds(start, width)
        tiles = width // 128
        cut = (tiles // 2 if flip else tiles - tiles // 2) * 128
        self.halves = [("xy", pl.ds(start, cut))]
        if cut < width:
            self.halves.append(("yx", pl.ds(start + cut, width - cut)))
        self.sems, self.base = sems, base

    def copy(self, slot, axis, step, source, target):
        send, recv = self.sems
        return pltpu.make_async_remote_copy(
            source, target, send.at[self.base + slot], recv.at[self.base + slot],
            device_id=self.place.device(self.place.at(axis, step)), device_id_type=MESH)

    def copies(self, stage):
        place = self.place
        if stage == 2:
            out = []
            for step in (1, 2, 3):
                source = self.held.at[place.at("z", step)["z"], place.y, place.x, :, self.cols]
                out.append(self.copy(
                    step - 1, "z", step, source, self.slots[2].at[step - 1, :, self.cols]))
            return out
        out = []
        for number, (order, cols) in enumerate(self.halves):
            axis = order[stage]
            spot = {"y": EVERY, "x": EVERY}
            if stage == 1:
                spot[order[0]] = getattr(place, order[0])
            spot[axis] = place.at(axis, 1)[axis]
            layer = EVERY if self.layer is None else self.layer
            land = (layer,) + (EVERY,) * (1 - stage) + (EVERY, cols)
            out.append(self.copy(
                2 * stage + number + (0 if self.layer is not None else 3), axis, 1,
                self.held.at[layer, spot["y"], spot["x"], :, cols], self.slots[stage].at[land]))
        return out

    def start(self, stage):
        for sent in self.copies(stage):
            sent.start()

    def add(self, stage):
        place, held, slots = self.place, self.held, self.slots[stage]
        for sent in self.copies(stage):
            sent.wait_recv()
        if stage == 2:
            value = held[place.z, place.y, place.x, :, self.cols].astype(F32)
            for step in range(3):
                value = value + slots[step, :, self.cols].astype(F32)
            self.result[:, self.cols] = value[:self.result.shape[0]]
            return
        for order, cols in self.halves:

            layers = 4 if self.layer is None else 1

            @pl.loop(0, layers * (2 - stage))
            def _(index):
                spot = {"y": place.y, "x": place.x}
                if stage == 0:
                    layer = index // 2 if self.layer is None else self.layer
                    spot[order[1]] = index % 2
                    arrived = slots[layer, index % 2, :, cols]
                else:
                    layer = index if self.layer is None else self.layer
                    arrived = slots[layer, :, cols]
                at = (layer, spot["y"], spot["x"], EVERY, cols)
                held[at] = (held[at].astype(F32) + arrived.astype(F32)).astype(held.dtype)

    def finish(self):
        for stage in range(self.stages[0], self.stages[1] + 1):
            for sent in self.copies(stage):
                sent.wait_send()


def advance(groups, *moves):
    for group, stage in moves:
        for chunk in groups[group]:
            if stage > chunk.stages[0]:
                chunk.add(stage - 1)
            if stage <= chunk.stages[1]:
                chunk.start(stage)


def split_dot(value, other):
    high = value.astype(BF)
    return dot(high, other) + dot((value - high.astype(F32)).astype(BF), other)


def picks(count, width):
    shape = (count, 128)
    lane = lax.broadcasted_iota(jnp.int32, shape, 0) % width
    return (lane == lax.broadcasted_iota(jnp.int32, shape, 1)).astype(F32).astype(BF)


def pack_rows(rows, right):
    rows = jnp.broadcast_to(rows[None], (16, 8, D)).reshape(128, D)
    iota = lambda axis: lax.broadcasted_iota(jnp.int32, (128, D), axis)
    rows = jnp.where(iota(1) // 24 == right(iota(0) // 8), rows, 0.0)
    return split_dot(rows, picks(D, 24)).reshape(4, 2, 2, 8, 128)


def pack_small(target, core, norm_sums, ffn_sums):
    target[:, :, :, 0:8, :] = pack_rows(norm_sums[...], lambda device: 2 * device + core)
    iota = lambda axis: lax.broadcasted_iota(jnp.int32, (16, FF), axis)
    ffn = jnp.where(iota(1) // 96 == iota(0) + 16 * core, ffn_sums[...], 0.0)
    target[:, :, :, 8:16, :] = jnp.zeros((4, 2, 2, 8, 128), F32)
    target[:, :, :, 8, :] = split_dot(ffn, picks(FF, 96)).reshape(4, 2, 2, 128)


def pack_heads(core, grad_head):
    return pack_rows(grad_head[...], lambda device: 16 * core + device)


def attend_back_pair(qkv, grad_context, probs, delta, grad_head, core, row, pair):
    lane = lax.broadcasted_iota(jnp.int32, (LEN, 128), 1)
    item = core * 3 + pair
    queries, keys, values = (trio(qkv, core, row, part, pair) for part in range(3))
    rows = pl.ds(pl.multiple_of(row * LEN, LEN), LEN)
    wide = pl.ds(pl.multiple_of(item * 128, 128), 128)
    grad = grad_context[rows, wide]
    flipped = keys.T
    grads_k, grads_v, grads_q = [], [], []
    for half, mask in enumerate(half_masks()):
        share = probs[half]
        grad_probs = dot_last(values * mask, grad) - delta[row, pl.ds(item * 2 + half, 1), :]
        grad_scores = (share.astype(F32) * grad_probs).astype(BF)
        grads_v.append(dot(share, grad))
        grads_k.append(dot(grad_scores, queries))
        grads_q.append(dot(flipped[half * HD:(half + 1) * HD, :], grad_scores))
    grad_q = (jnp.concatenate(grads_q, axis=0).T * HD ** -0.5).astype(BF)
    grad_k = jnp.where(lane < HD, grads_k[0], grads_k[1]).astype(BF)
    grad_v = jnp.where(lane < HD, grads_v[0], grads_v[1]).astype(BF)
    for part, value in enumerate((grad_q, grad_k, grad_v)):
        qkv[pair, rows, place_of(core, part, 128)] = value
    grad_head[0:1, wide] += jnp.sum(grad_q.astype(F32), axis=0, keepdims=True)
    grad_head[1:2, wide] += jnp.sum(grad_v.astype(F32), axis=0, keepdims=True)


def backward_scatter_kernel(*refs):
    refs = list(refs)
    take = lambda number: [refs.pop(0) for _ in range(number)]
    norm_given, norm = take(2)
    rows_old, cols_old = take(4), take(4)
    head_sq, ffn_sq, norm_sq, weight_sums = take(4)
    (act_any, branch_any, down_any, slope_any, up_any, two_any, normed_any, hidden_any, context_any,
     flip_any, token_any, qkv_any, weight_any, probs_any, scale_any, out_any) = take(16)
    results = take(5)
    lines, totals, input_any = take(3)
    held, other = take(6), take(6)
    slots = [take(3) for _ in range(6)]
    heads_sum = refs.pop(0)
    (wide, flip, flip_context, context, attended, qkv, weight, one, two, act, inner, probs, delta,
     grad_head, norm_sums, ffn_sums, scale_one, w_out) = take(18)
    (mine_early, plane_early, line_early, mine_one, land_one, mine_two, land_two, old_small) = take(8)
    send, recv, local = refs
    place = Place()
    greet_all()
    sems = (send, recv)
    partner = place.device(place.at("m", 1))
    mine, theirs = place.m, 1 - place.m
    loaded = {}

    def load(name, source, target):
        copy = pltpu.make_async_copy(source, target, local.at[len(loaded)])
        copy.start()
        loaded[name] = copy

    tile_rows = FF // 2 // 4
    act_slots, chunk_slots = 16, 18

    def act_load(index):
        core = jnp.where(index < 4, theirs, mine)
        start = pl.multiple_of(core * (FF // 2) + (index % 4) * tile_rows, tile_rows)
        return pltpu.make_async_copy(
            act_any.at[pl.ds(start, tile_rows)], act.at[index % 2], local.at[act_slots + index % 2])

    def down_tile(index):
        return qkv.at[0, pl.ds(pl.multiple_of(index % 2 * UP_CHUNK, UP_CHUNK), UP_CHUNK)]

    def slope_tile(index):
        return qkv.at[1 + index % 2, :, pl.ds(0, UP_CHUNK)]

    def up_tile(index):
        return weight.at[index % 2, :, pl.ds(0, UP_CHUNK)]

    def chunk_loads(index):
        core = jnp.where(index < 3, theirs, mine)
        inside = pl.ds(pl.multiple_of(index % 3 * UP_CHUNK, UP_CHUNK), UP_CHUNK)
        whole = pl.ds(
            pl.multiple_of(core * (FF // 2) + index % 3 * UP_CHUNK, UP_CHUNK), UP_CHUNK)
        slot = chunk_slots + 3 * (index % 2)
        return [
            pltpu.make_async_copy(down_any.at[whole], down_tile(index), local.at[slot]),
            pltpu.make_async_copy(slope_any.at[:, whole], slope_tile(index), local.at[slot + 1]),
            pltpu.make_async_copy(up_any.at[core, :, inside], up_tile(index), local.at[slot + 2]),
        ]

    load("branch", branch_any, wide)
    for index in range(2):
        act_load(index).start()

    small, qkv_held, out_held, up_held, down_held, heads = held
    small_other, qkv_other, out_other, up_other, down_other, heads_other = other
    base = 13

    def swap(slot, source, target):
        return pltpu.make_async_remote_copy(
            source, target, send.at[slot], recv.at[slot],
            device_id=partner, device_id_type=MESH)

    def down_swap(layer):
        return swap(layer, down_held.at[layer], down_other.at[layer])

    def up_swap(third):
        cols = pl.ds(pl.multiple_of(third * UP_CHUNK, UP_CHUNK), UP_CHUNK)
        at = (EVERY, EVERY, EVERY, EVERY, cols)
        return swap(4 + third, up_held.at[at], up_other.at[at])

    def qkv_swap(pair):
        at = (EVERY, EVERY, EVERY, EVERY, pl.ds(pl.multiple_of(pair * PAIR, PAIR), PAIR))
        return swap(8 + pair, qkv_held.at[at], qkv_other.at[at])

    out_swap = swap(7, out_held, out_other)
    small_swap = swap(11, small, small_other)
    heads_swap = swap(12, heads, heads_other)
    widths = (128, PAIR, D, UP_CHUNK, DOWN_CHUNK, 128)
    chunks = [[] for _ in range(6)]
    targets = results + [heads_sum]

    def collect(index, start, width, flip=False, layer=None, stages=(0, 2), count=Collect.COUNT):
        nonlocal base
        made = Collect(place, held[index], slots[index], targets[index], start, width, flip, sems,
                       base, layer, stages)
        base += count
        return made

    groups = [[collect(4, 0, D, layer=z, stages=(0, 1), count=4)] for z in range(4)]
    groups += [[collect(4, 0, D, stages=(2, 2), count=3)]]
    for index in (3, 2, 1):
        for start in range(0, held[index].shape[4], widths[index]):
            groups.append([collect(index, start, widths[index], index == 1 and start == PAIR)])
    groups[8].append(collect(0, 0, 128))
    groups.append([collect(5, 0, 128)])
    norm_sums[...] = norm_given[...]
    loaded["branch"].wait()
    meet_all()

    def down_tile_of(index):
        act_load(index).wait()
        value = dot(act[index % 2], wide[...]).reshape(2, 2, tile_rows // 4, D)

        @pl.when(index < 6)
        def _():
            act_load(index + 2).start()

        return value

    @pl.loop(0, 4)
    def _(layer):
        down_held[layer] = down_tile_of(layer).astype(BF)
        down_swap(layer).start()

    load("hidden", hidden_any, flip)
    for index in range(2):
        for copy in chunk_loads(index):
            copy.start()
    load("two", two_any, two)
    load("normed", normed_any, one)
    load("context", context_any, context)
    load("flip", flip_any, flip_context)
    load("scale", scale_any, scale_one)
    load("out", out_any, w_out)

    @pl.loop(0, 4)
    def _(layer):
        value = down_tile_of(layer + 4)
        down_swap(layer).wait()
        down_held[layer] = (value + down_other[layer].astype(F32)).astype(BF)
        for at, moves in ((0, ((0, 0),)), (2, ((1, 0),))):
            @pl.when(layer == at)
            def _():
                advance(groups, *moves)

    loaded["hidden"].wait()
    loaded["two"].wait()

    def feed_back(index):
        for copy in chunk_loads(index):
            copy.wait()
        core = jnp.where(index < 3, theirs, mine)
        whole = pl.ds(
            pl.multiple_of(core * (FF // 2) + index % 3 * UP_CHUNK, UP_CHUNK), UP_CHUNK)
        value = dot_last(wide[...], down_tile(index)[...])
        value = (value * slope_tile(index)[...].astype(F32)).astype(BF)
        inner[...] = value
        ffn_sums[:, whole] = jnp.sum(value.astype(F32), axis=0, keepdims=True)
        two[...] += dot_last(inner[...], up_tile(index)[...])
        return dot(flip[...], inner[...]).reshape(4, 2, 2, D // 16, UP_CHUNK)

    @pl.loop(0, 3)
    def _(third):
        cols = pl.ds(pl.multiple_of(third * UP_CHUNK, UP_CHUNK), UP_CHUNK)
        up_held[:, :, :, :, cols] = feed_back(third).astype(BF)
        up_swap(third).start()
        for copy in chunk_loads(third + 2):
            copy.start()

        for at, moves in (
            (0, ((2, 0),)),
            (1, ((0, 1), (3, 0))),
            (2, ((1, 1),)),
        ):
            @pl.when(third == at)
            def _():
                advance(groups, *moves)

    @pl.loop(0, 3)
    def _(third):
        at = (EVERY, EVERY, EVERY, EVERY,
              pl.ds(pl.multiple_of(third * UP_CHUNK, UP_CHUNK), UP_CHUNK))
        value = feed_back(third + 3)
        up_swap(third).wait()
        up_held[at] = (value + up_other[at].astype(F32)).astype(BF)

        @pl.when(third == 0)
        def _():
            for copy in chunk_loads(5):
                copy.start()

        for spot, moves in (
            (0, ((0, 2), (2, 1), (5, 0))),
            (1, ((3, 1),)),
            (2, ((1, 2), (2, 2), (6, 0))),
        ):
            @pl.when(third == spot)
            def _():
                advance(groups, *moves)

    def probs_load(item):
        pair, row = item // 4, item % 2
        core = jnp.where(item % 4 < 2, theirs, mine)
        return pltpu.make_async_copy(
            probs_any.at[pair * 4 + row * 2 + core], probs.at[item % 2], local.at[24 + item % 2])

    for item in range(2):
        probs_load(item).start()
    load("token", token_any, flip)
    load("qkv", qkv_any, qkv)
    load("weight", weight_any, weight)
    loaded["normed"].wait()
    for name in ("context", "scale", "out"):
        loaded[name].wait()
    for row in range(2):
        rows = slice(row * LEN, (row + 1) * LEN)
        back, gain, shift = norm_back(
            two[rows, :], one[rows, :], scale_one[rows, 0:1], norm[2:3, :])
        norm_sums[2:3, :] += gain
        norm_sums[3:4, :] += shift
        one[rows, :] = back
        back = back.astype(BF)
        attended[rows, :] = back
        norm_sums[0:1, :] += jnp.sum(back.astype(F32), axis=0, keepdims=True)
        back = dot_last(back, w_out[...]).astype(BF)
        wide[rows, :] = back
        product = back.astype(F32) * context[rows, :].astype(F32)
        high = product.astype(BF)
        low = (product - high.astype(F32)).astype(BF)
        head = lax.broadcasted_iota(jnp.int32, (16, D), 0)
        member = (lax.broadcasted_iota(jnp.int32, (16, D), 1) // HD == head).astype(F32).astype(BF)
        delta[row] = dot_last(member, high) + dot_last(member, low)
    loaded["flip"].wait()
    advance(groups, (5, 1))
    spare = out_held.shape[3] - D // 32

    def out_half(core):
        rows = pl.ds(pl.multiple_of(core * HALF, HALF), HALF)
        value = dot(flip_context[rows, :], attended[...]).reshape(16, D // 32, D)
        value = jnp.concatenate([value, jnp.zeros((16, spare, D), F32)], axis=1)
        return value.reshape(4, 2, 2, D // 32 + spare, D)

    out_held[...] = out_half(theirs).astype(BF)
    out_swap.start()
    pack_small(small, theirs, norm_sums, ffn_sums)
    small_swap.start()
    advance(groups, (3, 2), (4, 2))

    def out_mine():
        value = out_half(mine)
        out_swap.wait()
        out_held[...] = (value + out_other[...].astype(F32)).astype(BF)
        small_swap.wait()
        pack_small(small, mine, norm_sums, ffn_sums)
        small[...] += small_other[...]

    grad_head[...] = jnp.zeros(grad_head.shape, F32)
    for name in ("qkv", "token"):
        loaded[name].wait()

    def qkv_theirs(pair):
        cols = pl.ds(pl.multiple_of(pair * PAIR, PAIR), PAIR)
        value = dot(flip[...], qkv[pair, :, place_of(theirs, 0, PAIR)])
        qkv_held[:, :, :, :, cols] = value.reshape(4, 2, 2, D // 16, PAIR).astype(BF)
        qkv_swap(pair).start()

    def qkv_mine(pair):
        cols = pl.ds(pl.multiple_of(pair * PAIR, PAIR), PAIR)
        at = (EVERY, EVERY, EVERY, EVERY, cols)
        value = dot(flip[...], qkv[pair, :, place_of(mine, 0, PAIR)]).reshape(4, 2, 2, D // 16, PAIR)
        qkv_swap(pair).wait()
        qkv_held[at] = (value + qkv_other[at].astype(F32)).astype(BF)

    @pl.loop(0, 12)
    def _(item):
        pair, row = item // 4, item % 2
        core = jnp.where(item % 4 < 2, theirs, mine)

        @pl.when(item == 2)
        def _():
            out_mine()

        @pl.when(item % 4 == 2)
        def _():
            qkv_theirs(pair)

        @pl.when((item == 4) | (item == 8))
        def _():
            qkv_mine(pair - 1)

        for at, moves in (
            (1, ((7, 0),)),
            (2, ((5, 2), (6, 1))),
            (3, ((8, 0),)),
            (5, ((7, 1),)),
            (6, ((6, 2),)),
            (7, ((9, 0),)),
            (8, ((4, 3), (8, 1))),
            (10, ((5, 3), (7, 2), (10, 0))),
            (11, ((9, 1),)),
        ):
            @pl.when(item == at)
            def _():
                advance(groups, *moves)

        probs_load(item).wait()
        attend_back_pair(qkv, wide, probs.at[item % 2], delta, grad_head, core, row, pair)

        @pl.when(item < 10)
        def _():
            probs_load(item + 2).start()

    loaded["weight"].wait()

    def input_rows(row):
        rows = pl.ds(pl.multiple_of(row * LEN, LEN), LEN)
        one[rows, :] += (dot_last(qkv[0, rows, :], weight[0]) + dot_last(qkv[1, rows, :], weight[1])
                         + dot_last(qkv[2, rows, :], weight[2]))

    qkv_mine(2)
    advance(groups, (6, 3), (8, 2), (11, 0))
    heads[...] = pack_heads(theirs, grad_head)
    heads_swap.start()
    input_rows(0)
    heads_swap.wait()
    heads[...] = pack_heads(mine, grad_head) + heads_other[...]
    advance(groups, (12, 0))
    input_rows(1)
    input_done = pltpu.make_async_copy(one, input_any, local.at[12])
    input_done.start()
    advance(groups, (7, 3), (9, 2), (10, 1), (11, 1), (12, 1), (8, 3), (10, 2))
    small_sum, grads = results[0], results[1:]
    lines[...] = jnp.zeros(lines.shape, F32)

    def put_sums(index):
        grad = grads[index][...]
        square = grad * grad + EPS_SQUARE
        put_line(lines, COL_LINES[index], jnp.sum(square, axis=0, keepdims=True))
        if index in (0, 2):
            line = UP_ROWS if index else QKV_ROWS
            lines[line:line + 1, 0:grad.shape[0]] = to_row(jnp.sum(square, axis=1, keepdims=True))

    def ratio_of(index):
        (row,), (col,) = new_rows_cols(grads, rows_old, cols_old, lines, (index,))
        grad = grads[index][...]
        scaled = jnp.sum(grad * grad * (1.0 / col), axis=1, keepdims=True)
        share = 0.5 if index in (0, 2) else 1.0
        return (jnp.sum(scaled / row, axis=0, keepdims=True),
                jnp.sum(row, axis=0, keepdims=True) * share)

    for index in (1, 2, 3):
        put_sums(index)
    early = Exchange(place, mine_early, plane_early, line_early, sems, base)
    late = Broadcast(mine_one, land_one, sems, base + Exchange.COUNT, True)
    second = Broadcast(mine_two, land_two, sems, base + Exchange.COUNT + 1, False)
    value = lines[LATE:, :]
    early.start_plane(value)
    advance(groups, (9, 3), (11, 2), (12, 2))
    line = lax.broadcasted_iota(jnp.int32, value.shape, 0) + LATE
    same, cross = early.end_plane()
    paired = value + plane_early[theirs, place.y, place.x]
    early.start_line(jnp.where((line >= OUT_LINE) & (line < UP_ROWS), same + cross, same))
    advance(groups, (10, 3))
    lines[LATE:, :] = jnp.where(line >= UP_ROWS, paired, early.end_line())
    sums = {index: ratio_of(index) for index in (1, 2, 3)}
    place_small(old_small, norm_sq[...], head_sq[...], as_row(ffn_sq), 1.0)
    advance(groups, (11, 3), (12, 3))
    put_sums(0)
    value = lines[0:LATE, :]
    late.start(value)
    small_sum[6:8, :] = heads_sum[0:2, :]
    _, update = small_update(small_sum[...], old_small[...])
    others = small_sums(update)
    line = lax.broadcasted_iota(jnp.int32, value.shape, 0)
    late.end()
    paired = value + land_one[lax.axis_index("dp") * 2 + theirs]
    total = sum(land_one[2 * number + mine] for number in range(16))
    lines[0:LATE, :] = jnp.where(line >= QKV_ROWS, paired, total)
    sums[0] = ratio_of(0)
    second.start((
        scalars([sums[index][0] for index in range(4)] + [sums[index][1] for index in range(4)]
                + others) + weight_sums[...])[0:1])
    second.end()
    totals[...] = jnp.broadcast_to(jnp.sum(land_two[...], axis=0), totals.shape)
    input_done.wait()
    for group in groups:
        for chunk in group:
            chunk.finish()
    for exchange in (early, late, second):
        exchange.finish()


def backward_scatter(norm_sums, norm, rows_old, cols_old, squares,
                     weight_sums, large, rows, widths):
    count = large[1].shape[0]
    shape = jax.ShapeDtypeStruct
    some = pl.BlockSpec(memory_space=pl.ANY)
    kinds = [F32, BF, BF, BF, BF, F32]
    padded = [16, rows[1], 32, rows[3], rows[4], 8]
    wide = widths + [128]
    held = [pltpu.VMEM((4, 2, 2, r, w), k) for r, w, k in zip(padded, wide, kinds)]
    slots = []
    for r, w, k in zip(padded, wide, kinds):
        slots += [pltpu.VMEM((4, 2, r, w), k), pltpu.VMEM((4, r, w), k), pltpu.VMEM((3, r, w), k)]
    sems = 13 + 19 + 9 * Collect.COUNT + Exchange.COUNT + 2
    outs = [shape((r, w), F32) for r, w in zip(rows, widths)]
    outs += [shape((LINES, 128), F32), shape((8, 128), F32), shape((count, D), F32)]
    small = [norm_sums, norm, *rows_old, *cols_old, *squares, weight_sums]
    return pl.pallas_call(
        backward_scatter_kernel,
        out_shape=outs,
        in_specs=[VMEM] * len(small) + [some] * len(large),
        out_specs=[VMEM] * 7 + [some],
        scratch_shapes=held + held + slots + [
            pltpu.VMEM((8, 128), F32),
            pltpu.VMEM((count, D), BF),
            pltpu.VMEM((D, count), BF),
            pltpu.VMEM((D, count), BF),
            pltpu.VMEM((count, D), BF),
            pltpu.VMEM((count, D), BF),
            pltpu.VMEM((3, count, D), BF),
            pltpu.VMEM((3, D, D), BF),
            pltpu.VMEM((count, D), F32),
            pltpu.VMEM((count, D), F32),
            pltpu.VMEM((2, FF // 8, count), BF),
            pltpu.VMEM((count, UP_CHUNK), BF),
            pltpu.VMEM((2, 2, LEN, LEN), BF),
            pltpu.VMEM((2, 16, LEN), F32),
            pltpu.VMEM((8, D), F32),
            pltpu.VMEM((8, D), F32),
            pltpu.VMEM((1, FF), F32),
            pltpu.VMEM((count, 128), F32),
            pltpu.VMEM((D, D), BF),
        ] + [
            pltpu.VMEM(lead + (count, 128), F32)
            for count in (LINES - LATE,) for lead in ((2,), (2, 2, 2), (4,))
        ] + [
            pltpu.VMEM((LATE, 128), F32),
            pltpu.VMEM((32, LATE, 128), F32),
            pltpu.VMEM((1, 128), F32),
            pltpu.VMEM((32, 1, 128), F32),
            pltpu.VMEM((16, 128), F32),
            pltpu.SemaphoreType.DMA((sems,)),
            pltpu.SemaphoreType.DMA((sems,)),
            pltpu.SemaphoreType.DMA((26,)),
        ],
        compiler_params=pltpu.CompilerParams(
            collective_id=1, has_side_effects=True, vmem_limit_bytes=62 << 20),
        name="backward_scatter",
    )(*small, *large)


def small_block(norm, head, ffn):
    wide = lambda v: jnp.pad(v, [(0, 0)] * (v.ndim - 1) + [(0, 128 - v.shape[-1])])
    block = jnp.concatenate([wide(norm), wide(head), wide(ffn)], axis=-2)
    return jnp.pad(block, [(0, 0)] * (block.ndim - 2) + [(0, 16 - block.shape[-2]), (0, 0)])


def pair_major(weight):
    count = weight.shape[0]
    return weight.reshape(count, 3, 3, 128).transpose(0, 2, 1, 3).reshape(count, QKV_HALF)


def gather_plain(weights, vectors):
    head, ffn, norm = vectors
    qkv, out, up, down = (w.astype(BF) for w in weights)
    full = []
    for shard in (small_block(norm, head, ffn), pair_major(qkv), out, up, down):
        full.append(lax.all_gather(lax.all_gather(shard, "dp", axis=0), "mp", axis=0))
    return full


def scatter_plain(fulls):
    out = []
    for full in fulls:
        own = lax.psum_scatter(full.astype(F32), "mp", scatter_dimension=0)
        out.append(lax.psum_scatter(own, "dp", scatter_dimension=0))
    return out


def body(
    tokens, cotangent, seg_lengths, w_qkv, w_out, w_up, w_down, head_bias, ffn_bias, norm_bias,
    qkv_rows, qkv_cols, out_rows, out_cols, up_rows, up_cols, down_rows, down_cols,
    head_bias_sq, ffn_bias_sq, norm_sq,
):
    cores = lax.axis_size("mp")
    data = lax.axis_size("dp")
    rows_qkv = w_qkv.shape[0]
    fast = data == 16 and cores == 2
    weights = [w_qkv.transpose(1, 0, 2) if fast else w_qkv, w_out, w_up, w_down]
    vectors = [head_bias, ffn_bias if fast else ffn_bias.reshape(1, -1), norm_bias]
    rows_out = w_out.shape[0]
    if fast:
        (weight_sums, norm_full, ffn_full, scale_one, out_full, pooled, norm_sums, qkv_full,
         up_full, down_full, qkv, context_flip, token_flip, hidden_flip, normed_one, context,
         act_flip, slope, layer_out, grad_branch, grad_two, probs
         ) = forward_gather(weights, vectors, seg_lengths, tokens, cotangent)
        rows_old = [qkv_rows, out_rows, up_rows, down_rows]
        cols_old = [qkv_cols, out_cols, up_cols, down_cols]
        old = [head_bias_sq, ffn_bias_sq, norm_sq]
        *reduced, lines, totals, input_grad = backward_scatter(
            norm_sums, norm_full, rows_old, cols_old, old, weight_sums,
            [act_flip, grad_branch, down_full.reshape(FF, D), slope,
             up_full.reshape(2, D, FF // 2), grad_two, normed_one, hidden_flip, context,
             context_flip, token_flip, qkv, qkv_full.reshape(3, D, D), probs,
             scale_one, out_full],
            [16, rows_qkv, rows_out, rows_qkv, w_down.shape[0]],
            [128, QKV_HALF, D, w_up.shape[1], D])
        new = step(reduced, lines, totals, weights, rows_old, cols_old, vectors, old,
                   [layer_out, pooled, input_grad])
        new = list(new)
        grads, small_grads, rows_new, cols_new = new[:4], new[4:7], new[7:11], new[11:15]
        seconds, mats, fresh, passed = new[15:18], new[18:22], new[22:25], new[25:]
        grads[0], mats[0] = grads[0].transpose(1, 0, 2), mats[0].transpose(1, 0, 2)
        stats = [v for pair in zip(rows_new, cols_new) for v in pair]
        return (*passed, *grads, *small_grads, *stats, *seconds, *mats, *fresh)
    small, qkv_g, out_g, up_g, down_g = gather_plain(weights, vectors)
    small = small.astype(BF).astype(F32)
    own_head, own_ffn, own_norm = head_bias.shape[1], ffn_bias.shape[0], norm_bias.shape[1]
    norm_full = small[:, :, 0:6, :own_norm].transpose(2, 1, 0, 3).reshape(6, D)
    head_full = small[:, :, 6:8, :own_head].transpose(2, 0, 1, 3).reshape(2, 2, 3, 1, 128)
    ffn_full = small[:, :, 8, :own_ffn].reshape(1, FF)
    offsets = jnp.concatenate([head_full[0], jnp.zeros_like(head_full[0]), head_full[1]], axis=2)
    offsets = offsets.reshape(2, 1, QKV_HALF)
    qkv_full = qkv_g.reshape(2, D, QKV_HALF)
    up_full = up_g.reshape(2, D, FF // 2)
    down_full = down_g.reshape(FF, D)
    out_full = out_g.reshape(D, D)
    norm_full = jnp.pad(norm_full, ((0, 2), (0, 0)))
    qkv, context, lse = forward(tokens, qkv_full, offsets, seg_lengths)
    (layer_out, pooled, hidden_b, act, grad_branch, grad_inner, grad_attended, grad_context,
     grad_one, delta, norm_sums, ffn_sums) = middle_call(
        tokens, context, cotangent, seg_lengths, out_full, up_full, down_full, ffn_full,
        norm_full)
    grad_out, grad_up, grad_down = weight_grads(
        context.T, hidden_b.T, act.T, grad_branch, grad_inner, grad_attended,
        cores * data, rows_out)
    token_flip = tokens.T
    grad_qkv, input_grad, grad_head = backward(
        token_flip, qkv, grad_context, lse, delta, seg_lengths, qkv_full, grad_one)
    small_grads = small_block(
        norm_sums[:6].reshape(6, data, cores, -1).transpose(2, 1, 0, 3),
        grad_head.reshape(2, cores, data, -1).transpose(1, 2, 0, 3),
        ffn_sums.reshape(cores, data, 1, -1),
    )
    fulls = [
        small_grads,
        grad_qkv.reshape(cores, data, rows_qkv, QKV_HALF),
        grad_out.reshape(cores, data, rows_out, D),
        grad_up.reshape(cores, data, rows_qkv, FF // 2),
        grad_down.reshape(cores, data, -1, D),
    ]
    red_small, red_qkv, red_out, red_up, red_down = scatter_plain(fulls)
    norm_grad = red_small[0:6, :own_norm]
    red_qkv = pair_major(red_qkv)
    red_head = red_small[6:8, :own_head]
    red_ffn = red_small[8, :own_ffn]
    weights_flat = [w_qkv.reshape(rows_qkv, -1), w_out, w_up, w_down]
    grads_flat = [red_qkv, red_out, red_up, red_down]
    rows_old = [qkv_rows, out_rows, up_rows, down_rows]
    cols_old = [qkv_cols.reshape(-1), out_cols, up_cols, down_cols]
    col_count = [3 * D, D, FF, D]
    row_count = [D, D, D, FF]
    row_share = [cores, 1, cores, 1]
    squares = [grad * grad + EPS_SQUARE for grad in grads_flat]
    row_parts = [jnp.sum(square, axis=1) for square in squares]
    col_parts = [jnp.sum(square, axis=0) for square in squares]
    vec_weights = [head_bias, ffn_bias, norm_bias]
    vec_grads = [red_head, red_ffn, norm_grad]
    vec_old = [head_bias_sq, ffn_bias_sq, norm_sq]
    vec_counts = [2 * D, FF, 6 * D]
    vec_second = [
        DECAY * old + (1.0 - DECAY) * (grad * grad + EPS_SQUARE)
        for old, grad in zip(vec_old, vec_grads)
    ]
    vec_update = [grad * lax.rsqrt(second) for grad, second in zip(vec_grads, vec_second)]
    weight_parts = [jnp.sum(weight * weight) for weight in weights_flat + vec_weights]
    vec_parts = [jnp.sum(update * update) for update in vec_update]
    row_qkv, row_up = lax.psum((row_parts[0], row_parts[2]), "mp")
    col_qkv, col_up = lax.psum((col_parts[0], col_parts[2]), "dp")
    col_out, col_down = lax.psum((col_parts[1], col_parts[3]), ("dp", "mp"))
    row_sums = [row_qkv, row_parts[1], row_up, row_parts[3]]
    col_sums = [col_qkv, col_out, col_up, col_down]
    rows_new = [
        DECAY * rows_old[index] + (1.0 - DECAY) * row_sums[index] / col_count[index]
        for index in range(4)
    ]
    cols_new = [
        DECAY * cols_old[index] + (1.0 - DECAY) * col_sums[index] / row_count[index]
        for index in range(4)
    ]
    ratio_parts = [
        jnp.sum(
            grads_flat[index]
            * grads_flat[index]
            / (rows_new[index][:, None] * cols_new[index][None, :])
        )
        for index in range(4)
    ]
    extra_parts = (
        [jnp.sum(rows_new[index]) / row_share[index] for index in range(4)]
        + weight_parts
        + vec_parts
    )
    totals = lax.psum(jnp.stack(ratio_parts + extra_parts), ("dp", "mp"))
    row_means = [totals[4 + index] / row_count[index] for index in range(4)]
    weight_totals = [totals[8 + index] for index in range(7)]
    vec_totals = [totals[15 + index] for index in range(3)]
    new_mats = []
    for index in range(4):
        entries = row_count[index] * col_count[index]
        estimate = rows_new[index][:, None] * cols_new[index][None, :] / row_means[index]
        update = grads_flat[index] / jnp.sqrt(estimate)
        update_rms = jnp.sqrt(row_means[index] * totals[index] / entries)
        stride = (
            RATE * jnp.sqrt(weight_totals[index] / entries) / jnp.maximum(1.0, update_rms / CLIP)
        )
        new_mats.append(weights_flat[index] - stride * update)
    new_vecs = []
    for index in range(3):
        update_rms = jnp.sqrt(vec_totals[index] / vec_counts[index])
        stride = (
            RATE
            * jnp.sqrt(weight_totals[4 + index] / vec_counts[index])
            / jnp.maximum(1.0, update_rms / CLIP)
        )
        new_vecs.append(vec_weights[index] - stride * vec_update[index])
    return (
        layer_out,
        pooled,
        input_grad,
        red_qkv.reshape(w_qkv.shape),
        red_out,
        red_up,
        red_down,
        red_head,
        red_ffn,
        norm_grad,
        rows_new[0],
        cols_new[0].reshape(qkv_cols.shape),
        rows_new[1],
        cols_new[1],
        rows_new[2],
        cols_new[2],
        rows_new[3],
        cols_new[3],
        vec_second[0],
        vec_second[1],
        vec_second[2],
        new_mats[0].reshape(w_qkv.shape),
        new_mats[1],
        new_mats[2],
        new_mats[3],
        new_vecs[0],
        new_vecs[1],
        new_vecs[2],
    )


def solution(mesh):
    return jax.shard_map(
        body,
        mesh=mesh,
        in_specs=(
            P(("dp", "mp"), None),
            P(("dp", "mp"), None),
            P("dp", None),
            P("dp", None, "mp"),
            P(("mp", "dp"), None),
            P("dp", "mp"),
            P(("mp", "dp"), None),
            P(None, ("mp", "dp")),
            P(("mp", "dp")),
            P(None, ("dp", "mp")),
            P("dp"),
            P(None, "mp"),
            P(("mp", "dp")),
            P(),
            P("dp"),
            P("mp"),
            P(("mp", "dp")),
            P(),
            P(None, ("mp", "dp")),
            P(("mp", "dp")),
            P(None, ("dp", "mp")),
        ),
        out_specs=(
            P(("dp", "mp"), None),
            P(("dp", "mp"), None, None),
            P(("dp", "mp"), None),
            P("dp", None, "mp"),
            P(("mp", "dp"), None),
            P("dp", "mp"),
            P(("mp", "dp"), None),
            P(None, ("mp", "dp")),
            P(("mp", "dp")),
            P(None, ("dp", "mp")),
            P("dp"),
            P(None, "mp"),
            P(("mp", "dp")),
            P(),
            P("dp"),
            P("mp"),
            P(("mp", "dp")),
            P(),
            P(None, ("mp", "dp")),
            P(("mp", "dp")),
            P(None, ("dp", "mp")),
            P("dp", None, "mp"),
            P(("mp", "dp"), None),
            P("dp", "mp"),
            P(("mp", "dp"), None),
            P(None, ("mp", "dp")),
            P(("mp", "dp")),
            P(None, ("dp", "mp")),
        ),
        check_vma=False,
    )
```

```python
import functools

import jax
import jax.numpy as jnp
from jax import lax
from jax.experimental import pallas as pl
from jax.experimental.pallas import tpu as pltpu
from jax.sharding import PartitionSpec as P

D = 768
HD = 64
FF = 3072
LEN = 512
SEGS = 8

EPS_NORM = 1e-12
EPS_SQUARE = 1e-30
DECAY = 0.5
RATE = 3.0
CLIP = 0.3

MESH = pl.DeviceIdType.MESH
BF = jnp.bfloat16
F32 = jnp.float32
EVERY = slice(None)


PLANE = [(m, y, x) for m in range(2) for y in range(2) for x in range(2)][1:]


class Place:
    def __init__(self):
        d = lax.axis_index("dp")
        self.m = lax.axis_index("mp")
        self.z, self.y, self.x = d // 4, (d // 2) % 2, d % 2

    def at(self, axis, step):
        size = 4 if axis == "z" else 2
        spot = {"z": self.z, "y": self.y, "x": self.x, "m": self.m}
        spot[axis] = (spot[axis] + step) % size
        return spot

    def across(self, steps):
        m, y, x = steps
        return {"z": self.z, "m": (self.m + m) % 2, "y": (self.y + y) % 2, "x": (self.x + x) % 2}

    @staticmethod
    def device(spot):
        return (spot["z"] * 4 + spot["y"] * 2 + spot["x"], spot["m"])


def steps_of(axis):
    return (1, 2, 3) if axis == "z" else (1,)


def other_device(step):
    count = lax.axis_size("dp") * lax.axis_size("mp")
    number = (lax.axis_index("dp") * 2 + lax.axis_index("mp") + step) % count
    return (number // 2, number % 2)


def greet(place):
    barrier = pltpu.get_barrier_semaphore()
    for axis in "zyxm":
        for step in steps_of(axis):
            pl.semaphore_signal(
                barrier, inc=1, device_id=place.device(place.at(axis, step)), device_id_type=MESH)


def meet():
    pl.semaphore_wait(pltpu.get_barrier_semaphore(), 6)


def greet_all():
    barrier = pltpu.get_barrier_semaphore()

    @pl.loop(1, 32)
    def _(step):
        pl.semaphore_signal(
            barrier, inc=1, device_id=other_device(step), device_id_type=MESH)


def meet_all():
    pl.semaphore_wait(pltpu.get_barrier_semaphore(), 31)


def weight_sums_of(weights, small):
    parts = []
    for weight in weights:
        value = weight[...]
        if value.ndim == 3:
            parts.append(sum(all_sum(value[part] * value[part]) for part in range(3)))
        else:
            parts.append(all_sum(value * value))
    return scalars([jnp.zeros((1, 1), F32)] * 11 + parts + small_sums(small))


def as_row(ref):
    value = ref[...]
    return value.reshape(1, value.shape[0]) if value.ndim == 1 else value


def to_column(row):
    count = row.shape[1]
    here = lax.broadcasted_iota(jnp.int32, (count, count), 0)
    there = lax.broadcasted_iota(jnp.int32, (count, count), 1)
    return jnp.sum(jnp.where(here == there, row, 0.0), axis=1, keepdims=True)


def to_row(column):
    count = column.shape[0]
    here = lax.broadcasted_iota(jnp.int32, (count, count), 0)
    there = lax.broadcasted_iota(jnp.int32, (count, count), 1)
    return jnp.sum(jnp.where(here == there, column, 0.0), axis=0, keepdims=True)


def put_line(ref, line, row):
    for tile in range(row.shape[1] // 128):
        ref[line + tile:line + tile + 1, :] = row[:, tile * 128:(tile + 1) * 128]


def get_line(ref, line, width):
    tiles = width // 128
    return jnp.concatenate([ref[line + t:line + t + 1, :] for t in range(tiles)], axis=1)


def scalars(values):
    lane = lax.broadcasted_iota(jnp.int32, (8, 128), 1)
    out = jnp.zeros((8, 128), F32)
    for index, value in enumerate(values):
        out = jnp.where(lane == index, value, out)
    return out


def all_sum(values):
    return jnp.sum(jnp.sum(values, axis=1, keepdims=True), axis=0, keepdims=True)


class Exchange:
    COUNT = 10

    def __init__(self, place, mine, plane, line, sems, base, peers=PLANE):
        self.place, self.mine, self.plane, self.line = place, mine, plane, line
        self.peers = peers
        self.sems, self.base = sems, base

    def plane_copies(self):
        place = self.place
        send, recv = self.sems
        out = []
        for number, steps in enumerate(self.peers):
            spot = place.across(steps)
            slot = self.base + number
            device = place.device(spot)
            sent, arrives = (
                pltpu.make_async_remote_copy(
                    self.mine.at[0], self.plane.at[at["m"], at["y"], at["x"]],
                    send.at[slot], recv.at[slot], device_id=device, device_id_type=MESH)
                for at in ({"m": place.m, "y": place.y, "x": place.x}, spot))
            out.append((sent, arrives))
        return out

    def line_copies(self):
        place = self.place
        send, recv = self.sems
        out = []
        for step in (1, 2, 3):
            slot = self.base + 6 + step
            device = place.device(place.at("z", step))
            sent, arrives = (
                pltpu.make_async_remote_copy(
                    self.mine.at[1], self.line.at[layer], send.at[slot], recv.at[slot],
                    device_id=device, device_id_type=MESH)
                for layer in (place.z, place.at("z", -step)["z"]))
            out.append((sent, arrives))
        return out

    def start_plane(self, value):
        place = self.place
        self.mine[0] = value
        for sent, _ in self.plane_copies():
            sent.start()
        self.plane[place.m, place.y, place.x] = value

    def end_plane(self):
        plane, core = self.plane, self.place.m
        for _, arrives in self.plane_copies():
            arrives.wait_recv()
        cores = (core, 1 - core) if self.peers is PLANE else (core,)
        return [(plane[c, 0, 0] + plane[c, 0, 1]) + (plane[c, 1, 0] + plane[c, 1, 1])
                for c in cores]

    def start_line(self, value):
        self.mine[1] = value
        for sent, _ in self.line_copies():
            sent.start()
        self.line[self.place.z] = value

    def end_line(self):
        line = self.line
        for _, arrives in self.line_copies():
            arrives.wait_recv()
        return (line[0] + line[1]) + (line[2] + line[3])

    def finish(self):
        for sent, _ in self.plane_copies() + self.line_copies():
            sent.wait_send()


class Broadcast:
    def __init__(self, mine, land, sems, slot, core_only):
        self.mine, self.land, self.core_only = mine, land, core_only
        self.send, self.recv = (sem.at[slot] for sem in sems)
        self.number = lax.axis_index("dp") * 2 + lax.axis_index("mp")

    def copy(self, device):
        return pltpu.make_async_remote_copy(
            self.mine, self.land.at[self.number], self.send, self.recv,
            device_id=device, device_id_type=MESH)

    def start(self, value):
        self.mine[...] = value
        if self.core_only:
            @pl.loop(2, 32, step=2)
            def _(step):
                self.copy(other_device(step)).start()

            self.copy((self.number // 2, 1 - self.number % 2)).start()
        else:
            @pl.loop(1, 32)
            def _(step):
                self.copy(other_device(step)).start()

        self.land[self.number] = value

    def all_of_it(self):
        ref = self.land.at[pl.ds(0, 16 if self.core_only else 31)]
        return pltpu.make_async_remote_copy(
            ref, ref, self.send, self.recv, device_id=(0, 0), device_id_type=MESH)

    def end(self):
        self.all_of_it().wait_recv()

    def finish(self):
        self.all_of_it().wait_send()


QKV_LINE, QKV_ROWS, UP_LINE, OUT_LINE, DOWN_LINE, UP_ROWS = 0, 9, 16, 28, 34, 40
LATE, LINES = 16, 48
WIDTHS = (3 * D // 2, D, FF // 2, D)
COL_LINES = (QKV_LINE, OUT_LINE, UP_LINE, DOWN_LINE)
COL_COUNT = (3 * D, D, FF, D)
ROW_COUNT = (D, D, D, FF)


def pair_cuts():
    out = []
    for pair in range(3):
        for part in range(3):
            start = (pair * 3 + part) * 128
            out.append(((slice(part, part + 1), slice(pair * 128, (pair + 1) * 128)),
                        slice(start, start + 128)))
    return out


def new_rows_cols(grads, rows_old, cols_old, lines, which=range(4)):
    rows_new, cols_new = [], []
    for index in which:
        if index in (0, 2):
            line = UP_ROWS if index else QKV_ROWS
            count = rows_old[index].shape[0]
            row_sum = to_column(lines[line:line + 1, :count])
        else:
            grad = grads[index][...]
            row_sum = jnp.sum(grad * grad + EPS_SQUARE, axis=1, keepdims=True)
        rows_new.append(
            DECAY * to_column(as_row(rows_old[index])) + (1.0 - DECAY) * row_sum / COL_COUNT[index])
        col_sum = get_line(lines, COL_LINES[index], WIDTHS[index])
        if index == 0:
            old = jnp.concatenate([cols_old[0][at] for at, _ in pair_cuts()], axis=1)
        else:
            old = as_row(cols_old[index])
        cols_new.append(DECAY * old + (1.0 - DECAY) * col_sum / ROW_COUNT[index])
    return rows_new, cols_new


def place_small(ref, norm, head, ffn, fill):
    ref[...] = jnp.full(ref.shape, fill, F32)
    ref[0:6, 0:norm.shape[1]] = norm
    ref[6:8, 0:head.shape[1]] = head
    ref[8:9, 0:ffn.shape[1]] = ffn


def small_update(grad, old):
    second = DECAY * old + (1.0 - DECAY) * (grad * grad + EPS_SQUARE)
    return second, grad * lax.rsqrt(second)


def small_sums(values):
    line = lax.broadcasted_iota(jnp.int32, values.shape, 0)
    square = values * values
    return [
        all_sum(jnp.where((line >= 6) & (line < 8), square, 0.0)),
        all_sum(jnp.where(line == 8, square, 0.0)),
        all_sum(jnp.where(line < 6, square, 0.0)),
    ]


def step_kernel(*refs):
    refs = list(refs)
    take = lambda number: [refs.pop(0) for _ in range(number)]
    grads_any, weights_any = take(4), take(4)
    passed = take(3)
    small, lines, totals = take(3)
    rows_old, cols_old = take(4), take(4)
    head, ffn, norm, head_sq, ffn_sq, norm_sq = take(6)
    grads_out = take(4)
    head_grad, ffn_grad, norm_grad = take(3)
    rows_out, cols_out = take(4), take(4)
    head_second, ffn_second, norm_second = take(3)
    weights_out = take(4)
    head_new, ffn_new, norm_new = take(3)
    passed_out = take(3)
    grads, weights = take(4), take(4)
    old_small, weight_small, sems = refs
    loads = []
    for number, (source, target) in enumerate(
            zip(grads_any + weights_any + passed, grads + weights + passed_out)):
        copy = pltpu.make_async_copy(source, target, sems.at[number])
        copy.start()
        loads.append(copy)
    place_small(old_small, norm_sq[...], head_sq[...], as_row(ffn_sq), 1.0)
    place_small(weight_small, norm[...], head[...], as_row(ffn), 0.0)
    for copy in loads[:4]:
        copy.wait()
    rows_new, cols_new = new_rows_cols(grads, rows_old, cols_old, lines)
    total = lambda lane: totals[0:1, lane:lane + 1]
    for index in range(4):
        rows_out[index][...] = to_row(rows_new[index]).reshape(rows_out[index].shape)
        if index == 0:
            for at, cut in pair_cuts():
                cols_out[0][at] = cols_new[0][:, cut]
        else:
            cols_out[index][...] = cols_new[index].reshape(cols_out[index].shape)
        entries = ROW_COUNT[index] * COL_COUNT[index]
        row_mean = total(4 + index) / ROW_COUNT[index]
        update_rms = jnp.sqrt(row_mean * total(index) / entries)
        stride = (
            RATE * jnp.sqrt(total(11 + index) / entries) / jnp.maximum(1.0, update_rms / CLIP))
        scale_rows = lax.rsqrt(rows_new[index] / row_mean) * stride
        scale_cols = lax.rsqrt(cols_new[index])
        loads[4 + index].wait()
        if index == 0:
            for (part, cols), cut in pair_cuts():
                at = (part.start, EVERY, cols)
                grad = grads[0][:, cut]
                grads_out[0][at] = grad
                weights_out[0][at] = weights[0][at] - grad * scale_rows * scale_cols[:, cut]
        else:
            grad = grads[index][...]
            grads_out[index][...] = grad
            weights_out[index][...] = weights[index][...] - grad * scale_rows * scale_cols
    grad = small[...]
    second, update = small_update(grad, old_small[...])
    line = lax.broadcasted_iota(jnp.int32, grad.shape, 0)
    counts = (2 * D, FF, 6 * D)
    strides = []
    for index in range(3):
        update_rms = jnp.sqrt(total(8 + index) / counts[index])
        strides.append(
            RATE * jnp.sqrt(total(15 + index) / counts[index])
            / jnp.maximum(1.0, update_rms / CLIP))
    stride = jnp.where(line < 6, strides[2], jnp.where(line < 8, strides[0], strides[1]))
    fresh = weight_small[...] - stride * update
    for values, (norm_ref, head_ref, ffn_ref) in (
        (grad, (norm_grad, head_grad, ffn_grad)),
        (second, (norm_second, head_second, ffn_second)),
        (fresh, (norm_new, head_new, ffn_new)),
    ):
        norm_ref[...] = values[0:6, 0:norm_ref.shape[1]]
        head_ref[...] = values[6:8, 0:head_ref.shape[1]]
        ffn_ref[...] = values[8:9, 0:ffn_ref.shape[0]].reshape(ffn_ref.shape)
    for copy in loads[8:]:
        copy.wait()


def step(reduced, lines, totals, weights, rows_old, cols_old, vectors, squares, passed):
    vmem, some = pl.BlockSpec(memory_space=pltpu.VMEM), pl.BlockSpec(memory_space=pl.ANY)
    small, grads = reduced[0], reduced[1:]
    shapes = [w.shape for w in weights] + [v.shape for v in vectors]
    shapes += [r.shape for r in rows_old] + [c.shape for c in cols_old]
    shapes += [v.shape for v in vectors] + [w.shape for w in weights] + [v.shape for v in vectors]
    outs = [jax.ShapeDtypeStruct(s, F32) for s in shapes]
    large = [*grads, *weights, *passed]
    operands = [small, lines, totals, *rows_old, *cols_old, *vectors, *squares]
    return pl.pallas_call(
        step_kernel,
        out_shape=outs + [jax.ShapeDtypeStruct(v.shape, v.dtype) for v in passed],
        in_specs=[some] * len(large) + [vmem] * len(operands),
        out_specs=[vmem] * (len(shapes) + len(passed)),
        scratch_shapes=[pltpu.VMEM(v.shape, F32) for v in [*grads, *weights]] + [
            pltpu.VMEM((16, 128), F32), pltpu.VMEM((16, 128), F32),
            pltpu.SemaphoreType.DMA((11,)),
        ],
        compiler_params=pltpu.CompilerParams(vmem_limit_bytes=60 << 20),
        name="adafactor_step",
    )(*large, *operands)


HALF = D // 2
QKV_HALF = 3 * HALF
VMEM = pl.BlockSpec(memory_space=pltpu.VMEM)
SMEM = pl.BlockSpec(memory_space=pltpu.SMEM)


def dot(a, b):
    return jnp.dot(a, b, preferred_element_type=F32)


def dot_last(a, b):
    return lax.dot_general(a, b, (((1,), (1,)), ((), ())), preferred_element_type=F32)


def dot_first(a, b):
    return lax.dot_general(a, b, (((0,), (0,)), ((), ())), preferred_element_type=F32)


def ids_at(lengths, row, places):
    bound = jnp.int32(0)
    ids = jnp.zeros(places.shape, jnp.int32)
    for segment in range(SEGS):
        bound = bound + lengths[row, segment]
        ids = ids + (places >= bound).astype(jnp.int32)
    return ids


def set_bias(bias, lengths, row):
    down = ids_at(lengths, row, lax.broadcasted_iota(jnp.int32, (LEN, 1), 0))
    across = ids_at(lengths, row, lax.broadcasted_iota(jnp.int32, (1, LEN), 1))
    bias[...] = jnp.where(down == across, 0.0, -1e30)


def half_masks():
    lane = lax.broadcasted_iota(jnp.int32, (1, 128), 1)
    return [((lane // HD) == half).astype(F32).astype(BF) for half in range(2)]


PAIR = 3 * 128


def slab(ref, core, row, part, pair):
    return ref[core, pl.ds(pl.multiple_of(row * LEN, LEN), LEN),
               pl.ds(pl.multiple_of(pair * PAIR + part * 128, 128), 128)]


def project(tokens, weight, offsets, qkv, row):
    rows = pl.ds(pl.multiple_of(row * LEN, LEN), LEN)
    values = tokens[rows, :]
    for core in range(2):
        for pair in range(3):
            cut = slice(pair * PAIR, (pair + 1) * PAIR)
            out = (dot(values, weight[core, :, cut]) + offsets[core, :, cut]).astype(BF)
            scale = jnp.where(
                lax.broadcasted_iota(jnp.int32, (1, PAIR), 1) < 128, HD ** -0.5, 1.0).astype(BF)
            qkv[core, rows, cut] = out * scale


def attend(qkv, bias, context, lse, held, row):
    rows = pl.ds(pl.multiple_of(row * LEN, LEN), LEN)
    lane = lax.broadcasted_iota(jnp.int32, (LEN, 128), 1)
    held[...] = jnp.zeros(held.shape, F32)

    @pl.loop(0, 6)
    def _(item):
        core, pair = item // 3, item % 3
        queries, keys, values = (slab(qkv, core, row, part, pair) for part in range(3))
        wide = jnp.concatenate([values, jnp.ones_like(values)], axis=1)
        outs = []
        logs = held[...]
        for half, mask in enumerate(half_masks()):
            scores = dot_last(queries * mask, keys) + bias[...]
            peak = jnp.max(scores, axis=1, keepdims=True)
            raised = jnp.exp(scores - peak).astype(BF)
            both = dot(raised, wide)
            total = both[:, 128:]
            outs.append(both[:, :128] / total)
            logs = jnp.where(lane == item * 2 + half, peak + jnp.log(total), logs)
        held[...] = logs
        context[rows, pl.ds(pl.multiple_of(item * 128, 128), 128)] = jnp.where(
            lane < HD, outs[0], outs[1]).astype(BF)

    lse[row] = held[...].T[0:16, :]


def forward_kernel(tokens, weight, offsets, lengths, qkv, context, lse, bias, held):
    core = lax.axis_index("mp")

    @pl.loop(0, 2)
    def _(row):
        set_bias(bias, lengths, core * 2 + row)
        project(tokens, weight, offsets, qkv, row)
        attend(qkv, bias, context, lse, held, row)


def forward(tokens, weight, offsets, lengths):
    count = tokens.shape[0]
    return pl.pallas_call(
        forward_kernel,
        out_shape=[
            jax.ShapeDtypeStruct((2, count, QKV_HALF), BF),
            jax.ShapeDtypeStruct((count, D), BF),
            jax.ShapeDtypeStruct((count // LEN, 16, LEN), F32),
        ],
        in_specs=[VMEM, VMEM, VMEM, SMEM],
        out_specs=[VMEM] * 3,
        scratch_shapes=[pltpu.VMEM((LEN, LEN), F32), pltpu.VMEM((LEN, 128), F32)],
        compiler_params=pltpu.CompilerParams(vmem_limit_bytes=56 << 20),
        name="project_attend",
    )(tokens, weight, offsets, lengths)


def gelu_both(inner):
    cdf = 0.5 * (1.0 + lax.erf(inner * 0.7071067811865476))
    density = 0.3989422804014327 * jnp.exp(-0.5 * inner * inner)
    return inner * cdf, cdf + inner * density


def norm_parts(values):
    center = values - jnp.mean(values, axis=-1, keepdims=True)
    scale = lax.rsqrt(jnp.mean(center * center, axis=-1, keepdims=True) + EPS_NORM)
    return center * scale, scale


def norm_back(grad, normed, scale, gain):
    scaled = grad * gain
    mean = jnp.mean(scaled, axis=-1, keepdims=True)
    along = jnp.mean(scaled * normed, axis=-1, keepdims=True)
    return (
        (scaled - mean - normed * along) * scale,
        jnp.sum(grad * normed, axis=0, keepdims=True),
        jnp.sum(grad, axis=0, keepdims=True),
    )


CHUNK = 512


def middle(row, core, tokens, context, cotangent, lengths, w_out, w_up, w_down, ffn, norm, layer_out,
           pooled, hidden_b, act, grad_branch, grad_inner, grad_attended, grad_context,
           grad_one, delta, norm_sums, ffn_sums, slope, branch, hidden, normed_one, grad_two):
    rows = pl.ds(pl.multiple_of(row * LEN, LEN), LEN)
    attended = dot(context[rows, :], w_out[...]) + norm[0:1, :]
    normed, scale_one = norm_parts(tokens[rows, :].astype(F32) + attended)
    normed_one[...] = normed
    value = normed * norm[2:3, :] + norm[3:4, :]
    hidden[...] = value
    hidden_b[rows, :] = value.astype(BF)
    branch[...] = jnp.zeros(branch.shape, F32)
    for chunk in range(FF // CHUNK):
        core_of, start = chunk * CHUNK // (FF // 2), chunk * CHUNK % (FF // 2)
        cols = slice(chunk * CHUNK, (chunk + 1) * CHUNK)
        up = w_up[core_of, :, start:start + CHUNK]
        value, slope_value = gelu_both(dot(hidden_b[rows, :], up) + ffn[:, cols])
        value = value.astype(BF)
        act[rows, cols] = value
        slope[:, cols] = slope_value.astype(BF)
        branch[...] += dot(value, w_down[cols, :])
    normed, scale = norm_parts(hidden[...] + branch[...] + norm[1:2, :])
    output = normed * norm[4:5, :] + norm[5:6, :]
    high = output.astype(BF)
    layer_out[rows, :] = high
    low = (output - high.astype(F32)).astype(BF)
    place = lax.broadcasted_iota(jnp.int32, (SEGS, LEN), 1)
    segment = lax.broadcasted_iota(jnp.int32, (SEGS, 1), 0)
    ids = ids_at(lengths, core * 2 + row, place)
    member = (ids == segment).astype(F32)
    sizes = jnp.sum(member, axis=1, keepdims=True)
    member = member.astype(BF)
    pooled[row] = (dot(member, high) + dot(member, low)) / sizes
    back, gain, shift = norm_back(cotangent[rows, :].astype(F32), normed, scale, norm[4:5, :])
    norm_sums[4:5, :] += gain
    norm_sums[5:6, :] += shift
    grad_two[...] = back
    back = back.astype(BF)
    grad_branch[rows, :] = back
    norm_sums[1:2, :] += jnp.sum(back.astype(F32), axis=0, keepdims=True)
    for chunk in range(FF // CHUNK):
        core_of, start = chunk * CHUNK // (FF // 2), chunk * CHUNK % (FF // 2)
        cols = slice(chunk * CHUNK, (chunk + 1) * CHUNK)
        value = dot_last(grad_branch[rows, :], w_down[cols, :])
        value = (value * slope[:, cols].astype(F32)).astype(BF)
        grad_inner[rows, cols] = value
        ffn_sums[:, cols] += jnp.sum(value.astype(F32), axis=0, keepdims=True)
        grad_two[...] += dot_last(value, w_up[core_of, :, start:start + CHUNK])
    back, gain, shift = norm_back(grad_two[...], normed_one[...], scale_one, norm[2:3, :])
    norm_sums[2:3, :] += gain
    norm_sums[3:4, :] += shift
    grad_one[rows, :] = back
    back = back.astype(BF)
    grad_attended[rows, :] = back
    norm_sums[0:1, :] += jnp.sum(back.astype(F32), axis=0, keepdims=True)
    back = dot_last(back, w_out[...]).astype(BF)
    grad_context[rows, :] = back
    product = back.astype(F32) * context[rows, :].astype(F32)
    high = product.astype(BF)
    low = (product - high.astype(F32)).astype(BF)
    head = lax.broadcasted_iota(jnp.int32, (16, D), 0)
    member = (lax.broadcasted_iota(jnp.int32, (16, D), 1) // HD == head).astype(F32).astype(BF)
    delta[row] = dot_last(member, high) + dot_last(member, low)


def middle_kernel(*refs):
    core = lax.axis_index("mp")
    norm_sums, ffn_sums = refs[19], refs[20]
    norm_sums[...] = jnp.zeros(norm_sums.shape, F32)
    ffn_sums[...] = jnp.zeros(ffn_sums.shape, F32)

    @pl.loop(0, 2)
    def _(row):
        middle(row, core, *refs)


def middle_call(tokens, context, cotangent, lengths, w_out, w_up, w_down, ffn, norm):
    count = tokens.shape[0]
    shape = jax.ShapeDtypeStruct
    return pl.pallas_call(
        middle_kernel,
        out_shape=[
            shape((count, D), BF),
            shape((count // LEN, SEGS, D), F32),
            shape((count, D), BF),
            shape((count, FF), BF),
            shape((count, D), BF),
            shape((count, FF), BF),
            shape((count, D), BF),
            shape((count, D), BF),
            shape((count, D), F32),
            shape((count // LEN, 16, LEN), F32),
            shape((8, D), F32),
            shape((1, FF), F32),
        ],
        in_specs=[VMEM] * 3 + [SMEM] + [VMEM] * 5,
        out_specs=[VMEM] * 12,
        scratch_shapes=[
            pltpu.VMEM((LEN, FF), BF),
            pltpu.VMEM((LEN, D), F32),
            pltpu.VMEM((LEN, D), F32),
            pltpu.VMEM((LEN, D), F32),
            pltpu.VMEM((LEN, D), F32),
        ],
        compiler_params=pltpu.CompilerParams(vmem_limit_bytes=60 << 20),
        name="feed_forward",
    )(tokens, context, cotangent, lengths, w_out, w_up, w_down, ffn, norm)


def weight_grads_kernel(context, hidden_b, act, grad_branch, grad_inner, grad_attended,
                        out_grad, up_grad, down_grad):

    @pl.loop(0, FF // CHUNK)
    def _(chunk):
        half_chunks = FF // 2 // CHUNK
        cols = pl.ds(pl.multiple_of(chunk * CHUNK, CHUNK), CHUNK)
        local = pl.ds(pl.multiple_of((chunk % half_chunks) * CHUNK, CHUNK), CHUNK)
        up_grad[chunk // half_chunks, :, local] = dot(hidden_b[...], grad_inner[:, cols]).astype(BF)
        down_grad[cols, :] = dot(act[cols, :], grad_branch[...]).astype(BF)

    value = dot(context[...], grad_attended[...])
    rows, held = D // out_grad.shape[0], out_grad.shape[1]
    for block in range(out_grad.shape[0]):
        piece = value[block * rows:(block + 1) * rows, :]
        if held > rows:
            piece = jnp.concatenate([piece, jnp.zeros((held - rows, D), F32)], axis=0)
        out_grad[block] = piece.astype(BF)


def weight_grads(context, hidden_b, act, grad_branch, grad_inner, grad_attended, blocks, held):
    shape = jax.ShapeDtypeStruct
    return pl.pallas_call(
        weight_grads_kernel,
        out_shape=[shape((blocks, held, D), BF), shape((2, D, FF // 2), BF), shape((FF, D), BF)],
        in_specs=[VMEM] * 6,
        out_specs=[VMEM] * 3,
        compiler_params=pltpu.CompilerParams(vmem_limit_bytes=60 << 20),
        name="weight_grads",
    )(context, hidden_b, act, grad_branch, grad_inner, grad_attended)


def attend_back(qkv, grad_context, lse, delta, bias, grad_qkv, grad_head, row):
    rows = pl.ds(pl.multiple_of(row * LEN, LEN), LEN)
    lane = lax.broadcasted_iota(jnp.int32, (LEN, 128), 1)

    @pl.loop(0, 6)
    def _(item):
        core, pair = item // 3, item % 3
        queries, keys, values = (slab(qkv, core, row, part, pair) for part in range(3))
        wide = pl.ds(pl.multiple_of(item * 128, 128), 128)
        grad = grad_context[rows, wide]
        flipped = keys.T
        grads_k, grads_v, grads_q = [], [], []
        for half, mask in enumerate(half_masks()):
            head = item * 2 + half
            scores = dot_last(keys * mask, queries) + bias[...] - lse[row, pl.ds(head, 1), :]
            probs = jnp.exp(scores)
            grad_probs = dot_last(values * mask, grad)
            grad_scores = (probs * (grad_probs - delta[row, pl.ds(head, 1), :])).astype(BF)
            grads_v.append(dot(probs.astype(BF), grad))
            grads_k.append(dot(grad_scores, queries))
            grads_q.append(dot(flipped[half * HD:(half + 1) * HD, :], grad_scores))
        grad_q = (jnp.concatenate(grads_q, axis=0).T * HD ** -0.5).astype(BF)
        grad_k = jnp.where(lane < HD, grads_k[0], grads_k[1]).astype(BF)
        grad_v = jnp.where(lane < HD, grads_v[0], grads_v[1]).astype(BF)
        for part, value in enumerate((grad_q, grad_k, grad_v)):
            grad_qkv[core, rows, pl.ds(pl.multiple_of(pair * PAIR + part * 128, 128), 128)] = value
        grad_head[0:1, wide] += jnp.sum(grad_q.astype(F32), axis=0, keepdims=True)
        grad_head[1:2, wide] += jnp.sum(grad_v.astype(F32), axis=0, keepdims=True)


def backward_kernel(tokens, qkv, grad_context, lse, delta, lengths, weight, grad_one,
                    qkv_grad, input_grad, grad_head, grad_qkv, bias):
    core = lax.axis_index("mp")
    grad_head[...] = jnp.zeros(grad_head.shape, F32)

    @pl.loop(0, 2)
    def _(row):
        set_bias(bias, lengths, core * 2 + row)
        attend_back(qkv, grad_context, lse, delta, bias, grad_qkv, grad_head, row)
        rows = pl.ds(pl.multiple_of(row * LEN, LEN), LEN)
        input_grad[rows, :] = (
            grad_one[rows, :]
            + dot_last(grad_qkv[0, rows, :], weight[0])
            + dot_last(grad_qkv[1, rows, :], weight[1])
        )

    for core_of in range(2):
        for part in range(3):
            cut = slice(part * HALF, (part + 1) * HALF)
            qkv_grad[core_of, :, cut] = dot(tokens[...], grad_qkv[core_of, :, cut]).astype(BF)


def backward(tokens, qkv, grad_context, lse, delta, lengths, weight, grad_one):
    count = tokens.shape[1]
    shape = jax.ShapeDtypeStruct
    return pl.pallas_call(
        backward_kernel,
        out_shape=[shape((2, D, QKV_HALF), BF), shape((count, D), F32), shape((2, D), F32)],
        in_specs=[VMEM] * 5 + [SMEM] + [VMEM] * 2,
        out_specs=[VMEM] * 3,
        scratch_shapes=[
            pltpu.VMEM((2, count, QKV_HALF), BF),
            pltpu.VMEM((LEN, LEN), F32),
        ],
        compiler_params=pltpu.CompilerParams(vmem_limit_bytes=60 << 20),
        name="attend_back",
    )(tokens, qkv, grad_context, lse, delta, lengths, weight, grad_one)


UP_CHUNK = 512
DOWN_CHUNK = 256


class Spread:
    def __init__(self, place, full, start, width, flip, orders, sems, base):
        self.place, self.full = place, full
        self.cols = pl.ds(start, width)
        tiles = width // 128
        cut = (tiles // 2 if flip else tiles - tiles // 2) * 128
        self.halves = [(orders[0], pl.ds(start, cut))]
        if cut < width:
            self.halves.append((orders[1], pl.ds(start + cut, width - cut)))
        self.sems, self.base, self.slots = sems, base, {}
        self.count = sum(len(self.copies(stage)) for stage in range(4))

    def view(self, spot, cols):
        return self.full.at[spot["m"], spot["z"], spot["y"], spot["x"], :, cols]

    def copy(self, key, axis, step, spot, cols):
        place = self.place
        slot = self.base + self.slots.setdefault(key, len(self.slots))
        send, recv = self.sems
        send, recv = send.at[slot], recv.at[slot]
        device = place.device(place.at(axis, step))
        view = self.view(spot, cols)
        sent = pltpu.make_async_remote_copy(
            view, view, send, recv, device_id=device, device_id_type=MESH)
        land = dict(spot)
        land[axis] = place.at(axis, -step)[axis]
        land = self.view(land, cols)
        arrives = pltpu.make_async_remote_copy(
            land, land, send, recv, device_id=device, device_id_type=MESH)
        return sent, arrives

    def copies(self, stage):
        place = self.place
        here = {"z": place.z, "y": place.y, "x": place.x, "m": place.m}
        if stage == 3:
            here["z"] = here["y"] = here["x"] = EVERY
            return [self.copy((3, 0, 1), "m", 1, here, self.cols)]
        halves = self.halves
        if stage == 0 and halves[0][0][0] == "z":
            halves = [(halves[0][0], self.cols)]
        out = []
        for number, (order, cols) in enumerate(halves):
            spot = dict(here)
            for axis in order[:stage]:
                spot[axis] = EVERY
            for step in steps_of(order[stage]):
                out.append(self.copy((stage, number, step), order[stage], step, spot, cols))
        return out

    def start(self, stage):
        for sent, _ in self.copies(stage):
            sent.start()

    def arrived(self, stage):
        for _, arrives in self.copies(stage):
            arrives.wait_recv()

    def finish(self):
        for stage in range(4):
            for sent, _ in self.copies(stage):
                sent.wait_send()


def spread(groups, *moves):
    for group, stage in moves:
        for chunk in groups[group]:
            if stage:
                chunk.arrived(stage - 1)
            chunk.start(stage)


def unpack_small(small, norm_out, offsets, ffn_out):
    iota = lambda shape, axis: lax.broadcasted_iota(jnp.int32, shape, axis)
    pick = ((iota((128, D), 1) % 24 == iota((128, D), 0))).astype(F32).astype(BF)
    pick_ffn = ((iota((128, FF), 1) % 96 == iota((128, FF), 0))).astype(F32).astype(BF)
    total = jnp.zeros((16, D), F32)
    ffn = jnp.zeros((1, FF), F32)
    line, col = iota((256, D), 0), iota((256, D), 1) // 24
    device, kind = line // 16, line % 16
    for core in range(2):
        block = small[core].reshape(256, 128).astype(BF)
        wide = dot(block, pick)
        right = jnp.where(kind < 6, 2 * device + core, 16 * core + device)
        wide = jnp.where((col == right) & (kind < 8), wide, 0.0)
        total = total + jnp.sum(wide.reshape(16, 16, D), axis=0)
        wide = dot(small[core, :, :, :, 8, :].reshape(16, 128).astype(BF), pick_ffn)
        right = iota((16, FF), 1) // 96 == iota((16, FF), 0) + 16 * core
        ffn = ffn + jnp.sum(jnp.where(right, wide, 0.0), axis=0, keepdims=True)
    norm_out[0:6, :] = total[0:6, :]
    norm_out[6:8, :] = jnp.zeros((2, D), F32)
    ffn_out[...] = ffn
    offsets[...] = jnp.zeros(offsets.shape, F32)
    for core in range(2):
        for pair in range(3):
            source = core * HALF + pair * 128
            for part, row in ((0, 6), (2, 7)):
                start = pair * PAIR + part * 128
                offsets[core, :, start:start + 128] = total[row:row + 1, source:source + 128]


def place_of(core, part, width):
    return pl.ds(pl.multiple_of(core * PAIR + part * 128, 128), width)


def trio(ref, core, row, part, pair):
    return ref[pair, pl.ds(pl.multiple_of(row * LEN, LEN), LEN), place_of(core, part, 128)]


def project_pair(tokens, weight, offsets, qkv, pair):
    cols = pl.ds(pl.multiple_of(pair * PAIR, PAIR), PAIR)
    scale = jnp.where(
        lax.broadcasted_iota(jnp.int32, (1, PAIR), 1) < 128, HD ** -0.5, 1.0).astype(BF)
    for core in range(2):
        piece = weight[core, :, :, :, :, cols].reshape(D, PAIR)
        out = dot(tokens[...], piece) + offsets[core, :, cols]
        qkv[pair, :, place_of(core, 0, PAIR)] = out.astype(BF) * scale


def attend_pair(qkv, bias, probs, flip, core, row, pair):
    item = core * 3 + pair
    queries, keys, values = (trio(qkv, core, row, part, pair) for part in range(3))
    flipped = values.T
    cols = pl.ds(pl.multiple_of(row * LEN, LEN), LEN)
    for half, mask in enumerate(half_masks()):
        scores = dot_last(keys * mask, queries) + bias[row]
        raised = jnp.exp(scores - jnp.max(scores, axis=0, keepdims=True))
        share = (raised * (1.0 / jnp.sum(raised, axis=0, keepdims=True))).astype(BF)
        probs[half] = share
        lines = pl.ds(pl.multiple_of(item * 128 + half * HD, HD), HD)
        flip[lines, cols] = dot(flipped[half * HD:(half + 1) * HD, :], share).astype(BF)


FEED_MOVES = (
    ((8, 2),), ((9, 2),), (), ((6, 3),), ((7, 3),), ((8, 3),),
)


def forward_gather_kernel(*refs):
    refs = list(refs)
    take = lambda number: [refs.pop(0) for _ in range(number)]
    w_qkv, w_out, w_up, w_down, head, ffn, norm, lengths = take(8)
    tokens_any, cotangent_any = take(2)
    (sums, norm_out, ffn_out, hidden_scale, out_full, pooled, norm_sums) = take(7)
    (qkv_full, up_full, down_full, qkv_out, context_flip, token_flip, hidden_flip, normed_out,
     context_out, act_flip, slope_out, layer_out, branch_out, grad_two_out, probs_out) = take(15)
    (g_small, g_qkv, g_out, g_up, g_down, tokens, qkv, context, flip,
     hidden_b, normed_one, act, slope, flip_act, bias, probs, offsets, branch, flip_context) = take(19)
    send, recv, local = refs
    place = Place()
    greet(place)
    here = (place.m, place.z, place.y, place.x)
    used = [0]
    unwaited = []

    def keep(source, target):
        copy = pltpu.make_async_copy(source, target, local.at[used[0]])
        used[0] += 1
        copy.start()
        unwaited.append(copy)
        return copy

    def done(copy):
        copy.wait()
        unwaited[:] = [other for other in unwaited if other is not copy]

    tokens_loaded = keep(tokens_any, tokens)
    place_small(g_small.at[here], norm[...], head[...], as_row(ffn), 0.0)
    for part in range(3):
        for pair in range(3):
            start = pair * PAIR + part * 128
            g_qkv[here + (EVERY, slice(start, start + 128))] = w_qkv[
                part, :, pair * 128:(pair + 1) * 128].astype(BF)
    sems, base = (send, recv), [0]

    def chunk(full, start, width, flip=False, orders=("zxy", "zyx")):
        made = Spread(place, full, start, width, flip, orders, sems, base[0])
        base[0] += made.count
        return made

    groups = [[chunk(g_small, 0, 128), chunk(g_qkv, 0, PAIR)]]
    groups += [[chunk(g_qkv, pair * PAIR, PAIR, pair == 1)] for pair in (1, 2)]
    groups += [[chunk(g_out, 0, D)]]
    groups += [[chunk(g_up, at, UP_CHUNK)] for at in range(0, FF // 2, UP_CHUNK)]
    groups += [[chunk(g_down, at, DOWN_CHUNK)] for at in range(0, D, DOWN_CHUNK)]

    def ready(index):
        for made in groups[index]:
            made.arrived(3)

    meet()
    spread(groups, (0, 0), (1, 0))
    value = w_out[...]
    spare = g_out.shape[4] - value.shape[0]
    g_out[here] = jnp.concatenate([value, jnp.zeros((spare, D), F32)], axis=0).astype(BF)
    g_up[here] = w_up[...].astype(BF)
    g_down[here] = w_down[...].astype(BF)
    sums[...] = weight_sums_of([w_qkv, w_out, w_up, w_down], g_small[here])
    for row in range(2):
        set_bias(bias.at[row], lengths, place.m * 2 + row)
    done(tokens_loaded)
    flip[...] = tokens[...].T
    flip_kept = keep(flip, token_flip)
    spread(groups, (0, 1), (2, 0))
    spread(groups, (1, 1), (3, 0))
    spread(groups, (0, 2))
    spread(groups, (2, 1), (4, 0))
    spread(groups, (1, 2))
    spread(groups, (0, 3), (3, 1), (5, 0))
    ready(0)
    unpack_small(g_small, norm_out, offsets, ffn_out)

    @pl.loop(0, 12)
    def _(item):
        pair, row, core = item // 4, (item % 4) // 2, item % 2
        for at, moves in (
            (1, ((3, 2), (5, 1), (7, 0))),
            (4, ((2, 3),)),
            (6, ((7, 1), (9, 0))),
            (7, ((3, 3),)),
            (9, ((9, 1),)),
            (10, ((4, 3),)),
            (11, ((6, 2),)),
        ):
            @pl.when(item == at)
            def _():
                spread(groups, *moves)

        for at in (4, 8):
            @pl.when(item == at)
            def _():
                ready(at // 4)

        @pl.when(item % 4 == 0)
        def _():
            project_pair(tokens, g_qkv, offsets, qkv, pair)

        for at, moves in (
            (0, ((1, 3), (2, 2), (4, 1), (6, 0))),
            (4, ((4, 2), (6, 1), (8, 0))),
            (8, ((5, 2), (8, 1))),
        ):
            @pl.when(item == at)
            def _():
                spread(groups, *moves)

        def probs_copy(number):
            return pltpu.make_async_copy(
                probs.at[number % 2], probs_out.at[number], local.at[28 + number % 2])

        @pl.when(item >= 2)
        def _():
            probs_copy(item - 2).wait()

        attend_pair(qkv, bias, probs.at[item % 2], flip_context, core, row, pair)
        probs_copy(item).start()

    spread(groups, (7, 2))
    for core in range(2):
        for pair in range(3):
            cols = slice(pair * PAIR, (pair + 1) * PAIR)
            keep(g_qkv.at[core, :, :, :, :, cols],
                 qkv_full.at[pair, :, :, :, :, core * PAIR:(core + 1) * PAIR])
    keep(qkv, qkv_out)
    keep(flip_context, context_flip)
    context[...] = flip_context[...].T
    context_kept = keep(context, context_out)
    for slot in range(2):
        unwaited.append(
            pltpu.make_async_copy(probs.at[slot], probs_out.at[10 + slot], local.at[28 + slot]))
    ready(3)
    rows_out = w_out.shape[0]
    for core in range(2):
        value = g_out[core].reshape(16, g_out.shape[4], D).astype(F32)[:, :rows_out]
        out_full[core * HALF:(core + 1) * HALF, :] = value.reshape(HALF, D).astype(BF)
    halves = [slice(row * LEN, (row + 1) * LEN) for row in range(2)]
    for number, rows in enumerate(halves):
        attended = dot(context[rows, :], out_full[...]) + norm_out[0:1, :]
        normed, scale = norm_parts(tokens[rows, :].astype(F32) + attended)
        normed_one[rows, :] = normed
        hidden_scale[rows, :] = jnp.broadcast_to(scale, (LEN, 128))
        hidden_b[rows, :] = (normed * norm_out[2:3, :] + norm_out[3:4, :]).astype(BF)
        spread(groups, *(((), ((5, 3),)))[number])
    cotangent_loaded = keep(cotangent_any, tokens)
    keep(normed_one, normed_out)
    waiting = [[], []]
    for third in range(3):
        ready(4 + third)
        for core in range(2):
            for copy in waiting[core]:
                copy.wait()
            local_cols = slice(third * UP_CHUNK, (third + 1) * UP_CHUNK)
            start = core * (FF // 2) + third * UP_CHUNK
            cols = pl.ds(start, UP_CHUNK)
            up = g_up[core, :, :, :, :, local_cols].reshape(D, UP_CHUNK)

            @pl.loop(0, 2)
            def _(row):
                rows = pl.ds(pl.multiple_of(row * LEN, LEN), LEN)
                value, slope_value = gelu_both(
                    dot(hidden_b[rows, :], up) + ffn_out[:, start:start + UP_CHUNK])
                act[rows, cols] = value.astype(BF)
                slope[core, rows, :] = slope_value.astype(BF)

            flip_act[core] = act[:, cols].T
            slot = 24 + 2 * core
            waiting[core] = [
                pltpu.make_async_copy(slope.at[core], slope_out.at[:, cols], local.at[slot]),
                pltpu.make_async_copy(flip_act.at[core], act_flip.at[cols, :], local.at[slot + 1]),
            ]
            for copy in waiting[core]:
                copy.start()
            spread(groups, *FEED_MOVES[2 * third + core])
    done(flip_kept)
    flip[...] = hidden_b[...].T
    keep(flip, hidden_flip)
    for core in range(2):
        keep(g_up.at[core], up_full.at[core])
    for third in range(3):
        if third == 1:
            spread(groups, (9, 3))
        ready(7 + third)
        cols = slice(third * DOWN_CHUNK, (third + 1) * DOWN_CHUNK)
        down = g_down[:, :, :, :, :, cols].reshape(FF, DOWN_CHUNK)
        for rows in halves:
            branch[rows, cols] = dot(act[rows, :], down)
    for core in range(2):
        keep(g_down.at[core], down_full.at[core])
    norm_sums[...] = jnp.zeros(norm_sums.shape, F32)
    done(cotangent_loaded)
    done(context_kept)
    for row, rows in enumerate(halves):
        hidden = normed_one[rows, :] * norm_out[2:3, :] + norm_out[3:4, :]
        normed, scale = norm_parts(hidden + branch[rows, :] + norm_out[1:2, :])
        output = normed * norm_out[4:5, :] + norm_out[5:6, :]
        high = output.astype(BF)
        context[rows, :] = high
        keep(context.at[rows], layer_out.at[rows])
        low = (output - high.astype(F32)).astype(BF)
        spots = lax.broadcasted_iota(jnp.int32, (SEGS, LEN), 1)
        segment = lax.broadcasted_iota(jnp.int32, (SEGS, 1), 0)
        member = (ids_at(lengths, place.m * 2 + row, spots) == segment).astype(F32)
        sizes = jnp.sum(member, axis=1, keepdims=True)
        member = member.astype(BF)
        pooled[row] = (dot(member, high) + dot(member, low)) / sizes
        back, gain, shift = norm_back(tokens[rows, :].astype(F32), normed, scale, norm_out[4:5, :])
        norm_sums[4:5, :] += gain
        norm_sums[5:6, :] += shift
        branch[rows, :] = back
        keep(branch.at[rows], grad_two_out.at[rows])
        back = back.astype(BF)
        hidden_b[rows, :] = back
        keep(hidden_b.at[rows], branch_out.at[rows])
        norm_sums[1:2, :] += jnp.sum(back.astype(F32), axis=0, keepdims=True)
    for copy in unwaited + waiting[0] + waiting[1]:
        copy.wait()
    for group in groups:
        for made in group:
            made.finish()


def forward_gather(weights, vectors, lengths, tokens, cotangent):
    qkv, out, up, down = weights
    count = tokens.shape[0]
    shape = jax.ShapeDtypeStruct
    grid = (2, 4, 2, 2)
    rows = count // LEN
    flipped = shape((D, count), BF)
    small_outs = [
        shape((8, 128), F32), shape((8, D), F32), shape((1, FF), F32),
        shape((count, 128), F32), shape((D, D), BF), shape((rows, SEGS, D), F32), shape((8, D), F32),
    ]
    large_outs = [
        shape((3,) + grid[1:] + (qkv.shape[1], D), BF), shape(grid + up.shape, BF),
        shape(grid + down.shape, BF), shape((3, count, D), BF), flipped, flipped, flipped,
        shape((count, D), F32), shape((count, D), BF), shape((FF, count), BF),
        shape((count, FF), BF), shape((count, D), BF), shape((count, D), BF), shape((count, D), F32),
        shape((6 * rows, 2, LEN, LEN), BF),
    ]
    slots = 88
    some = pl.BlockSpec(memory_space=pl.ANY)
    return pl.pallas_call(
        forward_gather_kernel,
        out_shape=small_outs + large_outs,
        in_specs=[VMEM] * 7 + [SMEM] + [some] * 2,
        out_specs=[VMEM] * len(small_outs) + [some] * len(large_outs),
        scratch_shapes=[
            pltpu.VMEM(grid + (16, 128), F32),
            pltpu.VMEM(grid + (qkv.shape[1], QKV_HALF), BF),
            pltpu.VMEM(grid + (32, D), BF),
            pltpu.VMEM(grid + up.shape, BF),
            pltpu.VMEM(grid + down.shape, BF),
            pltpu.VMEM((count, D), BF),
            pltpu.VMEM((3, count, D), BF),
            pltpu.VMEM((count, D), BF),
            pltpu.VMEM((D, count), BF),
            pltpu.VMEM((count, D), BF),
            pltpu.VMEM((count, D), F32),
            pltpu.VMEM((count, FF), BF),
            pltpu.VMEM((2, count, UP_CHUNK), BF),
            pltpu.VMEM((2, UP_CHUNK, count), BF),
            pltpu.VMEM((2, LEN, LEN), F32),
            pltpu.VMEM((2, 2, LEN, LEN), BF),
            pltpu.VMEM((2, 1, QKV_HALF), F32),
            pltpu.VMEM((count, D), F32),
            pltpu.VMEM((D, count), BF),
            pltpu.SemaphoreType.DMA((slots,)),
            pltpu.SemaphoreType.DMA((slots,)),
            pltpu.SemaphoreType.DMA((30,)),
        ],
        compiler_params=pltpu.CompilerParams(
            collective_id=0, has_side_effects=True, vmem_limit_bytes=61 << 20),
        name="forward_gather",
    )(*weights, *vectors, lengths, tokens, cotangent)


class Collect:
    COUNT = 7

    def __init__(self, place, held, slots, result, start, width, flip, sems, base, layer=None,
                 stages=(0, 2)):
        self.place, self.held, self.slots, self.result = place, held, slots, result
        self.layer, self.stages = layer, stages
        self.cols = pl.ds(start, width)
        tiles = width // 128
        cut = (tiles // 2 if flip else tiles - tiles // 2) * 128
        self.halves = [("xy", pl.ds(start, cut))]
        if cut < width:
            self.halves.append(("yx", pl.ds(start + cut, width - cut)))
        self.sems, self.base = sems, base

    def copy(self, slot, axis, step, source, target):
        send, recv = self.sems
        return pltpu.make_async_remote_copy(
            source, target, send.at[self.base + slot], recv.at[self.base + slot],
            device_id=self.place.device(self.place.at(axis, step)), device_id_type=MESH)

    def copies(self, stage):
        place = self.place
        if stage == 2:
            out = []
            for step in (1, 2, 3):
                source = self.held.at[place.at("z", step)["z"], place.y, place.x, :, self.cols]
                out.append(self.copy(
                    step - 1, "z", step, source, self.slots[2].at[step - 1, :, self.cols]))
            return out
        out = []
        for number, (order, cols) in enumerate(self.halves):
            axis = order[stage]
            spot = {"y": EVERY, "x": EVERY}
            if stage == 1:
                spot[order[0]] = getattr(place, order[0])
            spot[axis] = place.at(axis, 1)[axis]
            layer = EVERY if self.layer is None else self.layer
            land = (layer,) + (EVERY,) * (1 - stage) + (EVERY, cols)
            out.append(self.copy(
                2 * stage + number + (0 if self.layer is not None else 3), axis, 1,
                self.held.at[layer, spot["y"], spot["x"], :, cols], self.slots[stage].at[land]))
        return out

    def start(self, stage):
        for sent in self.copies(stage):
            sent.start()

    def add(self, stage):
        place, held, slots = self.place, self.held, self.slots[stage]
        for sent in self.copies(stage):
            sent.wait_recv()
        if stage == 2:
            value = held[place.z, place.y, place.x, :, self.cols].astype(F32)
            for step in range(3):
                value = value + slots[step, :, self.cols].astype(F32)
            self.result[:, self.cols] = value[:self.result.shape[0]]
            return
        for order, cols in self.halves:

            layers = 4 if self.layer is None else 1

            @pl.loop(0, layers * (2 - stage))
            def _(index):
                spot = {"y": place.y, "x": place.x}
                if stage == 0:
                    layer = index // 2 if self.layer is None else self.layer
                    spot[order[1]] = index % 2
                    arrived = slots[layer, index % 2, :, cols]
                else:
                    layer = index if self.layer is None else self.layer
                    arrived = slots[layer, :, cols]
                at = (layer, spot["y"], spot["x"], EVERY, cols)
                held[at] = (held[at].astype(F32) + arrived.astype(F32)).astype(held.dtype)

    def finish(self):
        for stage in range(self.stages[0], self.stages[1] + 1):
            for sent in self.copies(stage):
                sent.wait_send()


def advance(groups, *moves):
    for group, stage in moves:
        for chunk in groups[group]:
            if stage > chunk.stages[0]:
                chunk.add(stage - 1)
            if stage <= chunk.stages[1]:
                chunk.start(stage)


def split_dot(value, other):
    high = value.astype(BF)
    return dot(high, other) + dot((value - high.astype(F32)).astype(BF), other)


def picks(count, width):
    shape = (count, 128)
    lane = lax.broadcasted_iota(jnp.int32, shape, 0) % width
    return (lane == lax.broadcasted_iota(jnp.int32, shape, 1)).astype(F32).astype(BF)


def pack_rows(rows, right):
    rows = jnp.broadcast_to(rows[None], (16, 8, D)).reshape(128, D)
    iota = lambda axis: lax.broadcasted_iota(jnp.int32, (128, D), axis)
    rows = jnp.where(iota(1) // 24 == right(iota(0) // 8), rows, 0.0)
    return split_dot(rows, picks(D, 24)).reshape(4, 2, 2, 8, 128)


def pack_small(target, core, norm_sums, ffn_sums):
    target[:, :, :, 0:8, :] = pack_rows(norm_sums[...], lambda device: 2 * device + core)
    iota = lambda axis: lax.broadcasted_iota(jnp.int32, (16, FF), axis)
    ffn = jnp.where(iota(1) // 96 == iota(0) + 16 * core, ffn_sums[...], 0.0)
    target[:, :, :, 8:16, :] = jnp.zeros((4, 2, 2, 8, 128), F32)
    target[:, :, :, 8, :] = split_dot(ffn, picks(FF, 96)).reshape(4, 2, 2, 128)


def pack_heads(core, grad_head):
    return pack_rows(grad_head[...], lambda device: 16 * core + device)


def attend_back_pair(qkv, grad_context, probs, delta, grad_head, core, row, pair):
    lane = lax.broadcasted_iota(jnp.int32, (LEN, 128), 1)
    item = core * 3 + pair
    queries, keys, values = (trio(qkv, core, row, part, pair) for part in range(3))
    rows = pl.ds(pl.multiple_of(row * LEN, LEN), LEN)
    wide = pl.ds(pl.multiple_of(item * 128, 128), 128)
    grad = grad_context[rows, wide]
    flipped = keys.T
    grads_k, grads_v, grads_q = [], [], []
    for half, mask in enumerate(half_masks()):
        share = probs[half]
        grad_probs = dot_last(values * mask, grad) - delta[row, pl.ds(item * 2 + half, 1), :]
        grad_scores = (share.astype(F32) * grad_probs).astype(BF)
        grads_v.append(dot(share, grad))
        grads_k.append(dot(grad_scores, queries))
        grads_q.append(dot(flipped[half * HD:(half + 1) * HD, :], grad_scores))
    grad_q = (jnp.concatenate(grads_q, axis=0).T * HD ** -0.5).astype(BF)
    grad_k = jnp.where(lane < HD, grads_k[0], grads_k[1]).astype(BF)
    grad_v = jnp.where(lane < HD, grads_v[0], grads_v[1]).astype(BF)
    for part, value in enumerate((grad_q, grad_k, grad_v)):
        qkv[pair, rows, place_of(core, part, 128)] = value
    grad_head[0:1, wide] += jnp.sum(grad_q.astype(F32), axis=0, keepdims=True)
    grad_head[1:2, wide] += jnp.sum(grad_v.astype(F32), axis=0, keepdims=True)


def backward_scatter_kernel(*refs):
    refs = list(refs)
    take = lambda number: [refs.pop(0) for _ in range(number)]
    norm_given, norm = take(2)
    rows_old, cols_old = take(4), take(4)
    head_sq, ffn_sq, norm_sq, weight_sums = take(4)
    (act_any, branch_any, down_any, slope_any, up_any, two_any, normed_any, hidden_any, context_any,
     flip_any, token_any, qkv_any, weight_any, probs_any, scale_any, out_any) = take(16)
    results = take(5)
    lines, totals, input_any = take(3)
    held, other = take(6), take(6)
    slots = [take(3) for _ in range(6)]
    heads_sum = refs.pop(0)
    (wide, flip, flip_context, context, attended, qkv, weight, one, two, act, inner, probs, delta,
     grad_head, norm_sums, ffn_sums, scale_one, w_out) = take(18)
    (mine_early, plane_early, line_early, mine_one, land_one, mine_two, land_two, old_small) = take(8)
    send, recv, local = refs
    place = Place()
    greet_all()
    sems = (send, recv)
    partner = place.device(place.at("m", 1))
    mine, theirs = place.m, 1 - place.m
    loaded = {}

    def load(name, source, target):
        copy = pltpu.make_async_copy(source, target, local.at[len(loaded)])
        copy.start()
        loaded[name] = copy

    tile_rows = FF // 2 // 4
    act_slots, chunk_slots = 16, 18

    def act_load(index):
        core = jnp.where(index < 4, theirs, mine)
        start = pl.multiple_of(core * (FF // 2) + (index % 4) * tile_rows, tile_rows)
        return pltpu.make_async_copy(
            act_any.at[pl.ds(start, tile_rows)], act.at[index % 2], local.at[act_slots + index % 2])

    def down_tile(index):
        return qkv.at[0, pl.ds(pl.multiple_of(index % 2 * UP_CHUNK, UP_CHUNK), UP_CHUNK)]

    def slope_tile(index):
        return qkv.at[1 + index % 2, :, pl.ds(0, UP_CHUNK)]

    def up_tile(index):
        return weight.at[index % 2, :, pl.ds(0, UP_CHUNK)]

    def chunk_loads(index):
        core = jnp.where(index < 3, theirs, mine)
        inside = pl.ds(pl.multiple_of(index % 3 * UP_CHUNK, UP_CHUNK), UP_CHUNK)
        whole = pl.ds(
            pl.multiple_of(core * (FF // 2) + index % 3 * UP_CHUNK, UP_CHUNK), UP_CHUNK)
        slot = chunk_slots + 3 * (index % 2)
        return [
            pltpu.make_async_copy(down_any.at[whole], down_tile(index), local.at[slot]),
            pltpu.make_async_copy(slope_any.at[:, whole], slope_tile(index), local.at[slot + 1]),
            pltpu.make_async_copy(up_any.at[core, :, inside], up_tile(index), local.at[slot + 2]),
        ]

    load("branch", branch_any, wide)
    for index in range(2):
        act_load(index).start()

    small, qkv_held, out_held, up_held, down_held, heads = held
    small_other, qkv_other, out_other, up_other, down_other, heads_other = other
    base = 13

    def swap(slot, source, target):
        return pltpu.make_async_remote_copy(
            source, target, send.at[slot], recv.at[slot],
            device_id=partner, device_id_type=MESH)

    def down_swap(layer):
        return swap(layer, down_held.at[layer], down_other.at[layer])

    def up_swap(third):
        cols = pl.ds(pl.multiple_of(third * UP_CHUNK, UP_CHUNK), UP_CHUNK)
        at = (EVERY, EVERY, EVERY, EVERY, cols)
        return swap(4 + third, up_held.at[at], up_other.at[at])

    def qkv_swap(pair):
        at = (EVERY, EVERY, EVERY, EVERY, pl.ds(pl.multiple_of(pair * PAIR, PAIR), PAIR))
        return swap(8 + pair, qkv_held.at[at], qkv_other.at[at])

    out_swap = swap(7, out_held, out_other)
    small_swap = swap(11, small, small_other)
    heads_swap = swap(12, heads, heads_other)
    widths = (128, PAIR, D, UP_CHUNK, DOWN_CHUNK, 128)
    chunks = [[] for _ in range(6)]
    targets = results + [heads_sum]

    def collect(index, start, width, flip=False, layer=None, stages=(0, 2), count=Collect.COUNT):
        nonlocal base
        made = Collect(place, held[index], slots[index], targets[index], start, width, flip, sems,
                       base, layer, stages)
        base += count
        return made

    groups = [[collect(4, 0, D, layer=z, stages=(0, 1), count=4)] for z in range(4)]
    groups += [[collect(4, 0, D, stages=(2, 2), count=3)]]
    for index in (3, 2, 1):
        for start in range(0, held[index].shape[4], widths[index]):
            groups.append([collect(index, start, widths[index], index == 1 and start == PAIR)])
    groups[8].append(collect(0, 0, 128))
    groups.append([collect(5, 0, 128)])
    norm_sums[...] = norm_given[...]
    loaded["branch"].wait()
    meet_all()

    def down_tile_of(index):
        act_load(index).wait()
        value = dot(act[index % 2], wide[...]).reshape(2, 2, tile_rows // 4, D)

        @pl.when(index < 6)
        def _():
            act_load(index + 2).start()

        return value

    @pl.loop(0, 4)
    def _(layer):
        down_held[layer] = down_tile_of(layer).astype(BF)
        down_swap(layer).start()

    load("hidden", hidden_any, flip)
    for index in range(2):
        for copy in chunk_loads(index):
            copy.start()
    load("two", two_any, two)
    load("normed", normed_any, one)
    load("context", context_any, context)
    load("flip", flip_any, flip_context)
    load("scale", scale_any, scale_one)
    load("out", out_any, w_out)

    @pl.loop(0, 4)
    def _(layer):
        value = down_tile_of(layer + 4)
        down_swap(layer).wait()
        down_held[layer] = (value + down_other[layer].astype(F32)).astype(BF)
        for at, moves in ((0, ((0, 0),)), (2, ((1, 0),))):
            @pl.when(layer == at)
            def _():
                advance(groups, *moves)

    loaded["hidden"].wait()
    loaded["two"].wait()

    def feed_back(index):
        for copy in chunk_loads(index):
            copy.wait()
        core = jnp.where(index < 3, theirs, mine)
        whole = pl.ds(
            pl.multiple_of(core * (FF // 2) + index % 3 * UP_CHUNK, UP_CHUNK), UP_CHUNK)
        value = dot_last(wide[...], down_tile(index)[...])
        value = (value * slope_tile(index)[...].astype(F32)).astype(BF)
        inner[...] = value
        ffn_sums[:, whole] = jnp.sum(value.astype(F32), axis=0, keepdims=True)
        two[...] += dot_last(inner[...], up_tile(index)[...])
        return dot(flip[...], inner[...]).reshape(4, 2, 2, D // 16, UP_CHUNK)

    @pl.loop(0, 3)
    def _(third):
        cols = pl.ds(pl.multiple_of(third * UP_CHUNK, UP_CHUNK), UP_CHUNK)
        up_held[:, :, :, :, cols] = feed_back(third).astype(BF)
        up_swap(third).start()
        for copy in chunk_loads(third + 2):
            copy.start()

        for at, moves in (
            (0, ((2, 0),)),
            (1, ((0, 1), (3, 0))),
            (2, ((1, 1),)),
        ):
            @pl.when(third == at)
            def _():
                advance(groups, *moves)

    @pl.loop(0, 3)
    def _(third):
        at = (EVERY, EVERY, EVERY, EVERY,
              pl.ds(pl.multiple_of(third * UP_CHUNK, UP_CHUNK), UP_CHUNK))
        value = feed_back(third + 3)
        up_swap(third).wait()
        up_held[at] = (value + up_other[at].astype(F32)).astype(BF)

        @pl.when(third == 0)
        def _():
            for copy in chunk_loads(5):
                copy.start()

        for spot, moves in (
            (0, ((0, 2), (2, 1), (5, 0))),
            (1, ((3, 1),)),
            (2, ((1, 2), (2, 2), (6, 0))),
        ):
            @pl.when(third == spot)
            def _():
                advance(groups, *moves)

    def probs_load(item):
        pair, row = item // 4, item % 2
        core = jnp.where(item % 4 < 2, theirs, mine)
        return pltpu.make_async_copy(
            probs_any.at[pair * 4 + row * 2 + core], probs.at[item % 2], local.at[24 + item % 2])

    for item in range(2):
        probs_load(item).start()
    load("token", token_any, flip)
    load("qkv", qkv_any, qkv)
    load("weight", weight_any, weight)
    loaded["normed"].wait()
    for name in ("context", "scale", "out"):
        loaded[name].wait()
    for row in range(2):
        rows = slice(row * LEN, (row + 1) * LEN)
        back, gain, shift = norm_back(
            two[rows, :], one[rows, :], scale_one[rows, 0:1], norm[2:3, :])
        norm_sums[2:3, :] += gain
        norm_sums[3:4, :] += shift
        one[rows, :] = back
        back = back.astype(BF)
        attended[rows, :] = back
        norm_sums[0:1, :] += jnp.sum(back.astype(F32), axis=0, keepdims=True)
        back = dot_last(back, w_out[...]).astype(BF)
        wide[rows, :] = back
        product = back.astype(F32) * context[rows, :].astype(F32)
        high = product.astype(BF)
        low = (product - high.astype(F32)).astype(BF)
        head = lax.broadcasted_iota(jnp.int32, (16, D), 0)
        member = (lax.broadcasted_iota(jnp.int32, (16, D), 1) // HD == head).astype(F32).astype(BF)
        delta[row] = dot_last(member, high) + dot_last(member, low)
    loaded["flip"].wait()
    advance(groups, (5, 1))
    spare = out_held.shape[3] - D // 32

    def out_half(core):
        rows = pl.ds(pl.multiple_of(core * HALF, HALF), HALF)
        value = dot(flip_context[rows, :], attended[...]).reshape(16, D // 32, D)
        value = jnp.concatenate([value, jnp.zeros((16, spare, D), F32)], axis=1)
        return value.reshape(4, 2, 2, D // 32 + spare, D)

    out_held[...] = out_half(theirs).astype(BF)
    out_swap.start()
    pack_small(small, theirs, norm_sums, ffn_sums)
    small_swap.start()
    advance(groups, (3, 2), (4, 2))

    def out_mine():
        value = out_half(mine)
        out_swap.wait()
        out_held[...] = (value + out_other[...].astype(F32)).astype(BF)
        small_swap.wait()
        pack_small(small, mine, norm_sums, ffn_sums)
        small[...] += small_other[...]

    grad_head[...] = jnp.zeros(grad_head.shape, F32)
    for name in ("qkv", "token"):
        loaded[name].wait()

    def qkv_theirs(pair):
        cols = pl.ds(pl.multiple_of(pair * PAIR, PAIR), PAIR)
        value = dot(flip[...], qkv[pair, :, place_of(theirs, 0, PAIR)])
        qkv_held[:, :, :, :, cols] = value.reshape(4, 2, 2, D // 16, PAIR).astype(BF)
        qkv_swap(pair).start()

    def qkv_mine(pair):
        cols = pl.ds(pl.multiple_of(pair * PAIR, PAIR), PAIR)
        at = (EVERY, EVERY, EVERY, EVERY, cols)
        value = dot(flip[...], qkv[pair, :, place_of(mine, 0, PAIR)]).reshape(4, 2, 2, D // 16, PAIR)
        qkv_swap(pair).wait()
        qkv_held[at] = (value + qkv_other[at].astype(F32)).astype(BF)

    @pl.loop(0, 12)
    def _(item):
        pair, row = item // 4, item % 2
        core = jnp.where(item % 4 < 2, theirs, mine)

        @pl.when(item == 2)
        def _():
            out_mine()

        @pl.when(item % 4 == 2)
        def _():
            qkv_theirs(pair)

        @pl.when((item == 5) | (item == 9))
        def _():
            qkv_mine(pair - 1)

        for at, moves in (
            (1, ((7, 0),)),
            (2, ((5, 2), (6, 1))),
            (3, ((8, 0),)),
            (5, ((7, 1),)),
            (6, ((6, 2),)),
            (7, ((9, 0),)),
            (8, ((4, 3), (8, 1))),
            (10, ((5, 3), (7, 2), (10, 0))),
            (11, ((9, 1),)),
        ):
            @pl.when(item == at)
            def _():
                advance(groups, *moves)

        probs_load(item).wait()
        attend_back_pair(qkv, wide, probs.at[item % 2], delta, grad_head, core, row, pair)

        @pl.when(item < 10)
        def _():
            probs_load(item + 2).start()

    loaded["weight"].wait()

    def input_rows(row):
        rows = pl.ds(pl.multiple_of(row * LEN, LEN), LEN)
        one[rows, :] += (dot_last(qkv[0, rows, :], weight[0]) + dot_last(qkv[1, rows, :], weight[1])
                         + dot_last(qkv[2, rows, :], weight[2]))

    qkv_mine(2)
    advance(groups, (6, 3), (8, 2), (11, 0))
    heads[...] = pack_heads(theirs, grad_head)
    heads_swap.start()
    input_rows(0)
    input_rows(1)
    heads_swap.wait()
    heads[...] = pack_heads(mine, grad_head) + heads_other[...]
    advance(groups, (12, 0))
    input_done = pltpu.make_async_copy(one, input_any, local.at[12])
    input_done.start()
    advance(groups, (7, 3), (9, 2), (10, 1), (11, 1), (8, 3), (10, 2), (12, 1))
    small_sum, grads = results[0], results[1:]
    lines[...] = jnp.zeros(lines.shape, F32)

    def put_sums(index):
        grad = grads[index][...]
        square = grad * grad + EPS_SQUARE
        put_line(lines, COL_LINES[index], jnp.sum(square, axis=0, keepdims=True))
        if index in (0, 2):
            line = UP_ROWS if index else QKV_ROWS
            lines[line:line + 1, 0:grad.shape[0]] = to_row(jnp.sum(square, axis=1, keepdims=True))

    def ratio_of(index):
        (row,), (col,) = new_rows_cols(grads, rows_old, cols_old, lines, (index,))
        grad = grads[index][...]
        scaled = jnp.sum(grad * grad * (1.0 / col), axis=1, keepdims=True)
        share = 0.5 if index in (0, 2) else 1.0
        return (jnp.sum(scaled / row, axis=0, keepdims=True),
                jnp.sum(row, axis=0, keepdims=True) * share)

    for index in (1, 2, 3):
        put_sums(index)
    early = Exchange(place, mine_early, plane_early, line_early, sems, base)
    late = Broadcast(mine_one, land_one, sems, base + Exchange.COUNT, True)
    second = Broadcast(mine_two, land_two, sems, base + Exchange.COUNT + 1, False)
    value = lines[LATE:, :]
    early.start_plane(value)
    advance(groups, (9, 3), (11, 2), (12, 2))
    line = lax.broadcasted_iota(jnp.int32, value.shape, 0) + LATE
    same, cross = early.end_plane()
    paired = value + plane_early[theirs, place.y, place.x]
    early.start_line(jnp.where((line >= OUT_LINE) & (line < UP_ROWS), same + cross, same))
    advance(groups, (10, 3))
    lines[LATE:, :] = jnp.where(line >= UP_ROWS, paired, early.end_line())
    sums = {index: ratio_of(index) for index in (1, 2, 3)}
    place_small(old_small, norm_sq[...], head_sq[...], as_row(ffn_sq), 1.0)
    advance(groups, (11, 3), (12, 3))
    put_sums(0)
    value = lines[0:LATE, :]
    late.start(value)
    small_sum[6:8, :] = heads_sum[0:2, :]
    _, update = small_update(small_sum[...], old_small[...])
    others = small_sums(update)
    line = lax.broadcasted_iota(jnp.int32, value.shape, 0)
    late.end()
    paired = value + land_one[lax.axis_index("dp") * 2 + theirs]
    total = sum(land_one[2 * number + mine] for number in range(16))
    lines[0:LATE, :] = jnp.where(line >= QKV_ROWS, paired, total)
    sums[0] = ratio_of(0)
    second.start((
        scalars([sums[index][0] for index in range(4)] + [sums[index][1] for index in range(4)]
                + others) + weight_sums[...])[0:1])
    second.end()
    totals[...] = jnp.broadcast_to(jnp.sum(land_two[...], axis=0), totals.shape)
    input_done.wait()
    for group in groups:
        for chunk in group:
            chunk.finish()
    for exchange in (early, late, second):
        exchange.finish()


def backward_scatter(norm_sums, norm, rows_old, cols_old, squares,
                     weight_sums, large, rows, widths):
    count = large[1].shape[0]
    shape = jax.ShapeDtypeStruct
    some = pl.BlockSpec(memory_space=pl.ANY)
    kinds = [F32, BF, BF, BF, BF, F32]
    padded = [16, rows[1], 32, rows[3], rows[4], 8]
    wide = widths + [128]
    held = [pltpu.VMEM((4, 2, 2, r, w), k) for r, w, k in zip(padded, wide, kinds)]
    slots = []
    for r, w, k in zip(padded, wide, kinds):
        slots += [pltpu.VMEM((4, 2, r, w), k), pltpu.VMEM((4, r, w), k), pltpu.VMEM((3, r, w), k)]
    sems = 13 + 19 + 9 * Collect.COUNT + Exchange.COUNT + 2
    outs = [shape((r, w), F32) for r, w in zip(rows, widths)]
    outs += [shape((LINES, 128), F32), shape((8, 128), F32), shape((count, D), F32)]
    small = [norm_sums, norm, *rows_old, *cols_old, *squares, weight_sums]
    return pl.pallas_call(
        backward_scatter_kernel,
        out_shape=outs,
        in_specs=[VMEM] * len(small) + [some] * len(large),
        out_specs=[VMEM] * 7 + [some],
        scratch_shapes=held + held + slots + [
            pltpu.VMEM((8, 128), F32),
            pltpu.VMEM((count, D), BF),
            pltpu.VMEM((D, count), BF),
            pltpu.VMEM((D, count), BF),
            pltpu.VMEM((count, D), BF),
            pltpu.VMEM((count, D), BF),
            pltpu.VMEM((3, count, D), BF),
            pltpu.VMEM((3, D, D), BF),
            pltpu.VMEM((count, D), F32),
            pltpu.VMEM((count, D), F32),
            pltpu.VMEM((2, FF // 8, count), BF),
            pltpu.VMEM((count, UP_CHUNK), BF),
            pltpu.VMEM((2, 2, LEN, LEN), BF),
            pltpu.VMEM((2, 16, LEN), F32),
            pltpu.VMEM((8, D), F32),
            pltpu.VMEM((8, D), F32),
            pltpu.VMEM((1, FF), F32),
            pltpu.VMEM((count, 128), F32),
            pltpu.VMEM((D, D), BF),
        ] + [
            pltpu.VMEM(lead + (count, 128), F32)
            for count in (LINES - LATE,) for lead in ((2,), (2, 2, 2), (4,))
        ] + [
            pltpu.VMEM((LATE, 128), F32),
            pltpu.VMEM((32, LATE, 128), F32),
            pltpu.VMEM((1, 128), F32),
            pltpu.VMEM((32, 1, 128), F32),
            pltpu.VMEM((16, 128), F32),
            pltpu.SemaphoreType.DMA((sems,)),
            pltpu.SemaphoreType.DMA((sems,)),
            pltpu.SemaphoreType.DMA((26,)),
        ],
        compiler_params=pltpu.CompilerParams(
            collective_id=1, has_side_effects=True, vmem_limit_bytes=62 << 20),
        name="backward_scatter",
    )(*small, *large)


def small_block(norm, head, ffn):
    wide = lambda v: jnp.pad(v, [(0, 0)] * (v.ndim - 1) + [(0, 128 - v.shape[-1])])
    block = jnp.concatenate([wide(norm), wide(head), wide(ffn)], axis=-2)
    return jnp.pad(block, [(0, 0)] * (block.ndim - 2) + [(0, 16 - block.shape[-2]), (0, 0)])


def pair_major(weight):
    count = weight.shape[0]
    return weight.reshape(count, 3, 3, 128).transpose(0, 2, 1, 3).reshape(count, QKV_HALF)


def gather_plain(weights, vectors):
    head, ffn, norm = vectors
    qkv, out, up, down = (w.astype(BF) for w in weights)
    full = []
    for shard in (small_block(norm, head, ffn), pair_major(qkv), out, up, down):
        full.append(lax.all_gather(lax.all_gather(shard, "dp", axis=0), "mp", axis=0))
    return full


def scatter_plain(fulls):
    out = []
    for full in fulls:
        own = lax.psum_scatter(full.astype(F32), "mp", scatter_dimension=0)
        out.append(lax.psum_scatter(own, "dp", scatter_dimension=0))
    return out


def body(
    tokens, cotangent, seg_lengths, w_qkv, w_out, w_up, w_down, head_bias, ffn_bias, norm_bias,
    qkv_rows, qkv_cols, out_rows, out_cols, up_rows, up_cols, down_rows, down_cols,
    head_bias_sq, ffn_bias_sq, norm_sq,
):
    cores = lax.axis_size("mp")
    data = lax.axis_size("dp")
    rows_qkv = w_qkv.shape[0]
    fast = data == 16 and cores == 2
    weights = [w_qkv.transpose(1, 0, 2) if fast else w_qkv, w_out, w_up, w_down]
    vectors = [head_bias, ffn_bias if fast else ffn_bias.reshape(1, -1), norm_bias]
    rows_out = w_out.shape[0]
    if fast:
        (weight_sums, norm_full, ffn_full, scale_one, out_full, pooled, norm_sums, qkv_full,
         up_full, down_full, qkv, context_flip, token_flip, hidden_flip, normed_one, context,
         act_flip, slope, layer_out, grad_branch, grad_two, probs
         ) = forward_gather(weights, vectors, seg_lengths, tokens, cotangent)
        rows_old = [qkv_rows, out_rows, up_rows, down_rows]
        cols_old = [qkv_cols, out_cols, up_cols, down_cols]
        old = [head_bias_sq, ffn_bias_sq, norm_sq]
        *reduced, lines, totals, input_grad = backward_scatter(
            norm_sums, norm_full, rows_old, cols_old, old, weight_sums,
            [act_flip, grad_branch, down_full.reshape(FF, D), slope,
             up_full.reshape(2, D, FF // 2), grad_two, normed_one, hidden_flip, context,
             context_flip, token_flip, qkv, qkv_full.reshape(3, D, D), probs,
             scale_one, out_full],
            [16, rows_qkv, rows_out, rows_qkv, w_down.shape[0]],
            [128, QKV_HALF, D, w_up.shape[1], D])
        new = step(reduced, lines, totals, weights, rows_old, cols_old, vectors, old,
                   [layer_out, pooled, input_grad])
        new = list(new)
        grads, small_grads, rows_new, cols_new = new[:4], new[4:7], new[7:11], new[11:15]
        seconds, mats, fresh, passed = new[15:18], new[18:22], new[22:25], new[25:]
        grads[0], mats[0] = grads[0].transpose(1, 0, 2), mats[0].transpose(1, 0, 2)
        stats = [v for pair in zip(rows_new, cols_new) for v in pair]
        return (*passed, *grads, *small_grads, *stats, *seconds, *mats, *fresh)
    small, qkv_g, out_g, up_g, down_g = gather_plain(weights, vectors)
    small = small.astype(BF).astype(F32)
    own_head, own_ffn, own_norm = head_bias.shape[1], ffn_bias.shape[0], norm_bias.shape[1]
    norm_full = small[:, :, 0:6, :own_norm].transpose(2, 1, 0, 3).reshape(6, D)
    head_full = small[:, :, 6:8, :own_head].transpose(2, 0, 1, 3).reshape(2, 2, 3, 1, 128)
    ffn_full = small[:, :, 8, :own_ffn].reshape(1, FF)
    offsets = jnp.concatenate([head_full[0], jnp.zeros_like(head_full[0]), head_full[1]], axis=2)
    offsets = offsets.reshape(2, 1, QKV_HALF)
    qkv_full = qkv_g.reshape(2, D, QKV_HALF)
    up_full = up_g.reshape(2, D, FF // 2)
    down_full = down_g.reshape(FF, D)
    out_full = out_g.reshape(D, D)
    norm_full = jnp.pad(norm_full, ((0, 2), (0, 0)))
    qkv, context, lse = forward(tokens, qkv_full, offsets, seg_lengths)
    (layer_out, pooled, hidden_b, act, grad_branch, grad_inner, grad_attended, grad_context,
     grad_one, delta, norm_sums, ffn_sums) = middle_call(
        tokens, context, cotangent, seg_lengths, out_full, up_full, down_full, ffn_full,
        norm_full)
    grad_out, grad_up, grad_down = weight_grads(
        context.T, hidden_b.T, act.T, grad_branch, grad_inner, grad_attended,
        cores * data, rows_out)
    token_flip = tokens.T
    grad_qkv, input_grad, grad_head = backward(
        token_flip, qkv, grad_context, lse, delta, seg_lengths, qkv_full, grad_one)
    small_grads = small_block(
        norm_sums[:6].reshape(6, data, cores, -1).transpose(2, 1, 0, 3),
        grad_head.reshape(2, cores, data, -1).transpose(1, 2, 0, 3),
        ffn_sums.reshape(cores, data, 1, -1),
    )
    fulls = [
        small_grads,
        grad_qkv.reshape(cores, data, rows_qkv, QKV_HALF),
        grad_out.reshape(cores, data, rows_out, D),
        grad_up.reshape(cores, data, rows_qkv, FF // 2),
        grad_down.reshape(cores, data, -1, D),
    ]
    red_small, red_qkv, red_out, red_up, red_down = scatter_plain(fulls)
    norm_grad = red_small[0:6, :own_norm]
    red_qkv = pair_major(red_qkv)
    red_head = red_small[6:8, :own_head]
    red_ffn = red_small[8, :own_ffn]
    weights_flat = [w_qkv.reshape(rows_qkv, -1), w_out, w_up, w_down]
    grads_flat = [red_qkv, red_out, red_up, red_down]
    rows_old = [qkv_rows, out_rows, up_rows, down_rows]
    cols_old = [qkv_cols.reshape(-1), out_cols, up_cols, down_cols]
    col_count = [3 * D, D, FF, D]
    row_count = [D, D, D, FF]
    row_share = [cores, 1, cores, 1]
    squares = [grad * grad + EPS_SQUARE for grad in grads_flat]
    row_parts = [jnp.sum(square, axis=1) for square in squares]
    col_parts = [jnp.sum(square, axis=0) for square in squares]
    vec_weights = [head_bias, ffn_bias, norm_bias]
    vec_grads = [red_head, red_ffn, norm_grad]
    vec_old = [head_bias_sq, ffn_bias_sq, norm_sq]
    vec_counts = [2 * D, FF, 6 * D]
    vec_second = [
        DECAY * old + (1.0 - DECAY) * (grad * grad + EPS_SQUARE)
        for old, grad in zip(vec_old, vec_grads)
    ]
    vec_update = [grad * lax.rsqrt(second) for grad, second in zip(vec_grads, vec_second)]
    weight_parts = [jnp.sum(weight * weight) for weight in weights_flat + vec_weights]
    vec_parts = [jnp.sum(update * update) for update in vec_update]
    row_qkv, row_up = lax.psum((row_parts[0], row_parts[2]), "mp")
    col_qkv, col_up = lax.psum((col_parts[0], col_parts[2]), "dp")
    col_out, col_down = lax.psum((col_parts[1], col_parts[3]), ("dp", "mp"))
    row_sums = [row_qkv, row_parts[1], row_up, row_parts[3]]
    col_sums = [col_qkv, col_out, col_up, col_down]
    rows_new = [
        DECAY * rows_old[index] + (1.0 - DECAY) * row_sums[index] / col_count[index]
        for index in range(4)
    ]
    cols_new = [
        DECAY * cols_old[index] + (1.0 - DECAY) * col_sums[index] / row_count[index]
        for index in range(4)
    ]
    ratio_parts = [
        jnp.sum(
            grads_flat[index]
            * grads_flat[index]
            / (rows_new[index][:, None] * cols_new[index][None, :])
        )
        for index in range(4)
    ]
    extra_parts = (
        [jnp.sum(rows_new[index]) / row_share[index] for index in range(4)]
        + weight_parts
        + vec_parts
    )
    totals = lax.psum(jnp.stack(ratio_parts + extra_parts), ("dp", "mp"))
    row_means = [totals[4 + index] / row_count[index] for index in range(4)]
    weight_totals = [totals[8 + index] for index in range(7)]
    vec_totals = [totals[15 + index] for index in range(3)]
    new_mats = []
    for index in range(4):
        entries = row_count[index] * col_count[index]
        estimate = rows_new[index][:, None] * cols_new[index][None, :] / row_means[index]
        update = grads_flat[index] / jnp.sqrt(estimate)
        update_rms = jnp.sqrt(row_means[index] * totals[index] / entries)
        stride = (
            RATE * jnp.sqrt(weight_totals[index] / entries) / jnp.maximum(1.0, update_rms / CLIP)
        )
        new_mats.append(weights_flat[index] - stride * update)
    new_vecs = []
    for index in range(3):
        update_rms = jnp.sqrt(vec_totals[index] / vec_counts[index])
        stride = (
            RATE
            * jnp.sqrt(weight_totals[4 + index] / vec_counts[index])
            / jnp.maximum(1.0, update_rms / CLIP)
        )
        new_vecs.append(vec_weights[index] - stride * vec_update[index])
    return (
        layer_out,
        pooled,
        input_grad,
        red_qkv.reshape(w_qkv.shape),
        red_out,
        red_up,
        red_down,
        red_head,
        red_ffn,
        norm_grad,
        rows_new[0],
        cols_new[0].reshape(qkv_cols.shape),
        rows_new[1],
        cols_new[1],
        rows_new[2],
        cols_new[2],
        rows_new[3],
        cols_new[3],
        vec_second[0],
        vec_second[1],
        vec_second[2],
        new_mats[0].reshape(w_qkv.shape),
        new_mats[1],
        new_mats[2],
        new_mats[3],
        new_vecs[0],
        new_vecs[1],
        new_vecs[2],
    )


def solution(mesh):
    return jax.shard_map(
        body,
        mesh=mesh,
        in_specs=(
            P(("dp", "mp"), None),
            P(("dp", "mp"), None),
            P("dp", None),
            P("dp", None, "mp"),
            P(("mp", "dp"), None),
            P("dp", "mp"),
            P(("mp", "dp"), None),
            P(None, ("mp", "dp")),
            P(("mp", "dp")),
            P(None, ("dp", "mp")),
            P("dp"),
            P(None, "mp"),
            P(("mp", "dp")),
            P(),
            P("dp"),
            P("mp"),
            P(("mp", "dp")),
            P(),
            P(None, ("mp", "dp")),
            P(("mp", "dp")),
            P(None, ("dp", "mp")),
        ),
        out_specs=(
            P(("dp", "mp"), None),
            P(("dp", "mp"), None, None),
            P(("dp", "mp"), None),
            P("dp", None, "mp"),
            P(("mp", "dp"), None),
            P("dp", "mp"),
            P(("mp", "dp"), None),
            P(None, ("mp", "dp")),
            P(("mp", "dp")),
            P(None, ("dp", "mp")),
            P("dp"),
            P(None, "mp"),
            P(("mp", "dp")),
            P(),
            P("dp"),
            P("mp"),
            P(("mp", "dp")),
            P(),
            P(None, ("mp", "dp")),
            P(("mp", "dp")),
            P(None, ("dp", "mp")),
            P("dp", None, "mp"),
            P(("mp", "dp"), None),
            P("dp", "mp"),
            P(("mp", "dp"), None),
            P(None, ("mp", "dp")),
            P(("mp", "dp")),
            P(None, ("dp", "mp")),
        ),
        check_vma=False,
    )
```
